32 devices in a mesh: dp: 16 (over z, x, core), mp: 2 (over y).
Axes of the slice: x: 2, y: 2, z: 4, core: 2. Of those that a mesh axis runs over, the one named last changes fastest.
Arguments:
- tokens: bfloat16 [16384, 1024], P(('dp', 'mp')), may hold values from -6 to 6
- memory: bfloat16 [65536, 1024], P(('dp', 'mp')), may hold values from -6 to 6
- cotangent: bfloat16 [16384, 1024], P(('dp', 'mp')), may hold values from -6 to 6
- target_lengths: int32 [64], P('dp'), may hold values from 1 to 256, as said below
- memory_lengths: int32 [64], P('dp'), may hold values from 40 to 1024, as said below
- norm_self: bfloat16 [1024], replicated, may hold values from 0.099609375 to 1.8984375
- query_self: bfloat16 [1024, 1024], P(None, 'mp'), may hold values from -0.046875 to 0.046875
- key_self: bfloat16 [1024, 1024], P(None, 'mp'), may hold values from -0.1875 to 0.1875
- value_self: bfloat16 [1024, 1024], P(None, 'mp'), may hold values from -0.1875 to 0.1875
- out_self: bfloat16 [1024, 1024], P('mp'), may hold values from -0.75 to 0.75
- bias_table: bfloat16 [32, 16], P(None, 'mp'), may hold values from -4 to 4
- norm_cross: bfloat16 [1024], replicated, may hold values from 0.099609375 to 1.8984375
- query_cross: bfloat16 [1024, 1024], P(None, 'mp'), may hold values from -0.046875 to 0.046875
- key_cross: bfloat16 [1024, 1024], P(None, 'mp'), may hold values from -0.1875 to 0.1875
- value_cross: bfloat16 [1024, 1024], P(None, 'mp'), may hold values from -0.1875 to 0.1875
- out_cross: bfloat16 [1024, 1024], P('mp'), may hold values from -1 to 1
- norm_ffn: bfloat16 [1024], replicated, may hold values from 0.099609375 to 1.8984375
- ffn_in: bfloat16 [1024, 4096], P(None, 'mp'), may hold values from -0.1875 to 0.1875
- ffn_out: bfloat16 [4096, 1024], P('mp'), may hold values from -0.09375 to 0.09375
Outputs:
- block_out: bfloat16 [16384, 1024], P(('dp', 'mp'))
- tokens_grad: bfloat16 [16384, 1024], P(('dp', 'mp'))
- memory_grad: bfloat16 [65536, 1024], P(('dp', 'mp'))
- norm_self_grad: float32 [1024], replicated
- query_self_grad: float32 [1024, 1024], P(None, 'mp')
- key_self_grad: float32 [1024, 1024], P(None, 'mp')
- value_self_grad: float32 [1024, 1024], P(None, 'mp')
- out_self_grad: float32 [1024, 1024], P('mp')
- bias_table_grad: float32 [32, 16], P(None, 'mp')
- norm_cross_grad: float32 [1024], replicated
- query_cross_grad: float32 [1024, 1024], P(None, 'mp')
- key_cross_grad: float32 [1024, 1024], P(None, 'mp')
- value_cross_grad: float32 [1024, 1024], P(None, 'mp')
- out_cross_grad: float32 [1024, 1024], P('mp')
- norm_ffn_grad: float32 [1024], replicated
- ffn_in_grad: float32 [1024, 4096], P(None, 'mp')
- ffn_out_grad: float32 [4096, 1024], P('mp')
The draws below stay inside these ranges and needn't reach their ends.
Inputs may be any that keep to these rules, and one draw needn't show every extreme that they name: `target_lengths`: in every group of 4 consecutive examples one example has target length 256. `memory_lengths`: the example of each group that has target length 256 has memory length 1024.
All inputs are finite; a program needn't handle non-finite values.
Results may differ from the reference program's by a relative error of at most 0.024.
The reference program's roundings to bfloat16 on the way count: a program that leaves them out, or rounds other values in their place, can miss the bound.
Values may be sent and summed in bfloat16 or wider, within the bound.
A program may use at most 384 MiB of HBM per device.

```python
import math
import jax
import jax.numpy as jnp
import numpy as np
from jax import lax

D = 1024
HEADS = 16
HEAD_DIM = 64
FF = 4096
BUCKETS = 32
TGT = 256
MEM = 1024
EX = 4
INNER = 1024
EXAMPLES = 64
TOKENS = 16384
MEMORY_ROWS = 65536


def full_slot(key):
    groups = EXAMPLES // EX
    return jax.random.randint(key, (groups,), 0, EX)


def draw_target_lengths(key, part):
    chosen = full_slot(key)
    key = jax.random.fold_in(key, 11)
    groups = EXAMPLES // EX
    level = jnp.arange(groups, dtype=jnp.int32)
    upper = jnp.maximum(TGT * (level + 1) // groups, 2)
    lower = jnp.maximum(upper // 2, 1)
    noise = jax.random.randint(key, (groups, EX), 0, 1 << 20)
    lengths = lower[:, None] + noise % (upper - lower + 1)[:, None]
    slots = jnp.arange(EX, dtype=jnp.int32)[None, :]
    lengths = jnp.where(slots == chosen[:, None], TGT, lengths)
    return lengths.reshape(EXAMPLES).astype(jnp.int32)


def draw_memory_lengths(key, part):
    chosen = full_slot(key)
    key = jax.random.fold_in(key, 23)
    groups = EXAMPLES // EX
    lower = max(1, MEM // 25)
    span = MEM - lower
    first_key, second_key = jax.random.split(key)
    first = jax.random.randint(first_key, (groups, EX), 0, span + 1)
    second = jax.random.randint(second_key, (groups, EX), span // 2, span + 1)
    lengths = lower + first * second // max(span, 1)
    slots = jnp.arange(EX, dtype=jnp.int32)[None, :]
    lengths = jnp.where(slots == chosen[:, None], MEM, lengths)
    return lengths.reshape(EXAMPLES).astype(jnp.int32)


def level_of(key, dims, pieces, least, high):
    loudness = 1.0
    for position, parts in pieces:
        heights = jax.random.uniform(jax.random.fold_in(jax.random.fold_in(key, 6), position), (parts,), jnp.float32, least / len(pieces), high / len(pieces))
        loudness = loudness * jnp.repeat(jnp.exp(heights), dims[position] // parts).reshape((-1,) + (1,) * (len(dims) - 1 - position))
    return loudness


def bell_draw(key, extent, deviation, bound, shards=(), kind=jnp.bfloat16):
    drawn = deviation * jax.random.normal(key, extent, jnp.float32)
    if shards:
        drawn = drawn * level_of(key, extent, shards, -0.22, 0.18)
    return jnp.clip(drawn, -bound, bound).astype(kind)


def setup_inputs(seed: int = 0) -> dict:
    splits = jax.random.split(jax.random.key(seed), 20)
    return {
        "tokens": bell_draw(splits[0], (TOKENS, D), 1.0, 6.0, ((0, 32),)),
        "memory": bell_draw(splits[1], (MEMORY_ROWS, D), 1.0, 6.0, ((0, 32),)),
        "cotangent": bell_draw(splits[2], (TOKENS, D), 1.0, 6.0, ((0, 32),)),
        "target_lengths": draw_target_lengths(jax.random.fold_in(splits[19], 71), 0),
        "memory_lengths": draw_memory_lengths(jax.random.fold_in(splits[19], 71), 0),
        "norm_self": jnp.clip(1.0 + 0.18 * jax.random.normal(splits[5], (D,), jnp.float32), 0.099609375, 1.8984375).astype(jnp.bfloat16),
        "query_self": bell_draw(splits[6], (D, INNER), (16 * D) ** -0.5, 0.046875, ((1, 2),)),
        "key_self": bell_draw(splits[7], (D, INNER), D ** -0.5, 0.1875, ((1, 2),)),
        "value_self": bell_draw(splits[8], (D, INNER), D ** -0.5, 0.1875, ((1, 2),)),
        "out_self": bell_draw(splits[9], (INNER, D), (INNER // 16) ** -0.5, 0.75, ((0, 2),)),
        "bias_table": bell_draw(splits[10], (BUCKETS, HEADS), 1.0, 4.0, ((1, 2),)),
        "norm_cross": jnp.clip(1.0 + 0.18 * jax.random.normal(splits[11], (D,), jnp.float32), 0.099609375, 1.8984375).astype(jnp.bfloat16),
        "query_cross": bell_draw(splits[12], (D, INNER), (16 * D) ** -0.5, 0.046875, ((1, 2),)),
        "key_cross": bell_draw(splits[13], (D, INNER), D ** -0.5, 0.1875, ((1, 2),)),
        "value_cross": bell_draw(splits[14], (D, INNER), D ** -0.5, 0.1875, ((1, 2),)),
        "out_cross": bell_draw(splits[15], (INNER, D), (INNER // 32) ** -0.5, 1.0, ((0, 2),)),
        "norm_ffn": jnp.clip(1.0 + 0.18 * jax.random.normal(splits[16], (D,), jnp.float32), 0.099609375, 1.8984375).astype(jnp.bfloat16),
        "ffn_in": bell_draw(splits[17], (D, FF), D ** -0.5, 0.1875, ((1, 2),)),
        "ffn_out": bell_draw(splits[18], (FF, D), FF ** -0.5, 0.09375, ((0, 2),)),
    }


@jax.custom_vjp
def low(v):
    return lax.optimization_barrier(v.astype(jnp.bfloat16)).astype(jnp.float32)

@jax.custom_vjp
def low_back(v):
    return v

def low_keep(v):
    return (low(v), None)

def low_pass(kept, grad):
    return (grad,)

def back_keep(v):
    return (v, None)

def back_low(kept, grad):
    return (low(grad),)
low.defvjp(low_keep, low_pass)
low_back.defvjp(back_keep, back_low)
epsilon = 1e-06
masked_score = -1e+30
highest = lax.Precision.HIGHEST

def bucket_edges():
    exact = list(range(1, 17))
    spaced = [int(math.ceil(16.0 * 8.0 ** ((level - 16) / 16.0))) for level in range(17, 32)]
    return np.array(exact + spaced, dtype=np.int32)

def rms_norm(value, gain):
    factor = lax.rsqrt(lax.optimization_barrier(jnp.mean(value * value, axis=-1, keepdims=True)) + epsilon)
    return value * factor * gain

def project(value, weight):
    return jnp.dot(value, weight, precision=highest)

def rounded_both(value):
    return low_back(low(value))

def attend(query, key_rows, value_rows, score_bias, mask):
    scores = jnp.einsum('pehd,kehd->ehpk', query, key_rows, precision=highest)
    if score_bias is not None:
        scores = scores + score_bias[None]
    scores = low_back(jnp.where(mask, scores, masked_score))
    row_max = lax.optimization_barrier(jnp.max(scores, axis=-1, keepdims=True))
    weights = jnp.exp(scores - row_max)
    probs = low(weights / lax.optimization_barrier(jnp.sum(weights, axis=-1, keepdims=True)))
    return jnp.einsum('ehpk,kehd->pehd', probs, value_rows, precision=highest)

def layer(tokens, memory, weights, target_len, memory_len):
    norm_self, query_self, key_self, value_self, out_self, bias_table, norm_cross, query_cross, key_cross, value_cross, out_cross, norm_ffn, ffn_in, ffn_out = weights

    def heads_view(value, length):
        return value.reshape(length, EX, HEADS, HEAD_DIM)
    target_pos = jnp.arange(TGT, dtype=jnp.int32)
    distance = jnp.maximum(target_pos[:, None] - target_pos[None, :], 0)
    buckets = lax.optimization_barrier(jnp.sum((distance[:, :, None] >= jnp.asarray(bucket_edges())[None, None, :]).astype(jnp.int32), axis=-1))
    score_bias = jnp.transpose(bias_table[buckets], (2, 0, 1))
    causal = target_pos[None, :] <= target_pos[:, None]
    self_mask = causal[None, None] & (target_pos[None, None, None, :] < target_len[:, None, None, None])
    memory_pos = jnp.arange(MEM, dtype=jnp.int32)
    cross_mask = memory_pos[None, None, None, :] < memory_len[:, None, None, None]
    normed = low(rms_norm(tokens, norm_self))
    query = heads_view(rounded_both(project(normed, query_self)), TGT)
    keys = heads_view(rounded_both(project(normed, key_self)), TGT)
    values = heads_view(rounded_both(project(normed, value_self)), TGT)
    mixed = rounded_both(attend(query, keys, values, score_bias, self_mask)).reshape(TGT * EX, INNER)
    resid_one = tokens + low_back(project(mixed, out_self))
    normed_two = low(rms_norm(resid_one, norm_cross))
    query_two = heads_view(rounded_both(project(normed_two, query_cross)), TGT)
    keys_two = heads_view(rounded_both(project(memory, key_cross)), MEM)
    values_two = heads_view(rounded_both(project(memory, value_cross)), MEM)
    mixed_two = rounded_both(attend(query_two, keys_two, values_two, None, cross_mask)).reshape(TGT * EX, INNER)
    resid_two = resid_one + low_back(project(mixed_two, out_cross))
    normed_three = low(rms_norm(resid_two, norm_ffn))
    hidden = low(jax.nn.gelu(low_back(project(normed_three, ffn_in))))
    return resid_two + low_back(project(hidden, ffn_out))

def reference(tokens, memory, cotangent, target_lengths, memory_lengths, norm_self, query_self, key_self, value_self, out_self, bias_table, norm_cross, query_cross, key_cross, value_cross, out_cross, norm_ffn, ffn_in, ffn_out):
    weights = tuple((w.astype(jnp.float32) for w in (norm_self, query_self, key_self, value_self, out_self, bias_table, norm_cross, query_cross, key_cross, value_cross, out_cross, norm_ffn, ffn_in, ffn_out)))
    groups = EXAMPLES // EX
    target_groups = target_lengths.reshape(groups, EX)
    memory_groups = memory_lengths.reshape(groups, EX)
    counts = lax.optimization_barrier(jnp.sum(target_groups, axis=1)).astype(jnp.float32)
    scales = groups * counts / jnp.sum(counts)
    token_groups = tokens.astype(jnp.float32).reshape(groups, TGT * EX, D)
    memory_rows = memory.astype(jnp.float32).reshape(groups, MEM * EX, D)
    cot_groups = cotangent.astype(jnp.float32).reshape(groups, TGT * EX, D)
    target_pos = jnp.arange(TGT, dtype=jnp.int32)

    def step(carry, item):
        tok_g, mem_g, cot_g, target_g, memory_g, scale_g = item

        def forward(tok_in, mem_in, weight_in):
            return layer(tok_in, mem_in, weight_in, target_g, memory_g)
        output, pullback = jax.vjp(forward, tok_g, mem_g, weights)
        live_rows = (target_pos[:, None] < target_g[None, :]).astype(jnp.float32).reshape(TGT * EX, 1)
        grad_tok, grad_mem, grad_weights = pullback(cot_g * live_rows * scale_g)
        carry = jax.tree.map(jnp.add, carry, grad_weights)
        return (carry, (output.astype(jnp.bfloat16), grad_tok.astype(jnp.bfloat16), grad_mem.astype(jnp.bfloat16)))
    zeros = jax.tree.map(jnp.zeros_like, weights)
    summed, results = lax.scan(step, zeros, (token_groups, memory_rows, cot_groups, target_groups, memory_groups, scales))
    block_out = results[0].reshape(TOKENS, D)
    tokens_grad = results[1].reshape(TOKENS, D)
    memory_grad = results[2].reshape(MEMORY_ROWS, D)
    return (block_out, tokens_grad, memory_grad, summed[0], summed[1], summed[2], summed[3], summed[4], summed[5], summed[6], summed[7], summed[8], summed[9], summed[10], summed[11], summed[12], summed[13])
```

```python
import functools
import math

import jax
import jax.numpy as jnp
import numpy as np
from jax import lax
from jax.experimental import pallas as pl
from jax.experimental.pallas import tpu as pltpu
from jax.sharding import PartitionSpec as P

HEAD_DIM = 64
BUCKETS = 32


epsilon = 1e-06
masked_score = -1e30
highest = lax.Precision.HIGHEST


def bucket_edges():
    exact = list(range(1, 17))
    spaced = [int(math.ceil(16.0 * 8.0 ** ((level - 16) / 16.0))) for level in range(17, 32)]
    return np.array(exact + spaced, dtype=np.int32)


def rms_norm(value, gain):
    factor = lax.rsqrt(jnp.mean(value * value, axis=-1, keepdims=True) + epsilon)
    return value * factor * gain


def gather_rows(value):
    return lax.all_gather(value, "mp", axis=0, tiled=True)


def spread_rows(value):
    return lax.psum_scatter(value, "mp", scatter_dimension=0, tiled=True)


def matmul(left, right):
    return jnp.dot(left, right, preferred_element_type=jnp.float32)


def left_product(left, right):
    return lax.dot_general(
        left, right, (((0,), (0,)), ((), ())), preferred_element_type=jnp.float32
    )


def right_product(left, right):
    return lax.dot_general(
        left, right, (((1,), (1,)), ((), ())), preferred_element_type=jnp.float32
    )


def attend_forward(query, key_rows, value_rows, score_bias, mask):
    scores = jnp.einsum("pehd,kehd->ehpk", query, key_rows, preferred_element_type=jnp.float32)
    if score_bias is not None:
        scores = scores + score_bias[None]
    scores = jnp.where(mask, scores, masked_score)
    row_max = jnp.max(scores, axis=-1, keepdims=True)
    weights = jnp.exp(scores - row_max)
    probs = weights / jnp.sum(weights, axis=-1, keepdims=True)
    probs_low = probs.astype(jnp.bfloat16)
    output = jnp.einsum(
        "ehpk,kehd->pehd", probs_low, value_rows, preferred_element_type=jnp.float32
    )
    return (probs, probs_low, output.astype(jnp.bfloat16))


def attend_backward(query, key_rows, value_rows, probs, probs_low, grad_mixed):
    grad_probs = jnp.einsum(
        "pehd,kehd->ehpk", grad_mixed, value_rows, preferred_element_type=jnp.float32
    )
    inner_sum = jnp.sum(probs * grad_probs, axis=-1, keepdims=True)
    grad_scores = (probs * (grad_probs - inner_sum)).astype(jnp.bfloat16)
    grad_query = jnp.einsum(
        "ehpk,kehd->pehd", grad_scores, key_rows, preferred_element_type=jnp.float32
    )
    grad_keys = jnp.einsum(
        "ehpk,pehd->kehd", grad_scores, query, preferred_element_type=jnp.float32
    )
    grad_values = jnp.einsum(
        "ehpk,pehd->kehd", probs_low, grad_mixed, preferred_element_type=jnp.float32
    )
    return (
        grad_scores,
        grad_query.astype(jnp.bfloat16),
        grad_keys.astype(jnp.bfloat16),
        grad_values.astype(jnp.bfloat16),
    )


def norm_backward(value, gain, grad_normed):
    pullback = jax.vjp(rms_norm, value, gain.astype(jnp.float32))[1]
    return pullback(grad_normed)


def on_device(
    tokens,
    memory,
    cotangent,
    target_lengths,
    memory_lengths,
    norm_self,
    query_self,
    key_self,
    value_self,
    out_self,
    bias_table,
    norm_cross,
    query_cross,
    key_cross,
    value_cross,
    out_cross,
    norm_ffn,
    ffn_in,
    ffn_out,
):
    examples = target_lengths.shape[0]
    local_rows = tokens.shape[0]
    parts = lax.axis_size("mp")
    device_rank = lax.axis_index("mp")
    local_pos = local_rows // examples
    total_pos = local_pos * parts
    memory_local = memory.shape[0]
    memory_total = memory_local * parts
    memory_pos = memory_total // examples
    inner_local = query_self.shape[1]
    heads = inner_local // HEAD_DIM
    total_rows = local_rows * parts
    group_count = jnp.sum(target_lengths).astype(jnp.float32)
    total_count = lax.psum(group_count, "dp")
    token_scale = lax.axis_size("dp") * group_count / total_count
    positions = device_rank * local_pos + jnp.arange(local_pos, dtype=jnp.int32)
    live_rows = (
        (positions[:, None] < target_lengths[None, :]).astype(jnp.float32).reshape(local_rows, 1)
    )
    target_pos = jnp.arange(total_pos, dtype=jnp.int32)
    distance = jnp.maximum(target_pos[:, None] - target_pos[None, :], 0)
    buckets = jnp.sum(
        (distance[:, :, None] >= jnp.asarray(bucket_edges())[None, None, :]).astype(jnp.int32),
        axis=-1,
    )
    table_hot = (buckets[:, :, None] == jnp.arange(BUCKETS, dtype=jnp.int32)[None, None, :]).astype(
        jnp.float32
    )
    causal = target_pos[None, :] <= target_pos[:, None]
    self_mask = causal[None, None] & (
        target_pos[None, None, None, :] < target_lengths[:, None, None, None]
    )
    cross_pos = jnp.arange(memory_pos, dtype=jnp.int32)
    cross_mask = cross_pos[None, None, None, :] < memory_lengths[:, None, None, None]
    score_bias = jnp.einsum(
        "qkb,bh->hqk", table_hot, bias_table.astype(jnp.float32), precision=highest
    )

    def target_view(value):
        return value.reshape(total_pos, examples, heads, HEAD_DIM)

    def memory_view(value):
        return value.reshape(memory_pos, examples, heads, HEAD_DIM)

    tokens_float = tokens.astype(jnp.float32)
    normed_one = rms_norm(tokens_float, norm_self.astype(jnp.float32)).astype(jnp.bfloat16)
    rows_one = gather_rows(normed_one)
    self_weights = jnp.concatenate([query_self, key_self, value_self], axis=1)
    projected = matmul(rows_one, self_weights).astype(jnp.bfloat16)
    query_one = target_view(projected[:, :inner_local])
    keys_one = target_view(projected[:, inner_local : 2 * inner_local])
    values_one = target_view(projected[:, 2 * inner_local :])
    probs_one, low_one, mixed_one = attend_forward(
        query_one, keys_one, values_one, score_bias, self_mask
    )
    mixed_rows_one = mixed_one.reshape(total_rows, inner_local)
    resid_one = tokens_float + spread_rows(matmul(mixed_rows_one, out_self))
    normed_two = rms_norm(resid_one, norm_cross.astype(jnp.float32)).astype(jnp.bfloat16)
    rows_two = gather_rows(normed_two)
    query_two = target_view(matmul(rows_two, query_cross).astype(jnp.bfloat16))
    memory_all = lax.all_gather(memory, "mp", axis=0, tiled=True)
    cross_kv = matmul(memory_all, jnp.concatenate([key_cross, value_cross], axis=1)).astype(
        jnp.bfloat16
    )
    keys_flat = cross_kv[:, :inner_local]
    values_flat = cross_kv[:, inner_local:]
    keys_two = memory_view(keys_flat)
    values_two = memory_view(values_flat)
    probs_two, low_two, mixed_two = attend_forward(
        query_two, keys_two, values_two, None, cross_mask
    )
    mixed_rows_two = mixed_two.reshape(total_rows, inner_local)
    resid_two = resid_one + spread_rows(matmul(mixed_rows_two, out_cross))
    normed_three = rms_norm(resid_two, norm_ffn.astype(jnp.float32)).astype(jnp.bfloat16)
    rows_three = gather_rows(normed_three)
    pre_act = matmul(rows_three, ffn_in)
    hidden = jax.nn.gelu(pre_act).astype(jnp.bfloat16)
    block_out = resid_two + spread_rows(matmul(hidden, ffn_out))
    grad_out = cotangent.astype(jnp.float32) * live_rows * token_scale
    grad_rows_three = gather_rows(grad_out.astype(jnp.bfloat16))
    ffn_out_grad = left_product(hidden, grad_rows_three)
    grad_hidden = right_product(grad_rows_three, ffn_out)
    gelu_back = jax.vjp(jax.nn.gelu, pre_act)[1]
    grad_pre = gelu_back(grad_hidden)[0].astype(jnp.bfloat16)
    ffn_in_grad = left_product(rows_three, grad_pre)
    grad_normed_three = spread_rows(right_product(grad_pre, ffn_in))
    grad_resid_three, gain_three = norm_backward(resid_two, norm_ffn, grad_normed_three)
    grad_two = grad_out + grad_resid_three
    grad_rows_two = gather_rows(grad_two.astype(jnp.bfloat16))
    out_cross_grad = left_product(mixed_rows_two, grad_rows_two)
    grad_mixed_two = target_view(right_product(grad_rows_two, out_cross).astype(jnp.bfloat16))
    cross_back = attend_backward(
        query_two, keys_two, values_two, probs_two, low_two, grad_mixed_two
    )
    grad_query_two = cross_back[1].reshape(total_rows, inner_local)
    grad_keys_two = cross_back[2].reshape(memory_total, inner_local)
    grad_values_two = cross_back[3].reshape(memory_total, inner_local)
    query_cross_grad = left_product(rows_two, grad_query_two)
    grad_normed_two = spread_rows(right_product(grad_query_two, query_cross))
    key_cross_grad = left_product(memory_all, grad_keys_two)
    value_cross_grad = left_product(memory_all, grad_values_two)
    memory_terms = right_product(grad_keys_two, key_cross) + right_product(
        grad_values_two, value_cross
    )
    memory_grad = lax.psum_scatter(memory_terms, "mp", scatter_dimension=0, tiled=True)
    grad_resid_two, gain_two = norm_backward(resid_one, norm_cross, grad_normed_two)
    grad_one = grad_two + grad_resid_two
    grad_rows_one = gather_rows(grad_one.astype(jnp.bfloat16))
    out_self_grad = left_product(mixed_rows_one, grad_rows_one)
    grad_mixed_one = target_view(right_product(grad_rows_one, out_self).astype(jnp.bfloat16))
    self_back = attend_backward(query_one, keys_one, values_one, probs_one, low_one, grad_mixed_one)
    bias_table_grad = jnp.einsum(
        "ehqk,qkb->bh", self_back[0].astype(jnp.float32), table_hot, precision=highest
    )
    grad_projected = jnp.concatenate(
        [
            self_back[1].reshape(total_rows, inner_local),
            self_back[2].reshape(total_rows, inner_local),
            self_back[3].reshape(total_rows, inner_local),
        ],
        axis=1,
    )
    self_weight_grad = left_product(rows_one, grad_projected)
    grad_normed_one = spread_rows(right_product(grad_projected, self_weights))
    grad_resid_one, gain_one = norm_backward(tokens_float, norm_self, grad_normed_one)
    tokens_grad = grad_one + grad_resid_one
    summed = lax.psum(
        (
            self_weight_grad[:, :inner_local],
            self_weight_grad[:, inner_local : 2 * inner_local],
            self_weight_grad[:, 2 * inner_local :],
            out_self_grad,
            bias_table_grad,
            query_cross_grad,
            key_cross_grad,
            value_cross_grad,
            out_cross_grad,
            ffn_in_grad,
            ffn_out_grad,
        ),
        "dp",
    )
    gains = lax.psum((gain_one, gain_two, gain_three), ("dp", "mp"))
    return (
        block_out.astype(jnp.bfloat16),
        tokens_grad.astype(jnp.bfloat16),
        memory_grad.astype(jnp.bfloat16),
        gains[0],
        summed[0],
        summed[1],
        summed[2],
        summed[3],
        summed[4],
        gains[1],
        summed[5],
        summed[6],
        summed[7],
        summed[8],
        gains[2],
        summed[9],
        summed[10],
    )


def links(dp_size):
    total = 2 * dp_size

    def swap(bit):
        return [(at, at ^ bit) for at in range(total)]

    def off_swap(bit):
        return [(at, at ^ bit) for at in range(total) if (at & 1) != ((at >> 1) & 1)]

    def turned(at):
        return (at & ~3) | ((at & 1) << 1) | ((at >> 1) & 1)

    def crossed(at):
        return (at & ~3) | ((1 - (at & 1)) << 1) | ((at >> 1) & 1)

    return {
        "turn": [(at, turned(at)) for at in range(total)],
        "cross": [(at, crossed(at)) for at in range(total)],
        "y": swap(1),
        "core": swap(2),
        "x": swap(4),
        "zl": swap(8),
        "zh": swap(16),
        "off_x": off_swap(4),
        "off_zl": off_swap(8),
    }


def permute(value, pairs):
    return lax.ppermute(value, ("dp", "mp"), pairs)


def reorder_kernel(inverse, examples, source, target):
    rows = source.shape[0] if not inverse else source.shape[0] * source.shape[1]
    chunk = rows // examples
    high = lax.broadcasted_iota(jnp.int32, (rows, rows), 0)
    low = lax.broadcasted_iota(jnp.int32, (rows, rows), 1)
    if inverse:
        hot = low == (high % examples) * chunk + high // examples
        value = source[...].reshape(rows, source.shape[2])
    else:
        hot = low == (high % chunk) * examples + high // chunk
        value = source[...]
    moved = jnp.dot(
        hot.astype(jnp.bfloat16), value, preferred_element_type=jnp.float32
    ).astype(jnp.bfloat16)
    target[...] = moved.reshape(target.shape)


def example_major(value, examples):
    rows, width = value.shape
    block = 256
    return pl.pallas_call(
        functools.partial(reorder_kernel, False, examples),
        grid=(rows // block,),
        in_specs=[pl.BlockSpec((block, width), lambda i: (i, 0))],
        out_specs=pl.BlockSpec((examples, block // examples, width), lambda i: (0, i, 0)),
        out_shape=jax.ShapeDtypeStruct((examples, rows // examples, width), value.dtype),
        compiler_params=pltpu.CompilerParams(vmem_limit_bytes=VMEM_LIMIT),
    )(value).reshape(rows, width)


def position_major(value, examples):
    rows, width = value.shape
    block = 256
    return pl.pallas_call(
        functools.partial(reorder_kernel, True, examples),
        grid=(rows // block,),
        in_specs=[
            pl.BlockSpec((examples, block // examples, width), lambda i: (0, i, 0))
        ],
        out_specs=pl.BlockSpec((block, width), lambda i: (i, 0)),
        out_shape=jax.ShapeDtypeStruct((rows, width), value.dtype),
        compiler_params=pltpu.CompilerParams(vmem_limit_bytes=VMEM_LIMIT),
    )(value.reshape(examples, rows // examples, width))


def nt(left, right):
    return lax.dot_general(
        left, right, (((1,), (1,)), ((), ())), preferred_element_type=jnp.float32
    )


def tn(left, right):
    return lax.dot_general(
        left, right, (((0,), (0,)), ((), ())), preferred_element_type=jnp.float32
    )


def nn(left, right):
    return jnp.dot(left, right, preferred_element_type=jnp.float32)


def one_head(value, head):
    lane = lax.broadcasted_iota(jnp.int32, value.shape, 1)
    return jnp.where(lane // HEAD_DIM == head, value, jnp.zeros_like(value))


def join_heads(first, second):
    return jnp.concatenate([first[:HEAD_DIM], second[HEAD_DIM:]], axis=0).T


def softmax_columns(scores):
    top = jnp.max(scores, axis=0, keepdims=True)
    weights = jnp.exp(scores - top)
    return weights * (1.0 / jnp.sum(weights, axis=0, keepdims=True))


def toeplitz(row, size):
    return pltpu.roll(jnp.broadcast_to(row, (size, size)), 0, 1, stride=1, stride_axis=0)


def diagonals(square):
    size = square.shape[0]
    row = lax.broadcasted_iota(jnp.int32, square.shape, 0)
    turned, step = square, 1
    while step < size:
        moved = pltpu.roll(turned, size - step, 1)
        turned = jnp.where((row & step) != 0, moved, turned)
        step *= 2
    return jnp.sum(turned, axis=0, keepdims=True)


def ordered(core, scratch, own, other):
    half = own.shape[0]
    scratch[pl.ds(pl.multiple_of(core * half, half), half), :] = own
    scratch[pl.ds(pl.multiple_of((1 - core) * half, half), half), :] = other
    return scratch[...]


def split_store(core, scratch, value, own, other):
    half = own.shape[0]
    scratch[...] = value
    own[...] = scratch[pl.ds(pl.multiple_of(core * half, half), half), :]
    other[...] = scratch[pl.ds(pl.multiple_of((1 - core) * half, half), half), :]


def self_scores(query, keys, bias_row, head, length):
    size = query.shape[0]
    scores = nt(keys, one_head(query, head)) + toeplitz(bias_row, size)
    key_at = lax.broadcasted_iota(jnp.int32, scores.shape, 0)
    query_at = lax.broadcasted_iota(jnp.int32, scores.shape, 1)
    return jnp.where((key_at <= query_at) & (key_at < length), scores, masked_score)


def self_forward_kernel(info, own, other, bias, out_own, out_other, scratch, out_scratch):
    core = info[0]
    length = info[1 + pl.program_id(1)]
    joined = ordered(core, scratch, own[...], other[...])
    query, keys, values = joined[:, :128], joined[:, 128:256], joined[:, 256:]
    mixed = []
    for head in range(2):
        probs = softmax_columns(
            self_scores(query, keys, bias[0, head : head + 1, :], head, length)
        )
        mixed.append(tn(values, probs.astype(jnp.bfloat16)))
    result = join_heads(*mixed).astype(jnp.bfloat16)
    split_store(core, out_scratch, result, out_own, out_other)


def self_backward_kernel(
    info,
    own,
    other,
    bias,
    grad_own,
    grad_other,
    out_own,
    out_other,
    out_bias,
    scratch,
    grad_scratch,
    out_scratch,
    bias_scratch,
):
    core = info[0]
    example = pl.program_id(1)
    length = info[1 + example]
    joined = ordered(core, scratch, own[...], other[...])
    query, keys, values = joined[:, :128], joined[:, 128:256], joined[:, 256:]
    grad = ordered(core, grad_scratch, grad_own[...], grad_other[...])
    grad_query, grad_keys, grad_values = [], [], []
    for head in range(2):
        probs = softmax_columns(
            self_scores(query, keys, bias[0, head : head + 1, :], head, length)
        )
        low = probs.astype(jnp.bfloat16)
        grad_head = one_head(grad, head)
        grad_probs = nt(values, grad_head)
        inner = jnp.sum(probs * grad_probs, axis=0, keepdims=True)
        grad_scores = (probs * (grad_probs - inner)).astype(jnp.bfloat16)
        grad_values.append(nn(low, grad_head))
        grad_keys.append(nn(grad_scores, one_head(query, head)))
        grad_query.append(tn(keys, grad_scores))
        square = grad_scores.astype(jnp.float32)

        @pl.when(example == 0)
        def _():
            bias_scratch[head] = square

        @pl.when(example > 0)
        def _():
            bias_scratch[head] = bias_scratch[head] + square

        @pl.when(example == pl.num_programs(1) - 1)
        def _():
            out_bias[0, head : head + 1, :] = diagonals(bias_scratch[head])

    result = jnp.concatenate(
        [
            join_heads(*grad_query),
            grad_keys[0] + grad_keys[1],
            grad_values[0] + grad_values[1],
        ],
        axis=1,
    ).astype(jnp.bfloat16)
    split_store(core, out_scratch, result, out_own, out_other)


def cross_scores(query, keys, head, core, length):
    scores = nt(keys, one_head(query, head))
    size = scores.shape[0]
    key_at = lax.broadcasted_iota(jnp.int32, scores.shape, 0)
    key_at = (key_at + core * (size // 2)) & (size - 1)
    return jnp.where(key_at < length, scores, masked_score)


def cross_forward_kernel(info, q_own, q_other, kv_own, kv_other, out_own, out_other):
    core = info[0]
    length = info[1 + pl.program_id(0)]
    query = jnp.concatenate([q_own[...], q_other[...]], axis=0)
    keys = jnp.concatenate([kv_own[:, :128], kv_other[:, :128]], axis=0)
    values = jnp.concatenate([kv_own[:, 128:], kv_other[:, 128:]], axis=0)
    mixed = []
    for head in range(2):
        probs = softmax_columns(cross_scores(query, keys, head, core, length))
        mixed.append(tn(values, probs.astype(jnp.bfloat16)))
    result = join_heads(*mixed).astype(jnp.bfloat16)
    half = out_own.shape[0]
    out_own[...] = result[:half]
    out_other[...] = result[half:]


def cross_backward_kernel(
    info,
    q_own,
    q_other,
    kv_own,
    kv_other,
    grad_own,
    grad_other,
    dq_own,
    dq_other,
    dkv_own,
    dkv_other,
):
    core = info[0]
    length = info[1 + pl.program_id(0)]
    query = jnp.concatenate([q_own[...], q_other[...]], axis=0)
    grad = jnp.concatenate([grad_own[...], grad_other[...]], axis=0)
    keys = jnp.concatenate([kv_own[:, :128], kv_other[:, :128]], axis=0)
    values = jnp.concatenate([kv_own[:, 128:], kv_other[:, 128:]], axis=0)
    grad_query, grad_keys, grad_values = [], [], []
    for head in range(2):
        probs = softmax_columns(cross_scores(query, keys, head, core, length))
        low = probs.astype(jnp.bfloat16)
        grad_head = one_head(grad, head)
        grad_probs = nt(values, grad_head)
        inner = jnp.sum(probs * grad_probs, axis=0, keepdims=True)
        grad_scores = (probs * (grad_probs - inner)).astype(jnp.bfloat16)
        grad_values.append(nn(low, grad_head))
        grad_keys.append(nn(grad_scores, one_head(query, head)))
        grad_query.append(tn(keys, grad_scores))
    half = dq_own.shape[0]
    result = join_heads(*grad_query).astype(jnp.bfloat16)
    dq_own[...] = result[:half]
    dq_other[...] = result[half:]
    result = jnp.concatenate(
        [grad_keys[0] + grad_keys[1], grad_values[0] + grad_values[1]], axis=1
    ).astype(jnp.bfloat16)
    half = dkv_own.shape[0]
    dkv_own[...] = result[:half]
    dkv_other[...] = result[half:]


VMEM_LIMIT = 56 * 1024 * 1024
SMEM_SPEC = pl.BlockSpec(memory_space=pltpu.SMEM)


def self_forward(info, own, other, bias, examples):
    rows, width = own.shape
    pairs, size = width // 384, rows // examples
    spec = pl.BlockSpec((size, 384), lambda h, e: (e, h))
    out = pl.BlockSpec((size, 128), lambda h, e: (e, h))
    return pl.pallas_call(
        self_forward_kernel,
        grid=(pairs, examples),
        in_specs=[SMEM_SPEC, spec, spec, pl.BlockSpec((1, 2, 2 * size), lambda h, e: (h, 0, 0))],
        out_specs=[out, out],
        out_shape=[jax.ShapeDtypeStruct((rows, pairs * 128), jnp.bfloat16)] * 2,
        scratch_shapes=[
            pltpu.VMEM((2 * size, 384), jnp.bfloat16),
            pltpu.VMEM((2 * size, 128), jnp.bfloat16),
        ],
        compiler_params=pltpu.CompilerParams(vmem_limit_bytes=VMEM_LIMIT),
    )(info, own, other, bias)


def self_backward(info, own, other, bias, grad_own, grad_other, examples):
    rows, width = own.shape
    pairs, size = width // 384, rows // examples
    spec = pl.BlockSpec((size, 384), lambda h, e: (e, h))
    low = pl.BlockSpec((size, 128), lambda h, e: (e, h))
    row = pl.BlockSpec((1, 2, 2 * size), lambda h, e: (h, 0, 0))
    return pl.pallas_call(
        self_backward_kernel,
        grid=(pairs, examples),
        in_specs=[SMEM_SPEC, spec, spec, row, low, low],
        out_specs=[spec, spec, row],
        out_shape=[jax.ShapeDtypeStruct((rows, width), jnp.bfloat16)] * 2
        + [jax.ShapeDtypeStruct((pairs, 2, 2 * size), jnp.float32)],
        scratch_shapes=[
            pltpu.VMEM((2 * size, 384), jnp.bfloat16),
            pltpu.VMEM((2 * size, 128), jnp.bfloat16),
            pltpu.VMEM((2 * size, 384), jnp.bfloat16),
            pltpu.VMEM((2, 2 * size, 2 * size), jnp.float32),
        ],
        compiler_params=pltpu.CompilerParams(vmem_limit_bytes=VMEM_LIMIT),
    )(info, own, other, bias, grad_own, grad_other)


def cross_forward(info, q_own, q_other, kv_own, kv_other, examples):
    rows, width = q_own.shape
    pairs, size, span = width // 128, rows // examples, kv_own.shape[0] // examples
    low = pl.BlockSpec((size, 128), lambda e, h: (e, h))
    wide = pl.BlockSpec((span, 256), lambda e, h: (e, h))
    return pl.pallas_call(
        cross_forward_kernel,
        grid=(examples, pairs),
        in_specs=[SMEM_SPEC, low, low, wide, wide],
        out_specs=[low, low],
        out_shape=[jax.ShapeDtypeStruct((rows, width), jnp.bfloat16)] * 2,
        compiler_params=pltpu.CompilerParams(vmem_limit_bytes=VMEM_LIMIT),
    )(info, q_own, q_other, kv_own, kv_other)


def cross_backward(info, q_own, q_other, kv_own, kv_other, grad_own, grad_other, examples):
    rows, width = q_own.shape
    pairs, size, span = width // 128, rows // examples, kv_own.shape[0] // examples
    low = pl.BlockSpec((size, 128), lambda e, h: (e, h))
    wide = pl.BlockSpec((span, 256), lambda e, h: (e, h))
    return pl.pallas_call(
        cross_backward_kernel,
        grid=(examples, pairs),
        in_specs=[SMEM_SPEC, low, low, wide, wide, low, low],
        out_specs=[low, low, wide, wide],
        out_shape=[jax.ShapeDtypeStruct((rows, width), jnp.bfloat16)] * 2
        + [jax.ShapeDtypeStruct(kv_own.shape, jnp.bfloat16)] * 2,
        compiler_params=pltpu.CompilerParams(vmem_limit_bytes=VMEM_LIMIT),
    )(info, q_own, q_other, kv_own, kv_other, grad_own, grad_other)


def assemble_kernel(info, held, first, second, target):
    part = pl.program_id(0) ^ info[0]

    @pl.when(info[1] == 1)
    def _():
        target[...] = held[...]

    @pl.when((info[1] == 0) & ((part & 1) == 0))
    def _():
        target[...] = first[...]

    @pl.when((info[1] == 0) & ((part & 1) == 1))
    def _():
        target[...] = second[...]


def bring(weight, place, net):
    rows, width = weight.shape
    part = rows // 4
    mine = place["x"] * 2 + place["zl"]
    start = mine * part
    first = permute(lax.dynamic_slice_in_dim(weight, start, part, 0), net["turn"])
    second = permute(first, net["off_x"])
    pair = jnp.concatenate([first, second], axis=0)
    far = permute(pair, net["off_zl"])
    info = jnp.stack([mine, (place["core"] == place["y"]).astype(jnp.int32)])
    block = (part, width)
    return pl.pallas_call(
        assemble_kernel,
        grid_spec=pltpu.PrefetchScalarGridSpec(
            num_scalar_prefetch=1,
            grid=(4,),
            in_specs=[
                pl.BlockSpec(block, lambda i, s: (i * s[1], 0)),
                pl.BlockSpec(block, lambda i, s: ((i ^ s[0]) >> 1, 0)),
                pl.BlockSpec(block, lambda i, s: ((i ^ s[0]) >> 1, 0)),
            ],
            out_specs=pl.BlockSpec(block, lambda i, s: (i, 0)),
        ),
        out_shape=jax.ShapeDtypeStruct(weight.shape, weight.dtype),
        compiler_params=pltpu.CompilerParams(vmem_limit_bytes=VMEM_LIMIT),
    )(info, weight, pair, far)


def add_low(left, right):
    return (left.astype(jnp.float32) + right.astype(jnp.float32)).astype(jnp.bfloat16)


def pick(value, index):
    return lax.dynamic_index_in_dim(value, index, 0, keepdims=False)


def reduce_pieces(value, place, net):
    count, rows, width = value.shape
    halves = value.reshape(2, count // 2, rows, width)
    near = permute(pick(halves, place["y"]), net["turn"])
    far = permute(pick(halves, 1 - place["y"]), net["cross"])
    total = add_low(near, far)
    for name in ("x", "zl", "zh"):
        view = total.reshape(2, total.shape[0] // 2, rows, width)
        sent = permute(pick(view, 1 - place[name]), net[name])
        total = add_low(pick(view, place[name]), sent)
    for name in ("zh", "zl", "x"):
        total = jnp.concatenate([total, permute(total, net[name])], axis=0)
    return total, permute(total, net["core"])


def finish_kernel(layout, info, own, other, *targets):
    mine = (pl.program_id(0) >> 3) == info[1]

    def write(source):
        for target, moves in zip(targets, layout):
            for row, rows, column, columns, at in moves:
                target[:, at : at + columns] = source[
                    0, row : row + rows, column : column + columns
                ].astype(jnp.float32)

    @pl.when(mine)
    def _():
        write(own)

    @pl.when(jnp.logical_not(mine))
    def _():
        write(other)


def finish(own, other, place, shapes, layout):
    count, rows, width = own.shape
    info = jnp.stack([place["x"] * 4 + place["zl"] * 2 + place["zh"], place["core"]])

    def at(held):
        def index(i, s):
            used = ((i >> 3) == s[1]) == held
            return (jnp.where(used, (i & 7) ^ s[0], s[0]), 0, 0)

        return index

    return pl.pallas_call(
        functools.partial(finish_kernel, layout),
        grid_spec=pltpu.PrefetchScalarGridSpec(
            num_scalar_prefetch=1,
            grid=(2 * count,),
            in_specs=[
                pl.BlockSpec((1, rows, width), at(True)),
                pl.BlockSpec((1, rows, width), at(False)),
            ],
            out_specs=[
                pl.BlockSpec((shape[0] // (2 * count), shape[1]), lambda i, s: (i, 0))
                for shape in shapes
            ],
        ),
        out_shape=[jax.ShapeDtypeStruct(shape, jnp.float32) for shape in shapes],
        compiler_params=pltpu.CompilerParams(vmem_limit_bytes=VMEM_LIMIT),
    )(info, own, other)


def pieces(*values):
    split = [v.reshape(16, v.shape[0] // 16, v.shape[1]) for v in values]
    return split[0] if len(split) == 1 else jnp.concatenate(split, axis=1)


def columns_together(*weights):
    rows = weights[0].shape[0]
    views = [w.reshape(rows, w.shape[1] // 128, 128) for w in weights]
    return jnp.stack(views, axis=2).reshape(rows, -1)


def low(value):
    return value.astype(jnp.bfloat16)


def on_chip_group(
    tokens,
    memory,
    cotangent,
    target_lengths,
    memory_lengths,
    norm_self,
    query_self,
    key_self,
    value_self,
    out_self,
    bias_table,
    norm_cross,
    query_cross,
    key_cross,
    value_cross,
    out_cross,
    norm_ffn,
    ffn_in,
    ffn_out,
):
    examples = target_lengths.shape[0]
    groups = lax.axis_size("dp")
    net = links(groups)
    index = lax.axis_index("dp")
    place = {
        "y": lax.axis_index("mp"),
        "core": index & 1,
        "x": (index >> 1) & 1,
        "zl": (index >> 2) & 1,
        "zh": (index >> 3) & 1,
    }
    core = place["core"]
    rows, width = tokens.shape
    half_pos = rows // examples

    def swap(value):
        return permute(value, net["core"])

    lengths = permute(jnp.concatenate([target_lengths, memory_lengths]), net["turn"])
    target_len, memory_len = lengths[:examples], lengths[examples:]
    group_count = jnp.sum(target_len).astype(jnp.float32)
    total_count = group_count.reshape(1, 1)
    for name in ("y", "x", "zl", "zh"):
        total_count = total_count + permute(total_count, net[name])
    token_scale = groups * group_count / total_count[0, 0]
    self_info = jnp.concatenate([core[None], target_len])
    cross_info = jnp.concatenate([core[None], memory_len])

    tok = permute(example_major(tokens, examples), net["turn"])
    self_in = bring(columns_together(query_self, key_self, value_self), place, net)
    outs = bring(jnp.concatenate([out_self, out_cross], axis=0), place, net)
    self_out, cross_out = outs[: out_self.shape[0]], outs[out_self.shape[0] :]
    mem = permute(example_major(memory, examples), net["turn"])
    kv_and_q = bring(
        jnp.concatenate([columns_together(key_cross, value_cross), query_cross], axis=1),
        place,
        net,
    )
    kv_width = 2 * key_cross.shape[1]
    cross_kv, cross_q = kv_and_q[:, :kv_width], kv_and_q[:, kv_width:]
    into = bring(ffn_in, place, net)
    outof = bring(ffn_out, place, net)
    cot = permute(example_major(cotangent, examples), net["turn"])
    table = bias_table
    table = jnp.where(core == place["y"], table, permute(table, net["turn"]))

    span = 2 * half_pos
    distance = jnp.arange(span, dtype=jnp.int32)
    level = jnp.sum(
        (distance[:, None] >= jnp.asarray(bucket_edges())[None, :]).astype(jnp.int32), axis=-1
    )
    level_hot = (level[:, None] == jnp.arange(BUCKETS, dtype=jnp.int32)[None, :]).astype(
        jnp.float32
    )
    bias = jnp.einsum(
        "db,bh->hd", level_hot, table.astype(jnp.float32), precision=highest
    ).reshape(-1, 2, span)

    tok_float = tok.astype(jnp.float32)
    n1 = low(rms_norm(tok_float, norm_self.astype(jnp.float32)))
    n1_far = swap(n1)
    qkv, qkv_far = low(nn(n1, self_in)), low(nn(n1_far, self_in))
    a1, a1_far = self_forward(self_info, qkv, qkv_far, bias, examples)
    r1 = tok_float + (nn(a1, self_out) + swap(nn(a1_far, self_out)))

    mem_far = swap(mem)
    kv, kv_far = low(nn(mem, cross_kv)), low(nn(mem_far, cross_kv))
    n2 = low(rms_norm(r1, norm_cross.astype(jnp.float32)))
    n2_far = swap(n2)
    q2, q2_far = low(nn(n2, cross_q)), low(nn(n2_far, cross_q))
    a2, a2_far = cross_forward(cross_info, q2, q2_far, kv, kv_far, examples)
    r2 = r1 + (nn(a2, cross_out) + swap(nn(a2_far, cross_out)))

    n3 = low(rms_norm(r2, norm_ffn.astype(jnp.float32)))
    n3_far = swap(n3)
    u, u_far = nn(n3, into), nn(n3_far, into)
    h, h_far = low(jax.nn.gelu(u)), low(jax.nn.gelu(u_far))
    block_out = low(r2 + (nn(h, outof) + swap(nn(h_far, outof))))
    block_out = position_major(permute(block_out, net["turn"]), examples)

    positions = core * half_pos + jnp.arange(half_pos, dtype=jnp.int32)
    live = (positions[None, :] < target_len[:, None]).astype(jnp.float32).reshape(rows, 1)
    dy = cot.astype(jnp.float32) * live * token_scale
    gy = low(dy)
    gy_far = swap(gy)
    ffn_out_part = low(tn(h, gy) + tn(h_far, gy_far))

    def through_gelu(pre, grad):
        return low(jax.vjp(jax.nn.gelu, pre)[1](nt(grad, outof))[0])

    du, du_far = through_gelu(u, gy), through_gelu(u_far, gy_far)
    ffn_in_part = low(tn(n3, du) + tn(n3_far, du_far))
    dn3 = nt(du, into) + swap(nt(du_far, into))
    back, gain_three = norm_backward(r2, norm_ffn, dn3)
    dr2 = dy + back
    ffn_out_done = reduce_pieces(pieces(ffn_out_part), place, net)
    ffn_in_done = reduce_pieces(pieces(ffn_in_part), place, net)

    g2 = low(dr2)
    g2_far = swap(g2)
    cross_out_part = low(tn(a2, g2) + tn(a2_far, g2_far))
    da2, da2_far = low(nt(g2, cross_out)), low(nt(g2_far, cross_out))
    dq2, dq2_far, dkv, dkv_far = cross_backward(
        cross_info, q2, q2_far, kv, kv_far, da2, da2_far, examples
    )
    cross_q_part = low(tn(dq2, n2) + tn(dq2_far, n2_far))
    cross_kv_part = low(tn(mem, dkv) + tn(mem_far, dkv_far))
    memory_grad = low(
        nt(dkv, cross_kv) + swap(low(nt(dkv_far, cross_kv))).astype(jnp.float32)
    )
    memory_grad = position_major(permute(memory_grad, net["turn"]), examples)
    dn2 = nt(dq2, cross_q) + swap(nt(dq2_far, cross_q))
    back, gain_two = norm_backward(r1, norm_cross, dn2)
    dr1 = dr2 + back

    g1 = low(dr1)
    g1_far = swap(g1)
    self_out_part = low(tn(a1, g1) + tn(a1_far, g1_far))
    middle_done = reduce_pieces(
        pieces(cross_kv_part, cross_out_part, self_out_part, cross_q_part), place, net
    )
    da1, da1_far = low(nt(g1, self_out)), low(nt(g1_far, self_out))
    dqkv, dqkv_far, by_distance = self_backward(
        self_info, qkv, qkv_far, bias, da1, da1_far, examples
    )
    self_in_part = low(tn(n1, dqkv) + tn(n1_far, dqkv_far))
    self_in_done = reduce_pieces(pieces(self_in_part), place, net)
    dn1 = nt(dqkv, self_in) + swap(nt(dqkv_far, self_in))
    back, gain_one = norm_backward(tok_float, norm_self, dn1)
    tokens_grad = low(dr1 + back)
    tokens_grad = position_major(permute(tokens_grad, net["turn"]), examples)

    bias_part = jnp.einsum(
        "hd,db->bh", by_distance.reshape(-1, span), level_hot, precision=highest
    )
    bias_row = jnp.pad(bias_part.reshape(1, -1), ((0, 0), (0, width - bias_part.size)))
    small = jnp.concatenate(
        [gain_one[None], gain_two[None], gain_three[None], bias_row], axis=0
    )
    for name in ("y", "x", "zl", "zh"):
        small = small + permute(small, net[name])
    small_far = swap(small)
    gains = small[:3] + small_far[:3]
    bias_sum = jnp.where(core == place["y"], small[3], small_far[3])
    bias_grad = bias_sum[: bias_part.size].reshape(bias_part.shape)

    (ffn_out_grad,) = finish(
        *ffn_out_done, place, [ffn_out.shape], [[(0, ffn_out.shape[0] // 16, 0, width, 0)]]
    )
    (ffn_in_grad,) = finish(
        *ffn_in_done,
        place,
        [ffn_in.shape],
        [[(0, width // 16, 0, ffn_in.shape[1], 0)]],
    )
    inner = key_cross.shape[1]
    wide, thin = width // 16, inner // 16
    key_moves = [(0, wide, 256 * i, 128, 128 * i) for i in range(inner // 128)]
    value_moves = [(0, wide, 256 * i + 128, 128, 128 * i) for i in range(inner // 128)]
    key_cross_grad, value_cross_grad, out_cross_grad, out_self_grad, query_rows = finish(
        *middle_done,
        place,
        [key_cross.shape, value_cross.shape, out_cross.shape, out_self.shape, (inner, width)],
        [
            key_moves,
            value_moves,
            [(wide, thin, 0, width, 0)],
            [(wide + thin, thin, 0, width, 0)],
            [(wide + 2 * thin, thin, 0, width, 0)],
        ],
    )
    query_cross_grad = query_rows.T
    query_self_grad, key_self_grad, value_self_grad = finish(
        *self_in_done,
        place,
        [query_self.shape, key_self.shape, value_self.shape],
        [
            [(0, wide, 384 * i + 128 * k, 128, 128 * i) for i in range(inner // 128)]
            for k in range(3)
        ],
    )
    return (
        block_out,
        tokens_grad,
        memory_grad,
        gains[0],
        query_self_grad,
        key_self_grad,
        value_self_grad,
        out_self_grad,
        bias_grad,
        gains[1],
        query_cross_grad,
        key_cross_grad,
        value_cross_grad,
        out_cross_grad,
        gains[2],
        ffn_in_grad,
        ffn_out_grad,
    )


def solution(mesh):
    placed = (
        P(("dp", "mp"), None),
        P(("dp", "mp"), None),
        P(("dp", "mp"), None),
        P("dp"),
        P("dp"),
        P(),
        P(None, "mp"),
        P(None, "mp"),
        P(None, "mp"),
        P("mp", None),
        P(None, "mp"),
        P(),
        P(None, "mp"),
        P(None, "mp"),
        P(None, "mp"),
        P("mp", None),
        P(),
        P(None, "mp"),
        P("mp", None),
    )
    near = mesh.shape["mp"] == 2 and mesh.shape["dp"] == 16
    return jax.shard_map(
        on_chip_group if near else on_device,
        mesh=mesh,
        in_specs=placed,
        out_specs=(
            P(("dp", "mp"), None),
            P(("dp", "mp"), None),
            P(("dp", "mp"), None),
            P(),
            P(None, "mp"),
            P(None, "mp"),
            P(None, "mp"),
            P("mp", None),
            P(None, "mp"),
            P(),
            P(None, "mp"),
            P(None, "mp"),
            P(None, "mp"),
            P("mp", None),
            P(),
            P(None, "mp"),
            P("mp", None),
        ),
        check_vma=False,
    )
```

```python
import functools
import math

import jax
import jax.numpy as jnp
import numpy as np
from jax import lax
from jax.experimental import pallas as pl
from jax.experimental.pallas import tpu as pltpu
from jax.sharding import PartitionSpec as P

HEAD_DIM = 64
BUCKETS = 32


epsilon = 1e-06
masked_score = -1e30
highest = lax.Precision.HIGHEST


def bucket_edges():
    exact = list(range(1, 17))
    spaced = [int(math.ceil(16.0 * 8.0 ** ((level - 16) / 16.0))) for level in range(17, 32)]
    return np.array(exact + spaced, dtype=np.int32)


def rms_norm(value, gain):
    factor = lax.rsqrt(jnp.mean(value * value, axis=-1, keepdims=True) + epsilon)
    return value * factor * gain


def gather_rows(value):
    return lax.all_gather(value, "mp", axis=0, tiled=True)


def spread_rows(value):
    return lax.psum_scatter(value, "mp", scatter_dimension=0, tiled=True)


def matmul(left, right):
    return jnp.dot(left, right, preferred_element_type=jnp.float32)


def left_product(left, right):
    return lax.dot_general(
        left, right, (((0,), (0,)), ((), ())), preferred_element_type=jnp.float32
    )


def right_product(left, right):
    return lax.dot_general(
        left, right, (((1,), (1,)), ((), ())), preferred_element_type=jnp.float32
    )


def attend_forward(query, key_rows, value_rows, score_bias, mask):
    scores = jnp.einsum("pehd,kehd->ehpk", query, key_rows, preferred_element_type=jnp.float32)
    if score_bias is not None:
        scores = scores + score_bias[None]
    scores = jnp.where(mask, scores, masked_score)
    row_max = jnp.max(scores, axis=-1, keepdims=True)
    weights = jnp.exp(scores - row_max)
    probs = weights / jnp.sum(weights, axis=-1, keepdims=True)
    probs_low = probs.astype(jnp.bfloat16)
    output = jnp.einsum(
        "ehpk,kehd->pehd", probs_low, value_rows, preferred_element_type=jnp.float32
    )
    return (probs, probs_low, output.astype(jnp.bfloat16))


def attend_backward(query, key_rows, value_rows, probs, probs_low, grad_mixed):
    grad_probs = jnp.einsum(
        "pehd,kehd->ehpk", grad_mixed, value_rows, preferred_element_type=jnp.float32
    )
    inner_sum = jnp.sum(probs * grad_probs, axis=-1, keepdims=True)
    grad_scores = (probs * (grad_probs - inner_sum)).astype(jnp.bfloat16)
    grad_query = jnp.einsum(
        "ehpk,kehd->pehd", grad_scores, key_rows, preferred_element_type=jnp.float32
    )
    grad_keys = jnp.einsum(
        "ehpk,pehd->kehd", grad_scores, query, preferred_element_type=jnp.float32
    )
    grad_values = jnp.einsum(
        "ehpk,pehd->kehd", probs_low, grad_mixed, preferred_element_type=jnp.float32
    )
    return (
        grad_scores,
        grad_query.astype(jnp.bfloat16),
        grad_keys.astype(jnp.bfloat16),
        grad_values.astype(jnp.bfloat16),
    )


def norm_backward(value, gain, grad_normed):
    pullback = jax.vjp(rms_norm, value, gain.astype(jnp.float32))[1]
    return pullback(grad_normed)


def on_device(
    tokens,
    memory,
    cotangent,
    target_lengths,
    memory_lengths,
    norm_self,
    query_self,
    key_self,
    value_self,
    out_self,
    bias_table,
    norm_cross,
    query_cross,
    key_cross,
    value_cross,
    out_cross,
    norm_ffn,
    ffn_in,
    ffn_out,
):
    examples = target_lengths.shape[0]
    local_rows = tokens.shape[0]
    parts = lax.axis_size("mp")
    device_rank = lax.axis_index("mp")
    local_pos = local_rows // examples
    total_pos = local_pos * parts
    memory_local = memory.shape[0]
    memory_total = memory_local * parts
    memory_pos = memory_total // examples
    inner_local = query_self.shape[1]
    heads = inner_local // HEAD_DIM
    total_rows = local_rows * parts
    group_count = jnp.sum(target_lengths).astype(jnp.float32)
    total_count = lax.psum(group_count, "dp")
    token_scale = lax.axis_size("dp") * group_count / total_count
    positions = device_rank * local_pos + jnp.arange(local_pos, dtype=jnp.int32)
    live_rows = (
        (positions[:, None] < target_lengths[None, :]).astype(jnp.float32).reshape(local_rows, 1)
    )
    target_pos = jnp.arange(total_pos, dtype=jnp.int32)
    distance = jnp.maximum(target_pos[:, None] - target_pos[None, :], 0)
    buckets = jnp.sum(
        (distance[:, :, None] >= jnp.asarray(bucket_edges())[None, None, :]).astype(jnp.int32),
        axis=-1,
    )
    table_hot = (buckets[:, :, None] == jnp.arange(BUCKETS, dtype=jnp.int32)[None, None, :]).astype(
        jnp.float32
    )
    causal = target_pos[None, :] <= target_pos[:, None]
    self_mask = causal[None, None] & (
        target_pos[None, None, None, :] < target_lengths[:, None, None, None]
    )
    cross_pos = jnp.arange(memory_pos, dtype=jnp.int32)
    cross_mask = cross_pos[None, None, None, :] < memory_lengths[:, None, None, None]
    score_bias = jnp.einsum(
        "qkb,bh->hqk", table_hot, bias_table.astype(jnp.float32), precision=highest
    )

    def target_view(value):
        return value.reshape(total_pos, examples, heads, HEAD_DIM)

    def memory_view(value):
        return value.reshape(memory_pos, examples, heads, HEAD_DIM)

    tokens_float = tokens.astype(jnp.float32)
    normed_one = rms_norm(tokens_float, norm_self.astype(jnp.float32)).astype(jnp.bfloat16)
    rows_one = gather_rows(normed_one)
    self_weights = jnp.concatenate([query_self, key_self, value_self], axis=1)
    projected = matmul(rows_one, self_weights).astype(jnp.bfloat16)
    query_one = target_view(projected[:, :inner_local])
    keys_one = target_view(projected[:, inner_local : 2 * inner_local])
    values_one = target_view(projected[:, 2 * inner_local :])
    probs_one, low_one, mixed_one = attend_forward(
        query_one, keys_one, values_one, score_bias, self_mask
    )
    mixed_rows_one = mixed_one.reshape(total_rows, inner_local)
    resid_one = tokens_float + spread_rows(matmul(mixed_rows_one, out_self))
    normed_two = rms_norm(resid_one, norm_cross.astype(jnp.float32)).astype(jnp.bfloat16)
    rows_two = gather_rows(normed_two)
    query_two = target_view(matmul(rows_two, query_cross).astype(jnp.bfloat16))
    memory_all = lax.all_gather(memory, "mp", axis=0, tiled=True)
    cross_kv = matmul(memory_all, jnp.concatenate([key_cross, value_cross], axis=1)).astype(
        jnp.bfloat16
    )
    keys_flat = cross_kv[:, :inner_local]
    values_flat = cross_kv[:, inner_local:]
    keys_two = memory_view(keys_flat)
    values_two = memory_view(values_flat)
    probs_two, low_two, mixed_two = attend_forward(
        query_two, keys_two, values_two, None, cross_mask
    )
    mixed_rows_two = mixed_two.reshape(total_rows, inner_local)
    resid_two = resid_one + spread_rows(matmul(mixed_rows_two, out_cross))
    normed_three = rms_norm(resid_two, norm_ffn.astype(jnp.float32)).astype(jnp.bfloat16)
    rows_three = gather_rows(normed_three)
    pre_act = matmul(rows_three, ffn_in)
    hidden = jax.nn.gelu(pre_act).astype(jnp.bfloat16)
    block_out = resid_two + spread_rows(matmul(hidden, ffn_out))
    grad_out = cotangent.astype(jnp.float32) * live_rows * token_scale
    grad_rows_three = gather_rows(grad_out.astype(jnp.bfloat16))
    ffn_out_grad = left_product(hidden, grad_rows_three)
    grad_hidden = right_product(grad_rows_three, ffn_out)
    gelu_back = jax.vjp(jax.nn.gelu, pre_act)[1]
    grad_pre = gelu_back(grad_hidden)[0].astype(jnp.bfloat16)
    ffn_in_grad = left_product(rows_three, grad_pre)
    grad_normed_three = spread_rows(right_product(grad_pre, ffn_in))
    grad_resid_three, gain_three = norm_backward(resid_two, norm_ffn, grad_normed_three)
    grad_two = grad_out + grad_resid_three
    grad_rows_two = gather_rows(grad_two.astype(jnp.bfloat16))
    out_cross_grad = left_product(mixed_rows_two, grad_rows_two)
    grad_mixed_two = target_view(right_product(grad_rows_two, out_cross).astype(jnp.bfloat16))
    cross_back = attend_backward(
        query_two, keys_two, values_two, probs_two, low_two, grad_mixed_two
    )
    grad_query_two = cross_back[1].reshape(total_rows, inner_local)
    grad_keys_two = cross_back[2].reshape(memory_total, inner_local)
    grad_values_two = cross_back[3].reshape(memory_total, inner_local)
    query_cross_grad = left_product(rows_two, grad_query_two)
    grad_normed_two = spread_rows(right_product(grad_query_two, query_cross))
    key_cross_grad = left_product(memory_all, grad_keys_two)
    value_cross_grad = left_product(memory_all, grad_values_two)
    memory_terms = right_product(grad_keys_two, key_cross) + right_product(
        grad_values_two, value_cross
    )
    memory_grad = lax.psum_scatter(memory_terms, "mp", scatter_dimension=0, tiled=True)
    grad_resid_two, gain_two = norm_backward(resid_one, norm_cross, grad_normed_two)
    grad_one = grad_two + grad_resid_two
    grad_rows_one = gather_rows(grad_one.astype(jnp.bfloat16))
    out_self_grad = left_product(mixed_rows_one, grad_rows_one)
    grad_mixed_one = target_view(right_product(grad_rows_one, out_self).astype(jnp.bfloat16))
    self_back = attend_backward(query_one, keys_one, values_one, probs_one, low_one, grad_mixed_one)
    bias_table_grad = jnp.einsum(
        "ehqk,qkb->bh", self_back[0].astype(jnp.float32), table_hot, precision=highest
    )
    grad_projected = jnp.concatenate(
        [
            self_back[1].reshape(total_rows, inner_local),
            self_back[2].reshape(total_rows, inner_local),
            self_back[3].reshape(total_rows, inner_local),
        ],
        axis=1,
    )
    self_weight_grad = left_product(rows_one, grad_projected)
    grad_normed_one = spread_rows(right_product(grad_projected, self_weights))
    grad_resid_one, gain_one = norm_backward(tokens_float, norm_self, grad_normed_one)
    tokens_grad = grad_one + grad_resid_one
    summed = lax.psum(
        (
            self_weight_grad[:, :inner_local],
            self_weight_grad[:, inner_local : 2 * inner_local],
            self_weight_grad[:, 2 * inner_local :],
            out_self_grad,
            bias_table_grad,
            query_cross_grad,
            key_cross_grad,
            value_cross_grad,
            out_cross_grad,
            ffn_in_grad,
            ffn_out_grad,
        ),
        "dp",
    )
    gains = lax.psum((gain_one, gain_two, gain_three), ("dp", "mp"))
    return (
        block_out.astype(jnp.bfloat16),
        tokens_grad.astype(jnp.bfloat16),
        memory_grad.astype(jnp.bfloat16),
        gains[0],
        summed[0],
        summed[1],
        summed[2],
        summed[3],
        summed[4],
        gains[1],
        summed[5],
        summed[6],
        summed[7],
        summed[8],
        gains[2],
        summed[9],
        summed[10],
    )


def links(dp_size):
    total = 2 * dp_size

    def swap(bit):
        return [(at, at ^ bit) for at in range(total)]

    def off_swap(bit):
        return [(at, at ^ bit) for at in range(total) if (at & 1) != ((at >> 1) & 1)]

    def turned(at):
        return (at & ~3) | ((at & 1) << 1) | ((at >> 1) & 1)

    def crossed(at):
        return (at & ~3) | ((1 - (at & 1)) << 1) | ((at >> 1) & 1)

    return {
        "turn": [(at, turned(at)) for at in range(total) if at != turned(at)],
        "cross": [(at, crossed(at)) for at in range(total)],
        "y": swap(1),
        "core": swap(2),
        "x": swap(4),
        "zl": swap(8),
        "zh": swap(16),
        "off_x": off_swap(4),
        "off_zl": off_swap(8),
    }


def permute(value, pairs):
    return lax.ppermute(value, ("dp", "mp"), pairs)


def reorder_kernel(inverse, examples, info, held, arrived, target):
    def write(source):
        if inverse:
            value = source[...].reshape(-1, source.shape[2])
        else:
            value = source[...]
        rows = value.shape[0]
        chunk = rows // examples
        high = lax.broadcasted_iota(jnp.int32, (rows, rows), 0)
        low = lax.broadcasted_iota(jnp.int32, (rows, rows), 1)
        if inverse:
            hot = low == (high % examples) * chunk + high // examples
        else:
            hot = low == (high % chunk) * examples + high // chunk
        moved = nn(hot.astype(jnp.bfloat16), value).astype(jnp.bfloat16)
        target[...] = moved.reshape(target.shape)

    @pl.when(info[0] == 1)
    def _():
        write(held)

    @pl.when(info[0] == 0)
    def _():
        write(arrived)


def reorder(inverse, held, arrived, settled, examples):
    rows, width = held.shape
    block = 256
    flat = pl.BlockSpec((block, width), lambda i, s: (i, 0))
    flat_shape = (rows, width)
    split_shape = (examples, rows // examples, width)
    split_block = (examples, block // examples, width)
    if inverse:
        held, arrived = held.reshape(split_shape), arrived.reshape(split_shape)
        in_specs = [
            pl.BlockSpec(split_block, lambda i, s: (0, i * s[0], 0)),
            pl.BlockSpec(split_block, lambda i, s: (0, i * (1 - s[0]), 0)),
        ]
        out_spec, out_shape = flat, flat_shape
    else:
        in_specs = [
            pl.BlockSpec((block, width), lambda i, s: (i * s[0], 0)),
            pl.BlockSpec((block, width), lambda i, s: (i * (1 - s[0]), 0)),
        ]
        out_spec = pl.BlockSpec(split_block, lambda i, s: (0, i, 0))
        out_shape = split_shape
    return pl.pallas_call(
        functools.partial(reorder_kernel, inverse, examples),
        grid_spec=pltpu.PrefetchScalarGridSpec(
            num_scalar_prefetch=1,
            grid=(rows // block,),
            in_specs=in_specs,
            out_specs=out_spec,
        ),
        out_shape=jax.ShapeDtypeStruct(out_shape, held.dtype),
        cost_estimate=cost(2 * rows * width * block, 4 * rows * width),
        compiler_params=pltpu.CompilerParams(vmem_limit_bytes=SMALL_VMEM),
    )(settled, held, arrived).reshape(flat_shape)


def nt(left, right):
    return lax.dot_general(
        left, right, (((1,), (1,)), ((), ())), preferred_element_type=jnp.float32
    )


def tn(left, right):
    return lax.dot_general(
        left, right, (((0,), (0,)), ((), ())), preferred_element_type=jnp.float32
    )


def nn(left, right):
    return jnp.dot(left, right, preferred_element_type=jnp.float32)


def one_head(value, head):
    lane = lax.broadcasted_iota(jnp.int32, value.shape, 1)
    return jnp.where(lane // HEAD_DIM == head, value, jnp.zeros_like(value))


def softmax_columns(scores):
    top = jnp.max(scores, axis=0, keepdims=True)
    weights = jnp.exp(scores - top)
    return weights * (1.0 / jnp.sum(weights, axis=0, keepdims=True))


def toeplitz(row, size):
    return pltpu.roll(jnp.broadcast_to(row, (size, size)), 0, 1, stride=1, stride_axis=0)


def diagonals(square):
    size = square.shape[0]
    row = lax.broadcasted_iota(jnp.int32, square.shape, 0)
    turned, step = square, 1
    while step < size:
        moved = pltpu.roll(turned, size - step, 1)
        turned = jnp.where((row & step) != 0, moved, turned)
        step *= 2
    return jnp.sum(turned, axis=0, keepdims=True)


def ordered(core, scratch, own, far):
    half = own.shape[0]
    scratch[pl.ds(pl.multiple_of(core * half, half), half), :] = own
    scratch[pl.ds(pl.multiple_of((1 - core) * half, half), half), :] = far
    return scratch[...]


def split_store(core, scratch, value, out):
    half = out.shape[1]
    scratch[...] = value
    out[0] = scratch[pl.ds(pl.multiple_of(core * half, half), half), :]
    out[1] = scratch[pl.ds(pl.multiple_of((1 - core) * half, half), half), :]


def self_scores(query, keys, bias, head, length):
    scores = nt(keys, one_head(query, head)) + bias
    key_at = lax.broadcasted_iota(jnp.int32, scores.shape, 0)
    query_at = lax.broadcasted_iota(jnp.int32, scores.shape, 1)
    return jnp.where((key_at <= query_at) & (key_at < length), scores, masked_score)


def heads_joined(first, second):
    return jnp.concatenate([first[:HEAD_DIM], second[HEAD_DIM:]], axis=0).T


def self_forward_kernel(info, rows, bias, out, scratch, out_scratch, bias_scratch):
    core = info[0]
    example = pl.program_id(1)
    length = info[1 + example]
    size = scratch.shape[0]

    @pl.when(example == 0)
    def _():
        for head in range(2):
            bias_scratch[head] = toeplitz(bias[0, head : head + 1, :], size)

    joined = ordered(core, scratch, rows[0], rows[1])
    query, keys, values = joined[:, :128], joined[:, 128:256], joined[:, 256:]
    mixed = []
    for head in range(2):
        probs = softmax_columns(self_scores(query, keys, bias_scratch[head], head, length))
        mixed.append(tn(values, probs.astype(jnp.bfloat16)))
    result = heads_joined(*mixed).astype(jnp.bfloat16)
    split_store(core, out_scratch, result, out)


def self_backward_kernel(
    info,
    rows,
    bias,
    grads,
    out,
    out_bias,
    scratch,
    grad_scratch,
    out_scratch,
    bias_scratch,
    sum_scratch,
):
    core = info[0]
    example = pl.program_id(1)
    length = info[1 + example]
    size = scratch.shape[0]

    @pl.when(example == 0)
    def _():
        for head in range(2):
            bias_scratch[head] = toeplitz(bias[0, head : head + 1, :], size)
        sum_scratch[...] = jnp.zeros_like(sum_scratch)

    joined = ordered(core, scratch, rows[0], rows[1])
    query, keys, values = joined[:, :128], joined[:, 128:256], joined[:, 256:]
    grad = ordered(core, grad_scratch, grads[0], grads[1])
    grad_query, grad_keys, grad_values, squares = [], [], [], []
    for head in range(2):
        probs = softmax_columns(self_scores(query, keys, bias_scratch[head], head, length))
        low = probs.astype(jnp.bfloat16)
        grad_head = one_head(grad, head)
        grad_probs = nt(values, grad_head)
        inner = jnp.sum(probs * grad_probs, axis=0, keepdims=True)
        grad_scores = (probs * (grad_probs - inner)).astype(jnp.bfloat16)
        grad_values.append(nn(low, grad_head))
        grad_keys.append(nn(grad_scores, one_head(query, head)))
        grad_query.append(tn(keys, grad_scores))
        squares.append(grad_scores.astype(jnp.float32))
    for head in range(2):
        sum_scratch[head] = sum_scratch[head] + squares[head]
    result = jnp.concatenate(
        [
            heads_joined(*grad_query),
            grad_keys[0] + grad_keys[1],
            grad_values[0] + grad_values[1],
        ],
        axis=1,
    ).astype(jnp.bfloat16)
    split_store(core, out_scratch, result, out)

    @pl.when(example == pl.num_programs(1) - 1)
    def _():
        for head in range(2):
            out_bias[0, head : head + 1, :] = diagonals(sum_scratch[head])


def cross_scores(query, keys, head, core, length):
    scores = nt(keys, one_head(query, head))
    size = scores.shape[0]
    key_at = lax.broadcasted_iota(jnp.int32, scores.shape, 0)
    key_at = (key_at + core * (size // 2)) & (size - 1)
    return jnp.where(key_at < length, scores, masked_score)


def cross_forward_kernel(info, queries, kv_own, kv_far, out):
    core = info[0]
    length = info[1 + pl.program_id(0)]
    query = queries[...].reshape(-1, 128)
    keys = jnp.concatenate([kv_own[:, :128], kv_far[:, :128]], axis=0)
    values = jnp.concatenate([kv_own[:, 128:], kv_far[:, 128:]], axis=0)
    mixed = []
    for head in range(2):
        probs = softmax_columns(cross_scores(query, keys, head, core, length))
        mixed.append(tn(values, probs.astype(jnp.bfloat16)))
    out[...] = heads_joined(*mixed).astype(jnp.bfloat16).reshape(out.shape)


def cross_backward_kernel(info, queries, kv_own, kv_far, grads, dq, dkv_own, dkv_far):
    core = info[0]
    length = info[1 + pl.program_id(0)]
    query = queries[...].reshape(-1, 128)
    grad = grads[...].reshape(-1, 128)
    keys = jnp.concatenate([kv_own[:, :128], kv_far[:, :128]], axis=0)
    values = jnp.concatenate([kv_own[:, 128:], kv_far[:, 128:]], axis=0)
    grad_query, grad_keys, grad_values = [], [], []
    for head in range(2):
        probs = softmax_columns(cross_scores(query, keys, head, core, length))
        low = probs.astype(jnp.bfloat16)
        grad_head = one_head(grad, head)
        grad_probs = nt(values, grad_head)
        inner = jnp.sum(probs * grad_probs, axis=0, keepdims=True)
        grad_scores = (probs * (grad_probs - inner)).astype(jnp.bfloat16)
        grad_values.append(nn(low, grad_head))
        grad_keys.append(nn(grad_scores, one_head(query, head)))
        grad_query.append(tn(keys, grad_scores))
    dq[...] = heads_joined(*grad_query).astype(jnp.bfloat16).reshape(dq.shape)
    result = jnp.concatenate(
        [grad_keys[0] + grad_keys[1], grad_values[0] + grad_values[1]], axis=1
    ).astype(jnp.bfloat16)
    half = dkv_own.shape[0]
    dkv_own[...] = result[:half]
    dkv_far[...] = result[half:]


MIB = 1024 * 1024


def cost(flops, moved, exps=0):
    return pl.CostEstimate(
        flops=int(flops), bytes_accessed=int(moved), transcendentals=int(exps)
    )


SMALL_VMEM = 12 * MIB
ATTEND_VMEM = 24 * MIB
FFN_VMEM = 44 * MIB
SETTLE_VMEM = 48 * MIB
MESH = pl.DeviceIdType.MESH
SMEM_SPEC = pl.BlockSpec(memory_space=pltpu.SMEM)


def self_forward(info, rows, bias, examples):
    _, count, width = rows.shape
    pairs, size = width // 384, count // examples
    return pl.pallas_call(
        self_forward_kernel,
        grid=(pairs, examples),
        in_specs=[
            SMEM_SPEC,
            pl.BlockSpec((2, size, 384), lambda h, e: (0, e, h)),
            pl.BlockSpec((1, 2, 2 * size), lambda h, e: (h, 0, 0)),
        ],
        out_specs=pl.BlockSpec((2, size, 128), lambda h, e: (0, e, h)),
        out_shape=jax.ShapeDtypeStruct((2, count, pairs * 128), jnp.bfloat16),
        scratch_shapes=[
            pltpu.VMEM((2 * size, 384), jnp.bfloat16),
            pltpu.VMEM((2 * size, 128), jnp.bfloat16),
            pltpu.VMEM((2, 2 * size, 2 * size), jnp.float32),
        ],
        cost_estimate=cost(2 * 2 * examples * 2 * pairs * (2 * size) ** 2 * 256 * 8, 8 * rows.size, examples * 2 * pairs * (2 * size) ** 2),
        compiler_params=pltpu.CompilerParams(vmem_limit_bytes=SMALL_VMEM),
    )(info, rows, bias)


def self_backward(info, rows, bias, grads, examples):
    _, count, width = rows.shape
    pairs, size = width // 384, count // examples
    row = pl.BlockSpec((1, 2, 2 * size), lambda h, e: (h, 0, 0))
    wide = pl.BlockSpec((2, size, 384), lambda h, e: (0, e, h))
    return pl.pallas_call(
        self_backward_kernel,
        grid=(pairs, examples),
        in_specs=[
            SMEM_SPEC,
            wide,
            row,
            pl.BlockSpec((2, size, 128), lambda h, e: (0, e, h)),
        ],
        out_specs=[wide, row],
        out_shape=[
            jax.ShapeDtypeStruct(rows.shape, jnp.bfloat16),
            jax.ShapeDtypeStruct((pairs, 2, 2 * size), jnp.float32),
        ],
        scratch_shapes=[
            pltpu.VMEM((2 * size, 384), jnp.bfloat16),
            pltpu.VMEM((2 * size, 128), jnp.bfloat16),
            pltpu.VMEM((2 * size, 384), jnp.bfloat16),
            pltpu.VMEM((2, 2 * size, 2 * size), jnp.float32),
            pltpu.VMEM((2, 2 * size, 2 * size), jnp.float32),
        ],
        cost_estimate=cost(5 * 2 * examples * 2 * pairs * (2 * size) ** 2 * 256 * 8, 12 * rows.size, examples * 2 * pairs * (2 * size) ** 2),
        compiler_params=pltpu.CompilerParams(vmem_limit_bytes=SMALL_VMEM),
    )(info, rows, bias, grads)


def cross_forward(info, queries, kv_own, kv_far, examples):
    _, count, width = queries.shape
    pairs, size, span = width // 128, count // examples, kv_own.shape[0] // examples
    thin = pl.BlockSpec((2, size, 128), lambda e, h: (0, e, h))
    wide = pl.BlockSpec((span, 256), lambda e, h: (e, h))
    return pl.pallas_call(
        cross_forward_kernel,
        grid=(examples, pairs),
        in_specs=[SMEM_SPEC, thin, wide, wide],
        out_specs=thin,
        out_shape=jax.ShapeDtypeStruct(queries.shape, jnp.bfloat16),
        cost_estimate=cost(2 * 2 * examples * 2 * pairs * 4 * size * span * 256 * 4, 8 * kv_own.size, examples * 2 * pairs * 4 * size * span),
        compiler_params=pltpu.CompilerParams(vmem_limit_bytes=ATTEND_VMEM),
    )(info, queries, kv_own, kv_far)


def cross_backward(info, queries, kv_own, kv_far, grads, examples):
    _, count, width = queries.shape
    pairs, size, span = width // 128, count // examples, kv_own.shape[0] // examples
    thin = pl.BlockSpec((2, size, 128), lambda e, h: (0, e, h))
    wide = pl.BlockSpec((span, 256), lambda e, h: (e, h))
    return pl.pallas_call(
        cross_backward_kernel,
        grid=(examples, pairs),
        in_specs=[SMEM_SPEC, thin, wide, wide, thin],
        out_specs=[thin, wide, wide],
        out_shape=[jax.ShapeDtypeStruct(queries.shape, jnp.bfloat16)]
        + [jax.ShapeDtypeStruct(kv_own.shape, jnp.bfloat16)] * 2,
        cost_estimate=cost(5 * 2 * examples * 2 * pairs * 4 * size * span * 256 * 2, 12 * kv_own.size, examples * 2 * pairs * 4 * size * span),
        compiler_params=pltpu.CompilerParams(vmem_limit_bytes=ATTEND_VMEM),
    )(info, queries, kv_own, kv_far, grads)


root = math.sqrt(2.0 / math.pi)
cubic = 0.044715


def ffn_kernel(
    n_own,
    n_far,
    g_own,
    g_far,
    into,
    outof,
    out_own,
    out_far,
    dn_own,
    dn_far,
    outof_grad,
    into_grad,
    turned,
    out_sum,
    dn_sum,
):
    step = pl.program_id(0)
    half = n_own.shape[0]

    @pl.when(step == 0)
    def _():
        turned[:, :half] = n_own[...].T
        turned[:, half:] = n_far[...].T
        out_own[...] = jnp.zeros_like(out_own)
        dn_own[...] = jnp.zeros_like(dn_own)
        out_sum[...] = jnp.zeros_like(out_sum)
        dn_sum[...] = jnp.zeros_like(dn_sum)

    grads, backs = [], []
    for normed, grad, out, back in (
        (n_own, g_own, out_own, dn_own),
        (n_far, g_far, out_sum, dn_sum),
    ):
        pre = nn(normed[...], into[...])
        grad_hidden = nt(grad[...], outof[...])
        bend = jnp.tanh(root * (pre + cubic * (pre * pre * pre)))
        hidden = (0.5 * pre * (1.0 + bend)).astype(jnp.bfloat16)
        slope = 0.5 * (1.0 + bend) + 0.5 * pre * (1.0 - bend * bend) * (
            root * (1.0 + 3.0 * cubic * (pre * pre))
        )
        grad_pre = (grad_hidden * slope).astype(jnp.bfloat16)
        out[...] += nn(hidden, outof[...])
        back[...] += nt(grad_pre, into[...])
        grads.append(tn(hidden, grad[...]))
        backs.append(nn(turned[:, : half] if normed is n_own else turned[:, half:], grad_pre))
    outof_grad[...] = (grads[0] + grads[1]).astype(jnp.bfloat16)
    into_grad[...] = (backs[0] + backs[1]).astype(jnp.bfloat16)

    @pl.when(step == pl.num_programs(0) - 1)
    def _():
        out_far[...] = out_sum[...].astype(jnp.bfloat16)
        dn_far[...] = dn_sum[...].astype(jnp.bfloat16)


def ffn(n_own, n_far, g_own, g_far, into, outof):
    rows, width = n_own.shape
    units = into.shape[1]
    tile = 256
    whole = pl.BlockSpec((rows, width), lambda i: (0, 0))
    tall = pl.BlockSpec((width, tile), lambda i: (0, i))
    flat = pl.BlockSpec((tile, width), lambda i: (i, 0))
    wide = jax.ShapeDtypeStruct((rows, width), jnp.float32)
    thin = jax.ShapeDtypeStruct((rows, width), jnp.bfloat16)
    return pl.pallas_call(
        ffn_kernel,
        grid=(units // tile,),
        in_specs=[whole, whole, whole, whole, tall, flat],
        out_specs=[whole, whole, whole, whole, flat, tall],
        out_shape=[
            wide,
            thin,
            wide,
            thin,
            jax.ShapeDtypeStruct(outof.shape, jnp.bfloat16),
            jax.ShapeDtypeStruct(into.shape, jnp.bfloat16),
        ],
        scratch_shapes=[
            pltpu.VMEM((width, 2 * rows), jnp.bfloat16),
            pltpu.VMEM((rows, width), jnp.float32),
            pltpu.VMEM((rows, width), jnp.float32),
        ],
        cost_estimate=cost(6 * 2 * 2 * rows * width * units, 24 * rows * width + 8 * width * units, 2 * rows * units),
        compiler_params=pltpu.CompilerParams(vmem_limit_bytes=FFN_VMEM),
    )(n_own, n_far, g_own, g_far, into, outof)


def assemble_kernel(count, moves, info, *refs):
    held, pair, far, targets = refs[:count], refs[count], refs[count + 1], refs[count + 2 :]
    part = pl.program_id(0) ^ info[0]

    @pl.when(info[1] == 1)
    def _():
        for source, column, _, _, target, at, columns in moves:
            targets[target][:, at : at + columns] = held[source][:, column : column + columns]

    def write(ref):
        for _, _, row, start, target, at, columns in moves:
            rows = targets[target].shape[0]
            targets[target][:, at : at + columns] = ref[
                0, row : row + rows, start : start + columns
            ]

    @pl.when((info[1] == 0) & ((part & 1) == 0))
    def _():
        write(pair)

    @pl.when((info[1] == 0) & ((part & 1) == 1))
    def _():
        write(far)


def bring(weights, pack, shapes, moves, place, net):
    mine = place["x"] * 2 + place["zl"]
    quarters = [
        lax.dynamic_slice_in_dim(w, mine * (w.shape[0] // 4), w.shape[0] // 4, 0)
        for w in weights
    ]
    first = permute(pack(*quarters)[None], net["turn"])
    pair = jnp.concatenate([first, permute(first, net["off_x"])], axis=0)
    far = permute(pair, net["off_zl"])
    info = jnp.stack([mine, place["settled"][0]])
    block = (1,) + first.shape[1:]

    def at(i, s):
        return ((i ^ s[0]) >> 1, 0, 0)

    return pl.pallas_call(
        functools.partial(assemble_kernel, len(weights), moves),
        grid_spec=pltpu.PrefetchScalarGridSpec(
            num_scalar_prefetch=1,
            grid=(4,),
            in_specs=[
                pl.BlockSpec((w.shape[0] // 4, w.shape[1]), lambda i, s: (i * s[1], 0))
                for w in weights
            ]
            + [pl.BlockSpec(block, at)] * 2,
            out_specs=[
                pl.BlockSpec((shape[0] // 4, shape[1]), lambda i, s: (i, 0)) for shape in shapes
            ],
        ),
        out_shape=[jax.ShapeDtypeStruct(shape, jnp.bfloat16) for shape in shapes],
        cost_estimate=cost(0, 4 * sum(w.size for w in weights)),
        compiler_params=pltpu.CompilerParams(vmem_limit_bytes=ATTEND_VMEM),
    )(info, *weights, pair, far)


def add_low(left, right):
    return (left.astype(jnp.float32) + right.astype(jnp.float32)).astype(jnp.bfloat16)


def pick(value, index):
    return lax.dynamic_index_in_dim(value, index, 0, keepdims=False)


def halve(total, name, place, net):
    view = total.reshape(2, total.shape[0] // 2, *total.shape[1:])
    sent = permute(pick(view, 1 - place[name]), net[name])
    return add_low(pick(view, place[name]), sent)


def spread_back(total, order, net):
    for name in reversed(order):
        total = jnp.concatenate([total, permute(total, net[name])], axis=0)
    return total, permute(total, net["core"])


def reduce_units(value, order, place, net):
    total = halve(value, "core", place, net)
    for name in order:
        total = halve(total, name, place, net)
    return spread_back(total, order, net)


def settle_kernel(groups, value, out, first, second, third, send, receive):
    index, y = lax.axis_index("dp"), lax.axis_index("mp")
    core, x, z = index % 2, (index // 2) % 2, index // 4
    deep = groups // 4
    chunks, rows = first.shape[0], first.shape[3]

    def at(c, yy, xx, zz):
        return (zz * 4 + xx * 2 + c, yy)

    def part(k):
        return pl.ds(pl.multiple_of(k * rows, rows), rows)

    partners = [at(1 - core, y, x, z), at(core, 1 - y, x, z), at(1 - core, 1 - y, x, z)]
    partners.append(at(core, y, 1 - x, z))
    for step in range(1, deep):
        partners.append(at(core, y, x, (z + step) % deep))
    barrier = pltpu.get_barrier_semaphore()
    for partner in partners:
        pl.semaphore_signal(barrier, inc=1, device_id=partner, device_id_type=MESH)
    pl.semaphore_wait(barrier, len(partners))

    def copy(source, target, slot, k, device):
        return pltpu.make_async_remote_copy(
            src_ref=source,
            dst_ref=target,
            send_sem=send.at[k, slot],
            recv_sem=receive.at[k, slot],
            device_id=device,
            device_id_type=MESH,
        )

    def quarter(k, q):
        return value.at[pl.ds(q * 8, 8), part(k)]

    def to_core(k):
        return copy(quarter(k, 1 - core), first.at[k, 0], 0, k, at(1 - core, core, x, z))

    def to_turned(k):
        return copy(quarter(k, 1 - core), first.at[k, 1], 1, k, at(1 - core, core, x, z))

    def to_same(k):
        return copy(quarter(k, core), first.at[k, 1], 2, k, at(core, core, x, z))

    def arrived(k, slot):
        return copy(quarter(k, core), first.at[k, 1 if slot else 0], slot, k, at(1 - core, y, x, z))

    def along_x(k):
        return copy(
            first.at[k, 1, pl.ds((1 - x) * 4, 4)], second.at[k], 3, k, at(core, y, 1 - x, z)
        )

    def along_z(k, step):
        far = (z + step) % deep
        return copy(
            second.at[k, far], third.at[k, step - 1], 3 + step, k, at(core, y, x, far)
        )

    def back_z(k, step):
        far = (z + step) % deep
        piece = core * 8 + x * 4 + z
        return copy(
            out.at[piece, part(k)], out.at[piece, part(k)], 6 + step, k, at(core, y, x, far)
        )

    def back_x(k):
        held = out.at[pl.ds(core * 8 + x * 4, 4), part(k)]
        return copy(held, held, 10, k, at(core, y, 1 - x, z))

    def back_core(k):
        held = out.at[pl.ds(core * 8, 8), part(k)]
        return copy(held, held, 11, k, at(1 - core, y, x, z))

    def start(k, carry):
        @pl.when(core == y)
        def _():
            to_core(k).start()

        @pl.when(core != y)
        def _():
            to_same(k).start()
            to_turned(k).start()

        return carry

    lax.fori_loop(0, chunks, start, 0)

    def total(left, right):
        return (left.astype(jnp.float32) + right.astype(jnp.float32)).astype(jnp.bfloat16)

    def tick(t, carry):
        @pl.when(t < chunks)
        def _():
            k = jnp.minimum(t, chunks - 1)

            @pl.when(core == y)
            def _():
                arrived(k, 2).wait_recv()

                def add(i, c):
                    first[k, 1, i] = total(value[core * 8 + i, part(k)], first[k, 1, i])
                    return c

                lax.fori_loop(0, 8, add, 0)

            @pl.when(core != y)
            def _():
                arrived(k, 0).wait_recv()
                arrived(k, 1).wait_recv()

                def add(i, c):
                    first[k, 1, i] = total(first[k, 0, i], first[k, 1, i])
                    return c

                lax.fori_loop(0, 8, add, 0)

            along_x(k).start()

        @pl.when((t >= 1) & (t < chunks + 1))
        def _():
            k = t - 1
            along_x(k).wait_recv()

            def add(i, c):
                second[k, i] = total(first[k, 1, x * 4 + i], second[k, i])
                return c

            lax.fori_loop(0, deep, add, 0)
            for step in range(1, deep):
                along_z(k, step).start()

        @pl.when((t >= 2) & (t < chunks + 2))
        def _():
            k = t - 2
            for step in range(1, deep):
                along_z(k, step).wait_recv()
            summed = second[k, z].astype(jnp.float32)
            for step in range(1, deep):
                summed = summed + third[k, step - 1].astype(jnp.float32)
            out[core * 8 + x * 4 + z, part(k)] = summed.astype(jnp.bfloat16)
            for step in range(1, deep):
                back_z(k, step).start()

        @pl.when((t >= 3) & (t < chunks + 3))
        def _():
            k = t - 3
            for step in range(1, deep):
                back_z(k, step).wait_recv()
            back_x(k).start()

        @pl.when((t >= 4) & (t < chunks + 4))
        def _():
            k = t - 4
            back_x(k).wait_recv()
            back_core(k).start()

        @pl.when(t >= 5)
        def _():
            back_core(t - 5).wait_recv()

        return carry

    lax.fori_loop(0, chunks + 5, tick, 0)

    def finish_sends(k, carry):
        @pl.when(core == y)
        def _():
            to_core(k).wait_send()

        @pl.when(core != y)
        def _():
            to_same(k).wait_send()
            to_turned(k).wait_send()

        along_x(k).wait_send()
        for step in range(1, deep):
            along_z(k, step).wait_send()
            back_z(k, step).wait_send()
        back_x(k).wait_send()
        back_core(k).wait_send()
        return carry

    lax.fori_loop(0, chunks, finish_sends, 0)


def settle(value, groups):
    count, rows, width = value.shape
    chunk = 32
    chunks = rows // chunk
    deep = groups // 4
    whole = pl.BlockSpec(memory_space=pltpu.VMEM)
    return pl.pallas_call(
        functools.partial(settle_kernel, groups),
        in_specs=[whole],
        out_specs=whole,
        out_shape=jax.ShapeDtypeStruct(value.shape, value.dtype),
        scratch_shapes=[
            pltpu.VMEM((chunks, 2, count // 2, chunk, width), value.dtype),
            pltpu.VMEM((chunks, deep, chunk, width), value.dtype),
            pltpu.VMEM((chunks, deep - 1, chunk, width), value.dtype),
            pltpu.SemaphoreType.DMA((chunks, 12)),
            pltpu.SemaphoreType.DMA((chunks, 12)),
        ],
        cost_estimate=cost(0, 60 * value.size),
        compiler_params=pltpu.CompilerParams(
            collective_id=0, has_side_effects=True, vmem_limit_bytes=SETTLE_VMEM
        ),
    )(value)


def unpack_kernel(pairs, source, key, val, cross_out, self_out, cross_q, *self_in):
    wide = key.shape[0] // 4
    thin = cross_out.shape[0] // 4

    def taken(row, rows):
        block = source[:, row : row + rows, :].astype(jnp.float32)
        return block.reshape(4 * rows, block.shape[2])

    kv = taken(0, wide)
    for i in range(pairs):
        key[:, 128 * i : 128 * i + 128] = kv[:, 256 * i : 256 * i + 128]
        val[:, 128 * i : 128 * i + 128] = kv[:, 256 * i + 128 : 256 * i + 256]
    cross_out[...] = taken(wide, thin)
    self_out[...] = taken(wide + thin, thin)
    cross_q[...] = taken(wide + 2 * thin, thin).T
    rest = taken(wide + 3 * thin, 3 * thin)
    for i in range(3):
        self_in[i][...] = rest[4 * thin * i : 4 * thin * (i + 1)].T


def unpack(value, inner):
    count, rows, width = value.shape
    tall = jax.ShapeDtypeStruct((width, inner), jnp.float32)
    flat = jax.ShapeDtypeStruct((inner, width), jnp.float32)
    by_row = pl.BlockSpec((width // 4, inner), lambda i: (i, 0))
    by_out = pl.BlockSpec((inner // 4, width), lambda i: (i, 0))
    by_column = pl.BlockSpec((width, inner // 4), lambda i: (0, i))
    return pl.pallas_call(
        functools.partial(unpack_kernel, inner // 128),
        grid=(4,),
        in_specs=[pl.BlockSpec((4, rows, width), lambda i: (i, 0, 0))],
        out_specs=[by_row, by_row, by_out, by_out] + [by_column] * 4,
        out_shape=[tall, tall, flat, flat] + [tall] * 4,
        cost_estimate=cost(0, 6 * value.size),
        compiler_params=pltpu.CompilerParams(vmem_limit_bytes=ATTEND_VMEM),
    )(value)


def finish_kernel(layout, info, own, other, *targets):
    mine = (pl.program_id(0) >> 3) == info[1]

    def write(source):
        for target, moves in zip(targets, layout):
            for row, rows, column, columns, at in moves:
                target[:, at : at + columns] = source[
                    0, row : row + rows, column : column + columns
                ].astype(jnp.float32)

    @pl.when(mine)
    def _():
        write(own)

    @pl.when(jnp.logical_not(mine))
    def _():
        write(other)


def finish(done, order, place, shapes, layout):
    own, other = done
    count, rows, width = own.shape
    mine = place[order[0]] * 4 + place[order[1]] * 2 + place[order[2]]
    info = jnp.stack([mine, place["core"]])

    def at(held):
        def index(i, s):
            used = ((i >> 3) == s[1]) == held
            return (jnp.where(used, (i & 7) ^ s[0], s[0]), 0, 0)

        return index

    return pl.pallas_call(
        functools.partial(finish_kernel, layout),
        grid_spec=pltpu.PrefetchScalarGridSpec(
            num_scalar_prefetch=1,
            grid=(2 * count,),
            in_specs=[
                pl.BlockSpec((1, rows, width), at(True)),
                pl.BlockSpec((1, rows, width), at(False)),
            ],
            out_specs=[
                pl.BlockSpec((shape[0] // (2 * count), shape[1]), lambda i, s: (i, 0))
                for shape in shapes
            ],
        ),
        out_shape=[jax.ShapeDtypeStruct(shape, jnp.float32) for shape in shapes],
        cost_estimate=cost(0, 4 * own.size * 6),
        compiler_params=pltpu.CompilerParams(vmem_limit_bytes=ATTEND_VMEM),
    )(info, own, other)


def pieces(*values):
    split = [v.reshape(16, v.shape[0] // 16, v.shape[1]) for v in values]
    return split[0] if len(split) == 1 else jnp.concatenate(split, axis=1)


def low(value):
    return value.astype(jnp.bfloat16)


def on_chip_group(
    tokens,
    memory,
    cotangent,
    target_lengths,
    memory_lengths,
    norm_self,
    query_self,
    key_self,
    value_self,
    out_self,
    bias_table,
    norm_cross,
    query_cross,
    key_cross,
    value_cross,
    out_cross,
    norm_ffn,
    ffn_in,
    ffn_out,
):
    examples = target_lengths.shape[0]
    groups = lax.axis_size("dp")
    net = links(groups)
    index = lax.axis_index("dp")
    place = {
        "y": lax.axis_index("mp"),
        "core": index & 1,
        "x": (index >> 1) & 1,
        "zl": (index >> 2) & 1,
        "zh": (index >> 3) & 1,
    }
    core = place["core"]
    settled = (core == place["y"]).astype(jnp.int32)
    place["settled"] = settled[None]
    rows, width = tokens.shape
    half_pos = rows // examples
    inner = query_self.shape[1]
    pairs = inner // 128

    def swap(value):
        return permute(value, net["core"])

    def both(value):
        return jnp.stack([value, swap(value)])

    def flat(value):
        return value.reshape(-1, value.shape[2])

    def turn(value):
        return permute(value, net["turn"])

    tok_raw = turn(tokens)
    qkv_moves = [
        (i, 128 * h, 0, inner * i + 128 * h, 0, 384 * h + 128 * i, 128)
        for h in range(pairs)
        for i in range(3)
    ]
    self_in, cross_q = bring(
        [query_self, key_self, value_self, query_cross],
        lambda *w: jnp.concatenate(w, axis=1),
        [(width, 3 * inner), (width, inner)],
        qkv_moves + [(3, 0, 0, 3 * inner, 1, 0, inner)],
        place,
        net,
    )
    kv_moves = [
        (i, 128 * h, 0, inner * i + 128 * h, 0, 256 * h + 128 * i, 128)
        for h in range(pairs)
        for i in range(2)
    ]
    quarter, thin = width // 4, inner // 4
    cross_kv, self_out, cross_out = bring(
        [key_cross, value_cross, out_self, out_cross],
        lambda k, v, a, b: jnp.concatenate([jnp.concatenate([k, v], axis=1), a, b], axis=0),
        [(width, 2 * inner), (inner, width), (inner, width)],
        kv_moves + [(2, 0, quarter, 0, 1, 0, width), (3, 0, quarter + thin, 0, 2, 0, width)],
        place,
        net,
    )
    mem_raw = turn(memory)
    cot_raw = turn(cotangent)
    facts = jnp.concatenate(
        [
            target_lengths.astype(jnp.float32),
            memory_lengths.astype(jnp.float32),
            bias_table.astype(jnp.float32).reshape(-1),
        ]
    )
    facts = jnp.where(settled == 1, facts, turn(facts))
    target_len = facts[:examples].astype(jnp.int32)
    memory_len = facts[examples : 2 * examples].astype(jnp.int32)
    table = facts[2 * examples :].reshape(bias_table.shape)
    group_count = jnp.sum(target_len).astype(jnp.float32)
    total_count = group_count.reshape(1, 1)
    for name in ("y", "x", "zl", "zh"):
        total_count = total_count + permute(total_count, net[name])
    token_scale = groups * group_count / total_count[0, 0]
    self_info = jnp.concatenate([core[None], target_len])
    cross_info = jnp.concatenate([core[None], memory_len])
    tok = reorder(False, tokens, tok_raw, place["settled"], examples)

    span = 2 * half_pos
    distance = jnp.arange(span, dtype=jnp.int32)
    level = jnp.sum(
        (distance[:, None] >= jnp.asarray(bucket_edges())[None, :]).astype(jnp.int32), axis=-1
    )
    level_hot = (level[:, None] == jnp.arange(BUCKETS, dtype=jnp.int32)[None, :]).astype(
        jnp.float32
    )
    bias = jnp.einsum("db,bh->hd", level_hot, table, precision=highest).reshape(-1, 2, span)

    tok_float = tok.astype(jnp.float32)
    n1 = both(low(rms_norm(tok_float, norm_self.astype(jnp.float32))))
    qkv = low(nn(flat(n1), self_in)).reshape(2, rows, -1)
    a1 = self_forward(self_info, qkv, bias, examples)
    r1 = tok_float + (nn(a1[0], self_out) + swap(nn(a1[1], self_out)))

    mem = reorder(False, memory, mem_raw, place["settled"], examples)
    mem_far = swap(mem)
    kv, kv_far = low(nn(mem, cross_kv)), low(nn(mem_far, cross_kv))
    n2 = both(low(rms_norm(r1, norm_cross.astype(jnp.float32))))
    q2 = low(nn(flat(n2), cross_q)).reshape(2, rows, -1)
    a2 = cross_forward(cross_info, q2, kv, kv_far, examples)
    r2 = r1 + (nn(a2[0], cross_out) + swap(nn(a2[1], cross_out)))

    cot = reorder(False, cotangent, cot_raw, place["settled"], examples)
    positions = core * half_pos + jnp.arange(half_pos, dtype=jnp.int32)
    live = (positions[None, :] < target_len[:, None]).astype(jnp.float32).reshape(rows, 1)
    dy = cot.astype(jnp.float32) * live * token_scale
    gy = low(dy)
    gy_far = permute(gy, net["y"])

    n3 = low(rms_norm(r2, norm_ffn.astype(jnp.float32)))
    n3_far = permute(n3, net["y"])
    out_own, out_far, dn_own, dn_far, ffn_out_part, ffn_in_part = ffn(
        n3, n3_far, gy, gy_far, ffn_in, ffn_out
    )
    dn3 = dn_own + permute(dn_far, net["y"]).astype(jnp.float32)
    back, gain_three = norm_backward(r2, norm_ffn, dn3)
    dr2 = dy + back
    block_out = low(r2 + (out_own + permute(out_far, net["y"]).astype(jnp.float32)))
    block_out = reorder(True, block_out, turn(block_out), place["settled"], examples)
    x_first, z_first = ("x", "zl", "zh"), ("zl", "zh", "x")
    ffn_out_done = reduce_units(pieces(ffn_out_part), x_first, place, net)
    ffn_in_done = reduce_units(pieces(ffn_in_part), z_first, place, net)

    g2 = both(low(dr2))
    da2 = low(nt(flat(g2), cross_out)).reshape(2, rows, -1)
    dq2, dkv, dkv_far = cross_backward(cross_info, q2, kv, kv_far, da2, examples)
    dn2 = nt(dq2[0], cross_q) + swap(nt(dq2[1], cross_q))
    back, gain_two = norm_backward(r1, norm_cross, dn2)
    dr1 = dr2 + back
    cross_out_part = low(tn(flat(a2), flat(g2)))
    cross_q_part = low(tn(flat(dq2), flat(n2)))
    cross_kv_part = low(tn(mem, dkv) + tn(mem_far, dkv_far))
    memory_grad = low(
        nt(dkv, cross_kv) + swap(low(nt(dkv_far, cross_kv))).astype(jnp.float32)
    )
    memory_grad = reorder(True, memory_grad, turn(memory_grad), place["settled"], examples)

    g1 = both(low(dr1))
    self_out_part = low(tn(flat(a1), flat(g1)))
    da1 = low(nt(flat(g1), self_out)).reshape(2, rows, -1)
    dqkv, by_distance = self_backward(self_info, qkv, bias, da1, examples)
    self_in_part = low(tn(flat(dqkv), flat(n1)))
    heads_done = settle(
        pieces(cross_kv_part, cross_out_part, self_out_part, cross_q_part, self_in_part), groups
    )
    dn1 = nt(dqkv[0], self_in) + swap(nt(dqkv[1], self_in))
    back, gain_one = norm_backward(tok_float, norm_self, dn1)
    tokens_grad = low(dr1 + back)
    tokens_grad = reorder(True, tokens_grad, turn(tokens_grad), place["settled"], examples)

    bias_part = jnp.einsum(
        "hd,db->bh", by_distance.reshape(-1, span), level_hot, precision=highest
    )
    bias_row = jnp.pad(bias_part.reshape(1, -1), ((0, 0), (0, width - bias_part.size)))
    small = jnp.concatenate(
        [gain_one[None], gain_two[None], gain_three[None], bias_row], axis=0
    )
    for name in ("y", "x", "zl", "zh"):
        small = small + permute(small, net[name])
    small_far = swap(small)
    gains = small[:3] + small_far[:3]
    bias_sum = jnp.where(settled == 1, small[3], small_far[3])
    bias_grad = bias_sum[: bias_part.size].reshape(bias_part.shape)

    (ffn_out_grad,) = finish(
        ffn_out_done,
        x_first,
        place,
        [ffn_out.shape],
        [[(0, ffn_out.shape[0] // 16, 0, width, 0)]],
    )
    (ffn_in_grad,) = finish(
        ffn_in_done,
        z_first,
        place,
        [ffn_in.shape],
        [[(0, width // 16, 0, ffn_in.shape[1], 0)]],
    )
    (
        key_cross_grad,
        value_cross_grad,
        out_cross_grad,
        out_self_grad,
        query_cross_grad,
        query_self_grad,
        key_self_grad,
        value_self_grad,
    ) = unpack(heads_done, inner)
    return (
        block_out,
        tokens_grad,
        memory_grad,
        gains[0],
        query_self_grad,
        key_self_grad,
        value_self_grad,
        out_self_grad,
        bias_grad,
        gains[1],
        query_cross_grad,
        key_cross_grad,
        value_cross_grad,
        out_cross_grad,
        gains[2],
        ffn_in_grad,
        ffn_out_grad,
    )


def solution(mesh):
    placed = (
        P(("dp", "mp"), None),
        P(("dp", "mp"), None),
        P(("dp", "mp"), None),
        P("dp"),
        P("dp"),
        P(),
        P(None, "mp"),
        P(None, "mp"),
        P(None, "mp"),
        P("mp", None),
        P(None, "mp"),
        P(),
        P(None, "mp"),
        P(None, "mp"),
        P(None, "mp"),
        P("mp", None),
        P(),
        P(None, "mp"),
        P("mp", None),
    )
    near = mesh.shape["mp"] == 2 and mesh.shape["dp"] == 16
    return jax.shard_map(
        on_chip_group if near else on_device,
        mesh=mesh,
        in_specs=placed,
        out_specs=(
            P(("dp", "mp"), None),
            P(("dp", "mp"), None),
            P(("dp", "mp"), None),
            P(),
            P(None, "mp"),
            P(None, "mp"),
            P(None, "mp"),
            P("mp", None),
            P(None, "mp"),
            P(),
            P(None, "mp"),
            P(None, "mp"),
            P(None, "mp"),
            P("mp", None),
            P(),
            P(None, "mp"),
            P("mp", None),
        ),
        check_vma=False,
    )
```

```python
import functools
import math

import jax
import jax.numpy as jnp
import numpy as np
from jax import lax
from jax.experimental import pallas as pl
from jax.experimental.pallas import tpu as pltpu
from jax.sharding import PartitionSpec as P

HEAD_DIM = 64
BUCKETS = 32


epsilon = 1e-06
masked_score = -1e30
highest = lax.Precision.HIGHEST


def bucket_edges():
    exact = list(range(1, 17))
    spaced = [int(math.ceil(16.0 * 8.0 ** ((level - 16) / 16.0))) for level in range(17, 32)]
    return np.array(exact + spaced, dtype=np.int32)


def rms_norm(value, gain):
    factor = lax.rsqrt(jnp.mean(value * value, axis=-1, keepdims=True) + epsilon)
    return value * factor * gain


def gather_rows(value):
    return lax.all_gather(value, "mp", axis=0, tiled=True)


def spread_rows(value):
    return lax.psum_scatter(value, "mp", scatter_dimension=0, tiled=True)


def matmul(left, right):
    return jnp.dot(left, right, preferred_element_type=jnp.float32)


def left_product(left, right):
    return lax.dot_general(
        left, right, (((0,), (0,)), ((), ())), preferred_element_type=jnp.float32
    )


def right_product(left, right):
    return lax.dot_general(
        left, right, (((1,), (1,)), ((), ())), preferred_element_type=jnp.float32
    )


def attend_forward(query, key_rows, value_rows, score_bias, mask):
    scores = jnp.einsum("pehd,kehd->ehpk", query, key_rows, preferred_element_type=jnp.float32)
    if score_bias is not None:
        scores = scores + score_bias[None]
    scores = jnp.where(mask, scores, masked_score)
    row_max = jnp.max(scores, axis=-1, keepdims=True)
    weights = jnp.exp(scores - row_max)
    probs = weights / jnp.sum(weights, axis=-1, keepdims=True)
    probs_low = probs.astype(jnp.bfloat16)
    output = jnp.einsum(
        "ehpk,kehd->pehd", probs_low, value_rows, preferred_element_type=jnp.float32
    )
    return (probs, probs_low, output.astype(jnp.bfloat16))


def attend_backward(query, key_rows, value_rows, probs, probs_low, grad_mixed):
    grad_probs = jnp.einsum(
        "pehd,kehd->ehpk", grad_mixed, value_rows, preferred_element_type=jnp.float32
    )
    inner_sum = jnp.sum(probs * grad_probs, axis=-1, keepdims=True)
    grad_scores = (probs * (grad_probs - inner_sum)).astype(jnp.bfloat16)
    grad_query = jnp.einsum(
        "ehpk,kehd->pehd", grad_scores, key_rows, preferred_element_type=jnp.float32
    )
    grad_keys = jnp.einsum(
        "ehpk,pehd->kehd", grad_scores, query, preferred_element_type=jnp.float32
    )
    grad_values = jnp.einsum(
        "ehpk,pehd->kehd", probs_low, grad_mixed, preferred_element_type=jnp.float32
    )
    return (
        grad_scores,
        grad_query.astype(jnp.bfloat16),
        grad_keys.astype(jnp.bfloat16),
        grad_values.astype(jnp.bfloat16),
    )


def norm_backward(value, gain, grad_normed):
    pullback = jax.vjp(rms_norm, value, gain.astype(jnp.float32))[1]
    return pullback(grad_normed)


def on_device(
    tokens,
    memory,
    cotangent,
    target_lengths,
    memory_lengths,
    norm_self,
    query_self,
    key_self,
    value_self,
    out_self,
    bias_table,
    norm_cross,
    query_cross,
    key_cross,
    value_cross,
    out_cross,
    norm_ffn,
    ffn_in,
    ffn_out,
):
    examples = target_lengths.shape[0]
    local_rows = tokens.shape[0]
    parts = lax.axis_size("mp")
    device_rank = lax.axis_index("mp")
    local_pos = local_rows // examples
    total_pos = local_pos * parts
    memory_local = memory.shape[0]
    memory_total = memory_local * parts
    memory_pos = memory_total // examples
    inner_local = query_self.shape[1]
    heads = inner_local // HEAD_DIM
    total_rows = local_rows * parts
    group_count = jnp.sum(target_lengths).astype(jnp.float32)
    total_count = lax.psum(group_count, "dp")
    token_scale = lax.axis_size("dp") * group_count / total_count
    positions = device_rank * local_pos + jnp.arange(local_pos, dtype=jnp.int32)
    live_rows = (
        (positions[:, None] < target_lengths[None, :]).astype(jnp.float32).reshape(local_rows, 1)
    )
    target_pos = jnp.arange(total_pos, dtype=jnp.int32)
    distance = jnp.maximum(target_pos[:, None] - target_pos[None, :], 0)
    buckets = jnp.sum(
        (distance[:, :, None] >= jnp.asarray(bucket_edges())[None, None, :]).astype(jnp.int32),
        axis=-1,
    )
    table_hot = (buckets[:, :, None] == jnp.arange(BUCKETS, dtype=jnp.int32)[None, None, :]).astype(
        jnp.float32
    )
    causal = target_pos[None, :] <= target_pos[:, None]
    self_mask = causal[None, None] & (
        target_pos[None, None, None, :] < target_lengths[:, None, None, None]
    )
    cross_pos = jnp.arange(memory_pos, dtype=jnp.int32)
    cross_mask = cross_pos[None, None, None, :] < memory_lengths[:, None, None, None]
    score_bias = jnp.einsum(
        "qkb,bh->hqk", table_hot, bias_table.astype(jnp.float32), precision=highest
    )

    def target_view(value):
        return value.reshape(total_pos, examples, heads, HEAD_DIM)

    def memory_view(value):
        return value.reshape(memory_pos, examples, heads, HEAD_DIM)

    tokens_float = tokens.astype(jnp.float32)
    normed_one = rms_norm(tokens_float, norm_self.astype(jnp.float32)).astype(jnp.bfloat16)
    rows_one = gather_rows(normed_one)
    self_weights = jnp.concatenate([query_self, key_self, value_self], axis=1)
    projected = matmul(rows_one, self_weights).astype(jnp.bfloat16)
    query_one = target_view(projected[:, :inner_local])
    keys_one = target_view(projected[:, inner_local : 2 * inner_local])
    values_one = target_view(projected[:, 2 * inner_local :])
    probs_one, low_one, mixed_one = attend_forward(
        query_one, keys_one, values_one, score_bias, self_mask
    )
    mixed_rows_one = mixed_one.reshape(total_rows, inner_local)
    resid_one = tokens_float + spread_rows(matmul(mixed_rows_one, out_self))
    normed_two = rms_norm(resid_one, norm_cross.astype(jnp.float32)).astype(jnp.bfloat16)
    rows_two = gather_rows(normed_two)
    query_two = target_view(matmul(rows_two, query_cross).astype(jnp.bfloat16))
    memory_all = lax.all_gather(memory, "mp", axis=0, tiled=True)
    cross_kv = matmul(memory_all, jnp.concatenate([key_cross, value_cross], axis=1)).astype(
        jnp.bfloat16
    )
    keys_flat = cross_kv[:, :inner_local]
    values_flat = cross_kv[:, inner_local:]
    keys_two = memory_view(keys_flat)
    values_two = memory_view(values_flat)
    probs_two, low_two, mixed_two = attend_forward(
        query_two, keys_two, values_two, None, cross_mask
    )
    mixed_rows_two = mixed_two.reshape(total_rows, inner_local)
    resid_two = resid_one + spread_rows(matmul(mixed_rows_two, out_cross))
    normed_three = rms_norm(resid_two, norm_ffn.astype(jnp.float32)).astype(jnp.bfloat16)
    rows_three = gather_rows(normed_three)
    pre_act = matmul(rows_three, ffn_in)
    hidden = jax.nn.gelu(pre_act).astype(jnp.bfloat16)
    block_out = resid_two + spread_rows(matmul(hidden, ffn_out))
    grad_out = cotangent.astype(jnp.float32) * live_rows * token_scale
    grad_rows_three = gather_rows(grad_out.astype(jnp.bfloat16))
    ffn_out_grad = left_product(hidden, grad_rows_three)
    grad_hidden = right_product(grad_rows_three, ffn_out)
    gelu_back = jax.vjp(jax.nn.gelu, pre_act)[1]
    grad_pre = gelu_back(grad_hidden)[0].astype(jnp.bfloat16)
    ffn_in_grad = left_product(rows_three, grad_pre)
    grad_normed_three = spread_rows(right_product(grad_pre, ffn_in))
    grad_resid_three, gain_three = norm_backward(resid_two, norm_ffn, grad_normed_three)
    grad_two = grad_out + grad_resid_three
    grad_rows_two = gather_rows(grad_two.astype(jnp.bfloat16))
    out_cross_grad = left_product(mixed_rows_two, grad_rows_two)
    grad_mixed_two = target_view(right_product(grad_rows_two, out_cross).astype(jnp.bfloat16))
    cross_back = attend_backward(
        query_two, keys_two, values_two, probs_two, low_two, grad_mixed_two
    )
    grad_query_two = cross_back[1].reshape(total_rows, inner_local)
    grad_keys_two = cross_back[2].reshape(memory_total, inner_local)
    grad_values_two = cross_back[3].reshape(memory_total, inner_local)
    query_cross_grad = left_product(rows_two, grad_query_two)
    grad_normed_two = spread_rows(right_product(grad_query_two, query_cross))
    key_cross_grad = left_product(memory_all, grad_keys_two)
    value_cross_grad = left_product(memory_all, grad_values_two)
    memory_terms = right_product(grad_keys_two, key_cross) + right_product(
        grad_values_two, value_cross
    )
    memory_grad = lax.psum_scatter(memory_terms, "mp", scatter_dimension=0, tiled=True)
    grad_resid_two, gain_two = norm_backward(resid_one, norm_cross, grad_normed_two)
    grad_one = grad_two + grad_resid_two
    grad_rows_one = gather_rows(grad_one.astype(jnp.bfloat16))
    out_self_grad = left_product(mixed_rows_one, grad_rows_one)
    grad_mixed_one = target_view(right_product(grad_rows_one, out_self).astype(jnp.bfloat16))
    self_back = attend_backward(query_one, keys_one, values_one, probs_one, low_one, grad_mixed_one)
    bias_table_grad = jnp.einsum(
        "ehqk,qkb->bh", self_back[0].astype(jnp.float32), table_hot, precision=highest
    )
    grad_projected = jnp.concatenate(
        [
            self_back[1].reshape(total_rows, inner_local),
            self_back[2].reshape(total_rows, inner_local),
            self_back[3].reshape(total_rows, inner_local),
        ],
        axis=1,
    )
    self_weight_grad = left_product(rows_one, grad_projected)
    grad_normed_one = spread_rows(right_product(grad_projected, self_weights))
    grad_resid_one, gain_one = norm_backward(tokens_float, norm_self, grad_normed_one)
    tokens_grad = grad_one + grad_resid_one
    summed = lax.psum(
        (
            self_weight_grad[:, :inner_local],
            self_weight_grad[:, inner_local : 2 * inner_local],
            self_weight_grad[:, 2 * inner_local :],
            out_self_grad,
            bias_table_grad,
            query_cross_grad,
            key_cross_grad,
            value_cross_grad,
            out_cross_grad,
            ffn_in_grad,
            ffn_out_grad,
        ),
        "dp",
    )
    gains = lax.psum((gain_one, gain_two, gain_three), ("dp", "mp"))
    return (
        block_out.astype(jnp.bfloat16),
        tokens_grad.astype(jnp.bfloat16),
        memory_grad.astype(jnp.bfloat16),
        gains[0],
        summed[0],
        summed[1],
        summed[2],
        summed[3],
        summed[4],
        gains[1],
        summed[5],
        summed[6],
        summed[7],
        summed[8],
        gains[2],
        summed[9],
        summed[10],
    )


def links(dp_size):
    total = 2 * dp_size

    def swap(bit):
        return [(at, at ^ bit) for at in range(total)]

    def off_swap(bit):
        return [(at, at ^ bit) for at in range(total) if (at & 1) != ((at >> 1) & 1)]

    def turned(at):
        return (at & ~3) | ((at & 1) << 1) | ((at >> 1) & 1)

    def crossed(at):
        return (at & ~3) | ((1 - (at & 1)) << 1) | ((at >> 1) & 1)

    return {
        "turn": [(at, turned(at)) for at in range(total) if at != turned(at)],
        "cross": [(at, crossed(at)) for at in range(total)],
        "y": swap(1),
        "core": swap(2),
        "x": swap(4),
        "zl": swap(8),
        "zh": swap(16),
        "off_x": off_swap(4),
        "off_zl": off_swap(8),
    }


def permute(value, pairs):
    return lax.ppermute(value, ("dp", "mp"), pairs)


def reorder_kernel(inverse, examples, info, held, arrived, target):
    def write(source):
        if inverse:
            value = source[...].reshape(-1, source.shape[2])
        else:
            value = source[...]
        rows = value.shape[0]
        chunk = rows // examples
        high = lax.broadcasted_iota(jnp.int32, (rows, rows), 0)
        low = lax.broadcasted_iota(jnp.int32, (rows, rows), 1)
        if inverse:
            hot = low == (high % examples) * chunk + high // examples
        else:
            hot = low == (high % chunk) * examples + high // chunk
        moved = nn(hot.astype(jnp.bfloat16), value).astype(jnp.bfloat16)
        target[...] = moved.reshape(target.shape)

    @pl.when(info[0] == 1)
    def _():
        write(held)

    @pl.when(info[0] == 0)
    def _():
        write(arrived)


def reorder(inverse, held, arrived, settled, examples):
    rows, width = held.shape
    block = 256
    flat = pl.BlockSpec((block, width), lambda i, s: (i, 0))
    flat_shape = (rows, width)
    split_shape = (examples, rows // examples, width)
    split_block = (examples, block // examples, width)
    if inverse:
        held, arrived = held.reshape(split_shape), arrived.reshape(split_shape)
        in_specs = [
            pl.BlockSpec(split_block, lambda i, s: (0, i * s[0], 0)),
            pl.BlockSpec(split_block, lambda i, s: (0, i * (1 - s[0]), 0)),
        ]
        out_spec, out_shape = flat, flat_shape
    else:
        in_specs = [
            pl.BlockSpec((block, width), lambda i, s: (i * s[0], 0)),
            pl.BlockSpec((block, width), lambda i, s: (i * (1 - s[0]), 0)),
        ]
        out_spec = pl.BlockSpec(split_block, lambda i, s: (0, i, 0))
        out_shape = split_shape
    return pl.pallas_call(
        functools.partial(reorder_kernel, inverse, examples),
        grid_spec=pltpu.PrefetchScalarGridSpec(
            num_scalar_prefetch=1,
            grid=(rows // block,),
            in_specs=in_specs,
            out_specs=out_spec,
        ),
        out_shape=jax.ShapeDtypeStruct(out_shape, held.dtype),
        cost_estimate=cost(2 * rows * width * block, 4 * rows * width),
        compiler_params=pltpu.CompilerParams(vmem_limit_bytes=SMALL_VMEM),
    )(settled, held, arrived).reshape(flat_shape)


def nt(left, right):
    return lax.dot_general(
        left, right, (((1,), (1,)), ((), ())), preferred_element_type=jnp.float32
    )


def tn(left, right):
    return lax.dot_general(
        left, right, (((0,), (0,)), ((), ())), preferred_element_type=jnp.float32
    )


def nn(left, right):
    return jnp.dot(left, right, preferred_element_type=jnp.float32)


def one_head(value, head):
    lane = lax.broadcasted_iota(jnp.int32, value.shape, 1)
    return jnp.where(lane // HEAD_DIM == head, value, jnp.zeros_like(value))


def softmax_columns(scores):
    top = jnp.max(scores, axis=0, keepdims=True)
    weights = jnp.exp(scores - top)
    return weights * (1.0 / jnp.sum(weights, axis=0, keepdims=True))


def toeplitz(row, size):
    return pltpu.roll(jnp.broadcast_to(row, (size, size)), 0, 1, stride=1, stride_axis=0)


def diagonals(square):
    size = square.shape[0]
    row = lax.broadcasted_iota(jnp.int32, square.shape, 0)
    turned, step = square, 1
    while step < size:
        moved = pltpu.roll(turned, size - step, 1)
        turned = jnp.where((row & step) != 0, moved, turned)
        step *= 2
    return jnp.sum(turned, axis=0, keepdims=True)


def ordered(core, scratch, own, far):
    half = own.shape[0]
    scratch[pl.ds(pl.multiple_of(core * half, half), half), :] = own
    scratch[pl.ds(pl.multiple_of((1 - core) * half, half), half), :] = far
    return scratch[...]


def split_store(core, scratch, value, out):
    half = out.shape[1]
    scratch[...] = value
    out[0] = scratch[pl.ds(pl.multiple_of(core * half, half), half), :]
    out[1] = scratch[pl.ds(pl.multiple_of((1 - core) * half, half), half), :]


def self_scores(query, keys, bias, head, length):
    scores = nt(keys, one_head(query, head)) + bias
    key_at = lax.broadcasted_iota(jnp.int32, scores.shape, 0)
    query_at = lax.broadcasted_iota(jnp.int32, scores.shape, 1)
    return jnp.where((key_at <= query_at) & (key_at < length), scores, masked_score)


def heads_joined(first, second):
    return jnp.concatenate([first[:HEAD_DIM], second[HEAD_DIM:]], axis=0).T


def self_forward_kernel(info, rows, bias, out, scratch, out_scratch, bias_scratch):
    core = info[0]
    example = pl.program_id(1)
    length = info[1 + example]
    size = scratch.shape[0]

    @pl.when(example == 0)
    def _():
        for head in range(2):
            bias_scratch[head] = toeplitz(bias[0, head : head + 1, :], size)

    joined = ordered(core, scratch, rows[0], rows[1])
    query, keys, values = joined[:, :128], joined[:, 128:256], joined[:, 256:]
    mixed = []
    for head in range(2):
        probs = softmax_columns(self_scores(query, keys, bias_scratch[head], head, length))
        mixed.append(tn(values, probs.astype(jnp.bfloat16)))
    result = heads_joined(*mixed).astype(jnp.bfloat16)
    split_store(core, out_scratch, result, out)


def self_backward_kernel(
    info,
    rows,
    bias,
    grads,
    out,
    out_bias,
    scratch,
    grad_scratch,
    out_scratch,
    bias_scratch,
    sum_scratch,
):
    core = info[0]
    example = pl.program_id(1)
    length = info[1 + example]
    size = scratch.shape[0]

    @pl.when(example == 0)
    def _():
        for head in range(2):
            bias_scratch[head] = toeplitz(bias[0, head : head + 1, :], size)
        sum_scratch[...] = jnp.zeros_like(sum_scratch)

    joined = ordered(core, scratch, rows[0], rows[1])
    query, keys, values = joined[:, :128], joined[:, 128:256], joined[:, 256:]
    grad = ordered(core, grad_scratch, grads[0], grads[1])
    grad_query, grad_keys, grad_values, squares = [], [], [], []
    for head in range(2):
        probs = softmax_columns(self_scores(query, keys, bias_scratch[head], head, length))
        low = probs.astype(jnp.bfloat16)
        grad_head = one_head(grad, head)
        grad_probs = nt(values, grad_head)
        inner = jnp.sum(probs * grad_probs, axis=0, keepdims=True)
        grad_scores = (probs * (grad_probs - inner)).astype(jnp.bfloat16)
        grad_values.append(nn(low, grad_head))
        grad_keys.append(nn(grad_scores, one_head(query, head)))
        grad_query.append(tn(keys, grad_scores))
        squares.append(grad_scores.astype(jnp.float32))
    for head in range(2):
        sum_scratch[head] = sum_scratch[head] + squares[head]
    result = jnp.concatenate(
        [
            heads_joined(*grad_query),
            grad_keys[0] + grad_keys[1],
            grad_values[0] + grad_values[1],
        ],
        axis=1,
    ).astype(jnp.bfloat16)
    split_store(core, out_scratch, result, out)

    @pl.when(example == pl.num_programs(1) - 1)
    def _():
        for head in range(2):
            out_bias[0, head : head + 1, :] = diagonals(sum_scratch[head])


def cross_scores(query, keys, head, core, length):
    scores = nt(keys, one_head(query, head))
    size = scores.shape[0]
    key_at = lax.broadcasted_iota(jnp.int32, scores.shape, 0)
    key_at = (key_at + core * (size // 2)) & (size - 1)
    return jnp.where(key_at < length, scores, masked_score)


def cross_forward_kernel(info, queries, kv_own, kv_far, out):
    core = info[0]
    length = info[1 + pl.program_id(0)]
    query = queries[...].reshape(-1, 128)
    keys = jnp.concatenate([kv_own[:, :128], kv_far[:, :128]], axis=0)
    values = jnp.concatenate([kv_own[:, 128:], kv_far[:, 128:]], axis=0)
    mixed = []
    for head in range(2):
        probs = softmax_columns(cross_scores(query, keys, head, core, length))
        mixed.append(tn(values, probs.astype(jnp.bfloat16)))
    out[...] = heads_joined(*mixed).astype(jnp.bfloat16).reshape(out.shape)


def cross_backward_kernel(info, queries, kv_own, kv_far, grads, dq, dkv_own, dkv_far):
    core = info[0]
    length = info[1 + pl.program_id(0)]
    query = queries[...].reshape(-1, 128)
    grad = grads[...].reshape(-1, 128)
    keys = jnp.concatenate([kv_own[:, :128], kv_far[:, :128]], axis=0)
    values = jnp.concatenate([kv_own[:, 128:], kv_far[:, 128:]], axis=0)
    grad_query, grad_keys, grad_values = [], [], []
    for head in range(2):
        probs = softmax_columns(cross_scores(query, keys, head, core, length))
        low = probs.astype(jnp.bfloat16)
        grad_head = one_head(grad, head)
        grad_probs = nt(values, grad_head)
        inner = jnp.sum(probs * grad_probs, axis=0, keepdims=True)
        grad_scores = (probs * (grad_probs - inner)).astype(jnp.bfloat16)
        grad_values.append(nn(low, grad_head))
        grad_keys.append(nn(grad_scores, one_head(query, head)))
        grad_query.append(tn(keys, grad_scores))
    dq[...] = heads_joined(*grad_query).astype(jnp.bfloat16).reshape(dq.shape)
    result = jnp.concatenate(
        [grad_keys[0] + grad_keys[1], grad_values[0] + grad_values[1]], axis=1
    ).astype(jnp.bfloat16)
    half = dkv_own.shape[0]
    dkv_own[...] = result[:half]
    dkv_far[...] = result[half:]


MIB = 1024 * 1024


def cost(flops, moved, exps=0):
    return pl.CostEstimate(
        flops=int(flops), bytes_accessed=int(moved), transcendentals=int(exps)
    )


SMALL_VMEM = 12 * MIB
ATTEND_VMEM = 24 * MIB
FFN_VMEM = 44 * MIB
SETTLE_VMEM = 48 * MIB
MESH = pl.DeviceIdType.MESH
SMEM_SPEC = pl.BlockSpec(memory_space=pltpu.SMEM)


def self_forward(info, rows, bias, examples):
    _, count, width = rows.shape
    pairs, size = width // 384, count // examples
    return pl.pallas_call(
        self_forward_kernel,
        grid=(pairs, examples),
        in_specs=[
            SMEM_SPEC,
            pl.BlockSpec((2, size, 384), lambda h, e: (0, e, h)),
            pl.BlockSpec((1, 2, 2 * size), lambda h, e: (h, 0, 0)),
        ],
        out_specs=pl.BlockSpec((2, size, 128), lambda h, e: (0, e, h)),
        out_shape=jax.ShapeDtypeStruct((2, count, pairs * 128), jnp.bfloat16),
        scratch_shapes=[
            pltpu.VMEM((2 * size, 384), jnp.bfloat16),
            pltpu.VMEM((2 * size, 128), jnp.bfloat16),
            pltpu.VMEM((2, 2 * size, 2 * size), jnp.float32),
        ],
        cost_estimate=cost(2 * 2 * examples * 2 * pairs * (2 * size) ** 2 * 256 * 8, 8 * rows.size, examples * 2 * pairs * (2 * size) ** 2),
        compiler_params=pltpu.CompilerParams(vmem_limit_bytes=SMALL_VMEM),
    )(info, rows, bias)


def self_backward(info, rows, bias, grads, examples):
    _, count, width = rows.shape
    pairs, size = width // 384, count // examples
    row = pl.BlockSpec((1, 2, 2 * size), lambda h, e: (h, 0, 0))
    wide = pl.BlockSpec((2, size, 384), lambda h, e: (0, e, h))
    return pl.pallas_call(
        self_backward_kernel,
        grid=(pairs, examples),
        in_specs=[
            SMEM_SPEC,
            wide,
            row,
            pl.BlockSpec((2, size, 128), lambda h, e: (0, e, h)),
        ],
        out_specs=[wide, row],
        out_shape=[
            jax.ShapeDtypeStruct(rows.shape, jnp.bfloat16),
            jax.ShapeDtypeStruct((pairs, 2, 2 * size), jnp.float32),
        ],
        scratch_shapes=[
            pltpu.VMEM((2 * size, 384), jnp.bfloat16),
            pltpu.VMEM((2 * size, 128), jnp.bfloat16),
            pltpu.VMEM((2 * size, 384), jnp.bfloat16),
            pltpu.VMEM((2, 2 * size, 2 * size), jnp.float32),
            pltpu.VMEM((2, 2 * size, 2 * size), jnp.float32),
        ],
        cost_estimate=cost(5 * 2 * examples * 2 * pairs * (2 * size) ** 2 * 256 * 8, 12 * rows.size, examples * 2 * pairs * (2 * size) ** 2),
        compiler_params=pltpu.CompilerParams(vmem_limit_bytes=SMALL_VMEM),
    )(info, rows, bias, grads)


def cross_forward(info, queries, kv_own, kv_far, examples):
    _, count, width = queries.shape
    pairs, size, span = width // 128, count // examples, kv_own.shape[0] // examples
    thin = pl.BlockSpec((2, size, 128), lambda e, h: (0, e, h))
    wide = pl.BlockSpec((span, 256), lambda e, h: (e, h))
    return pl.pallas_call(
        cross_forward_kernel,
        grid=(examples, pairs),
        in_specs=[SMEM_SPEC, thin, wide, wide],
        out_specs=thin,
        out_shape=jax.ShapeDtypeStruct(queries.shape, jnp.bfloat16),
        cost_estimate=cost(2 * 2 * examples * 2 * pairs * 4 * size * span * 256 * 4, 8 * kv_own.size, examples * 2 * pairs * 4 * size * span),
        compiler_params=pltpu.CompilerParams(vmem_limit_bytes=ATTEND_VMEM),
    )(info, queries, kv_own, kv_far)


def cross_backward(info, queries, kv_own, kv_far, grads, examples):
    _, count, width = queries.shape
    pairs, size, span = width // 128, count // examples, kv_own.shape[0] // examples
    thin = pl.BlockSpec((2, size, 128), lambda e, h: (0, e, h))
    wide = pl.BlockSpec((span, 256), lambda e, h: (e, h))
    return pl.pallas_call(
        cross_backward_kernel,
        grid=(examples, pairs),
        in_specs=[SMEM_SPEC, thin, wide, wide, thin],
        out_specs=[thin, wide, wide],
        out_shape=[jax.ShapeDtypeStruct(queries.shape, jnp.bfloat16)]
        + [jax.ShapeDtypeStruct(kv_own.shape, jnp.bfloat16)] * 2,
        cost_estimate=cost(5 * 2 * examples * 2 * pairs * 4 * size * span * 256 * 2, 12 * kv_own.size, examples * 2 * pairs * 4 * size * span),
        compiler_params=pltpu.CompilerParams(vmem_limit_bytes=ATTEND_VMEM),
    )(info, queries, kv_own, kv_far, grads)


root = math.sqrt(2.0 / math.pi)
cubic = 0.044715


def ffn_kernel(
    n_own,
    n_far,
    g_own,
    g_far,
    into,
    outof,
    out_own,
    out_far,
    dn_own,
    dn_far,
    outof_grad,
    into_grad,
    turned,
    out_sum,
    dn_sum,
):
    step = pl.program_id(0)
    half = n_own.shape[0]

    @pl.when(step == 0)
    def _():
        turned[:, :half] = n_own[...].T
        turned[:, half:] = n_far[...].T
        out_own[...] = jnp.zeros_like(out_own)
        dn_own[...] = jnp.zeros_like(dn_own)
        out_sum[...] = jnp.zeros_like(out_sum)
        dn_sum[...] = jnp.zeros_like(dn_sum)

    grads, backs = [], []
    for normed, grad, out, back in (
        (n_own, g_own, out_own, dn_own),
        (n_far, g_far, out_sum, dn_sum),
    ):
        pre = nn(normed[...], into[...])
        grad_hidden = nt(grad[...], outof[...])
        bend = jnp.tanh(root * (pre + cubic * (pre * pre * pre)))
        hidden = (0.5 * pre * (1.0 + bend)).astype(jnp.bfloat16)
        slope = 0.5 * (1.0 + bend) + 0.5 * pre * (1.0 - bend * bend) * (
            root * (1.0 + 3.0 * cubic * (pre * pre))
        )
        grad_pre = (grad_hidden * slope).astype(jnp.bfloat16)
        out[...] += nn(hidden, outof[...])
        back[...] += nt(grad_pre, into[...])
        grads.append(tn(hidden, grad[...]))
        backs.append(nn(turned[:, : half] if normed is n_own else turned[:, half:], grad_pre))
    outof_grad[...] = (grads[0] + grads[1]).astype(jnp.bfloat16)
    into_grad[...] = (backs[0] + backs[1]).astype(jnp.bfloat16)

    @pl.when(step == pl.num_programs(0) - 1)
    def _():
        out_far[...] = out_sum[...].astype(jnp.bfloat16)
        dn_far[...] = dn_sum[...].astype(jnp.bfloat16)


def ffn(n_own, n_far, g_own, g_far, into, outof):
    rows, width = n_own.shape
    units = into.shape[1]
    tile = 256
    whole = pl.BlockSpec((rows, width), lambda i: (0, 0))
    tall = pl.BlockSpec((width, tile), lambda i: (0, i))
    flat = pl.BlockSpec((tile, width), lambda i: (i, 0))
    wide = jax.ShapeDtypeStruct((rows, width), jnp.float32)
    thin = jax.ShapeDtypeStruct((rows, width), jnp.bfloat16)
    return pl.pallas_call(
        ffn_kernel,
        grid=(units // tile,),
        in_specs=[whole, whole, whole, whole, tall, flat],
        out_specs=[whole, whole, whole, whole, flat, tall],
        out_shape=[
            wide,
            thin,
            wide,
            thin,
            jax.ShapeDtypeStruct(outof.shape, jnp.bfloat16),
            jax.ShapeDtypeStruct(into.shape, jnp.bfloat16),
        ],
        scratch_shapes=[
            pltpu.VMEM((width, 2 * rows), jnp.bfloat16),
            pltpu.VMEM((rows, width), jnp.float32),
            pltpu.VMEM((rows, width), jnp.float32),
        ],
        cost_estimate=cost(6 * 2 * 2 * rows * width * units, 24 * rows * width + 8 * width * units, 2 * rows * units),
        compiler_params=pltpu.CompilerParams(vmem_limit_bytes=FFN_VMEM),
    )(n_own, n_far, g_own, g_far, into, outof)


def gather_kernel(groups, examples, tokens, facts, counts, *refs):
    weights, refs = refs[:8], refs[8:]
    tok_out, facts_out, counts_out, self_in, cross_q, cross_kv, self_out, cross_out = refs[:8]
    raw, landed, round_in, near_send, near_get, send, get = refs[8:]
    index, y = lax.axis_index("dp"), lax.axis_index("mp")
    core, x, z = index % 2, (index // 2) % 2, index // 4
    deep = groups // 4

    def at(c, yy, xx, zz):
        return (zz * 4 + xx * 2 + c, yy)

    z_near = z + 1 - 2 * (z % 2)
    x_side, z_side = at(core, y, 1 - x, z), at(core, y, x, z_near)
    turned = at(1 - core, 1 - y, x, z)
    rounds = [at(1 - core, y, x, z), x_side, z_side]
    step = 2
    while step < deep:
        rounds.append(at(core, y, x, z + step - 2 * step * ((z // step) % 2)))
        step *= 2
    barrier = pltpu.get_barrier_semaphore()
    for partner in rounds:
        pl.semaphore_signal(barrier, inc=1, device_id=partner, device_id_type=MESH)

    @pl.when(core != y)
    def _():
        pl.semaphore_signal(barrier, inc=1, device_id=turned, device_id_type=MESH)
        pl.semaphore_wait(barrier, len(rounds) + 1)

    @pl.when(core == y)
    def _():
        pl.semaphore_wait(barrier, len(rounds))

    homes = [raw.at[0], raw.at[1], raw.at[2], cross_q, raw.at[3], raw.at[4], self_out, cross_out]

    def remote(source, target, sems, slot, device):
        return pltpu.make_async_remote_copy(
            src_ref=source,
            dst_ref=target,
            send_sem=sems[0].at[slot],
            recv_sem=sems[1].at[slot],
            device_id=device,
            device_id_type=MESH,
        )

    mine = x * 2 + z % 2

    def quarter(w, which, first=0, parts=1):
        rows = homes[w].shape[0] // 4
        size = rows // parts
        return homes[w].at[pl.ds(pl.multiple_of(which * rows + first * size, size), size)]

    def along_y(w):
        rows = homes[w].shape[0] // 4
        sent = mine * rows
        return remote(
            weights[w].at[pl.ds(pl.multiple_of(sent, rows), rows)],
            quarter(w, mine),
            (send, get),
            w,
            turned,
        )

    def direct(w, which):
        piece = quarter(w, mine)
        return remote(piece, piece, (send, get), 8 + 2 * w + which, (x_side, z_side)[which])

    def passed(w, which):
        other = mine + (2 - 4 * x if which == 0 else 1 - 2 * (z % 2))
        piece = quarter(w, other, which, 2)
        return remote(piece, piece, (send, get), 24 + 2 * w + which, (z_side, x_side)[which])

    token_copy = remote(tokens, landed, (send, get), 40, turned)
    facts_copy = remote(facts, facts_out, (send, get), 41, turned)

    @pl.when(core != y)
    def _():
        facts_copy.start()
        for w in range(8):
            along_y(w).start()
        token_copy.start()

    @pl.when(core == y)
    def _():
        pltpu.make_async_copy(tokens, landed, near_get.at[0]).start()
        pltpu.make_async_copy(facts, facts_out, near_get.at[1]).start()
        for w in range(8):
            pltpu.make_async_copy(weights[w], homes[w], near_get.at[2 + w]).start()

    counts_out[...] = counts[...]
    for i, partner in enumerate(rounds):
        swap = remote(counts_out, round_in.at[i], (near_send, get), 42 + i, partner)
        swap.start()
        swap.wait()
        counts_out[...] += round_in[i]

    @pl.when(core == y)
    def _():
        pltpu.make_async_copy(tokens, landed, near_get.at[0]).wait()
        pltpu.make_async_copy(facts, facts_out, near_get.at[1]).wait()
        for w in range(8):
            pltpu.make_async_copy(weights[w], homes[w], near_get.at[2 + w]).wait()

    @pl.when(core != y)
    def _():
        facts_copy.wait()
        for w in range(9):
            if w < 8:
                along_y(w).wait()
                for which in range(2):
                    direct(w, which).start()
            if w > 0:
                for which in range(2):
                    direct(w - 1, which).wait()
                for which in range(2):
                    passed(w - 1, which).start()
        token_copy.wait()

    rows = landed.shape[0]
    block = 256
    chunk = block // examples
    high = lax.broadcasted_iota(jnp.int32, (block, block), 0)
    low = lax.broadcasted_iota(jnp.int32, (block, block), 1)
    hot = (low == (high % chunk) * examples + high // chunk).astype(jnp.bfloat16)
    for i in range(rows // block):
        moved = nn(hot, landed[pl.ds(i * block, block), :]).astype(jnp.bfloat16)
        tok_out[:, pl.ds(i * chunk, chunk), :] = moved.reshape(examples, chunk, moved.shape[1])

    @pl.when(core != y)
    def _():
        for w in range(8):
            for which in range(2):
                passed(w, which).wait()

    for h in range(raw.shape[2] // 128):
        for i in range(3):
            self_in[:, 384 * h + 128 * i : 384 * h + 128 * i + 128] = raw[
                i, :, 128 * h : 128 * h + 128
            ]
        for i in range(2):
            cross_kv[:, 256 * h + 128 * i : 256 * h + 128 * i + 128] = raw[
                3 + i, :, 128 * h : 128 * h + 128
            ]


def gather(tokens, facts, counts, weights, groups, examples):
    rows, width = tokens.shape
    inner = weights[0].shape[1]
    rounds = 2 + (groups // 4).bit_length() - 1
    anywhere = pl.BlockSpec(memory_space=pl.ANY)
    whole = pl.BlockSpec(memory_space=pltpu.VMEM)

    def half(*shape):
        return jax.ShapeDtypeStruct(shape, jnp.bfloat16)

    return pl.pallas_call(
        functools.partial(gather_kernel, groups, examples),
        in_specs=[anywhere, whole, whole] + [anywhere] * 8,
        out_specs=[whole] * 8,
        out_shape=[
            half(examples, rows // examples, width),
            jax.ShapeDtypeStruct(facts.shape, facts.dtype),
            jax.ShapeDtypeStruct(counts.shape, counts.dtype),
            half(width, 3 * inner),
            half(width, inner),
            half(width, 2 * inner),
            half(inner, width),
            half(inner, width),
        ],
        scratch_shapes=[
            pltpu.VMEM((5, width, inner), jnp.bfloat16),
            pltpu.VMEM((rows, width), jnp.bfloat16),
            pltpu.VMEM((rounds,) + counts.shape, counts.dtype),
            pltpu.SemaphoreType.DMA((42 + rounds,)),
            pltpu.SemaphoreType.DMA((10,)),
            pltpu.SemaphoreType.DMA((42,)),
            pltpu.SemaphoreType.DMA((42 + rounds,)),
        ],
        cost_estimate=cost(0, 150 * MIB),
        compiler_params=pltpu.CompilerParams(
            collective_id=1, has_side_effects=True, vmem_limit_bytes=SETTLE_VMEM
        ),
    )(tokens, facts, counts, *weights)


def add_low(left, right):
    return (left.astype(jnp.float32) + right.astype(jnp.float32)).astype(jnp.bfloat16)


def pick(value, index):
    return lax.dynamic_index_in_dim(value, index, 0, keepdims=False)


def part_out(total, name, place, net):
    view = total.reshape(2, total.shape[0] // 2, *total.shape[1:])
    return permute(pick(view, 1 - place[name]), net[name])


def part_in(total, arrived, name, place):
    view = total.reshape(2, total.shape[0] // 2, *total.shape[1:])
    return add_low(pick(view, place[name]), arrived)


def halve(total, name, place, net):
    return part_in(total, part_out(total, name, place, net), name, place)


def beside(own, arrived):
    return jnp.concatenate([own, arrived], axis=0)


def tie(*values):
    return lax.optimization_barrier(values)


def settle_kernel(groups, value, small, out, small_out, first, second, third, small_in, send, receive, small_send, small_get):
    index, y = lax.axis_index("dp"), lax.axis_index("mp")
    core, x, z = index % 2, (index // 2) % 2, index // 4
    deep = groups // 4
    chunks, rows = first.shape[0], first.shape[3]

    def at(c, yy, xx, zz):
        return (zz * 4 + xx * 2 + c, yy)

    def part(k):
        return pl.ds(pl.multiple_of(k * rows, rows), rows)

    partners = [at(1 - core, y, x, z), at(core, 1 - y, x, z), at(1 - core, 1 - y, x, z)]
    partners.append(at(core, y, 1 - x, z))
    for step in range(1, deep):
        partners.append(at(core, y, x, (z + step) % deep))
    barrier = pltpu.get_barrier_semaphore()
    for partner in partners:
        pl.semaphore_signal(barrier, inc=1, device_id=partner, device_id_type=MESH)
    pl.semaphore_wait(barrier, len(partners))

    def copy(source, target, slot, k, device):
        return pltpu.make_async_remote_copy(
            src_ref=source,
            dst_ref=target,
            send_sem=send.at[k, slot],
            recv_sem=receive.at[k, slot],
            device_id=device,
            device_id_type=MESH,
        )

    def quarter(k, q):
        return value.at[pl.ds(q * 8, 8), part(k)]

    def to_core(k):
        return copy(quarter(k, 1 - core), first.at[k, 0], 0, k, at(1 - core, core, x, z))

    def to_turned(k):
        return copy(quarter(k, 1 - core), first.at[k, 1], 1, k, at(1 - core, core, x, z))

    def to_same(k):
        return copy(quarter(k, core), first.at[k, 1], 2, k, at(core, core, x, z))

    def arrived(k, slot):
        return copy(quarter(k, core), first.at[k, 1 if slot else 0], slot, k, at(1 - core, y, x, z))

    def along_x(k):
        return copy(
            first.at[k, 1, pl.ds((1 - x) * 4, 4)], second.at[k], 3, k, at(core, y, 1 - x, z)
        )

    def along_z(k, step):
        far = (z + step) % deep
        return copy(
            second.at[k, far], third.at[k, step - 1], 3 + step, k, at(core, y, x, far)
        )

    def back_z(k, step):
        far = (z + step) % deep
        piece = core * 8 + x * 4 + z
        return copy(
            out.at[piece, part(k)], out.at[piece, part(k)], 6 + step, k, at(core, y, x, far)
        )

    def back_x(k):
        held = out.at[pl.ds(core * 8 + x * 4, 4), part(k)]
        return copy(held, held, 10, k, at(core, y, 1 - x, z))

    def back_core(k):
        held = out.at[pl.ds(core * 8, 8), part(k)]
        return copy(held, held, 11, k, at(1 - core, y, x, z))

    rounds = [at(core, 1 - y, x, z), at(core, y, 1 - x, z)]
    step = 1
    while step < deep:
        rounds.append(at(core, y, x, z + step - 2 * step * ((z // step) % 2)))
        step *= 2
    rounds.append(at(1 - core, y, x, z))
    small_out[0] = small[...]

    def small_round(i):
        swap = pltpu.make_async_remote_copy(
            src_ref=small_out.at[0],
            dst_ref=small_in.at[i],
            send_sem=small_send.at[i],
            recv_sem=small_get.at[i],
            device_id=rounds[i],
            device_id_type=MESH,
        )
        swap.start()
        swap.wait()
        if i < len(rounds) - 1:
            small_out[0] = small_out[0] + small_in[i]
        else:
            small_out[1] = small_in[i]

    small_round(0)

    def start(k, carry):
        @pl.when(core == y)
        def _():
            to_core(k).start()

        @pl.when(core != y)
        def _():
            to_same(k).start()
            to_turned(k).start()

        return carry

    lax.fori_loop(0, chunks, start, 0)
    for i in range(1, len(rounds)):
        small_round(i)

    def total(left, right):
        return (left.astype(jnp.float32) + right.astype(jnp.float32)).astype(jnp.bfloat16)

    def tick(t, carry):
        @pl.when(t < chunks)
        def _():
            k = jnp.minimum(t, chunks - 1)

            @pl.when(core == y)
            def _():
                arrived(k, 2).wait_recv()

                def add(i, c):
                    first[k, 1, i] = total(value[core * 8 + i, part(k)], first[k, 1, i])
                    return c

                lax.fori_loop(0, 8, add, 0)

            @pl.when(core != y)
            def _():
                arrived(k, 0).wait_recv()
                arrived(k, 1).wait_recv()

                def add(i, c):
                    first[k, 1, i] = total(first[k, 0, i], first[k, 1, i])
                    return c

                lax.fori_loop(0, 8, add, 0)

            along_x(k).start()

        @pl.when((t >= 1) & (t < chunks + 1))
        def _():
            k = t - 1
            along_x(k).wait_recv()

            def add(i, c):
                second[k, i] = total(first[k, 1, x * 4 + i], second[k, i])
                return c

            lax.fori_loop(0, deep, add, 0)
            for step in range(1, deep):
                along_z(k, step).start()

        @pl.when((t >= 2) & (t < chunks + 2))
        def _():
            k = t - 2
            for step in range(1, deep):
                along_z(k, step).wait_recv()
            summed = second[k, z].astype(jnp.float32)
            for step in range(1, deep):
                summed = summed + third[k, step - 1].astype(jnp.float32)
            out[core * 8 + x * 4 + z, part(k)] = summed.astype(jnp.bfloat16)
            for step in range(1, deep):
                back_z(k, step).start()

        @pl.when((t >= 3) & (t < chunks + 3))
        def _():
            k = t - 3
            for step in range(1, deep):
                back_z(k, step).wait_recv()
            back_x(k).start()

        @pl.when((t >= 4) & (t < chunks + 4))
        def _():
            k = t - 4
            back_x(k).wait_recv()
            back_core(k).start()

        @pl.when(t >= 5)
        def _():
            back_core(t - 5).wait_recv()

        return carry

    lax.fori_loop(0, chunks + 5, tick, 0)

    def finish_sends(k, carry):
        @pl.when(core == y)
        def _():
            to_core(k).wait_send()

        @pl.when(core != y)
        def _():
            to_same(k).wait_send()
            to_turned(k).wait_send()

        along_x(k).wait_send()
        for step in range(1, deep):
            along_z(k, step).wait_send()
            back_z(k, step).wait_send()
        back_x(k).wait_send()
        back_core(k).wait_send()
        return carry

    lax.fori_loop(0, chunks, finish_sends, 0)


def settle(value, small, groups):
    count, rows, width = value.shape
    chunk = 32
    chunks = rows // chunk
    deep = groups // 4
    rounds = 3 + deep.bit_length() - 1
    whole = pl.BlockSpec(memory_space=pltpu.VMEM)
    return pl.pallas_call(
        functools.partial(settle_kernel, groups),
        in_specs=[whole, whole],
        out_specs=[whole, whole],
        out_shape=[
            jax.ShapeDtypeStruct(value.shape, value.dtype),
            jax.ShapeDtypeStruct((2,) + small.shape, small.dtype),
        ],
        scratch_shapes=[
            pltpu.VMEM((chunks, 2, count // 2, chunk, width), value.dtype),
            pltpu.VMEM((chunks, deep, chunk, width), value.dtype),
            pltpu.VMEM((chunks, deep - 1, chunk, width), value.dtype),
            pltpu.VMEM((rounds,) + small.shape, small.dtype),
            pltpu.SemaphoreType.DMA((chunks, 12)),
            pltpu.SemaphoreType.DMA((chunks, 12)),
            pltpu.SemaphoreType.DMA((rounds,)),
            pltpu.SemaphoreType.DMA((rounds,)),
        ],
        cost_estimate=cost(0, 60 * value.size),
        compiler_params=pltpu.CompilerParams(
            collective_id=0, has_side_effects=True, vmem_limit_bytes=SETTLE_VMEM
        ),
    )(value, small)


def unpack_kernel(pairs, source, key, val, cross_out, self_out, cross_q, *self_in):
    wide = key.shape[0] // 4
    thin = cross_out.shape[0] // 4

    def taken(row, rows):
        block = source[:, row : row + rows, :].astype(jnp.float32)
        return block.reshape(4 * rows, block.shape[2])

    kv = taken(0, wide)
    for i in range(pairs):
        key[:, 128 * i : 128 * i + 128] = kv[:, 256 * i : 256 * i + 128]
        val[:, 128 * i : 128 * i + 128] = kv[:, 256 * i + 128 : 256 * i + 256]
    cross_out[...] = taken(wide, thin)
    self_out[...] = taken(wide + thin, thin)
    cross_q[...] = taken(wide + 2 * thin, thin).T
    rest = taken(wide + 3 * thin, 3 * thin)
    for i in range(3):
        self_in[i][...] = rest[4 * thin * i : 4 * thin * (i + 1)].T


def unpack(value, inner):
    count, rows, width = value.shape
    tall = jax.ShapeDtypeStruct((width, inner), jnp.float32)
    flat = jax.ShapeDtypeStruct((inner, width), jnp.float32)
    by_row = pl.BlockSpec((width // 4, inner), lambda i: (i, 0))
    by_out = pl.BlockSpec((inner // 4, width), lambda i: (i, 0))
    by_column = pl.BlockSpec((width, inner // 4), lambda i: (0, i))
    return pl.pallas_call(
        functools.partial(unpack_kernel, inner // 128),
        grid=(4,),
        in_specs=[pl.BlockSpec((4, rows, width), lambda i: (i, 0, 0))],
        out_specs=[by_row, by_row, by_out, by_out] + [by_column] * 4,
        out_shape=[tall, tall, flat, flat] + [tall] * 4,
        cost_estimate=cost(0, 6 * value.size),
        compiler_params=pltpu.CompilerParams(vmem_limit_bytes=ATTEND_VMEM),
    )(value)


def finish_kernel(info, *refs):
    target = refs[4]
    rows = refs[0].shape[1]
    which = 2 * ((pl.program_id(0) >> 1) ^ info[1]) + ((pl.program_id(0) & 1) ^ (info[0] >> 2))

    for held in range(4):

        @pl.when(which == held)
        def _():
            for i in range(4):
                target[rows * i : rows * (i + 1), :] = refs[held][i ^ (info[0] & 3)].astype(
                    jnp.float32
                )


def finish(done, order, place, shape):
    count, rows, width = done[0].shape
    mine = place[order[0]] * 4 + place[order[1]] * 2
    info = jnp.stack([mine, place["core"]])
    return pl.pallas_call(
        finish_kernel,
        grid_spec=pltpu.PrefetchScalarGridSpec(
            num_scalar_prefetch=1,
            grid=(4,),
            in_specs=[pl.BlockSpec((4, rows, width), lambda i, s: (0, 0, 0))] * 4,
            out_specs=pl.BlockSpec((shape[0] // 4, shape[1]), lambda i, s: (i, 0)),
        ),
        out_shape=jax.ShapeDtypeStruct(shape, jnp.float32),
        cost_estimate=cost(0, 4 * done[0].size * 12),
        compiler_params=pltpu.CompilerParams(vmem_limit_bytes=ATTEND_VMEM),
    )(info, *done)


def pieces(*values):
    split = [v.reshape(16, v.shape[0] // 16, v.shape[1]) for v in values]
    return split[0] if len(split) == 1 else jnp.concatenate(split, axis=1)


def low(value):
    return value.astype(jnp.bfloat16)


def on_chip_group(
    tokens,
    memory,
    cotangent,
    target_lengths,
    memory_lengths,
    norm_self,
    query_self,
    key_self,
    value_self,
    out_self,
    bias_table,
    norm_cross,
    query_cross,
    key_cross,
    value_cross,
    out_cross,
    norm_ffn,
    ffn_in,
    ffn_out,
):
    examples = target_lengths.shape[0]
    groups = lax.axis_size("dp")
    net = links(groups)
    index = lax.axis_index("dp")
    place = {
        "y": lax.axis_index("mp"),
        "core": index & 1,
        "x": (index >> 1) & 1,
        "zl": (index >> 2) & 1,
        "zh": (index >> 3) & 1,
    }
    core = place["core"]
    settled = (core == place["y"]).astype(jnp.int32)
    place["settled"] = settled[None]
    rows, width = tokens.shape
    half_pos = rows // examples
    inner = query_self.shape[1]
    pairs = inner // 128

    def swap(value):
        return permute(value, net["core"])

    def both(value):
        return jnp.stack([value, swap(value)])

    def flat(value):
        return value.reshape(-1, value.shape[2])

    def turn(value):
        return permute(value, net["turn"])

    lengths = jnp.concatenate([target_lengths, memory_lengths]).astype(jnp.float32)
    table_rows = bias_table.astype(jnp.float32).reshape(-1, 128)
    facts = jnp.concatenate(
        [jnp.pad(lengths, (0, 128 - lengths.size))[None], table_rows], axis=0
    )
    facts = jnp.pad(facts, ((0, 8 - facts.shape[0]), (0, 0)))
    counts = jnp.broadcast_to(jnp.sum(target_lengths).astype(jnp.float32), (8, 128))
    tok, facts, counts, self_in, cross_q, cross_kv, self_out, cross_out = gather(
        tokens,
        facts,
        counts,
        [query_self, key_self, value_self, query_cross, key_cross, value_cross, out_self, out_cross],
        groups,
        examples,
    )
    tok = tok.reshape(rows, width)
    target_len = facts[0, :examples].astype(jnp.int32)
    memory_len = facts[0, examples : 2 * examples].astype(jnp.int32)
    table = facts[1 : 1 + table_rows.shape[0]].reshape(bias_table.shape)
    group_count = jnp.sum(target_len).astype(jnp.float32)
    token_scale = groups * group_count / counts[0, 0]
    self_info = jnp.concatenate([core[None], target_len])
    cross_info = jnp.concatenate([core[None], memory_len])
    memory_after, tok = tie(memory, tok)
    mem_raw = turn(memory_after)

    span = 2 * half_pos
    distance = jnp.arange(span, dtype=jnp.int32)
    level = jnp.sum(
        (distance[:, None] >= jnp.asarray(bucket_edges())[None, :]).astype(jnp.int32), axis=-1
    )
    level_hot = (level[:, None] == jnp.arange(BUCKETS, dtype=jnp.int32)[None, :]).astype(
        jnp.float32
    )
    bias = jnp.einsum("db,bh->hd", level_hot, table, precision=highest).reshape(-1, 2, span)

    tok_float = tok.astype(jnp.float32)
    n1 = both(low(rms_norm(tok_float, norm_self.astype(jnp.float32))))
    qkv = low(nn(flat(n1), self_in)).reshape(2, rows, -1)
    cot_after, qkv = tie(cotangent, qkv)
    cot_raw = turn(cot_after)
    a1 = self_forward(self_info, qkv, bias, examples)
    r1 = tok_float + (nn(a1[0], self_out) + swap(nn(a1[1], self_out)))

    mem = reorder(False, memory, mem_raw, place["settled"], examples)
    mem_far = swap(mem)
    kv, kv_far = low(nn(mem, cross_kv)), low(nn(mem_far, cross_kv))
    n2 = both(low(rms_norm(r1, norm_cross.astype(jnp.float32))))
    q2 = low(nn(flat(n2), cross_q)).reshape(2, rows, -1)

    cot = reorder(False, cotangent, cot_raw, place["settled"], examples)
    positions = core * half_pos + jnp.arange(half_pos, dtype=jnp.int32)
    live = (positions[None, :] < target_len[:, None]).astype(jnp.float32).reshape(rows, 1)
    dy = cot.astype(jnp.float32) * live * token_scale
    gy, q2 = tie(low(dy), q2)
    gy_far = permute(gy, net["y"])

    a2 = cross_forward(cross_info, q2, kv, kv_far, examples)
    a2, gy_far = tie(a2, gy_far)
    r2 = r1 + (nn(a2[0], cross_out) + swap(nn(a2[1], cross_out)))

    n3 = low(rms_norm(r2, norm_ffn.astype(jnp.float32)))
    n3_far = permute(n3, net["y"])
    out_own, out_far, dn_own, dn_far, ffn_out_part, ffn_in_part = ffn(
        n3, n3_far, gy, gy_far, ffn_in, ffn_out
    )
    dn_far = permute(dn_far, net["y"])
    first = pieces(ffn_out_part)
    second = pieces(ffn_in_part)
    first, second = halve(first, "core", place, net), halve(second, "core", place, net)
    first_in, second_in = part_out(first, "x", place, net), part_out(second, "zl", place, net)
    dn3 = dn_own + dn_far.astype(jnp.float32)
    back, gain_three = norm_backward(r2, norm_ffn, dn3)
    dr2 = dy + back

    g2 = both(low(dr2))
    da2 = low(nt(flat(g2), cross_out)).reshape(2, rows, -1)
    out_far = permute(out_far, net["y"])
    dq2, dkv, dkv_far = cross_backward(cross_info, q2, kv, kv_far, da2, examples)
    dq2, first_in, second_in, out_far = tie(dq2, first_in, second_in, out_far)
    first = part_in(first, first_in, "x", place)
    second = part_in(second, second_in, "zl", place)
    first_in, second_in = part_out(first, "zl", place, net), part_out(second, "zh", place, net)
    block_out = low(r2 + (out_own + out_far.astype(jnp.float32)))
    block_back = turn(block_out)
    memory_grad = low(
        nt(dkv, cross_kv) + swap(low(nt(dkv_far, cross_kv))).astype(jnp.float32)
    )
    memory_back = turn(memory_grad)
    dn2 = nt(dq2[0], cross_q) + swap(nt(dq2[1], cross_q))
    back, gain_two = norm_backward(r1, norm_cross, dn2)
    dr1 = dr2 + back
    cross_kv_part = low(tn(mem, dkv) + tn(mem_far, dkv_far))
    cross_out_part = low(tn(flat(a2), flat(g2)))
    cross_q_part = low(tn(flat(dq2), flat(n2)))

    g1 = both(low(dr1))
    self_out_part = low(tn(flat(a1), flat(g1)))
    da1 = low(nt(flat(g1), self_out)).reshape(2, rows, -1)
    head_parts = pieces(cross_kv_part, cross_out_part, self_out_part, cross_q_part)
    da1, first_in, second_in, head_parts, memory_grad = tie(
        da1, first_in, second_in, head_parts, memory_grad
    )
    first = part_in(first, first_in, "zl", place)
    second = part_in(second, second_in, "zh", place)
    first_in, second_in = permute(first, net["zh"]), permute(second, net["x"])
    dqkv, by_distance = self_backward(self_info, qkv, bias, da1, examples)
    dqkv, first_in, second_in = tie(dqkv, first_in, second_in)
    first, second = add_low(first, first_in), add_low(second, second_in)
    first_in, second_in = permute(first, net["zl"]), permute(second, net["zh"])
    self_in_part = low(tn(flat(dqkv), flat(n1)))
    dn1 = nt(dqkv[0], self_in) + swap(nt(dqkv[1], self_in))
    back, gain_one = norm_backward(tok_float, norm_self, dn1)
    tokens_grad = low(dr1 + back)
    tokens_back = turn(tokens_grad)

    bias_part = jnp.einsum(
        "hd,db->bh", by_distance.reshape(-1, span), level_hot, precision=highest
    )
    bias_row = jnp.pad(bias_part.reshape(1, -1), ((0, 0), (0, width - bias_part.size)))
    small = jnp.concatenate(
        [gain_one[None], gain_two[None], gain_three[None], bias_row, jnp.zeros((4, width))], axis=0
    )
    head_parts = jnp.concatenate([head_parts, pieces(self_in_part)], axis=1)
    head_parts, small, first_in, second_in = tie(head_parts, small, first_in, second_in)
    first, second = beside(first, first_in), beside(second, second_in)
    first_in, second_in = permute(first, net["x"]), permute(second, net["zl"])
    first_far, second_far = swap(first), swap(second)
    heads_done, small = settle(head_parts, small, groups)
    small, first_in, second_in, first_far, second_far = tie(
        small, first_in, second_in, first_far, second_far
    )
    first = (first, first_in, first_far, swap(first_in))
    second = (second, second_in, second_far, swap(second_in))
    gains = small[0, :3] + small[1, :3]
    bias_sum = jnp.where(settled == 1, small[0, 3], small[1, 3])
    bias_grad = bias_sum[: bias_part.size].reshape(bias_part.shape)
    block_out = reorder(True, block_out, block_back, place["settled"], examples)
    tokens_grad = reorder(True, tokens_grad, tokens_back, place["settled"], examples)
    memory_grad = reorder(True, memory_grad, memory_back, place["settled"], examples)

    ffn_out_grad = finish(first, ("x", "zl"), place, ffn_out.shape)
    ffn_in_grad = finish(second, ("zl", "zh"), place, ffn_in.shape)
    (
        key_cross_grad,
        value_cross_grad,
        out_cross_grad,
        out_self_grad,
        query_cross_grad,
        query_self_grad,
        key_self_grad,
        value_self_grad,
    ) = unpack(heads_done, inner)
    return (
        block_out,
        tokens_grad,
        memory_grad,
        gains[0],
        query_self_grad,
        key_self_grad,
        value_self_grad,
        out_self_grad,
        bias_grad,
        gains[1],
        query_cross_grad,
        key_cross_grad,
        value_cross_grad,
        out_cross_grad,
        gains[2],
        ffn_in_grad,
        ffn_out_grad,
    )


def solution(mesh):
    placed = (
        P(("dp", "mp"), None),
        P(("dp", "mp"), None),
        P(("dp", "mp"), None),
        P("dp"),
        P("dp"),
        P(),
        P(None, "mp"),
        P(None, "mp"),
        P(None, "mp"),
        P("mp", None),
        P(None, "mp"),
        P(),
        P(None, "mp"),
        P(None, "mp"),
        P(None, "mp"),
        P("mp", None),
        P(),
        P(None, "mp"),
        P("mp", None),
    )
    near = mesh.shape["mp"] == 2 and mesh.shape["dp"] == 16
    return jax.shard_map(
        on_chip_group if near else on_device,
        mesh=mesh,
        in_specs=placed,
        out_specs=(
            P(("dp", "mp"), None),
            P(("dp", "mp"), None),
            P(("dp", "mp"), None),
            P(),
            P(None, "mp"),
            P(None, "mp"),
            P(None, "mp"),
            P("mp", None),
            P(None, "mp"),
            P(),
            P(None, "mp"),
            P(None, "mp"),
            P(None, "mp"),
            P("mp", None),
            P(),
            P(None, "mp"),
            P("mp", None),
        ),
        check_vma=False,
    )
```

```python
import functools
import math

import jax
import jax.numpy as jnp
import numpy as np
from jax import lax
from jax.experimental import pallas as pl
from jax.experimental.pallas import tpu as pltpu
from jax.sharding import PartitionSpec as P

HEAD_DIM = 64
BUCKETS = 32


epsilon = 1e-06
masked_score = -1e30
highest = lax.Precision.HIGHEST


def bucket_edges():
    exact = list(range(1, 17))
    spaced = [int(math.ceil(16.0 * 8.0 ** ((level - 16) / 16.0))) for level in range(17, 32)]
    return np.array(exact + spaced, dtype=np.int32)


def rms_norm(value, gain):
    factor = lax.rsqrt(jnp.mean(value * value, axis=-1, keepdims=True) + epsilon)
    return value * factor * gain


def gather_rows(value):
    return lax.all_gather(value, "mp", axis=0, tiled=True)


def spread_rows(value):
    return lax.psum_scatter(value, "mp", scatter_dimension=0, tiled=True)


def matmul(left, right):
    return jnp.dot(left, right, preferred_element_type=jnp.float32)


def left_product(left, right):
    return lax.dot_general(
        left, right, (((0,), (0,)), ((), ())), preferred_element_type=jnp.float32
    )


def right_product(left, right):
    return lax.dot_general(
        left, right, (((1,), (1,)), ((), ())), preferred_element_type=jnp.float32
    )


def attend_forward(query, key_rows, value_rows, score_bias, mask):
    scores = jnp.einsum("pehd,kehd->ehpk", query, key_rows, preferred_element_type=jnp.float32)
    if score_bias is not None:
        scores = scores + score_bias[None]
    scores = jnp.where(mask, scores, masked_score)
    row_max = jnp.max(scores, axis=-1, keepdims=True)
    weights = jnp.exp(scores - row_max)
    probs = weights / jnp.sum(weights, axis=-1, keepdims=True)
    probs_low = probs.astype(jnp.bfloat16)
    output = jnp.einsum(
        "ehpk,kehd->pehd", probs_low, value_rows, preferred_element_type=jnp.float32
    )
    return (probs, probs_low, output.astype(jnp.bfloat16))


def attend_backward(query, key_rows, value_rows, probs, probs_low, grad_mixed):
    grad_probs = jnp.einsum(
        "pehd,kehd->ehpk", grad_mixed, value_rows, preferred_element_type=jnp.float32
    )
    inner_sum = jnp.sum(probs * grad_probs, axis=-1, keepdims=True)
    grad_scores = (probs * (grad_probs - inner_sum)).astype(jnp.bfloat16)
    grad_query = jnp.einsum(
        "ehpk,kehd->pehd", grad_scores, key_rows, preferred_element_type=jnp.float32
    )
    grad_keys = jnp.einsum(
        "ehpk,pehd->kehd", grad_scores, query, preferred_element_type=jnp.float32
    )
    grad_values = jnp.einsum(
        "ehpk,pehd->kehd", probs_low, grad_mixed, preferred_element_type=jnp.float32
    )
    return (
        grad_scores,
        grad_query.astype(jnp.bfloat16),
        grad_keys.astype(jnp.bfloat16),
        grad_values.astype(jnp.bfloat16),
    )


def norm_backward(value, gain, grad_normed):
    pullback = jax.vjp(rms_norm, value, gain.astype(jnp.float32))[1]
    return pullback(grad_normed)


def on_device(
    tokens,
    memory,
    cotangent,
    target_lengths,
    memory_lengths,
    norm_self,
    query_self,
    key_self,
    value_self,
    out_self,
    bias_table,
    norm_cross,
    query_cross,
    key_cross,
    value_cross,
    out_cross,
    norm_ffn,
    ffn_in,
    ffn_out,
):
    examples = target_lengths.shape[0]
    local_rows = tokens.shape[0]
    parts = lax.axis_size("mp")
    device_rank = lax.axis_index("mp")
    local_pos = local_rows // examples
    total_pos = local_pos * parts
    memory_local = memory.shape[0]
    memory_total = memory_local * parts
    memory_pos = memory_total // examples
    inner_local = query_self.shape[1]
    heads = inner_local // HEAD_DIM
    total_rows = local_rows * parts
    group_count = jnp.sum(target_lengths).astype(jnp.float32)
    total_count = lax.psum(group_count, "dp")
    token_scale = lax.axis_size("dp") * group_count / total_count
    positions = device_rank * local_pos + jnp.arange(local_pos, dtype=jnp.int32)
    live_rows = (
        (positions[:, None] < target_lengths[None, :]).astype(jnp.float32).reshape(local_rows, 1)
    )
    target_pos = jnp.arange(total_pos, dtype=jnp.int32)
    distance = jnp.maximum(target_pos[:, None] - target_pos[None, :], 0)
    buckets = jnp.sum(
        (distance[:, :, None] >= jnp.asarray(bucket_edges())[None, None, :]).astype(jnp.int32),
        axis=-1,
    )
    table_hot = (buckets[:, :, None] == jnp.arange(BUCKETS, dtype=jnp.int32)[None, None, :]).astype(
        jnp.float32
    )
    causal = target_pos[None, :] <= target_pos[:, None]
    self_mask = causal[None, None] & (
        target_pos[None, None, None, :] < target_lengths[:, None, None, None]
    )
    cross_pos = jnp.arange(memory_pos, dtype=jnp.int32)
    cross_mask = cross_pos[None, None, None, :] < memory_lengths[:, None, None, None]
    score_bias = jnp.einsum(
        "qkb,bh->hqk", table_hot, bias_table.astype(jnp.float32), precision=highest
    )

    def target_view(value):
        return value.reshape(total_pos, examples, heads, HEAD_DIM)

    def memory_view(value):
        return value.reshape(memory_pos, examples, heads, HEAD_DIM)

    tokens_float = tokens.astype(jnp.float32)
    normed_one = rms_norm(tokens_float, norm_self.astype(jnp.float32)).astype(jnp.bfloat16)
    rows_one = gather_rows(normed_one)
    self_weights = jnp.concatenate([query_self, key_self, value_self], axis=1)
    projected = matmul(rows_one, self_weights).astype(jnp.bfloat16)
    query_one = target_view(projected[:, :inner_local])
    keys_one = target_view(projected[:, inner_local : 2 * inner_local])
    values_one = target_view(projected[:, 2 * inner_local :])
    probs_one, low_one, mixed_one = attend_forward(
        query_one, keys_one, values_one, score_bias, self_mask
    )
    mixed_rows_one = mixed_one.reshape(total_rows, inner_local)
    resid_one = tokens_float + spread_rows(matmul(mixed_rows_one, out_self))
    normed_two = rms_norm(resid_one, norm_cross.astype(jnp.float32)).astype(jnp.bfloat16)
    rows_two = gather_rows(normed_two)
    query_two = target_view(matmul(rows_two, query_cross).astype(jnp.bfloat16))
    memory_all = lax.all_gather(memory, "mp", axis=0, tiled=True)
    cross_kv = matmul(memory_all, jnp.concatenate([key_cross, value_cross], axis=1)).astype(
        jnp.bfloat16
    )
    keys_flat = cross_kv[:, :inner_local]
    values_flat = cross_kv[:, inner_local:]
    keys_two = memory_view(keys_flat)
    values_two = memory_view(values_flat)
    probs_two, low_two, mixed_two = attend_forward(
        query_two, keys_two, values_two, None, cross_mask
    )
    mixed_rows_two = mixed_two.reshape(total_rows, inner_local)
    resid_two = resid_one + spread_rows(matmul(mixed_rows_two, out_cross))
    normed_three = rms_norm(resid_two, norm_ffn.astype(jnp.float32)).astype(jnp.bfloat16)
    rows_three = gather_rows(normed_three)
    pre_act = matmul(rows_three, ffn_in)
    hidden = jax.nn.gelu(pre_act).astype(jnp.bfloat16)
    block_out = resid_two + spread_rows(matmul(hidden, ffn_out))
    grad_out = cotangent.astype(jnp.float32) * live_rows * token_scale
    grad_rows_three = gather_rows(grad_out.astype(jnp.bfloat16))
    ffn_out_grad = left_product(hidden, grad_rows_three)
    grad_hidden = right_product(grad_rows_three, ffn_out)
    gelu_back = jax.vjp(jax.nn.gelu, pre_act)[1]
    grad_pre = gelu_back(grad_hidden)[0].astype(jnp.bfloat16)
    ffn_in_grad = left_product(rows_three, grad_pre)
    grad_normed_three = spread_rows(right_product(grad_pre, ffn_in))
    grad_resid_three, gain_three = norm_backward(resid_two, norm_ffn, grad_normed_three)
    grad_two = grad_out + grad_resid_three
    grad_rows_two = gather_rows(grad_two.astype(jnp.bfloat16))
    out_cross_grad = left_product(mixed_rows_two, grad_rows_two)
    grad_mixed_two = target_view(right_product(grad_rows_two, out_cross).astype(jnp.bfloat16))
    cross_back = attend_backward(
        query_two, keys_two, values_two, probs_two, low_two, grad_mixed_two
    )
    grad_query_two = cross_back[1].reshape(total_rows, inner_local)
    grad_keys_two = cross_back[2].reshape(memory_total, inner_local)
    grad_values_two = cross_back[3].reshape(memory_total, inner_local)
    query_cross_grad = left_product(rows_two, grad_query_two)
    grad_normed_two = spread_rows(right_product(grad_query_two, query_cross))
    key_cross_grad = left_product(memory_all, grad_keys_two)
    value_cross_grad = left_product(memory_all, grad_values_two)
    memory_terms = right_product(grad_keys_two, key_cross) + right_product(
        grad_values_two, value_cross
    )
    memory_grad = lax.psum_scatter(memory_terms, "mp", scatter_dimension=0, tiled=True)
    grad_resid_two, gain_two = norm_backward(resid_one, norm_cross, grad_normed_two)
    grad_one = grad_two + grad_resid_two
    grad_rows_one = gather_rows(grad_one.astype(jnp.bfloat16))
    out_self_grad = left_product(mixed_rows_one, grad_rows_one)
    grad_mixed_one = target_view(right_product(grad_rows_one, out_self).astype(jnp.bfloat16))
    self_back = attend_backward(query_one, keys_one, values_one, probs_one, low_one, grad_mixed_one)
    bias_table_grad = jnp.einsum(
        "ehqk,qkb->bh", self_back[0].astype(jnp.float32), table_hot, precision=highest
    )
    grad_projected = jnp.concatenate(
        [
            self_back[1].reshape(total_rows, inner_local),
            self_back[2].reshape(total_rows, inner_local),
            self_back[3].reshape(total_rows, inner_local),
        ],
        axis=1,
    )
    self_weight_grad = left_product(rows_one, grad_projected)
    grad_normed_one = spread_rows(right_product(grad_projected, self_weights))
    grad_resid_one, gain_one = norm_backward(tokens_float, norm_self, grad_normed_one)
    tokens_grad = grad_one + grad_resid_one
    summed = lax.psum(
        (
            self_weight_grad[:, :inner_local],
            self_weight_grad[:, inner_local : 2 * inner_local],
            self_weight_grad[:, 2 * inner_local :],
            out_self_grad,
            bias_table_grad,
            query_cross_grad,
            key_cross_grad,
            value_cross_grad,
            out_cross_grad,
            ffn_in_grad,
            ffn_out_grad,
        ),
        "dp",
    )
    gains = lax.psum((gain_one, gain_two, gain_three), ("dp", "mp"))
    return (
        block_out.astype(jnp.bfloat16),
        tokens_grad.astype(jnp.bfloat16),
        memory_grad.astype(jnp.bfloat16),
        gains[0],
        summed[0],
        summed[1],
        summed[2],
        summed[3],
        summed[4],
        gains[1],
        summed[5],
        summed[6],
        summed[7],
        summed[8],
        gains[2],
        summed[9],
        summed[10],
    )


def links(dp_size):
    total = 2 * dp_size

    def swap(bit):
        return [(at, at ^ bit) for at in range(total)]

    def turned(at):
        return (at & ~3) | ((at & 1) << 1) | ((at >> 1) & 1)

    return {
        "turn": [(at, turned(at)) for at in range(total) if at != turned(at)],
        "give": [(at, at ^ 2) for at in range(total) if (at & 1) == ((at >> 1) & 1)],
        "take": [(at, at ^ 2) for at in range(total) if (at & 1) != ((at >> 1) & 1)],
        "y": swap(1),
        "core": swap(2),
        "x": swap(4),
        "zl": swap(8),
        "zh": swap(16),
    }


def permute(value, pairs):
    return lax.ppermute(value, ("dp", "mp"), pairs)


def reorder_kernel(inverse, examples, info, held, arrived, target):
    def write(source):
        if inverse:
            value = source[...].reshape(-1, source.shape[2])
        else:
            value = source[...]
        rows = value.shape[0]
        chunk = rows // examples
        high = lax.broadcasted_iota(jnp.int32, (rows, rows), 0)
        low = lax.broadcasted_iota(jnp.int32, (rows, rows), 1)
        if inverse:
            hot = low == (high % examples) * chunk + high // examples
        else:
            hot = low == (high % chunk) * examples + high // chunk
        moved = nn(hot.astype(jnp.bfloat16), value).astype(jnp.bfloat16)
        target[...] = moved.reshape(target.shape)

    @pl.when(info[0] == 1)
    def _():
        write(held)

    @pl.when(info[0] == 0)
    def _():
        write(arrived)


def reorder(inverse, held, arrived, settled, examples):
    rows, width = held.shape
    block = 256
    flat = pl.BlockSpec((block, width), lambda i, s: (i, 0))
    flat_shape = (rows, width)
    split_shape = (examples, rows // examples, width)
    split_block = (examples, block // examples, width)
    if inverse:
        held, arrived = held.reshape(split_shape), arrived.reshape(split_shape)
        in_specs = [
            pl.BlockSpec(split_block, lambda i, s: (0, i * s[0], 0)),
            pl.BlockSpec(split_block, lambda i, s: (0, i * (1 - s[0]), 0)),
        ]
        out_spec, out_shape = flat, flat_shape
    else:
        in_specs = [
            pl.BlockSpec((block, width), lambda i, s: (i * s[0], 0)),
            pl.BlockSpec((block, width), lambda i, s: (i * (1 - s[0]), 0)),
        ]
        out_spec = pl.BlockSpec(split_block, lambda i, s: (0, i, 0))
        out_shape = split_shape
    return pl.pallas_call(
        functools.partial(reorder_kernel, inverse, examples),
        grid_spec=pltpu.PrefetchScalarGridSpec(
            num_scalar_prefetch=1,
            grid=(rows // block,),
            in_specs=in_specs,
            out_specs=out_spec,
        ),
        out_shape=jax.ShapeDtypeStruct(out_shape, held.dtype),
        cost_estimate=cost(2 * rows * width * block, 4 * rows * width),
        compiler_params=pltpu.CompilerParams(vmem_limit_bytes=SMALL_VMEM),
    )(settled, held, arrived).reshape(flat_shape)


def memory_kernel(examples, info, *refs):
    sources, weight, rows_out, kv_out = refs[:6], refs[6], refs[7], refs[8]
    block = 256
    chunk = block // examples
    high = lax.broadcasted_iota(jnp.int32, (block, block), 0)
    low = lax.broadcasted_iota(jnp.int32, (block, block), 1)
    hot = (low == (high % chunk) * examples + high // chunk).astype(jnp.bfloat16)

    def write(source):
        parts = []
        for start in range(0, source.shape[0], block):
            moved = nn(hot, source[start : start + block, :]).astype(jnp.bfloat16)
            parts.append(moved.reshape(examples, chunk, moved.shape[1]))
        moved = jnp.concatenate(parts, axis=1)
        rows_out[...] = moved.reshape(rows_out.shape)
        moved = nn(moved.reshape(source.shape), weight[...]).astype(jnp.bfloat16)
        kv_out[...] = moved.reshape(kv_out.shape)

    late = pl.program_id(1) >= 1
    kind = jnp.where(pl.program_id(0) == 0, 0, jnp.where(late, 4, 2)) + info[1]
    for i in range(6):
        pl.when(kind == i)(functools.partial(write, sources[i]))


def memory_rows(y_half, settled, sources, weight, examples):
    rows, width = sources[0].shape
    block = 512
    blocks = rows // block
    shape = (2, examples, rows // examples, width)
    kv_shape = shape[:3] + (weight.shape[1],)

    def source(which):
        half, part = (0, 0) if which < 2 else (1, which // 2 - 1)
        start = part
        last = (blocks if half == 0 else 1 if part == 0 else blocks - 1) - 1

        def index(p, i, s):
            held = jnp.clip(i - start, 0, last)
            return (jnp.where((p == half) & (s[1] == which % 2), held, 0), 0)

        return pl.BlockSpec((block, width), index)

    def out(columns):
        return pl.BlockSpec(
            (1, examples, block // examples, columns),
            lambda p, i, s: ((p + s[0]) & 1, 0, i, 0),
        )

    return pl.pallas_call(
        functools.partial(memory_kernel, examples),
        grid_spec=pltpu.PrefetchScalarGridSpec(
            num_scalar_prefetch=1,
            grid=(2, blocks),
            in_specs=[source(i) for i in range(6)]
            + [pl.BlockSpec(weight.shape, lambda p, i, s: (0, 0))],
            out_specs=[out(width), out(weight.shape[1])],
        ),
        out_shape=[
            jax.ShapeDtypeStruct(shape, weight.dtype),
            jax.ShapeDtypeStruct(kv_shape, weight.dtype),
        ],
        cost_estimate=cost(4 * rows * width * (weight.shape[1] + 256), 12 * rows * width),
        compiler_params=pltpu.CompilerParams(vmem_limit_bytes=ATTEND_VMEM),
    )(jnp.stack([y_half, settled]), *sources, weight)


def nt(left, right):
    return lax.dot_general(
        left, right, (((1,), (1,)), ((), ())), preferred_element_type=jnp.float32
    )


def tn(left, right):
    return lax.dot_general(
        left, right, (((0,), (0,)), ((), ())), preferred_element_type=jnp.float32
    )


def nn(left, right):
    return jnp.dot(left, right, preferred_element_type=jnp.float32)


def one_head(value, head):
    lane = lax.broadcasted_iota(jnp.int32, value.shape, 1)
    return jnp.where(lane // HEAD_DIM == head, value, jnp.zeros_like(value))


def toeplitz(row, size):
    return pltpu.roll(jnp.broadcast_to(row, (size, size)), 0, 1, stride=1, stride_axis=0)


def diagonals(square):
    size = square.shape[0]
    row = lax.broadcasted_iota(jnp.int32, square.shape, 0)
    turned, step = square, 1
    while step < size:
        moved = pltpu.roll(turned, size - step, 1)
        turned = jnp.where((row & step) != 0, moved, turned)
        step *= 2
    return jnp.sum(turned, axis=0, keepdims=True)


def heads_joined(first, second):
    return jnp.concatenate([first, second], axis=0).T


def head_rows(value, head):
    return value[HEAD_DIM * head : HEAD_DIM * (head + 1)]


def self_heads(core, rows, scratch, example):
    half = scratch.shape[1] // 2
    at = pl.ds(example * half, half)
    scratch[example, pl.ds(pl.multiple_of(core * half, half), half), :] = rows[0, at, :]
    scratch[example, pl.ds(pl.multiple_of((1 - core) * half, half), half), :] = rows[1, at, :]
    return scratch[example]


def self_store(core, value, scratch, out, example):
    half = scratch.shape[1] // 2
    at = pl.ds(example * half, half)
    scratch[example] = value
    out[0, at, :] = scratch[example, pl.ds(pl.multiple_of(core * half, half), half), :]
    out[1, at, :] = scratch[example, pl.ds(pl.multiple_of((1 - core) * half, half), half), :]


def self_masks(size, length):
    key_at = lax.broadcasted_iota(jnp.int32, (size, size), 0)
    query_at = lax.broadcasted_iota(jnp.int32, (size, size), 1)
    return jnp.where((key_at <= query_at) & (key_at < length), 0.0, masked_score)


def side_by_side(value):
    return jnp.concatenate([one_head(value, head) for head in range(2)], axis=0)


def own_blocks(value, size):
    return value[:HEAD_DIM, :size], value[HEAD_DIM:, size:]


def self_forward_kernel(examples, info, rows, bias, out, mixed, level, scratch, out_scratch):
    core = info[0]
    size = scratch.shape[1]
    slopes = jnp.concatenate(
        [toeplitz(bias[0, head : head + 1, :], size) for head in range(2)], axis=1
    )
    for example in range(examples):
        joined = self_heads(core, rows, scratch, example)
        query, keys = joined[:, :128], joined[:, 128:256]
        mask = self_masks(size, info[1 + example])
        scores = nt(keys, side_by_side(query)) + slopes + jnp.concatenate([mask, mask], axis=1)
        top = jnp.max(scores, axis=0, keepdims=True)
        weights = jnp.exp(scores - top)
        total = jnp.sum(weights, axis=0, keepdims=True)
        probs = (weights * (1.0 / total)).astype(jnp.bfloat16)
        sums = nn(joined[:, 256:].T, probs)
        parts = own_blocks(sums, size)
        levels = top + jnp.log(total)
        for head in range(2):
            level[0, example, head : head + 1, :] = levels[:, size * head : size * (head + 1)]
            mixed[0, example, HEAD_DIM * head : HEAD_DIM * (head + 1), :] = parts[head]
        result = heads_joined(*parts).astype(jnp.bfloat16)
        self_store(core, result, out_scratch, out, example)


def self_backward_kernel(
    examples,
    info,
    rows,
    bias,
    grads,
    mixed,
    level,
    out,
    out_bias,
    scratch,
    grad_scratch,
    out_scratch,
):
    core = info[0]
    size = scratch.shape[1]
    slopes = jnp.concatenate(
        [toeplitz(bias[0, head : head + 1, :], size) for head in range(2)], axis=1
    )
    sums = None
    for example in range(examples):
        joined = self_heads(core, rows, scratch, example)
        query, keys, values = joined[:, :128], joined[:, 128:256], joined[:, 256:]
        grad = self_heads(core, grads, grad_scratch, example)
        products = grad.astype(jnp.float32).T * mixed[0, example]
        inner = jnp.concatenate(
            [jnp.sum(head_rows(products, head), axis=0, keepdims=True) for head in range(2)],
            axis=1,
        )
        levels = jnp.concatenate([level[0, example, 0:1, :], level[0, example, 1:2, :]], axis=1)
        mask = self_masks(size, info[1 + example])
        heads, grad_heads = side_by_side(query), side_by_side(grad)
        scores = nt(keys, heads) + slopes + jnp.concatenate([mask, mask], axis=1)
        probs = jnp.exp(scores - levels)
        grad_scores = (probs * (nt(values, grad_heads) - inner)).astype(jnp.bfloat16)
        square = grad_scores.astype(jnp.float32)
        sums = square if sums is None else sums + square
        result = jnp.concatenate(
            [
                heads_joined(*own_blocks(nn(keys.T, grad_scores), size)),
                nn(grad_scores, heads),
                nn(probs.astype(jnp.bfloat16), grad_heads),
            ],
            axis=1,
        ).astype(jnp.bfloat16)
        self_store(core, result, out_scratch, out, example)
    for head in range(2):
        out_bias[0, head : head + 1, :] = diagonals(sums[:, size * head : size * (head + 1)])


def by_length(length, span, body):
    quarter = span // 4
    for part in range(1, 5):
        keys = part * quarter
        inside = length > keys - quarter
        if part < 4:
            inside = inside & (length <= keys)

        @pl.when(inside)
        def _():
            body(keys)


def masked_tail(scores, length, quarter):
    keys, count = scores.shape
    key_at = keys - quarter + lax.broadcasted_iota(jnp.int32, (quarter, count), 0)
    tail = scores[keys - quarter :] + jnp.where(key_at < length, 0.0, masked_score)
    if keys == quarter:
        return tail
    return jnp.concatenate([scores[: keys - quarter], tail], axis=0)


def cross_forward_kernel(info, queries, kv, out, mixed, level):
    length = info[pl.program_id(0)]
    query = queries[...].reshape(-1, 128)
    count = query.shape[0]
    span = 2 * kv.shape[1]
    heads = side_by_side(query)

    def body(keys):
        joined = kv[...].reshape(span, 256)[:keys]
        scores = masked_tail(nt(joined[:, :128], heads), length, span // 4)
        top = jnp.max(scores, axis=0, keepdims=True)
        weights = jnp.exp(scores - top)
        total = jnp.sum(weights, axis=0, keepdims=True)
        probs = (weights * (1.0 / total)).astype(jnp.bfloat16)
        sums = nn(joined[:, 128:].T, probs)
        parts = own_blocks(sums, count)
        levels = top + jnp.log(total)
        for head in range(2):
            mixed[0, 0, HEAD_DIM * head : HEAD_DIM * (head + 1), :] = parts[head]
            level[0, 0, head : head + 1, :] = levels[:, count * head : count * (head + 1)]
        out[...] = heads_joined(*parts).astype(jnp.bfloat16).reshape(out.shape)

    by_length(length, span, body)


def cross_backward_kernel(info, queries, kv, grads, mixed, level, dq, dkv):
    length = info[pl.program_id(0)]
    query = queries[...].reshape(-1, 128)
    count = query.shape[0]
    grad = grads[...].reshape(-1, 128)
    span = 2 * kv.shape[1]
    heads, grad_heads = side_by_side(query), side_by_side(grad)
    products = grad.astype(jnp.float32).T * mixed[0, 0]
    inner = jnp.concatenate(
        [jnp.sum(head_rows(products, head), axis=0, keepdims=True) for head in range(2)], axis=1
    )
    levels = jnp.concatenate([level[0, 0, 0:1, :], level[0, 0, 1:2, :]], axis=1)

    def body(keys):
        joined = kv[...].reshape(span, 256)[:keys]
        scores = masked_tail(nt(joined[:, :128], heads), length, span // 4)
        probs = jnp.exp(scores - levels)
        grad_scores = (probs * (nt(joined[:, 128:], grad_heads) - inner)).astype(jnp.bfloat16)
        result = jnp.concatenate(
            [nn(grad_scores, heads), nn(probs.astype(jnp.bfloat16), grad_heads)], axis=1
        ).astype(jnp.bfloat16)
        if keys < span:
            result = jnp.concatenate(
                [result, jnp.zeros((span - keys, 256), jnp.bfloat16)], axis=0
            )
        dkv[...] = result.reshape(dkv.shape)
        sums = nn(joined[:, :128].T, grad_scores)
        dq[...] = heads_joined(*own_blocks(sums, count)).astype(jnp.bfloat16).reshape(dq.shape)

    by_length(length, span, body)


MIB = 1024 * 1024


def cost(flops, moved, exps=0):
    return pl.CostEstimate(
        flops=int(flops), bytes_accessed=int(moved), transcendentals=int(exps)
    )


SMALL_VMEM = 12 * MIB
ATTEND_VMEM = 24 * MIB
FFN_VMEM = 44 * MIB
SETTLE_VMEM = 48 * MIB
MESH = pl.DeviceIdType.MESH
SMEM_SPEC = pl.BlockSpec(memory_space=pltpu.SMEM)


def self_forward(info, rows, bias, examples):
    _, count, width = rows.shape
    pairs, size = width // 384, count // examples
    return pl.pallas_call(
        functools.partial(self_forward_kernel, examples),
        grid=(pairs,),
        in_specs=[
            SMEM_SPEC,
            pl.BlockSpec((2, count, 384), lambda h: (0, 0, h)),
            pl.BlockSpec((1, 2, 2 * size), lambda h: (h, 0, 0)),
        ],
        out_specs=[
            pl.BlockSpec((2, count, 128), lambda h: (0, 0, h)),
            pl.BlockSpec((1, examples, 128, 2 * size), lambda h: (h, 0, 0, 0)),
            pl.BlockSpec((1, examples, 2, 2 * size), lambda h: (h, 0, 0, 0)),
        ],
        out_shape=[
            jax.ShapeDtypeStruct((2, count, pairs * 128), jnp.bfloat16),
            jax.ShapeDtypeStruct((pairs, examples, 128, 2 * size), jnp.float32),
            jax.ShapeDtypeStruct((pairs, examples, 2, 2 * size), jnp.float32),
        ],
        scratch_shapes=[
            pltpu.VMEM((examples, 2 * size, 384), jnp.bfloat16),
            pltpu.VMEM((examples, 2 * size, 128), jnp.bfloat16),
        ],
        cost_estimate=cost(
            2 * 2 * examples * 2 * pairs * (2 * size) ** 2 * 256 * 2,
            8 * rows.size,
            examples * 2 * pairs * (2 * size) ** 2,
        ),
        compiler_params=pltpu.CompilerParams(vmem_limit_bytes=ATTEND_VMEM),
    )(info, rows, bias)


def self_backward(info, rows, bias, grads, mixed, level, examples):
    _, count, width = rows.shape
    pairs, size = width // 384, count // examples
    row = pl.BlockSpec((1, 2, 2 * size), lambda h: (h, 0, 0))
    wide = pl.BlockSpec((2, count, 384), lambda h: (0, 0, h))
    return pl.pallas_call(
        functools.partial(self_backward_kernel, examples),
        grid=(pairs,),
        in_specs=[
            SMEM_SPEC,
            wide,
            row,
            pl.BlockSpec((2, count, 128), lambda h: (0, 0, h)),
            pl.BlockSpec((1, examples, 128, 2 * size), lambda h: (h, 0, 0, 0)),
            pl.BlockSpec((1, examples, 2, 2 * size), lambda h: (h, 0, 0, 0)),
        ],
        out_specs=[wide, row],
        out_shape=[
            jax.ShapeDtypeStruct(rows.shape, jnp.bfloat16),
            jax.ShapeDtypeStruct((pairs, 2, 2 * size), jnp.float32),
        ],
        scratch_shapes=[
            pltpu.VMEM((examples, 2 * size, 384), jnp.bfloat16),
            pltpu.VMEM((examples, 2 * size, 128), jnp.bfloat16),
            pltpu.VMEM((examples, 2 * size, 384), jnp.bfloat16),
        ],
        cost_estimate=cost(
            5 * 2 * examples * 2 * pairs * (2 * size) ** 2 * 256 * 2,
            12 * rows.size,
            examples * 2 * pairs * (2 * size) ** 2,
        ),
        compiler_params=pltpu.CompilerParams(vmem_limit_bytes=ATTEND_VMEM),
    )(info, rows, bias, grads, mixed, level)


def cross_forward(info, queries, kv, examples):
    _, count, width = queries.shape
    pairs, size, span = width // 128, count // examples, kv.shape[1] // examples
    thin = pl.BlockSpec((2, size, 128), lambda e, h: (0, e, h))
    wide = pl.BlockSpec((2, span, 256), lambda e, h: (0, e, h))
    return pl.pallas_call(
        cross_forward_kernel,
        grid=(examples, pairs),
        in_specs=[SMEM_SPEC, thin, wide],
        out_specs=[
            thin,
            pl.BlockSpec((1, 1, 128, 2 * size), lambda e, h: (e, h, 0, 0)),
            pl.BlockSpec((1, 1, 2, 2 * size), lambda e, h: (e, h, 0, 0)),
        ],
        out_shape=[
            jax.ShapeDtypeStruct(queries.shape, jnp.bfloat16),
            jax.ShapeDtypeStruct((examples, pairs, 128, 2 * size), jnp.float32),
            jax.ShapeDtypeStruct((examples, pairs, 2, 2 * size), jnp.float32),
        ],
        cost_estimate=cost(
            2 * 2 * examples * 2 * pairs * 4 * size * span * 256,
            4 * kv.size,
            examples * 2 * pairs * 4 * size * span,
        ),
        compiler_params=pltpu.CompilerParams(vmem_limit_bytes=ATTEND_VMEM),
    )(info, queries, kv)


def cross_backward(info, queries, kv, grads, mixed, level, examples):
    _, count, width = queries.shape
    pairs, size, span = width // 128, count // examples, kv.shape[1] // examples
    thin = pl.BlockSpec((2, size, 128), lambda e, h: (0, e, h))
    wide = pl.BlockSpec((2, span, 256), lambda e, h: (0, e, h))
    return pl.pallas_call(
        cross_backward_kernel,
        grid=(examples, pairs),
        in_specs=[
            SMEM_SPEC,
            thin,
            wide,
            thin,
            pl.BlockSpec((1, 1, 128, 2 * size), lambda e, h: (e, h, 0, 0)),
            pl.BlockSpec((1, 1, 2, 2 * size), lambda e, h: (e, h, 0, 0)),
        ],
        out_specs=[thin, wide],
        out_shape=[
            jax.ShapeDtypeStruct(queries.shape, jnp.bfloat16),
            jax.ShapeDtypeStruct(kv.shape, jnp.bfloat16),
        ],
        cost_estimate=cost(
            5 * 2 * examples * 2 * pairs * 4 * size * span * 256,
            6 * kv.size,
            examples * 2 * pairs * 4 * size * span,
        ),
        compiler_params=pltpu.CompilerParams(vmem_limit_bytes=ATTEND_VMEM),
    )(info, queries, kv, grads, mixed, level)


root = math.sqrt(2.0 / math.pi)
cubic = 0.044715


def ffn_rows_kernel(normed, grad, into, outof, out, back, hidden_out, pre_out, out_sum, back_sum):
    step = pl.program_id(0)

    @pl.when(step == 0)
    def _():
        out_sum[...] = jnp.zeros_like(out_sum)
        back_sum[...] = jnp.zeros_like(back_sum)

    pre = nn(normed[...], into[...])
    grad_hidden = nt(grad[...], outof[...])
    bend = jnp.tanh(root * (pre + cubic * (pre * pre * pre)))
    hidden = (0.5 * pre * (1.0 + bend)).astype(jnp.bfloat16)
    slope = 0.5 * (1.0 + bend) + 0.5 * pre * (1.0 - bend * bend) * (
        root * (1.0 + 3.0 * cubic * (pre * pre))
    )
    grad_pre = (grad_hidden * slope).astype(jnp.bfloat16)
    hidden_out[...] = hidden
    pre_out[...] = grad_pre
    out_sum[...] += nn(hidden, outof[...])
    back_sum[...] += nt(grad_pre, into[...])

    @pl.when(step == pl.num_programs(0) - 1)
    def _():
        out[...] = out_sum[...].astype(out.dtype)
        back[...] = back_sum[...].astype(back.dtype)


def ffn_rows(normed, grad, into, outof, kind):
    rows, width = normed.shape
    units = into.shape[1]
    tile = 512
    whole = pl.BlockSpec((rows, width), lambda i: (0, 0))
    tall = pl.BlockSpec((width, tile), lambda i: (0, i))
    flat = pl.BlockSpec((tile, width), lambda i: (i, 0))
    thin = pl.BlockSpec((rows, tile), lambda i: (0, i))
    return pl.pallas_call(
        ffn_rows_kernel,
        grid=(units // tile,),
        in_specs=[whole, whole, tall, flat],
        out_specs=[whole, whole, thin, thin],
        out_shape=[jax.ShapeDtypeStruct((rows, width), kind)] * 2
        + [jax.ShapeDtypeStruct((rows, units), jnp.bfloat16)] * 2,
        scratch_shapes=[pltpu.VMEM((rows, width), jnp.float32)] * 2,
        cost_estimate=cost(
            4 * 2 * rows * width * units, 12 * rows * width + 4 * width * units, rows * units
        ),
        compiler_params=pltpu.CompilerParams(vmem_limit_bytes=ATTEND_VMEM),
    )(normed, grad, into, outof)


def ffn_weights_kernel(
    n_own, n_far, g_own, g_far, h_own, h_far, p_own, p_far, outof_grad, into_grad, turned
):
    half = n_own.shape[0]

    @pl.when(pl.program_id(0) == 0)
    def _():
        turned[:, :half] = n_own[...].T
        turned[:, half:] = n_far[...].T

    outof_grad[...] = (tn(h_own[...], g_own[...]) + tn(h_far[...], g_far[...])).astype(
        jnp.bfloat16
    )
    into_grad[...] = (
        nn(turned[:, :half], p_own[...]) + nn(turned[:, half:], p_far[...])
    ).astype(jnp.bfloat16)


def ffn_weights(normed, grads, hiddens, pres):
    rows, width = normed[0].shape
    units = hiddens[0].shape[1]
    tile = 512
    whole = pl.BlockSpec((rows, width), lambda i: (0, 0))
    thin = pl.BlockSpec((rows, tile), lambda i: (0, i))
    return pl.pallas_call(
        ffn_weights_kernel,
        grid=(units // tile,),
        in_specs=[whole] * 4 + [thin] * 4,
        out_specs=[
            pl.BlockSpec((tile, width), lambda i: (i, 0)),
            pl.BlockSpec((width, tile), lambda i: (0, i)),
        ],
        out_shape=[
            jax.ShapeDtypeStruct((units, width), jnp.bfloat16),
            jax.ShapeDtypeStruct((width, units), jnp.bfloat16),
        ],
        scratch_shapes=[pltpu.VMEM((width, 2 * rows), jnp.bfloat16)],
        cost_estimate=cost(
            4 * 2 * rows * width * units, 8 * rows * width + 4 * width * units
        ),
        compiler_params=pltpu.CompilerParams(vmem_limit_bytes=30 * MIB),
    )(*normed, *grads, *hiddens, *pres)


def gather_kernel(groups, examples, tokens, memory, facts, counts, *refs):
    weights, refs = refs[:8], refs[8:]
    tok_out, mem_out, facts_out, counts_out, self_in, cross_q, cross_kv = refs[:7]
    self_out, cross_out = refs[7:9]
    raw, landed, round_in, near_send, near_get, send, get = refs[9:]
    index, y = lax.axis_index("dp"), lax.axis_index("mp")
    core, x, z = index % 2, (index // 2) % 2, index // 4
    deep = groups // 4

    def at(c, yy, xx, zz):
        return (zz * 4 + xx * 2 + c, yy)

    z_near = z + 1 - 2 * (z % 2)
    x_side, z_side = at(core, y, 1 - x, z), at(core, y, x, z_near)
    turned = at(1 - core, 1 - y, x, z)
    rounds = [at(1 - core, y, x, z), x_side, z_side]
    step = 2
    while step < deep:
        rounds.append(at(core, y, x, z + step - 2 * step * ((z // step) % 2)))
        step *= 2
    barrier = pltpu.get_barrier_semaphore()
    for partner in rounds:
        pl.semaphore_signal(barrier, inc=1, device_id=partner, device_id_type=MESH)

    @pl.when(core != y)
    def _():
        pl.semaphore_signal(barrier, inc=1, device_id=turned, device_id_type=MESH)
        pl.semaphore_wait(barrier, len(rounds) + 1)

    @pl.when(core == y)
    def _():
        pl.semaphore_wait(barrier, len(rounds))

    homes = [raw.at[0], raw.at[1], raw.at[2], cross_q, raw.at[3], raw.at[4], self_out, cross_out]

    def remote(source, target, sems, slot, device):
        return pltpu.make_async_remote_copy(
            src_ref=source,
            dst_ref=target,
            send_sem=sems[0].at[slot],
            recv_sem=sems[1].at[slot],
            device_id=device,
            device_id_type=MESH,
        )

    mine = x * 2 + z % 2

    def quarter(w, which, first=0, parts=1):
        rows = homes[w].shape[0] // 4
        size = rows // parts
        return homes[w].at[pl.ds(pl.multiple_of(which * rows + first * size, size), size)]

    def along_y(w):
        rows = homes[w].shape[0] // 4
        sent = mine * rows
        return remote(
            weights[w].at[pl.ds(pl.multiple_of(sent, rows), rows)],
            quarter(w, mine),
            (send, get),
            w,
            turned,
        )

    def direct(w, which):
        piece = quarter(w, mine)
        return remote(piece, piece, (send, get), 8 + 2 * w + which, (x_side, z_side)[which])

    def passed(w, which):
        other = mine + (2 - 4 * x if which == 0 else 1 - 2 * (z % 2))
        piece = quarter(w, other, which, 2)
        return remote(piece, piece, (send, get), 24 + 2 * w + which, (z_side, x_side)[which])

    token_copy = remote(tokens, landed, (send, get), 40, turned)
    facts_copy = remote(facts, facts_out, (send, get), 41, turned)
    early = memory.at[pl.ds(0, mem_out.shape[0])]
    memory_copy = remote(early, mem_out, (send, get), 42 + len(rounds), turned)

    @pl.when(core != y)
    def _():
        facts_copy.start()
        for w in range(8):
            along_y(w).start()
        token_copy.start()
        memory_copy.start()

    @pl.when(core == y)
    def _():
        pltpu.make_async_copy(tokens, landed, near_get.at[0]).start()
        pltpu.make_async_copy(facts, facts_out, near_get.at[1]).start()
        for w in range(8):
            pltpu.make_async_copy(weights[w], homes[w], near_get.at[2 + w]).start()

    def count_copy(i):
        return remote(counts_out, round_in.at[i], (near_send, get), 42 + i, rounds[i])

    def count_round(w):
        if w % 2 == 1 and w // 2 < len(rounds):
            count_copy(w // 2).start()
        if w % 2 == 0 and 0 < w <= 2 * len(rounds):
            count_copy(w // 2 - 1).wait()
            counts_out[...] += round_in[w // 2 - 1]

    counts_out[...] = counts[...]
    @pl.when(core == y)
    def _():
        pltpu.make_async_copy(tokens, landed, near_get.at[0]).wait()
        pltpu.make_async_copy(facts, facts_out, near_get.at[1]).wait()
        for w in range(8):
            pltpu.make_async_copy(weights[w], homes[w], near_get.at[2 + w]).wait()

    def share(w):
        if w < 8:
            along_y(w).wait()
            for which in range(2):
                direct(w, which).start()
        if w > 0:
            for which in range(2):
                direct(w - 1, which).wait()
            for which in range(2):
                passed(w - 1, which).start()

    for w in range(9):
        pl.when(core != y)(functools.partial(share, w))
        count_round(w)

    @pl.when(core != y)
    def _():
        facts_copy.wait()
        token_copy.wait()

    rows = landed.shape[0]
    block = 256
    chunk = block // examples
    high = lax.broadcasted_iota(jnp.int32, (block, block), 0)
    low = lax.broadcasted_iota(jnp.int32, (block, block), 1)
    hot = (low == (high % chunk) * examples + high // chunk).astype(jnp.bfloat16)
    for i in range(rows // block):
        moved = nn(hot, landed[pl.ds(i * block, block), :]).astype(jnp.bfloat16)
        tok_out[:, pl.ds(i * chunk, chunk), :] = moved.reshape(examples, chunk, moved.shape[1])

    @pl.when(core != y)
    def _():
        for w in range(8):
            for which in range(2):
                passed(w, which).wait()
        memory_copy.wait()

    for h in range(raw.shape[2] // 128):
        for i in range(3):
            self_in[:, 384 * h + 128 * i : 384 * h + 128 * i + 128] = raw[
                i, :, 128 * h : 128 * h + 128
            ]
        for i in range(2):
            cross_kv[:, 256 * h + 128 * i : 256 * h + 128 * i + 128] = raw[
                3 + i, :, 128 * h : 128 * h + 128
            ]


def gather(tokens, memory, facts, counts, weights, groups, examples):
    rows, width = tokens.shape
    inner = weights[0].shape[1]
    rounds = 2 + (groups // 4).bit_length() - 1
    anywhere = pl.BlockSpec(memory_space=pl.ANY)
    whole = pl.BlockSpec(memory_space=pltpu.VMEM)

    def half(*shape):
        return jax.ShapeDtypeStruct(shape, jnp.bfloat16)

    return pl.pallas_call(
        functools.partial(gather_kernel, groups, examples),
        in_specs=[anywhere, anywhere, whole, whole] + [anywhere] * 8,
        out_specs=[whole] * 9,
        out_shape=[
            half(examples, rows // examples, width),
            half(memory.shape[0] // 4, width),
            jax.ShapeDtypeStruct(facts.shape, facts.dtype),
            jax.ShapeDtypeStruct(counts.shape, counts.dtype),
            half(width, 3 * inner),
            half(width, inner),
            half(width, 2 * inner),
            half(inner, width),
            half(inner, width),
        ],
        scratch_shapes=[
            pltpu.VMEM((5, width, inner), jnp.bfloat16),
            pltpu.VMEM((rows, width), jnp.bfloat16),
            pltpu.VMEM((rounds,) + counts.shape, counts.dtype),
            pltpu.SemaphoreType.DMA((42 + rounds,)),
            pltpu.SemaphoreType.DMA((10,)),
            pltpu.SemaphoreType.DMA((43 + rounds,)),
            pltpu.SemaphoreType.DMA((43 + rounds,)),
        ],
        cost_estimate=cost(0, 150 * MIB),
        compiler_params=pltpu.CompilerParams(
            collective_id=1, has_side_effects=True, vmem_limit_bytes=SETTLE_VMEM
        ),
    )(tokens, memory, facts, counts, *weights)


def add_low(left, right):
    return (left.astype(jnp.float32) + right.astype(jnp.float32)).astype(jnp.bfloat16)


def pick(value, index):
    return lax.dynamic_index_in_dim(value, index, 0, keepdims=False)


axis_of = {"zh": 0, "zl": 1, "x": 2, "core": 3}


def part_sent(total, name, place):
    return lax.dynamic_index_in_dim(total, 1 - place[name], axis_of[name])


def part_out(total, name, place, net):
    return permute(part_sent(total, name, place), net[name])


def part_in(total, arrived, name, place):
    kept = lax.dynamic_index_in_dim(total, place[name], axis_of[name])
    return add_low(kept, arrived)


def halve(total, name, place, net):
    return part_in(total, part_out(total, name, place, net), name, place)


def by_device(value):
    return value.reshape(2, 2, 2, 2, value.shape[0] // 16, value.shape[1])


def tie(*values):
    return lax.optimization_barrier(values)


def settle_kernel(groups, *refs):
    count = len(refs) - 13
    parts, small, refs = refs[:count], refs[count], refs[count + 1 :]
    out, small_out, value, first, second, third, small_in = refs[:7]
    send, receive, small_send, small_get, load = refs[7:]
    index, y = lax.axis_index("dp"), lax.axis_index("mp")
    core, x, z = index % 2, (index // 2) % 2, index // 4
    deep = groups // 4
    chunks, rows = first.shape[0], first.shape[3]

    def at(c, yy, xx, zz):
        return (zz * 4 + xx * 2 + c, yy)

    def part(k):
        return pl.ds(pl.multiple_of(k * rows, rows), rows)

    loads, starts = [], [0]
    for i, ref in enumerate(parts):
        size = ref.shape[1]
        target = value.at[:, pl.ds(starts[-1], size)]
        loads.append(pltpu.make_async_copy(ref, target, load.at[i]))
        loads[-1].start()
        starts.append(starts[-1] + size)
    partners = [at(1 - core, y, x, z), at(core, 1 - y, x, z), at(1 - core, 1 - y, x, z)]
    partners.append(at(core, y, 1 - x, z))
    for step in range(1, deep):
        partners.append(at(core, y, x, (z + step) % deep))
    barrier = pltpu.get_barrier_semaphore()
    for partner in partners:
        pl.semaphore_signal(barrier, inc=1, device_id=partner, device_id_type=MESH)
    pl.semaphore_wait(barrier, len(partners))

    def copy(source, target, slot, k, device):
        return pltpu.make_async_remote_copy(
            src_ref=source,
            dst_ref=target,
            send_sem=send.at[k, slot],
            recv_sem=receive.at[k, slot],
            device_id=device,
            device_id_type=MESH,
        )

    def quarter(k, q):
        return value.at[pl.ds(q * 8, 8), part(k)]

    def to_core(k):
        return copy(quarter(k, 1 - core), first.at[k, 0], 0, k, at(1 - core, core, x, z))

    def to_turned(k):
        return copy(quarter(k, 1 - core), first.at[k, 1], 1, k, at(1 - core, core, x, z))

    def to_same(k):
        return copy(quarter(k, core), first.at[k, 1], 2, k, at(core, core, x, z))

    def arrived(k, slot):
        return copy(quarter(k, core), first.at[k, 1 if slot else 0], slot, k, at(1 - core, y, x, z))

    def along_x(k):
        return copy(
            first.at[k, 1, pl.ds((1 - x) * 4, 4)], second.at[k], 3, k, at(core, y, 1 - x, z)
        )

    def along_z(k, step):
        far = (z + step) % deep
        return copy(
            second.at[k, far], third.at[k, step - 1], 3 + step, k, at(core, y, x, far)
        )

    def back_z(k, step):
        far = (z + step) % deep
        piece = core * 8 + x * 4 + z
        return copy(
            out.at[piece, part(k)], out.at[piece, part(k)], 6 + step, k, at(core, y, x, far)
        )

    def back_x(k):
        held = out.at[pl.ds(core * 8 + x * 4, 4), part(k)]
        return copy(held, held, 10, k, at(core, y, 1 - x, z))

    def back_core(k):
        held = out.at[pl.ds(core * 8, 8), part(k)]
        return copy(held, held, 11, k, at(1 - core, y, x, z))

    rounds = [at(core, 1 - y, x, z), at(core, y, 1 - x, z)]
    step = 1
    while step < deep:
        rounds.append(at(core, y, x, z + step - 2 * step * ((z // step) % 2)))
        step *= 2
    rounds.append(at(1 - core, y, x, z))
    small_out[0] = small[...]

    def small_round(i):
        swap = pltpu.make_async_remote_copy(
            src_ref=small_out.at[0],
            dst_ref=small_in.at[i],
            send_sem=small_send.at[i],
            recv_sem=small_get.at[i],
            device_id=rounds[i],
            device_id_type=MESH,
        )
        swap.start()
        swap.wait()
        if i < len(rounds) - 1:
            small_out[0] = small_out[0] + small_in[i]
        else:
            small_out[1] = small_in[i]

    small_round(0)

    def start(k, carry):
        @pl.when(core == y)
        def _():
            to_core(k).start()

        @pl.when(core != y)
        def _():
            to_same(k).start()
            to_turned(k).start()

        return carry

    for i in range(count):
        loads[i].wait()
        lax.fori_loop(starts[i] // rows, starts[i + 1] // rows, start, 0)
    for i in range(1, len(rounds)):
        small_round(i)

    def total(left, right):
        return (left.astype(jnp.float32) + right.astype(jnp.float32)).astype(jnp.bfloat16)

    def tick(t, carry):
        @pl.when(t < chunks)
        def _():
            k = jnp.minimum(t, chunks - 1)

            @pl.when(core == y)
            def _():
                arrived(k, 2).wait_recv()

                def add(i, c):
                    first[k, 1, i] = total(value[core * 8 + i, part(k)], first[k, 1, i])
                    return c

                lax.fori_loop(0, 8, add, 0)

            @pl.when(core != y)
            def _():
                arrived(k, 0).wait_recv()
                arrived(k, 1).wait_recv()

                def add(i, c):
                    first[k, 1, i] = total(first[k, 0, i], first[k, 1, i])
                    return c

                lax.fori_loop(0, 8, add, 0)

            along_x(k).start()

        @pl.when((t >= 1) & (t < chunks + 1))
        def _():
            k = t - 1
            along_x(k).wait_recv()

            def add(i, c):
                second[k, i] = total(first[k, 1, x * 4 + i], second[k, i])
                return c

            lax.fori_loop(0, deep, add, 0)
            for step in range(1, deep):
                along_z(k, step).start()

        @pl.when((t >= 2) & (t < chunks + 2))
        def _():
            k = t - 2
            for step in range(1, deep):
                along_z(k, step).wait_recv()
            summed = second[k, z].astype(jnp.float32)
            for step in range(1, deep):
                summed = summed + third[k, step - 1].astype(jnp.float32)
            out[core * 8 + x * 4 + z, part(k)] = summed.astype(jnp.bfloat16)
            for step in range(1, deep):
                back_z(k, step).start()

        @pl.when((t >= 3) & (t < chunks + 3))
        def _():
            k = t - 3
            for step in range(1, deep):
                back_z(k, step).wait_recv()
            back_x(k).start()

        @pl.when((t >= 4) & (t < chunks + 4))
        def _():
            k = t - 4
            back_x(k).wait_recv()
            back_core(k).start()

        @pl.when(t >= 5)
        def _():
            back_core(t - 5).wait_recv()

        return carry

    lax.fori_loop(0, chunks + 5, tick, 0)

    def finish_sends(k, carry):
        @pl.when(core == y)
        def _():
            to_core(k).wait_send()

        @pl.when(core != y)
        def _():
            to_same(k).wait_send()
            to_turned(k).wait_send()

        along_x(k).wait_send()
        for step in range(1, deep):
            along_z(k, step).wait_send()
            back_z(k, step).wait_send()
        back_x(k).wait_send()
        back_core(k).wait_send()
        return carry

    lax.fori_loop(0, chunks, finish_sends, 0)


def settle(parts, small, groups):
    count, _, width = parts[0].shape
    kind = parts[0].dtype
    rows = sum(part.shape[1] for part in parts)
    chunk = 16
    chunks = rows // chunk
    deep = groups // 4
    rounds = 3 + deep.bit_length() - 1
    whole = pl.BlockSpec(memory_space=pltpu.VMEM)
    return pl.pallas_call(
        functools.partial(settle_kernel, groups),
        in_specs=[pl.BlockSpec(memory_space=pl.ANY)] * len(parts) + [whole],
        out_specs=[whole, whole],
        out_shape=[
            jax.ShapeDtypeStruct((count, rows, width), kind),
            jax.ShapeDtypeStruct((2,) + small.shape, small.dtype),
        ],
        scratch_shapes=[
            pltpu.VMEM((count, rows, width), kind),
            pltpu.VMEM((chunks, 2, count // 2, chunk, width), kind),
            pltpu.VMEM((chunks, deep, chunk, width), kind),
            pltpu.VMEM((chunks, deep - 1, chunk, width), kind),
            pltpu.VMEM((rounds,) + small.shape, small.dtype),
            pltpu.SemaphoreType.DMA((chunks, 12)),
            pltpu.SemaphoreType.DMA((chunks, 12)),
            pltpu.SemaphoreType.DMA((rounds,)),
            pltpu.SemaphoreType.DMA((rounds,)),
            pltpu.SemaphoreType.DMA((len(parts),)),
        ],
        cost_estimate=cost(0, 60 * count * rows * width),
        compiler_params=pltpu.CompilerParams(
            collective_id=0, has_side_effects=True, vmem_limit_bytes=SETTLE_VMEM
        ),
    )(*parts, small)


def unpack_kernel(pairs, source, key, val, cross_out, self_out, cross_q, *self_in):
    wide = key.shape[0] // 4
    thin = cross_out.shape[0] // 4

    def taken(row, rows):
        block = source[:, row : row + rows, :].astype(jnp.float32)
        return block.reshape(4 * rows, block.shape[2])

    kv = taken(0, wide)
    for i in range(pairs):
        key[:, 128 * i : 128 * i + 128] = kv[:, 256 * i : 256 * i + 128]
        val[:, 128 * i : 128 * i + 128] = kv[:, 256 * i + 128 : 256 * i + 256]
    cross_out[...] = taken(wide, thin)
    self_out[...] = taken(wide + thin, thin)
    cross_q[...] = taken(wide + 2 * thin, thin).T
    rest = taken(wide + 3 * thin, 3 * thin)
    for i in range(3):
        self_in[i][...] = rest[4 * thin * i : 4 * thin * (i + 1)].T


def unpack(value, inner):
    count, rows, width = value.shape
    tall = jax.ShapeDtypeStruct((width, inner), jnp.float32)
    flat = jax.ShapeDtypeStruct((inner, width), jnp.float32)
    by_row = pl.BlockSpec((width // 4, inner), lambda i: (i, 0))
    by_out = pl.BlockSpec((inner // 4, width), lambda i: (i, 0))
    by_column = pl.BlockSpec((width, inner // 4), lambda i: (0, i))
    return pl.pallas_call(
        functools.partial(unpack_kernel, inner // 128),
        grid=(4,),
        in_specs=[pl.BlockSpec((4, rows, width), lambda i: (i, 0, 0))],
        out_specs=[by_row, by_row, by_out, by_out] + [by_column] * 4,
        out_shape=[tall, tall, flat, flat] + [tall] * 4,
        cost_estimate=cost(0, 6 * value.size),
        compiler_params=pltpu.CompilerParams(vmem_limit_bytes=ATTEND_VMEM),
    )(value)


def widen_kernel(source, target):
    target[...] = source[...].astype(jnp.float32)


def widen(value, shape):
    rows, width = shape
    block = rows // 4
    spec = pl.BlockSpec((block, width), lambda i: (i, 0))
    return pl.pallas_call(
        widen_kernel,
        grid=(4,),
        in_specs=[spec],
        out_specs=spec,
        out_shape=jax.ShapeDtypeStruct(shape, jnp.float32),
        cost_estimate=cost(0, 6 * rows * width),
        compiler_params=pltpu.CompilerParams(vmem_limit_bytes=ATTEND_VMEM),
    )(value.reshape(shape))


def pieces(value):
    return value.reshape(16, value.shape[0] // 16, value.shape[1])


def low(value):
    return value.astype(jnp.bfloat16)


def on_chip_group(
    tokens,
    memory,
    cotangent,
    target_lengths,
    memory_lengths,
    norm_self,
    query_self,
    key_self,
    value_self,
    out_self,
    bias_table,
    norm_cross,
    query_cross,
    key_cross,
    value_cross,
    out_cross,
    norm_ffn,
    ffn_in,
    ffn_out,
):
    examples = target_lengths.shape[0]
    groups = lax.axis_size("dp")
    net = links(groups)
    index = lax.axis_index("dp")
    place = {
        "y": lax.axis_index("mp"),
        "core": index & 1,
        "x": (index >> 1) & 1,
        "zl": (index >> 2) & 1,
        "zh": (index >> 3) & 1,
    }
    core = place["core"]
    settled = (core == place["y"]).astype(jnp.int32)
    place["settled"] = settled[None]
    rows, width = tokens.shape
    half_pos = rows // examples
    inner = query_self.shape[1]
    pairs = inner // 128

    def swap(value):
        return permute(value, net["core"])

    def both(value):
        return jnp.stack([value, swap(value)])

    def flat(value):
        return value.reshape(-1, value.shape[2])

    def turn(value):
        return permute(value, net["turn"])

    lengths = jnp.concatenate([target_lengths, memory_lengths]).astype(jnp.float32)
    table_rows = bias_table.astype(jnp.float32).reshape(-1, 128)
    facts = jnp.concatenate(
        [jnp.pad(lengths, (0, 128 - lengths.size))[None], table_rows], axis=0
    )
    facts = jnp.pad(facts, ((0, 8 - facts.shape[0]), (0, 0)))
    counts = jnp.broadcast_to(jnp.sum(target_lengths).astype(jnp.float32), (8, 128))
    mem_near = permute(memory, net["give"])
    held = gather(
        tokens,
        memory,
        facts,
        counts,
        [query_self, key_self, value_self, query_cross, key_cross, value_cross, out_self, out_cross],
        groups,
        examples,
    )
    tok, mem_first, facts, counts, self_in, cross_q, cross_kv = held[:7]
    self_out, cross_out = held[7:]
    tok = tok.reshape(rows, width)
    target_len = facts[0, :examples].astype(jnp.int32)
    memory_len = facts[0, examples : 2 * examples].astype(jnp.int32)
    table = facts[1 : 1 + table_rows.shape[0]].reshape(bias_table.shape)
    group_count = jnp.sum(target_len).astype(jnp.float32)
    token_scale = groups * group_count / counts[0, 0]
    self_info = jnp.concatenate([core[None], target_len])
    mem_sent, tok = tie(memory[mem_first.shape[0] :], tok)
    mem_rest = turn(mem_sent)
    first_far = permute(mem_first, net["take"])

    span = 2 * half_pos
    distance = jnp.arange(span, dtype=jnp.int32)
    level = jnp.sum(
        (distance[:, None] >= jnp.asarray(bucket_edges())[None, :]).astype(jnp.int32), axis=-1
    )
    level_hot = (level[:, None] == jnp.arange(BUCKETS, dtype=jnp.int32)[None, :]).astype(
        jnp.float32
    )
    bias = jnp.einsum("db,bh->hd", level_hot, table, precision=highest).reshape(-1, 2, span)

    tok_float = tok.astype(jnp.float32)
    n1 = both(low(rms_norm(tok_float, norm_self.astype(jnp.float32))))
    qkv = low(nn(flat(n1), self_in)).reshape(2, rows, -1)
    cot_after, qkv = tie(cotangent, qkv)
    cot_raw = turn(cot_after)
    a1, mixed_one, level_one = self_forward(self_info, qkv, bias, examples)
    r1 = tok_float + (nn(a1[0], self_out) + swap(low(nn(a1[1], self_out))).astype(jnp.float32))

    rest_far = permute(mem_rest, net["take"])
    mem, kv = memory_rows(
        place["y"],
        settled,
        [mem_near, memory, mem_first, first_far, mem_rest, rest_far],
        cross_kv,
        examples,
    )
    mem = mem.reshape(2, -1, width)
    kv = kv.reshape(2, -1, 2 * inner)
    n2 = both(low(rms_norm(r1, norm_cross.astype(jnp.float32))))
    q2 = low(nn(flat(n2), cross_q)).reshape(2, rows, -1)

    kv, cot_raw = tie(kv, cot_raw)
    cot = reorder(False, cotangent, cot_raw, place["settled"], examples)
    positions = core * half_pos + jnp.arange(half_pos, dtype=jnp.int32)
    live = (positions[None, :] < target_len[:, None]).astype(jnp.float32).reshape(rows, 1)
    dy = cot.astype(jnp.float32) * live * token_scale
    gy = low(dy)
    gy_far = permute(gy, net["y"])

    a2, mixed_two, level_two = cross_forward(memory_len, q2, kv, examples)
    a2, gy_far = tie(a2, gy_far)
    r2 = r1 + (nn(a2[0], cross_out) + swap(low(nn(a2[1], cross_out))).astype(jnp.float32))

    n3 = low(rms_norm(r2, norm_ffn.astype(jnp.float32)))
    n3_far = permute(n3, net["y"])
    out_own, dn_own, h_own, p_own = ffn_rows(n3, gy, ffn_in, ffn_out, jnp.float32)
    out_own, n3_far = tie(out_own, n3_far)
    out_far, dn_far, h_far, p_far = ffn_rows(n3_far, gy_far, ffn_in, ffn_out, jnp.bfloat16)
    dn_far = permute(dn_far, net["y"])
    ffn_out_part, ffn_in_part = ffn_weights(
        (n3, n3_far), (gy, gy_far), (h_own, h_far), (p_own, p_far)
    )
    dn_far, ffn_out_part = tie(dn_far, ffn_out_part)
    first = lax.psum_scatter(ffn_out_part, "dp", scatter_dimension=0, tiled=True)
    second = lax.psum_scatter(ffn_in_part, "dp", scatter_dimension=0, tiled=True)
    dn3 = dn_own + dn_far.astype(jnp.float32)
    back, gain_three = norm_backward(r2, norm_ffn, dn3)
    dr2 = dy + back

    g2 = both(low(dr2))
    da2 = low(nt(flat(g2), cross_out)).reshape(2, rows, -1)
    da2, out_far = tie(da2, out_far)
    out_far = permute(out_far, net["y"])
    dq2, dkv = cross_backward(memory_len, q2, kv, da2, mixed_two, level_two, examples)
    dkv, out_far = tie(dkv, out_far)
    block_out = low(r2 + (out_own + out_far.astype(jnp.float32)))
    block_back = turn(block_out)
    dkv_swapped = swap(low(nt(pick(dkv, 1 - core), cross_kv)))
    cross_kv_part = low(tn(flat(mem), flat(dkv)))
    dkv_swapped, cross_kv_part = tie(dkv_swapped, cross_kv_part)
    memory_grad = low(nt(pick(dkv, core), cross_kv) + dkv_swapped.astype(jnp.float32))
    memory_grad, cross_kv_part, dq2, first = tie(memory_grad, cross_kv_part, dq2, first)
    first = lax.all_gather(first, "dp", axis=0, tiled=True)
    memory_back = turn(memory_grad)
    dn2 = nt(dq2[0], cross_q) + swap(low(nt(dq2[1], cross_q))).astype(jnp.float32)
    back, gain_two = norm_backward(r1, norm_cross, dn2)
    dr1 = dr2 + back
    cross_out_part = low(tn(flat(a2), flat(g2)))
    cross_q_part = low(tn(flat(dq2), flat(n2)))

    g1 = both(low(dr1))
    self_out_part = low(tn(flat(a1), flat(g1)))
    da1 = low(nt(flat(g1), self_out)).reshape(2, rows, -1)
    head_parts = [cross_kv_part, cross_out_part, self_out_part, cross_q_part]
    da1, head_parts = tie(da1, head_parts)
    dqkv, by_distance = self_backward(
        self_info, qkv, bias, da1, mixed_one, level_one, examples
    )
    self_in_part = low(tn(flat(dqkv), flat(n1)))
    dqkv, self_in_part, memory_back, block_back = tie(
        dqkv, self_in_part, memory_back, block_back
    )
    dn1 = nt(dqkv[0], self_in) + swap(low(nt(dqkv[1], self_in))).astype(jnp.float32)
    back, gain_one = norm_backward(tok_float, norm_self, dn1)
    tokens_grad = low(dr1 + back)
    tokens_back = turn(tokens_grad)

    bias_part = jnp.einsum(
        "hd,db->bh", by_distance.reshape(-1, span), level_hot, precision=highest
    )
    bias_row = jnp.pad(bias_part.reshape(1, -1), ((0, 0), (0, width - bias_part.size)))
    small = jnp.concatenate(
        [gain_one[None], gain_two[None], gain_three[None], bias_row, jnp.zeros((4, width))], axis=0
    )
    head_parts = [pieces(part) for part in head_parts + [self_in_part]]
    head_parts, second = tie(head_parts, second)
    second = lax.all_gather(second, "dp", axis=0, tiled=True)
    heads_done, small = settle(head_parts, small, groups)
    small, first, second, block_back, tokens_back, memory_back = tie(
        small, first, second, block_back, tokens_back, memory_back
    )
    gains = small[0, :3] + small[1, :3]
    bias_sum = jnp.where(settled == 1, small[0, 3], small[1, 3])
    bias_grad = bias_sum[: bias_part.size].reshape(bias_part.shape)
    block_out = reorder(True, block_out, block_back, place["settled"], examples)
    tokens_grad = reorder(True, tokens_grad, tokens_back, place["settled"], examples)
    memory_grad = reorder(True, memory_grad, memory_back, place["settled"], examples)

    ffn_out_grad = widen(first, ffn_out.shape)
    ffn_in_grad = widen(second, ffn_in.shape)
    (
        key_cross_grad,
        value_cross_grad,
        out_cross_grad,
        out_self_grad,
        query_cross_grad,
        query_self_grad,
        key_self_grad,
        value_self_grad,
    ) = unpack(heads_done, inner)
    return (
        block_out,
        tokens_grad,
        memory_grad,
        gains[0],
        query_self_grad,
        key_self_grad,
        value_self_grad,
        out_self_grad,
        bias_grad,
        gains[1],
        query_cross_grad,
        key_cross_grad,
        value_cross_grad,
        out_cross_grad,
        gains[2],
        ffn_in_grad,
        ffn_out_grad,
    )


def solution(mesh):
    placed = (
        P(("dp", "mp"), None),
        P(("dp", "mp"), None),
        P(("dp", "mp"), None),
        P("dp"),
        P("dp"),
        P(),
        P(None, "mp"),
        P(None, "mp"),
        P(None, "mp"),
        P("mp", None),
        P(None, "mp"),
        P(),
        P(None, "mp"),
        P(None, "mp"),
        P(None, "mp"),
        P("mp", None),
        P(),
        P(None, "mp"),
        P("mp", None),
    )
    near = mesh.shape["mp"] == 2 and mesh.shape["dp"] == 16
    return jax.shard_map(
        on_chip_group if near else on_device,
        mesh=mesh,
        in_specs=placed,
        out_specs=(
            P(("dp", "mp"), None),
            P(("dp", "mp"), None),
            P(("dp", "mp"), None),
            P(),
            P(None, "mp"),
            P(None, "mp"),
            P(None, "mp"),
            P("mp", None),
            P(None, "mp"),
            P(),
            P(None, "mp"),
            P(None, "mp"),
            P(None, "mp"),
            P("mp", None),
            P(),
            P(None, "mp"),
            P("mp", None),
        ),
        check_vma=False,
    )
```

```python
import functools
import math

import jax
import jax.numpy as jnp
import numpy as np
from jax import lax
from jax.experimental import pallas as pl
from jax.experimental.pallas import tpu as pltpu
from jax.sharding import PartitionSpec as P

HEAD_DIM = 64
BUCKETS = 32


epsilon = 1e-06
masked_score = -1e30
highest = lax.Precision.HIGHEST


def bucket_edges():
    exact = list(range(1, 17))
    spaced = [int(math.ceil(16.0 * 8.0 ** ((level - 16) / 16.0))) for level in range(17, 32)]
    return np.array(exact + spaced, dtype=np.int32)


def rms_norm(value, gain):
    factor = lax.rsqrt(jnp.mean(value * value, axis=-1, keepdims=True) + epsilon)
    return value * factor * gain


def gather_rows(value):
    return lax.all_gather(value, "mp", axis=0, tiled=True)


def spread_rows(value):
    return lax.psum_scatter(value, "mp", scatter_dimension=0, tiled=True)


def matmul(left, right):
    return jnp.dot(left, right, preferred_element_type=jnp.float32)


def left_product(left, right):
    return lax.dot_general(
        left, right, (((0,), (0,)), ((), ())), preferred_element_type=jnp.float32
    )


def right_product(left, right):
    return lax.dot_general(
        left, right, (((1,), (1,)), ((), ())), preferred_element_type=jnp.float32
    )


def attend_forward(query, key_rows, value_rows, score_bias, mask):
    scores = jnp.einsum("pehd,kehd->ehpk", query, key_rows, preferred_element_type=jnp.float32)
    if score_bias is not None:
        scores = scores + score_bias[None]
    scores = jnp.where(mask, scores, masked_score)
    row_max = jnp.max(scores, axis=-1, keepdims=True)
    weights = jnp.exp(scores - row_max)
    probs = weights / jnp.sum(weights, axis=-1, keepdims=True)
    probs_low = probs.astype(jnp.bfloat16)
    output = jnp.einsum(
        "ehpk,kehd->pehd", probs_low, value_rows, preferred_element_type=jnp.float32
    )
    return (probs, probs_low, output.astype(jnp.bfloat16))


def attend_backward(query, key_rows, value_rows, probs, probs_low, grad_mixed):
    grad_probs = jnp.einsum(
        "pehd,kehd->ehpk", grad_mixed, value_rows, preferred_element_type=jnp.float32
    )
    inner_sum = jnp.sum(probs * grad_probs, axis=-1, keepdims=True)
    grad_scores = (probs * (grad_probs - inner_sum)).astype(jnp.bfloat16)
    grad_query = jnp.einsum(
        "ehpk,kehd->pehd", grad_scores, key_rows, preferred_element_type=jnp.float32
    )
    grad_keys = jnp.einsum(
        "ehpk,pehd->kehd", grad_scores, query, preferred_element_type=jnp.float32
    )
    grad_values = jnp.einsum(
        "ehpk,pehd->kehd", probs_low, grad_mixed, preferred_element_type=jnp.float32
    )
    return (
        grad_scores,
        grad_query.astype(jnp.bfloat16),
        grad_keys.astype(jnp.bfloat16),
        grad_values.astype(jnp.bfloat16),
    )


def norm_backward(value, gain, grad_normed):
    pullback = jax.vjp(rms_norm, value, gain.astype(jnp.float32))[1]
    return pullback(grad_normed)


def on_device(
    tokens,
    memory,
    cotangent,
    target_lengths,
    memory_lengths,
    norm_self,
    query_self,
    key_self,
    value_self,
    out_self,
    bias_table,
    norm_cross,
    query_cross,
    key_cross,
    value_cross,
    out_cross,
    norm_ffn,
    ffn_in,
    ffn_out,
):
    examples = target_lengths.shape[0]
    local_rows = tokens.shape[0]
    parts = lax.axis_size("mp")
    device_rank = lax.axis_index("mp")
    local_pos = local_rows // examples
    total_pos = local_pos * parts
    memory_local = memory.shape[0]
    memory_total = memory_local * parts
    memory_pos = memory_total // examples
    inner_local = query_self.shape[1]
    heads = inner_local // HEAD_DIM
    total_rows = local_rows * parts
    group_count = jnp.sum(target_lengths).astype(jnp.float32)
    total_count = lax.psum(group_count, "dp")
    token_scale = lax.axis_size("dp") * group_count / total_count
    positions = device_rank * local_pos + jnp.arange(local_pos, dtype=jnp.int32)
    live_rows = (
        (positions[:, None] < target_lengths[None, :]).astype(jnp.float32).reshape(local_rows, 1)
    )
    target_pos = jnp.arange(total_pos, dtype=jnp.int32)
    distance = jnp.maximum(target_pos[:, None] - target_pos[None, :], 0)
    buckets = jnp.sum(
        (distance[:, :, None] >= jnp.asarray(bucket_edges())[None, None, :]).astype(jnp.int32),
        axis=-1,
    )
    table_hot = (buckets[:, :, None] == jnp.arange(BUCKETS, dtype=jnp.int32)[None, None, :]).astype(
        jnp.float32
    )
    causal = target_pos[None, :] <= target_pos[:, None]
    self_mask = causal[None, None] & (
        target_pos[None, None, None, :] < target_lengths[:, None, None, None]
    )
    cross_pos = jnp.arange(memory_pos, dtype=jnp.int32)
    cross_mask = cross_pos[None, None, None, :] < memory_lengths[:, None, None, None]
    score_bias = jnp.einsum(
        "qkb,bh->hqk", table_hot, bias_table.astype(jnp.float32), precision=highest
    )

    def target_view(value):
        return value.reshape(total_pos, examples, heads, HEAD_DIM)

    def memory_view(value):
        return value.reshape(memory_pos, examples, heads, HEAD_DIM)

    tokens_float = tokens.astype(jnp.float32)
    normed_one = rms_norm(tokens_float, norm_self.astype(jnp.float32)).astype(jnp.bfloat16)
    rows_one = gather_rows(normed_one)
    self_weights = jnp.concatenate([query_self, key_self, value_self], axis=1)
    projected = matmul(rows_one, self_weights).astype(jnp.bfloat16)
    query_one = target_view(projected[:, :inner_local])
    keys_one = target_view(projected[:, inner_local : 2 * inner_local])
    values_one = target_view(projected[:, 2 * inner_local :])
    probs_one, low_one, mixed_one = attend_forward(
        query_one, keys_one, values_one, score_bias, self_mask
    )
    mixed_rows_one = mixed_one.reshape(total_rows, inner_local)
    resid_one = tokens_float + spread_rows(matmul(mixed_rows_one, out_self))
    normed_two = rms_norm(resid_one, norm_cross.astype(jnp.float32)).astype(jnp.bfloat16)
    rows_two = gather_rows(normed_two)
    query_two = target_view(matmul(rows_two, query_cross).astype(jnp.bfloat16))
    memory_all = lax.all_gather(memory, "mp", axis=0, tiled=True)
    cross_kv = matmul(memory_all, jnp.concatenate([key_cross, value_cross], axis=1)).astype(
        jnp.bfloat16
    )
    keys_flat = cross_kv[:, :inner_local]
    values_flat = cross_kv[:, inner_local:]
    keys_two = memory_view(keys_flat)
    values_two = memory_view(values_flat)
    probs_two, low_two, mixed_two = attend_forward(
        query_two, keys_two, values_two, None, cross_mask
    )
    mixed_rows_two = mixed_two.reshape(total_rows, inner_local)
    resid_two = resid_one + spread_rows(matmul(mixed_rows_two, out_cross))
    normed_three = rms_norm(resid_two, norm_ffn.astype(jnp.float32)).astype(jnp.bfloat16)
    rows_three = gather_rows(normed_three)
    pre_act = matmul(rows_three, ffn_in)
    hidden = jax.nn.gelu(pre_act).astype(jnp.bfloat16)
    block_out = resid_two + spread_rows(matmul(hidden, ffn_out))
    grad_out = cotangent.astype(jnp.float32) * live_rows * token_scale
    grad_rows_three = gather_rows(grad_out.astype(jnp.bfloat16))
    ffn_out_grad = left_product(hidden, grad_rows_three)
    grad_hidden = right_product(grad_rows_three, ffn_out)
    gelu_back = jax.vjp(jax.nn.gelu, pre_act)[1]
    grad_pre = gelu_back(grad_hidden)[0].astype(jnp.bfloat16)
    ffn_in_grad = left_product(rows_three, grad_pre)
    grad_normed_three = spread_rows(right_product(grad_pre, ffn_in))
    grad_resid_three, gain_three = norm_backward(resid_two, norm_ffn, grad_normed_three)
    grad_two = grad_out + grad_resid_three
    grad_rows_two = gather_rows(grad_two.astype(jnp.bfloat16))
    out_cross_grad = left_product(mixed_rows_two, grad_rows_two)
    grad_mixed_two = target_view(right_product(grad_rows_two, out_cross).astype(jnp.bfloat16))
    cross_back = attend_backward(
        query_two, keys_two, values_two, probs_two, low_two, grad_mixed_two
    )
    grad_query_two = cross_back[1].reshape(total_rows, inner_local)
    grad_keys_two = cross_back[2].reshape(memory_total, inner_local)
    grad_values_two = cross_back[3].reshape(memory_total, inner_local)
    query_cross_grad = left_product(rows_two, grad_query_two)
    grad_normed_two = spread_rows(right_product(grad_query_two, query_cross))
    key_cross_grad = left_product(memory_all, grad_keys_two)
    value_cross_grad = left_product(memory_all, grad_values_two)
    memory_terms = right_product(grad_keys_two, key_cross) + right_product(
        grad_values_two, value_cross
    )
    memory_grad = lax.psum_scatter(memory_terms, "mp", scatter_dimension=0, tiled=True)
    grad_resid_two, gain_two = norm_backward(resid_one, norm_cross, grad_normed_two)
    grad_one = grad_two + grad_resid_two
    grad_rows_one = gather_rows(grad_one.astype(jnp.bfloat16))
    out_self_grad = left_product(mixed_rows_one, grad_rows_one)
    grad_mixed_one = target_view(right_product(grad_rows_one, out_self).astype(jnp.bfloat16))
    self_back = attend_backward(query_one, keys_one, values_one, probs_one, low_one, grad_mixed_one)
    bias_table_grad = jnp.einsum(
        "ehqk,qkb->bh", self_back[0].astype(jnp.float32), table_hot, precision=highest
    )
    grad_projected = jnp.concatenate(
        [
            self_back[1].reshape(total_rows, inner_local),
            self_back[2].reshape(total_rows, inner_local),
            self_back[3].reshape(total_rows, inner_local),
        ],
        axis=1,
    )
    self_weight_grad = left_product(rows_one, grad_projected)
    grad_normed_one = spread_rows(right_product(grad_projected, self_weights))
    grad_resid_one, gain_one = norm_backward(tokens_float, norm_self, grad_normed_one)
    tokens_grad = grad_one + grad_resid_one
    summed = lax.psum(
        (
            self_weight_grad[:, :inner_local],
            self_weight_grad[:, inner_local : 2 * inner_local],
            self_weight_grad[:, 2 * inner_local :],
            out_self_grad,
            bias_table_grad,
            query_cross_grad,
            key_cross_grad,
            value_cross_grad,
            out_cross_grad,
            ffn_in_grad,
            ffn_out_grad,
        ),
        "dp",
    )
    gains = lax.psum((gain_one, gain_two, gain_three), ("dp", "mp"))
    return (
        block_out.astype(jnp.bfloat16),
        tokens_grad.astype(jnp.bfloat16),
        memory_grad.astype(jnp.bfloat16),
        gains[0],
        summed[0],
        summed[1],
        summed[2],
        summed[3],
        summed[4],
        gains[1],
        summed[5],
        summed[6],
        summed[7],
        summed[8],
        gains[2],
        summed[9],
        summed[10],
    )


def links(dp_size):
    total = 2 * dp_size

    def swap(bit):
        return [(at, at ^ bit) for at in range(total)]

    def turned(at):
        return (at & ~3) | ((at & 1) << 1) | ((at >> 1) & 1)

    return {
        "turn": [(at, turned(at)) for at in range(total) if at != turned(at)],
        "give": [(at, at ^ 2) for at in range(total) if (at & 1) == ((at >> 1) & 1)],
        "take": [(at, at ^ 2) for at in range(total) if (at & 1) != ((at >> 1) & 1)],
        "y": swap(1),
        "core": swap(2),
        "x": swap(4),
        "zl": swap(8),
        "zh": swap(16),
    }


def permute(value, pairs):
    return lax.ppermute(value, ("dp", "mp"), pairs)


def reorder_kernel(inverse, examples, info, held, arrived, target):
    def write(source):
        if inverse:
            value = source[...].reshape(-1, source.shape[2])
        else:
            value = source[...]
        rows = value.shape[0]
        chunk = rows // examples
        high = lax.broadcasted_iota(jnp.int32, (rows, rows), 0)
        low = lax.broadcasted_iota(jnp.int32, (rows, rows), 1)
        if inverse:
            hot = low == (high % examples) * chunk + high // examples
        else:
            hot = low == (high % chunk) * examples + high // chunk
        moved = nn(hot.astype(jnp.bfloat16), value).astype(jnp.bfloat16)
        target[...] = moved.reshape(target.shape)

    @pl.when(info[0] == 1)
    def _():
        write(held)

    @pl.when(info[0] == 0)
    def _():
        write(arrived)


def reorder(inverse, held, arrived, settled, examples):
    rows, width = held.shape
    block = 256
    flat = pl.BlockSpec((block, width), lambda i, s: (i, 0))
    flat_shape = (rows, width)
    split_shape = (examples, rows // examples, width)
    split_block = (examples, block // examples, width)
    if inverse:
        held, arrived = held.reshape(split_shape), arrived.reshape(split_shape)
        in_specs = [
            pl.BlockSpec(split_block, lambda i, s: (0, i * s[0], 0)),
            pl.BlockSpec(split_block, lambda i, s: (0, i * (1 - s[0]), 0)),
        ]
        out_spec, out_shape = flat, flat_shape
    else:
        in_specs = [
            pl.BlockSpec((block, width), lambda i, s: (i * s[0], 0)),
            pl.BlockSpec((block, width), lambda i, s: (i * (1 - s[0]), 0)),
        ]
        out_spec = pl.BlockSpec(split_block, lambda i, s: (0, i, 0))
        out_shape = split_shape
    return pl.pallas_call(
        functools.partial(reorder_kernel, inverse, examples),
        grid_spec=pltpu.PrefetchScalarGridSpec(
            num_scalar_prefetch=1,
            grid=(rows // block,),
            in_specs=in_specs,
            out_specs=out_spec,
        ),
        out_shape=jax.ShapeDtypeStruct(out_shape, held.dtype),
        cost_estimate=cost(2 * rows * width * block, 4 * rows * width),
        compiler_params=pltpu.CompilerParams(vmem_limit_bytes=SMALL_VMEM),
    )(settled, held, arrived).reshape(flat_shape)


def memory_kernel(examples, info, *refs):
    sources, weight, rows_out, kv_out = refs[:6], refs[6], refs[7], refs[8]
    block = 256
    chunk = block // examples
    high = lax.broadcasted_iota(jnp.int32, (block, block), 0)
    low = lax.broadcasted_iota(jnp.int32, (block, block), 1)
    hot = (low == (high % chunk) * examples + high // chunk).astype(jnp.bfloat16)

    def write(source):
        parts = []
        for start in range(0, source.shape[0], block):
            moved = nn(hot, source[start : start + block, :]).astype(jnp.bfloat16)
            parts.append(moved.reshape(examples, chunk, moved.shape[1]))
        moved = jnp.concatenate(parts, axis=1)
        rows_out[...] = moved.reshape(rows_out.shape)
        moved = nn(moved.reshape(source.shape), weight[...]).astype(jnp.bfloat16)
        kv_out[...] = moved.reshape(kv_out.shape)

    late = pl.program_id(1) >= 1
    kind = jnp.where(pl.program_id(0) == 0, 0, jnp.where(late, 4, 2)) + info[1]
    for i in range(6):
        pl.when(kind == i)(functools.partial(write, sources[i]))


def memory_rows(y_half, settled, sources, weight, examples):
    rows, width = sources[0].shape
    block = 512
    blocks = rows // block
    shape = (2, examples, rows // examples, width)
    kv_shape = shape[:3] + (weight.shape[1],)

    def source(which):
        half, part = (0, 0) if which < 2 else (1, which // 2 - 1)
        start = part
        last = (blocks if half == 0 else 1 if part == 0 else blocks - 1) - 1

        def index(p, i, s):
            held = jnp.clip(i - start, 0, last)
            return (jnp.where((p == half) & (s[1] == which % 2), held, 0), 0)

        return pl.BlockSpec((block, width), index)

    def out(columns):
        return pl.BlockSpec(
            (1, examples, block // examples, columns),
            lambda p, i, s: ((p + s[0]) & 1, 0, i, 0),
        )

    return pl.pallas_call(
        functools.partial(memory_kernel, examples),
        grid_spec=pltpu.PrefetchScalarGridSpec(
            num_scalar_prefetch=1,
            grid=(2, blocks),
            in_specs=[source(i) for i in range(6)]
            + [pl.BlockSpec(weight.shape, lambda p, i, s: (0, 0))],
            out_specs=[out(width), out(weight.shape[1])],
        ),
        out_shape=[
            jax.ShapeDtypeStruct(shape, weight.dtype),
            jax.ShapeDtypeStruct(kv_shape, weight.dtype),
        ],
        cost_estimate=cost(4 * rows * width * (weight.shape[1] + 256), 12 * rows * width),
        compiler_params=pltpu.CompilerParams(vmem_limit_bytes=ATTEND_VMEM),
    )(jnp.stack([y_half, settled]), *sources, weight)


def nt(left, right):
    return lax.dot_general(
        left, right, (((1,), (1,)), ((), ())), preferred_element_type=jnp.float32
    )


def tn(left, right):
    return lax.dot_general(
        left, right, (((0,), (0,)), ((), ())), preferred_element_type=jnp.float32
    )


def nn(left, right):
    return jnp.dot(left, right, preferred_element_type=jnp.float32)


def one_head(value, head):
    lane = lax.broadcasted_iota(jnp.int32, value.shape, 1)
    return jnp.where(lane // HEAD_DIM == head, value, jnp.zeros_like(value))


def toeplitz(row, size):
    return pltpu.roll(jnp.broadcast_to(row, (size, size)), 0, 1, stride=1, stride_axis=0)


def diagonals(square):
    size = square.shape[0]
    row = lax.broadcasted_iota(jnp.int32, square.shape, 0)
    turned, step = square, 1
    while step < size:
        moved = pltpu.roll(turned, size - step, 1)
        turned = jnp.where((row & step) != 0, moved, turned)
        step *= 2
    return jnp.sum(turned, axis=0, keepdims=True)


def heads_joined(first, second):
    return jnp.concatenate([first, second], axis=0).T


def head_rows(value, head):
    return value[HEAD_DIM * head : HEAD_DIM * (head + 1)]


def self_heads(core, rows, scratch, example):
    half = scratch.shape[1] // 2
    at = pl.ds(example * half, half)
    scratch[example, pl.ds(pl.multiple_of(core * half, half), half), :] = rows[0, at, :]
    scratch[example, pl.ds(pl.multiple_of((1 - core) * half, half), half), :] = rows[1, at, :]
    return scratch[example]


def self_store(core, value, scratch, out, example):
    half = scratch.shape[1] // 2
    at = pl.ds(example * half, half)
    scratch[example] = value
    out[0, at, :] = scratch[example, pl.ds(pl.multiple_of(core * half, half), half), :]
    out[1, at, :] = scratch[example, pl.ds(pl.multiple_of((1 - core) * half, half), half), :]


def self_masks(size, length):
    key_at = lax.broadcasted_iota(jnp.int32, (size, size), 0)
    query_at = lax.broadcasted_iota(jnp.int32, (size, size), 1)
    return jnp.where((key_at <= query_at) & (key_at < length), 0.0, masked_score)


def side_by_side(value):
    return jnp.concatenate([one_head(value, head) for head in range(2)], axis=0)


def own_blocks(value, size):
    return value[:HEAD_DIM, :size], value[HEAD_DIM:, size:]


def self_forward_kernel(examples, info, rows, bias, out, mixed, level, scratch, out_scratch):
    core = info[0]
    size = scratch.shape[1]
    slopes = jnp.concatenate(
        [toeplitz(bias[0, head : head + 1, :], size) for head in range(2)], axis=1
    )
    for example in range(examples):
        joined = self_heads(core, rows, scratch, example)
        query, keys = joined[:, :128], joined[:, 128:256]
        mask = self_masks(size, info[1 + example])
        scores = nt(keys, side_by_side(query)) + slopes + jnp.concatenate([mask, mask], axis=1)
        top = jnp.max(scores, axis=0, keepdims=True)
        weights = jnp.exp(scores - top)
        total = jnp.sum(weights, axis=0, keepdims=True)
        probs = (weights * (1.0 / total)).astype(jnp.bfloat16)
        sums = nn(joined[:, 256:].T, probs)
        parts = own_blocks(sums, size)
        levels = top + jnp.log(total)
        for head in range(2):
            level[0, example, head : head + 1, :] = levels[:, size * head : size * (head + 1)]
            mixed[0, example, HEAD_DIM * head : HEAD_DIM * (head + 1), :] = parts[head]
        result = heads_joined(*parts).astype(jnp.bfloat16)
        self_store(core, result, out_scratch, out, example)


def by_length(length, span, body):
    quarter = span // 4
    for part in range(1, 5):
        keys = part * quarter
        inside = length > keys - quarter
        if part < 4:
            inside = inside & (length <= keys)

        @pl.when(inside)
        def _():
            body(keys)


def masked_tail(scores, length, quarter):
    keys, count = scores.shape
    key_at = keys - quarter + lax.broadcasted_iota(jnp.int32, (quarter, count), 0)
    tail = scores[keys - quarter :] + jnp.where(key_at < length, 0.0, masked_score)
    if keys == quarter:
        return tail
    return jnp.concatenate([scores[: keys - quarter], tail], axis=0)


def cross_forward_kernel(info, queries, kv, out, mixed, level):
    length = info[pl.program_id(0)]
    query = queries[...].reshape(-1, 128)
    count = query.shape[0]
    span = 2 * kv.shape[1]
    heads = side_by_side(query)

    def body(keys):
        joined = kv[...].reshape(span, 256)[:keys]
        scores = masked_tail(nt(joined[:, :128], heads), length, span // 4)
        top = jnp.max(scores, axis=0, keepdims=True)
        weights = jnp.exp(scores - top)
        total = jnp.sum(weights, axis=0, keepdims=True)
        probs = (weights * (1.0 / total)).astype(jnp.bfloat16)
        sums = nn(joined[:, 128:].T, probs)
        parts = own_blocks(sums, count)
        levels = top + jnp.log(total)
        for head in range(2):
            mixed[0, 0, HEAD_DIM * head : HEAD_DIM * (head + 1), :] = parts[head]
            level[0, 0, head : head + 1, :] = levels[:, count * head : count * (head + 1)]
        out[...] = heads_joined(*parts).astype(jnp.bfloat16).reshape(out.shape)

    by_length(length, span, body)


def cross_backward_kernel(info, queries, kv, grads, mixed, level, dq, dkv):
    length = info[pl.program_id(0)]
    query = queries[...].reshape(-1, 128)
    count = query.shape[0]
    grad = grads[...].reshape(-1, 128)
    span = 2 * kv.shape[1]
    heads, grad_heads = side_by_side(query), side_by_side(grad)
    products = grad.astype(jnp.float32).T * mixed[0, 0]
    inner = jnp.concatenate(
        [jnp.sum(head_rows(products, head), axis=0, keepdims=True) for head in range(2)], axis=1
    )
    levels = jnp.concatenate([level[0, 0, 0:1, :], level[0, 0, 1:2, :]], axis=1)

    def body(keys):
        joined = kv[...].reshape(span, 256)[:keys]
        scores = masked_tail(nt(joined[:, :128], heads), length, span // 4)
        probs = jnp.exp(scores - levels)
        grad_scores = (probs * (nt(joined[:, 128:], grad_heads) - inner)).astype(jnp.bfloat16)
        result = jnp.concatenate(
            [nn(grad_scores, heads), nn(probs.astype(jnp.bfloat16), grad_heads)], axis=1
        ).astype(jnp.bfloat16)
        if keys < span:
            result = jnp.concatenate(
                [result, jnp.zeros((span - keys, 256), jnp.bfloat16)], axis=0
            )
        dkv[...] = result.reshape(dkv.shape)
        sums = nn(joined[:, :128].T, grad_scores)
        dq[...] = heads_joined(*own_blocks(sums, count)).astype(jnp.bfloat16).reshape(dq.shape)

    by_length(length, span, body)


MIB = 1024 * 1024


def cost(flops, moved, exps=0):
    return pl.CostEstimate(
        flops=int(flops), bytes_accessed=int(moved), transcendentals=int(exps)
    )


SMALL_VMEM = 12 * MIB
ATTEND_VMEM = 24 * MIB
FFN_VMEM = 44 * MIB
SETTLE_VMEM = 48 * MIB
MESH = pl.DeviceIdType.MESH
SMEM_SPEC = pl.BlockSpec(memory_space=pltpu.SMEM)


def self_forward(info, rows, bias, examples):
    _, count, width = rows.shape
    pairs, size = width // 384, count // examples
    return pl.pallas_call(
        functools.partial(self_forward_kernel, examples),
        grid=(pairs,),
        in_specs=[
            SMEM_SPEC,
            pl.BlockSpec((2, count, 384), lambda h: (0, 0, h)),
            pl.BlockSpec((1, 2, 2 * size), lambda h: (h, 0, 0)),
        ],
        out_specs=[
            pl.BlockSpec((2, count, 128), lambda h: (0, 0, h)),
            pl.BlockSpec((1, examples, 128, 2 * size), lambda h: (h, 0, 0, 0)),
            pl.BlockSpec((1, examples, 2, 2 * size), lambda h: (h, 0, 0, 0)),
        ],
        out_shape=[
            jax.ShapeDtypeStruct((2, count, pairs * 128), jnp.bfloat16),
            jax.ShapeDtypeStruct((pairs, examples, 128, 2 * size), jnp.float32),
            jax.ShapeDtypeStruct((pairs, examples, 2, 2 * size), jnp.float32),
        ],
        scratch_shapes=[
            pltpu.VMEM((examples, 2 * size, 384), jnp.bfloat16),
            pltpu.VMEM((examples, 2 * size, 128), jnp.bfloat16),
        ],
        cost_estimate=cost(
            2 * 2 * examples * 2 * pairs * (2 * size) ** 2 * 256 * 2,
            8 * rows.size,
            examples * 2 * pairs * (2 * size) ** 2,
        ),
        compiler_params=pltpu.CompilerParams(vmem_limit_bytes=ATTEND_VMEM),
    )(info, rows, bias)


def cross_forward(info, queries, kv, examples):
    _, count, width = queries.shape
    pairs, size, span = width // 128, count // examples, kv.shape[1] // examples
    thin = pl.BlockSpec((2, size, 128), lambda e, h: (0, e, h))
    wide = pl.BlockSpec((2, span, 256), lambda e, h: (0, e, h))
    return pl.pallas_call(
        cross_forward_kernel,
        grid=(examples, pairs),
        in_specs=[SMEM_SPEC, thin, wide],
        out_specs=[
            thin,
            pl.BlockSpec((1, 1, 128, 2 * size), lambda e, h: (e, h, 0, 0)),
            pl.BlockSpec((1, 1, 2, 2 * size), lambda e, h: (e, h, 0, 0)),
        ],
        out_shape=[
            jax.ShapeDtypeStruct(queries.shape, jnp.bfloat16),
            jax.ShapeDtypeStruct((examples, pairs, 128, 2 * size), jnp.float32),
            jax.ShapeDtypeStruct((examples, pairs, 2, 2 * size), jnp.float32),
        ],
        cost_estimate=cost(
            2 * 2 * examples * 2 * pairs * 4 * size * span * 256,
            4 * kv.size,
            examples * 2 * pairs * 4 * size * span,
        ),
        compiler_params=pltpu.CompilerParams(vmem_limit_bytes=ATTEND_VMEM),
    )(info, queries, kv)


def cross_backward(info, queries, kv, grads, mixed, level, examples):
    _, count, width = queries.shape
    pairs, size, span = width // 128, count // examples, kv.shape[1] // examples
    thin = pl.BlockSpec((2, size, 128), lambda e, h: (0, e, h))
    wide = pl.BlockSpec((2, span, 256), lambda e, h: (0, e, h))
    return pl.pallas_call(
        cross_backward_kernel,
        grid=(examples, pairs),
        in_specs=[
            SMEM_SPEC,
            thin,
            wide,
            thin,
            pl.BlockSpec((1, 1, 128, 2 * size), lambda e, h: (e, h, 0, 0)),
            pl.BlockSpec((1, 1, 2, 2 * size), lambda e, h: (e, h, 0, 0)),
        ],
        out_specs=[thin, wide],
        out_shape=[
            jax.ShapeDtypeStruct(queries.shape, jnp.bfloat16),
            jax.ShapeDtypeStruct(kv.shape, jnp.bfloat16),
        ],
        cost_estimate=cost(
            5 * 2 * examples * 2 * pairs * 4 * size * span * 256,
            6 * kv.size,
            examples * 2 * pairs * 4 * size * span,
        ),
        compiler_params=pltpu.CompilerParams(vmem_limit_bytes=ATTEND_VMEM),
    )(info, queries, kv, grads, mixed, level)


root = math.sqrt(2.0 / math.pi)
cubic = 0.044715


def ffn_rows_kernel(normed, grad, into, outof, out, back, hidden_out, pre_out, out_sum, back_sum):
    step = pl.program_id(0)

    @pl.when(step == 0)
    def _():
        out_sum[...] = jnp.zeros_like(out_sum)
        back_sum[...] = jnp.zeros_like(back_sum)

    pre = nn(normed[...], into[...])
    grad_hidden = nt(grad[...], outof[...])
    bend = jnp.tanh(root * (pre + cubic * (pre * pre * pre)))
    hidden = (0.5 * pre * (1.0 + bend)).astype(jnp.bfloat16)
    slope = 0.5 * (1.0 + bend) + 0.5 * pre * (1.0 - bend * bend) * (
        root * (1.0 + 3.0 * cubic * (pre * pre))
    )
    grad_pre = (grad_hidden * slope).astype(jnp.bfloat16)
    hidden_out[...] = hidden
    pre_out[...] = grad_pre
    out_sum[...] += nn(hidden, outof[...])
    back_sum[...] += nt(grad_pre, into[...])

    @pl.when(step == pl.num_programs(0) - 1)
    def _():
        out[...] = out_sum[...].astype(out.dtype)
        back[...] = back_sum[...].astype(back.dtype)


def ffn_rows(normed, grad, into, outof, kind):
    rows, width = normed.shape
    units = into.shape[1]
    tile = 512
    whole = pl.BlockSpec((rows, width), lambda i: (0, 0))
    tall = pl.BlockSpec((width, tile), lambda i: (0, i))
    flat = pl.BlockSpec((tile, width), lambda i: (i, 0))
    thin = pl.BlockSpec((rows, tile), lambda i: (0, i))
    return pl.pallas_call(
        ffn_rows_kernel,
        grid=(units // tile,),
        in_specs=[whole, whole, tall, flat],
        out_specs=[whole, whole, thin, thin],
        out_shape=[jax.ShapeDtypeStruct((rows, width), kind)] * 2
        + [jax.ShapeDtypeStruct((rows, units), jnp.bfloat16)] * 2,
        scratch_shapes=[pltpu.VMEM((rows, width), jnp.float32)] * 2,
        cost_estimate=cost(
            4 * 2 * rows * width * units, 12 * rows * width + 4 * width * units, rows * units
        ),
        compiler_params=pltpu.CompilerParams(vmem_limit_bytes=ATTEND_VMEM),
    )(normed, grad, into, outof)


def ffn_weights_kernel(n_own, n_far, g_own, g_far, h_own, h_far, p_own, p_far, out):
    step = pl.program_id(0)
    half = pl.num_programs(0) // 2

    @pl.when(step < half)
    def _():
        out[...] = (tn(h_own[...], g_own[...]) + tn(h_far[...], g_far[...])).astype(out.dtype)

    @pl.when(step >= half)
    def _():
        out[...] = (tn(p_own[...], n_own[...]) + tn(p_far[...], n_far[...])).astype(out.dtype)


def ffn_weights(normed, grads, hiddens, pres):
    rows, width = normed[0].shape
    units = hiddens[0].shape[1]
    tile = 512
    steps = units // tile
    whole = pl.BlockSpec((rows, width), lambda i: (0, 0))
    first = pl.BlockSpec((rows, tile), lambda i: (0, jnp.minimum(i, steps - 1)))
    second = pl.BlockSpec((rows, tile), lambda i: (0, jnp.maximum(i - steps, 0)))
    return pl.pallas_call(
        ffn_weights_kernel,
        grid=(2 * steps,),
        in_specs=[whole] * 4 + [first] * 2 + [second] * 2,
        out_specs=pl.BlockSpec((tile, width), lambda i: (i, 0)),
        out_shape=jax.ShapeDtypeStruct((2 * units, width), jnp.bfloat16),
        cost_estimate=cost(
            4 * 2 * rows * width * units, 8 * rows * width + 4 * width * units
        ),
        compiler_params=pltpu.CompilerParams(vmem_limit_bytes=30 * MIB),
    )(*normed, *grads, *hiddens, *pres)


def gather_kernel(groups, examples, tokens, memory, facts, counts, *refs):
    weights, refs = refs[:8], refs[8:]
    tok_out, mem_out, facts_out, counts_out, self_in, cross_q, cross_kv = refs[:7]
    self_out, cross_out = refs[7:9]
    raw, landed, round_in, near_send, near_get, send, get = refs[9:]
    index, y = lax.axis_index("dp"), lax.axis_index("mp")
    core, x, z = index % 2, (index // 2) % 2, index // 4
    deep = groups // 4

    def at(c, yy, xx, zz):
        return (zz * 4 + xx * 2 + c, yy)

    z_near = z + 1 - 2 * (z % 2)
    x_side, z_side = at(core, y, 1 - x, z), at(core, y, x, z_near)
    turned = at(1 - core, 1 - y, x, z)
    rounds = [at(1 - core, y, x, z), x_side, z_side]
    step = 2
    while step < deep:
        rounds.append(at(core, y, x, z + step - 2 * step * ((z // step) % 2)))
        step *= 2
    barrier = pltpu.get_barrier_semaphore()
    for partner in rounds:
        pl.semaphore_signal(barrier, inc=1, device_id=partner, device_id_type=MESH)

    @pl.when(core != y)
    def _():
        pl.semaphore_signal(barrier, inc=1, device_id=turned, device_id_type=MESH)
        pl.semaphore_wait(barrier, len(rounds) + 1)

    @pl.when(core == y)
    def _():
        pl.semaphore_wait(barrier, len(rounds))

    homes = [raw.at[0], raw.at[1], raw.at[2], cross_q, raw.at[3], raw.at[4], self_out, cross_out]

    def remote(source, target, sems, slot, device):
        return pltpu.make_async_remote_copy(
            src_ref=source,
            dst_ref=target,
            send_sem=sems[0].at[slot],
            recv_sem=sems[1].at[slot],
            device_id=device,
            device_id_type=MESH,
        )

    mine = x * 2 + z % 2

    def quarter(w, which, first=0, parts=1):
        rows = homes[w].shape[0] // 4
        size = rows // parts
        return homes[w].at[pl.ds(pl.multiple_of(which * rows + first * size, size), size)]

    def along_y(w):
        rows = homes[w].shape[0] // 4
        sent = mine * rows
        return remote(
            weights[w].at[pl.ds(pl.multiple_of(sent, rows), rows)],
            quarter(w, mine),
            (send, get),
            w,
            turned,
        )

    def direct(w, which):
        piece = quarter(w, mine)
        return remote(piece, piece, (send, get), 8 + 2 * w + which, (x_side, z_side)[which])

    def passed(w, which):
        other = mine + (2 - 4 * x if which == 0 else 1 - 2 * (z % 2))
        piece = quarter(w, other, which, 2)
        return remote(piece, piece, (send, get), 24 + 2 * w + which, (z_side, x_side)[which])

    token_copy = remote(tokens, landed, (send, get), 40, turned)
    facts_copy = remote(facts, facts_out, (send, get), 41, turned)
    early = memory.at[pl.ds(0, mem_out.shape[0])]
    memory_copy = remote(early, mem_out, (send, get), 42 + len(rounds), turned)

    @pl.when(core != y)
    def _():
        facts_copy.start()
        for w in range(8):
            along_y(w).start()
        token_copy.start()
        memory_copy.start()

    @pl.when(core == y)
    def _():
        pltpu.make_async_copy(tokens, landed, near_get.at[0]).start()
        pltpu.make_async_copy(facts, facts_out, near_get.at[1]).start()
        for w in range(8):
            pltpu.make_async_copy(weights[w], homes[w], near_get.at[2 + w]).start()

    def count_copy(i):
        return remote(counts_out, round_in.at[i], (near_send, get), 42 + i, rounds[i])

    def count_round(w):
        if w % 2 == 1 and w // 2 < len(rounds):
            count_copy(w // 2).start()
        if w % 2 == 0 and 0 < w <= 2 * len(rounds):
            count_copy(w // 2 - 1).wait()
            counts_out[...] += round_in[w // 2 - 1]

    counts_out[...] = counts[...]
    @pl.when(core == y)
    def _():
        pltpu.make_async_copy(tokens, landed, near_get.at[0]).wait()
        pltpu.make_async_copy(facts, facts_out, near_get.at[1]).wait()
        for w in range(8):
            pltpu.make_async_copy(weights[w], homes[w], near_get.at[2 + w]).wait()

    def share(w):
        if w < 8:
            along_y(w).wait()
            for which in range(2):
                direct(w, which).start()
        if w > 0:
            for which in range(2):
                direct(w - 1, which).wait()
            for which in range(2):
                passed(w - 1, which).start()

    for w in range(9):
        pl.when(core != y)(functools.partial(share, w))
        count_round(w)

    @pl.when(core != y)
    def _():
        facts_copy.wait()
        token_copy.wait()

    rows = landed.shape[0]
    block = 256
    chunk = block // examples
    high = lax.broadcasted_iota(jnp.int32, (block, block), 0)
    low = lax.broadcasted_iota(jnp.int32, (block, block), 1)
    hot = (low == (high % chunk) * examples + high // chunk).astype(jnp.bfloat16)
    for i in range(rows // block):
        moved = nn(hot, landed[pl.ds(i * block, block), :]).astype(jnp.bfloat16)
        tok_out[:, pl.ds(i * chunk, chunk), :] = moved.reshape(examples, chunk, moved.shape[1])

    @pl.when(core != y)
    def _():
        for w in range(8):
            for which in range(2):
                passed(w, which).wait()
        memory_copy.wait()

    for h in range(raw.shape[2] // 128):
        for i in range(3):
            self_in[:, 384 * h + 128 * i : 384 * h + 128 * i + 128] = raw[
                i, :, 128 * h : 128 * h + 128
            ]
        for i in range(2):
            cross_kv[:, 256 * h + 128 * i : 256 * h + 128 * i + 128] = raw[
                3 + i, :, 128 * h : 128 * h + 128
            ]


def gather(tokens, memory, facts, counts, weights, groups, examples):
    rows, width = tokens.shape
    inner = weights[0].shape[1]
    rounds = 2 + (groups // 4).bit_length() - 1
    anywhere = pl.BlockSpec(memory_space=pl.ANY)
    whole = pl.BlockSpec(memory_space=pltpu.VMEM)

    def half(*shape):
        return jax.ShapeDtypeStruct(shape, jnp.bfloat16)

    return pl.pallas_call(
        functools.partial(gather_kernel, groups, examples),
        in_specs=[anywhere, anywhere, whole, whole] + [anywhere] * 8,
        out_specs=[whole] * 9,
        out_shape=[
            half(examples, rows // examples, width),
            half(memory.shape[0] // 4, width),
            jax.ShapeDtypeStruct(facts.shape, facts.dtype),
            jax.ShapeDtypeStruct(counts.shape, counts.dtype),
            half(width, 3 * inner),
            half(width, inner),
            half(width, 2 * inner),
            half(inner, width),
            half(inner, width),
        ],
        scratch_shapes=[
            pltpu.VMEM((5, width, inner), jnp.bfloat16),
            pltpu.VMEM((rows, width), jnp.bfloat16),
            pltpu.VMEM((rounds,) + counts.shape, counts.dtype),
            pltpu.SemaphoreType.DMA((42 + rounds,)),
            pltpu.SemaphoreType.DMA((10,)),
            pltpu.SemaphoreType.DMA((43 + rounds,)),
            pltpu.SemaphoreType.DMA((43 + rounds,)),
        ],
        cost_estimate=cost(0, 150 * MIB),
        compiler_params=pltpu.CompilerParams(
            collective_id=1, has_side_effects=True, vmem_limit_bytes=SETTLE_VMEM
        ),
    )(tokens, memory, facts, counts, *weights)


def add_low(left, right):
    return (left.astype(jnp.float32) + right.astype(jnp.float32)).astype(jnp.bfloat16)


def pick(value, index):
    return lax.dynamic_index_in_dim(value, index, 0, keepdims=False)


def tie(*values):
    return lax.optimization_barrier(values)


def settle_kernel(groups, examples, *refs):
    parts, small, info, qkv = refs[:4], refs[4], refs[5], refs[6]
    bias, grads, mixed, level, normed, self_in, tok, grad_rest, gain = refs[7:16]
    out, small_out, tok_grad, tok_back = refs[16:20]
    value, first, second, third, small_in, rows_held, placed, grad_placed, result = refs[20:29]
    far_sent, far_found, send, receive, small_send, small_get, load, single = refs[29:]
    count = len(parts)
    index, y = lax.axis_index("dp"), lax.axis_index("mp")
    core, x, z = index % 2, (index // 2) % 2, index // 4
    deep = groups // 4
    chunks, rows = first.shape[0], first.shape[3]

    def at(c, yy, xx, zz):
        return (zz * 4 + xx * 2 + c, yy)

    def part(k):
        return pl.ds(pl.multiple_of(k * rows, rows), rows)

    fetch = pltpu.make_async_copy(qkv, rows_held, load.at[count])
    fetch.start()
    loads, starts = [], [0]
    for i, ref in enumerate(parts):
        size = ref.shape[1]
        target = value.at[:, pl.ds(starts[-1], size)]
        loads.append(pltpu.make_async_copy(ref, target, load.at[i]))
        loads[-1].start()
        starts.append(starts[-1] + size)
    partners = [at(1 - core, y, x, z), at(core, 1 - y, x, z), at(1 - core, 1 - y, x, z)]
    partners.append(at(core, y, 1 - x, z))
    for step in range(1, deep):
        partners.append(at(core, y, x, (z + step) % deep))
    barrier = pltpu.get_barrier_semaphore()
    for partner in partners:
        pl.semaphore_signal(barrier, inc=1, device_id=partner, device_id_type=MESH)
    pl.semaphore_wait(barrier, len(partners))

    def copy(source, target, slot, k, device):
        return pltpu.make_async_remote_copy(
            src_ref=source,
            dst_ref=target,
            send_sem=send.at[k, slot],
            recv_sem=receive.at[k, slot],
            device_id=device,
            device_id_type=MESH,
        )

    def quarter(k, q):
        return value.at[pl.ds(q * 8, 8), part(k)]

    def to_core(k):
        return copy(quarter(k, 1 - core), first.at[k, 0], 0, k, at(1 - core, core, x, z))

    def to_turned(k):
        return copy(quarter(k, 1 - core), first.at[k, 1], 1, k, at(1 - core, core, x, z))

    def to_same(k):
        return copy(quarter(k, core), first.at[k, 1], 2, k, at(core, core, x, z))

    def arrived(k, slot):
        return copy(quarter(k, core), first.at[k, 1 if slot else 0], slot, k, at(1 - core, y, x, z))

    def along_x(k):
        return copy(
            first.at[k, 1, pl.ds((1 - x) * 4, 4)], second.at[k], 3, k, at(core, y, 1 - x, z)
        )

    def along_z(k, step):
        far = (z + step) % deep
        return copy(
            second.at[k, far], third.at[k, step - 1], 3 + step, k, at(core, y, x, far)
        )

    def back_z(k, step):
        far = (z + step) % deep
        piece = core * 8 + x * 4 + z
        return copy(
            out.at[piece, part(k)], out.at[piece, part(k)], 6 + step, k, at(core, y, x, far)
        )

    def back_x(k):
        held = out.at[pl.ds(core * 8 + x * 4, 4), part(k)]
        return copy(held, held, 10, k, at(core, y, 1 - x, z))

    def back_core(k):
        held = out.at[pl.ds(core * 8, 8), part(k)]
        return copy(held, held, 11, k, at(1 - core, y, x, z))

    rounds = [at(core, 1 - y, x, z), at(core, y, 1 - x, z)]
    step = 1
    while step < deep:
        rounds.append(at(core, y, x, z + step - 2 * step * ((z // step) % 2)))
        step *= 2
    rounds.append(at(1 - core, y, x, z))
    small_out[0] = small[...]

    def small_copy(i):
        return pltpu.make_async_remote_copy(
            src_ref=small_out.at[0],
            dst_ref=small_in.at[i],
            send_sem=small_send.at[i],
            recv_sem=small_get.at[i],
            device_id=rounds[i],
            device_id_type=MESH,
        )

    def small_wait(i):
        small_copy(i).wait()
        if i < len(rounds) - 1:
            small_out[0] = small_out[0] + small_in[i]
        else:
            small_out[1] = small_in[i]

    def single_copy(i, source, target, device):
        return pltpu.make_async_remote_copy(
            src_ref=source,
            dst_ref=target,
            send_sem=single.at[i, 0],
            recv_sem=single.at[i, 1],
            device_id=device,
            device_id_type=MESH,
        )

    far_copy = single_copy(0, far_sent, far_found, at(1 - core, y, x, z))
    turn_copy = single_copy(1, tok_grad, tok_back, at(1 - core, 1 - y, x, z))
    width = tok.shape[1]

    def attend(pair):
        size = placed.shape[1]
        half = size // 2
        columns = slice(384 * pair, 384 * (pair + 1))
        near = pl.ds(pl.multiple_of(core * half, half), half)
        away = pl.ds(pl.multiple_of((1 - core) * half, half), half)
        slopes = jnp.concatenate(
            [toeplitz(bias[pair, head : head + 1, :], size) for head in range(2)], axis=1
        )
        sums = None
        for example in range(examples):
            held = slice(half * example, half * (example + 1))
            placed[example, near, :] = rows_held[0, held, columns]
            placed[example, away, :] = rows_held[1, held, columns]
            grad_placed[example, near, :] = grads[0, held, 128 * pair : 128 * (pair + 1)]
            grad_placed[example, away, :] = grads[1, held, 128 * pair : 128 * (pair + 1)]
            joined, grad = placed[example], grad_placed[example]
            query, keys, values = joined[:, :128], joined[:, 128:256], joined[:, 256:]
            products = grad.astype(jnp.float32).T * mixed[pair, example]
            inner = jnp.concatenate(
                [jnp.sum(head_rows(products, head), axis=0, keepdims=True) for head in range(2)],
                axis=1,
            )
            levels = jnp.concatenate(
                [level[pair, example, 0:1, :], level[pair, example, 1:2, :]], axis=1
            )
            mask = self_masks(size, info[example])
            heads, grad_heads = side_by_side(query), side_by_side(grad)
            scores = nt(keys, heads) + slopes + jnp.concatenate([mask, mask], axis=1)
            probs = jnp.exp(scores - levels)
            grad_scores = (probs * (nt(values, grad_heads) - inner)).astype(jnp.bfloat16)
            square = grad_scores.astype(jnp.float32)
            sums = square if sums is None else sums + square
            result[example] = jnp.concatenate(
                [
                    heads_joined(*own_blocks(nn(keys.T, grad_scores), size)),
                    nn(grad_scores, heads),
                    nn(probs.astype(jnp.bfloat16), grad_heads),
                ],
                axis=1,
            ).astype(jnp.bfloat16)
            rows_held[0, held, columns] = result[example, near, :]
            rows_held[1, held, columns] = result[example, away, :]
        for head in range(2):
            at_column = 512 * (pair % 2) + 256 * head
            small_out[0, 4 + pair // 2 : 5 + pair // 2, at_column : at_column + size] = diagonals(
                sums[:, size * head : size * (head + 1)]
            )
        both_rows = rows_held[:, :, columns].reshape(-1, 384)
        piece = tn(both_rows, normed[...].reshape(-1, width)).astype(jnp.bfloat16)
        value[4 * pair : 4 * pair + 4, starts[count] :, :] = piece.reshape(4, 96, width)

    def heads_sent():
        lax.fori_loop(starts[count] // rows, chunks, start, 0)
        far_sent[...] = nt(rows_held[1], self_in[...]).astype(jnp.bfloat16)
        far_copy.start()

    def tokens_done():
        far_copy.wait()
        back = nt(rows_held[0], self_in[...]) + far_found[...].astype(jnp.float32)
        held = tok[...].astype(jnp.float32)
        size = lax.rsqrt(jnp.mean(held * held, axis=-1, keepdims=True) + epsilon)
        small_out[0, 0:1, :] = jnp.sum(back * held * size, axis=0, keepdims=True)
        back = back * gain[...]
        inner = jnp.mean(back * held, axis=-1, keepdims=True)
        back = back * size - held * (size * size * size * inner)
        tok_grad[...] = (grad_rest[...] + back).astype(jnp.bfloat16)
        small_copy(0).start()

        @pl.when(core != y)
        def _():
            turn_copy.start()

    def start(k, carry):
        @pl.when(core == y)
        def _():
            to_core(k).start()

        @pl.when(core != y)
        def _():
            to_same(k).start()
            to_turned(k).start()

        return carry

    for i in range(count):
        loads[i].wait()
        lax.fori_loop(starts[i] // rows, starts[i + 1] // rows, start, 0)
    fetch.wait()

    def total(left, right):
        return (left.astype(jnp.float32) + right.astype(jnp.float32)).astype(jnp.bfloat16)

    pairs = bias.shape[0]
    work = [functools.partial(attend, pair) for pair in range(pairs)] + [heads_sent, tokens_done]

    def tick(t, carry):
        for i, piece_of_work in enumerate(work):
            pl.when(t == i)(piece_of_work)
        for i in range(len(rounds) - 1):

            @pl.when(t == chunks + 1 + i)
            def _():
                small_wait(i)
                small_copy(i + 1).start()

        @pl.when(t < chunks)
        def _():
            k = jnp.minimum(t, chunks - 1)

            @pl.when(core == y)
            def _():
                arrived(k, 2).wait_recv()

                def add(i, c):
                    first[k, 1, i] = total(value[core * 8 + i, part(k)], first[k, 1, i])
                    return c

                lax.fori_loop(0, 8, add, 0)

            @pl.when(core != y)
            def _():
                arrived(k, 0).wait_recv()
                arrived(k, 1).wait_recv()

                def add(i, c):
                    first[k, 1, i] = total(first[k, 0, i], first[k, 1, i])
                    return c

                lax.fori_loop(0, 8, add, 0)

            along_x(k).start()

        @pl.when((t >= 1) & (t < chunks + 1))
        def _():
            k = t - 1
            along_x(k).wait_recv()

            def add(i, c):
                second[k, i] = total(first[k, 1, x * 4 + i], second[k, i])
                return c

            lax.fori_loop(0, deep, add, 0)
            for step in range(1, deep):
                along_z(k, step).start()

        @pl.when((t >= 2) & (t < chunks + 2))
        def _():
            k = t - 2
            for step in range(1, deep):
                along_z(k, step).wait_recv()
            summed = second[k, z].astype(jnp.float32)
            for step in range(1, deep):
                summed = summed + third[k, step - 1].astype(jnp.float32)
            out[core * 8 + x * 4 + z, part(k)] = summed.astype(jnp.bfloat16)
            for step in range(1, deep):
                back_z(k, step).start()

        @pl.when((t >= 3) & (t < chunks + 3))
        def _():
            k = t - 3
            for step in range(1, deep):
                back_z(k, step).wait_recv()
            back_x(k).start()

        @pl.when((t >= 4) & (t < chunks + 4))
        def _():
            k = t - 4
            back_x(k).wait_recv()
            back_core(k).start()

        @pl.when(t >= 5)
        def _():
            back_core(t - 5).wait_recv()

        return carry

    lax.fori_loop(0, chunks + 5, tick, 0)
    small_wait(len(rounds) - 1)

    @pl.when(core != y)
    def _():
        turn_copy.wait()


    def finish_sends(k, carry):
        @pl.when(core == y)
        def _():
            to_core(k).wait_send()

        @pl.when(core != y)
        def _():
            to_same(k).wait_send()
            to_turned(k).wait_send()

        along_x(k).wait_send()
        for step in range(1, deep):
            along_z(k, step).wait_send()
            back_z(k, step).wait_send()
        back_x(k).wait_send()
        back_core(k).wait_send()
        return carry

    lax.fori_loop(0, chunks, finish_sends, 0)


def settle(parts, small, info, attention, rows_in, groups, examples):
    qkv, bias, grads, mixed, level = attention
    normed, self_in, tok, grad_rest, gain = rows_in
    count, _, width = parts[0].shape
    kind = parts[0].dtype
    rows = sum(part.shape[1] for part in parts) + qkv.shape[2] // count
    chunk = 16
    chunks = rows // chunk
    deep = groups // 4
    rounds = 3 + deep.bit_length() - 1
    size = 2 * qkv.shape[1] // examples
    whole = pl.BlockSpec(memory_space=pltpu.VMEM)
    anywhere = pl.BlockSpec(memory_space=pl.ANY)
    return pl.pallas_call(
        functools.partial(settle_kernel, groups, examples),
        in_specs=[anywhere] * len(parts) + [whole, SMEM_SPEC, anywhere] + [whole] * 9,
        out_specs=[whole] * 4,
        out_shape=[
            jax.ShapeDtypeStruct((count, rows, width), kind),
            jax.ShapeDtypeStruct((2,) + small.shape, small.dtype),
            jax.ShapeDtypeStruct(tok.shape, tok.dtype),
            jax.ShapeDtypeStruct(tok.shape, tok.dtype),
        ],
        scratch_shapes=[
            pltpu.VMEM((count, rows, width), kind),
            pltpu.VMEM((chunks, 2, count // 2, chunk, width), kind),
            pltpu.VMEM((chunks, deep, chunk, width), kind),
            pltpu.VMEM((chunks, deep - 1, chunk, width), kind),
            pltpu.VMEM((rounds,) + small.shape, small.dtype),
            pltpu.VMEM(qkv.shape, kind),
            pltpu.VMEM((examples, size, 384), kind),
            pltpu.VMEM((examples, size, 128), kind),
            pltpu.VMEM((examples, size, 384), kind),
            pltpu.VMEM(tok.shape, kind),
            pltpu.VMEM(tok.shape, kind),
            pltpu.SemaphoreType.DMA((chunks, 12)),
            pltpu.SemaphoreType.DMA((chunks, 12)),
            pltpu.SemaphoreType.DMA((rounds,)),
            pltpu.SemaphoreType.DMA((rounds,)),
            pltpu.SemaphoreType.DMA((len(parts) + 1,)),
            pltpu.SemaphoreType.DMA((2, 2)),
        ],
        cost_estimate=cost(0, 60 * count * rows * width),
        compiler_params=pltpu.CompilerParams(
            collective_id=0, has_side_effects=True, vmem_limit_bytes=62 * MIB
        ),
    )(*parts, small, info, qkv, bias, grads, mixed, level, normed, self_in, tok, grad_rest, gain)


def unpack_kernel(pairs, source, key, val, cross_out, self_out, cross_q, *self_in):
    wide = key.shape[0] // 4
    thin = cross_out.shape[0] // 4

    def taken(row, rows):
        block = source[:, row : row + rows, :].astype(jnp.float32)
        return block.reshape(4 * rows, block.shape[2])

    kv = taken(0, wide)
    for i in range(pairs):
        key[:, 128 * i : 128 * i + 128] = kv[:, 256 * i : 256 * i + 128]
        val[:, 128 * i : 128 * i + 128] = kv[:, 256 * i + 128 : 256 * i + 256]
    cross_out[...] = taken(wide, thin)
    self_out[...] = taken(wide + thin, thin)
    cross_q[...] = taken(wide + 2 * thin, thin).T
    rest = taken(wide + 3 * thin, 3 * thin)
    for i in range(3):
        self_in[i][...] = rest[4 * thin * i : 4 * thin * (i + 1)].T


def unpack(value, inner):
    count, rows, width = value.shape
    tall = jax.ShapeDtypeStruct((width, inner), jnp.float32)
    flat = jax.ShapeDtypeStruct((inner, width), jnp.float32)
    by_row = pl.BlockSpec((width // 4, inner), lambda i: (i, 0))
    by_out = pl.BlockSpec((inner // 4, width), lambda i: (i, 0))
    by_column = pl.BlockSpec((width, inner // 4), lambda i: (0, i))
    return pl.pallas_call(
        functools.partial(unpack_kernel, inner // 128),
        grid=(4,),
        in_specs=[pl.BlockSpec((4, rows, width), lambda i: (i, 0, 0))],
        out_specs=[by_row, by_row, by_out, by_out] + [by_column] * 4,
        out_shape=[tall, tall, flat, flat] + [tall] * 4,
        cost_estimate=cost(0, 6 * value.size),
        compiler_params=pltpu.CompilerParams(vmem_limit_bytes=ATTEND_VMEM),
    )(value)


def widen_kernel(first, second, out_first, out_second):
    out_first[...] = first[...].astype(jnp.float32)
    out_second[...] = second[...].astype(jnp.float32).T


def widen(value):
    rows, width = value.shape[0] // 2, value.shape[1]
    steps = 4
    block = rows // steps
    return pl.pallas_call(
        widen_kernel,
        grid=(steps,),
        in_specs=[
            pl.BlockSpec((block, width), lambda i: (i, 0)),
            pl.BlockSpec((block, width), lambda i: (steps + i, 0)),
        ],
        out_specs=[
            pl.BlockSpec((block, width), lambda i: (i, 0)),
            pl.BlockSpec((width, block), lambda i: (0, i)),
        ],
        out_shape=[
            jax.ShapeDtypeStruct((rows, width), jnp.float32),
            jax.ShapeDtypeStruct((width, rows), jnp.float32),
        ],
        cost_estimate=cost(0, 12 * rows * width),
        compiler_params=pltpu.CompilerParams(vmem_limit_bytes=ATTEND_VMEM),
    )(value, value)


def pieces(value):
    return value.reshape(16, value.shape[0] // 16, value.shape[1])


def low(value):
    return value.astype(jnp.bfloat16)


def on_chip_group(
    tokens,
    memory,
    cotangent,
    target_lengths,
    memory_lengths,
    norm_self,
    query_self,
    key_self,
    value_self,
    out_self,
    bias_table,
    norm_cross,
    query_cross,
    key_cross,
    value_cross,
    out_cross,
    norm_ffn,
    ffn_in,
    ffn_out,
):
    examples = target_lengths.shape[0]
    groups = lax.axis_size("dp")
    net = links(groups)
    index = lax.axis_index("dp")
    place = {
        "y": lax.axis_index("mp"),
        "core": index & 1,
        "x": (index >> 1) & 1,
        "zl": (index >> 2) & 1,
        "zh": (index >> 3) & 1,
    }
    core = place["core"]
    settled = (core == place["y"]).astype(jnp.int32)
    place["settled"] = settled[None]
    rows, width = tokens.shape
    half_pos = rows // examples
    inner = query_self.shape[1]
    pairs = inner // 128

    def swap(value):
        return permute(value, net["core"])

    def both(value):
        return jnp.stack([value, swap(value)])

    def flat(value):
        return value.reshape(-1, value.shape[2])

    def turn(value):
        return permute(value, net["turn"])

    lengths = jnp.concatenate([target_lengths, memory_lengths]).astype(jnp.float32)
    table_rows = bias_table.astype(jnp.float32).reshape(-1, 128)
    facts = jnp.concatenate(
        [jnp.pad(lengths, (0, 128 - lengths.size))[None], table_rows], axis=0
    )
    facts = jnp.pad(facts, ((0, 8 - facts.shape[0]), (0, 0)))
    counts = jnp.broadcast_to(jnp.sum(target_lengths).astype(jnp.float32), (8, 128))
    mem_near = permute(memory, net["give"])
    held = gather(
        tokens,
        memory,
        facts,
        counts,
        [query_self, key_self, value_self, query_cross, key_cross, value_cross, out_self, out_cross],
        groups,
        examples,
    )
    tok, mem_first, facts, counts, self_in, cross_q, cross_kv = held[:7]
    self_out, cross_out = held[7:]
    tok = tok.reshape(rows, width)
    target_len = facts[0, :examples].astype(jnp.int32)
    memory_len = facts[0, examples : 2 * examples].astype(jnp.int32)
    table = facts[1 : 1 + table_rows.shape[0]].reshape(bias_table.shape)
    group_count = jnp.sum(target_len).astype(jnp.float32)
    token_scale = groups * group_count / counts[0, 0]
    self_info = jnp.concatenate([core[None], target_len])
    mem_sent, tok = tie(memory[mem_first.shape[0] :], tok)
    mem_rest = turn(mem_sent)
    first_far = permute(mem_first, net["take"])

    span = 2 * half_pos
    distance = jnp.arange(span, dtype=jnp.int32)
    level = jnp.sum(
        (distance[:, None] >= jnp.asarray(bucket_edges())[None, :]).astype(jnp.int32), axis=-1
    )
    level_hot = (level[:, None] == jnp.arange(BUCKETS, dtype=jnp.int32)[None, :]).astype(
        jnp.float32
    )
    bias = jnp.einsum("db,bh->hd", level_hot, table, precision=highest).reshape(-1, 2, span)

    tok_float = tok.astype(jnp.float32)
    n1 = both(low(rms_norm(tok_float, norm_self.astype(jnp.float32))))
    qkv = low(nn(flat(n1), self_in)).reshape(2, rows, -1)
    cot_after, qkv = tie(cotangent, qkv)
    cot_raw = turn(cot_after)
    a1, mixed_one, level_one = self_forward(self_info, qkv, bias, examples)
    r1 = tok_float + (nn(a1[0], self_out) + swap(low(nn(a1[1], self_out))).astype(jnp.float32))

    rest_far = permute(mem_rest, net["take"])
    mem, kv = memory_rows(
        place["y"],
        settled,
        [mem_near, memory, mem_first, first_far, mem_rest, rest_far],
        cross_kv,
        examples,
    )
    mem = mem.reshape(2, -1, width)
    kv = kv.reshape(2, -1, 2 * inner)
    n2 = both(low(rms_norm(r1, norm_cross.astype(jnp.float32))))
    q2 = low(nn(flat(n2), cross_q)).reshape(2, rows, -1)

    kv, cot_raw = tie(kv, cot_raw)
    cot = reorder(False, cotangent, cot_raw, place["settled"], examples)
    positions = core * half_pos + jnp.arange(half_pos, dtype=jnp.int32)
    live = (positions[None, :] < target_len[:, None]).astype(jnp.float32).reshape(rows, 1)
    dy = cot.astype(jnp.float32) * live * token_scale
    gy = low(dy)
    gy_far = permute(gy, net["y"])

    a2, mixed_two, level_two = cross_forward(memory_len, q2, kv, examples)
    a2, gy_far = tie(a2, gy_far)
    r2 = r1 + (nn(a2[0], cross_out) + swap(low(nn(a2[1], cross_out))).astype(jnp.float32))

    n3 = low(rms_norm(r2, norm_ffn.astype(jnp.float32)))
    n3_far = permute(n3, net["y"])
    out_own, dn_own, h_own, p_own = ffn_rows(n3, gy, ffn_in, ffn_out, jnp.float32)
    out_own, n3_far = tie(out_own, n3_far)
    out_far, dn_far, h_far, p_far = ffn_rows(n3_far, gy_far, ffn_in, ffn_out, jnp.bfloat16)
    dn_far = permute(dn_far, net["y"])
    ffn_part = ffn_weights((n3, n3_far), (gy, gy_far), (h_own, h_far), (p_own, p_far))
    dn_far, ffn_part = tie(dn_far, ffn_part)
    ffn_piece = lax.psum_scatter(ffn_part, "dp", scatter_dimension=0, tiled=True)
    dn3 = dn_own + dn_far.astype(jnp.float32)
    back, gain_three = norm_backward(r2, norm_ffn, dn3)
    dr2 = dy + back

    g2 = both(low(dr2))
    da2 = low(nt(flat(g2), cross_out)).reshape(2, rows, -1)
    da2, out_far = tie(da2, out_far)
    out_far = permute(out_far, net["y"])
    dq2, dkv = cross_backward(memory_len, q2, kv, da2, mixed_two, level_two, examples)
    dkv, out_far = tie(dkv, out_far)
    block_out = low(r2 + (out_own + out_far.astype(jnp.float32)))
    block_back = turn(block_out)
    dkv_swapped = swap(low(nt(pick(dkv, 1 - core), cross_kv)))
    cross_kv_part = low(tn(flat(mem), flat(dkv)))
    dkv_swapped, cross_kv_part = tie(dkv_swapped, cross_kv_part)
    memory_grad = low(nt(pick(dkv, core), cross_kv) + dkv_swapped.astype(jnp.float32))
    memory_grad, cross_kv_part, dq2 = tie(memory_grad, cross_kv_part, dq2)
    memory_back = turn(memory_grad)
    dn2 = nt(dq2[0], cross_q) + swap(low(nt(dq2[1], cross_q))).astype(jnp.float32)
    back, gain_two = norm_backward(r1, norm_cross, dn2)
    dr1 = dr2 + back
    cross_out_part = low(tn(flat(a2), flat(g2)))
    cross_q_part = low(tn(flat(dq2), flat(n2)))

    g1 = both(low(dr1))
    self_out_part = low(tn(flat(a1), flat(g1)))
    da1 = low(nt(flat(g1), self_out)).reshape(2, rows, -1)
    head_parts = [cross_kv_part, cross_out_part, self_out_part, cross_q_part]
    head_parts = [pieces(part) for part in head_parts]
    zero = jnp.zeros((1, width), jnp.float32)
    small = jnp.concatenate([zero, gain_two[None], gain_three[None], jnp.tile(zero, (5, 1))])
    da1, head_parts, small, ffn_piece, block_back = tie(
        da1, head_parts, small, ffn_piece, block_back
    )
    ffn_whole = lax.all_gather(ffn_piece, "dp", axis=0, tiled=True)

    heads_done, small, tokens_grad, tokens_back = settle(
        head_parts,
        small,
        target_len,
        (qkv, bias, da1, mixed_one, level_one),
        (n1, self_in, tok, dr1, norm_self.astype(jnp.float32)[None]),
        groups,
        examples,
    )
    small, ffn_whole, block_back, memory_back = tie(small, ffn_whole, block_back, memory_back)
    gains = small[0, :3] + small[1, :3]
    by_distance = jnp.where(settled == 1, small[0, 4:6], small[1, 4:6]).reshape(-1, span)
    bias_grad = jnp.einsum("hd,db->bh", by_distance, level_hot, precision=highest)
    block_out = reorder(True, block_out, block_back, place["settled"], examples)
    tokens_grad = reorder(True, tokens_grad, tokens_back, place["settled"], examples)
    memory_grad = reorder(True, memory_grad, memory_back, place["settled"], examples)

    ffn_out_grad, ffn_in_grad = widen(ffn_whole)
    (
        key_cross_grad,
        value_cross_grad,
        out_cross_grad,
        out_self_grad,
        query_cross_grad,
        query_self_grad,
        key_self_grad,
        value_self_grad,
    ) = unpack(heads_done, inner)
    return (
        block_out,
        tokens_grad,
        memory_grad,
        gains[0],
        query_self_grad,
        key_self_grad,
        value_self_grad,
        out_self_grad,
        bias_grad,
        gains[1],
        query_cross_grad,
        key_cross_grad,
        value_cross_grad,
        out_cross_grad,
        gains[2],
        ffn_in_grad,
        ffn_out_grad,
    )


def solution(mesh):
    placed = (
        P(("dp", "mp"), None),
        P(("dp", "mp"), None),
        P(("dp", "mp"), None),
        P("dp"),
        P("dp"),
        P(),
        P(None, "mp"),
        P(None, "mp"),
        P(None, "mp"),
        P("mp", None),
        P(None, "mp"),
        P(),
        P(None, "mp"),
        P(None, "mp"),
        P(None, "mp"),
        P("mp", None),
        P(),
        P(None, "mp"),
        P("mp", None),
    )
    near = mesh.shape["mp"] == 2 and mesh.shape["dp"] == 16
    return jax.shard_map(
        on_chip_group if near else on_device,
        mesh=mesh,
        in_specs=placed,
        out_specs=(
            P(("dp", "mp"), None),
            P(("dp", "mp"), None),
            P(("dp", "mp"), None),
            P(),
            P(None, "mp"),
            P(None, "mp"),
            P(None, "mp"),
            P("mp", None),
            P(None, "mp"),
            P(),
            P(None, "mp"),
            P(None, "mp"),
            P(None, "mp"),
            P("mp", None),
            P(),
            P(None, "mp"),
            P("mp", None),
        ),
        check_vma=False,
    )
```

```python
import functools
import math

import jax
import jax.numpy as jnp
import numpy as np
from jax import lax
from jax.experimental import pallas as pl
from jax.experimental.pallas import tpu as pltpu
from jax.sharding import PartitionSpec as P

HEAD_DIM = 64
BUCKETS = 32


epsilon = 1e-06
masked_score = -1e30
highest = lax.Precision.HIGHEST


def bucket_edges():
    exact = list(range(1, 17))
    spaced = [int(math.ceil(16.0 * 8.0 ** ((level - 16) / 16.0))) for level in range(17, 32)]
    return np.array(exact + spaced, dtype=np.int32)


def rms_norm(value, gain):
    factor = lax.rsqrt(jnp.mean(value * value, axis=-1, keepdims=True) + epsilon)
    return value * factor * gain


def gather_rows(value):
    return lax.all_gather(value, "mp", axis=0, tiled=True)


def spread_rows(value):
    return lax.psum_scatter(value, "mp", scatter_dimension=0, tiled=True)


def matmul(left, right):
    return jnp.dot(left, right, preferred_element_type=jnp.float32)


def left_product(left, right):
    return lax.dot_general(
        left, right, (((0,), (0,)), ((), ())), preferred_element_type=jnp.float32
    )


def right_product(left, right):
    return lax.dot_general(
        left, right, (((1,), (1,)), ((), ())), preferred_element_type=jnp.float32
    )


def attend_forward(query, key_rows, value_rows, score_bias, mask):
    scores = jnp.einsum("pehd,kehd->ehpk", query, key_rows, preferred_element_type=jnp.float32)
    if score_bias is not None:
        scores = scores + score_bias[None]
    scores = jnp.where(mask, scores, masked_score)
    row_max = jnp.max(scores, axis=-1, keepdims=True)
    weights = jnp.exp(scores - row_max)
    probs = weights / jnp.sum(weights, axis=-1, keepdims=True)
    probs_low = probs.astype(jnp.bfloat16)
    output = jnp.einsum(
        "ehpk,kehd->pehd", probs_low, value_rows, preferred_element_type=jnp.float32
    )
    return (probs, probs_low, output.astype(jnp.bfloat16))


def attend_backward(query, key_rows, value_rows, probs, probs_low, grad_mixed):
    grad_probs = jnp.einsum(
        "pehd,kehd->ehpk", grad_mixed, value_rows, preferred_element_type=jnp.float32
    )
    inner_sum = jnp.sum(probs * grad_probs, axis=-1, keepdims=True)
    grad_scores = (probs * (grad_probs - inner_sum)).astype(jnp.bfloat16)
    grad_query = jnp.einsum(
        "ehpk,kehd->pehd", grad_scores, key_rows, preferred_element_type=jnp.float32
    )
    grad_keys = jnp.einsum(
        "ehpk,pehd->kehd", grad_scores, query, preferred_element_type=jnp.float32
    )
    grad_values = jnp.einsum(
        "ehpk,pehd->kehd", probs_low, grad_mixed, preferred_element_type=jnp.float32
    )
    return (
        grad_scores,
        grad_query.astype(jnp.bfloat16),
        grad_keys.astype(jnp.bfloat16),
        grad_values.astype(jnp.bfloat16),
    )


def norm_backward(value, gain, grad_normed):
    pullback = jax.vjp(rms_norm, value, gain.astype(jnp.float32))[1]
    return pullback(grad_normed)


def on_device(
    tokens,
    memory,
    cotangent,
    target_lengths,
    memory_lengths,
    norm_self,
    query_self,
    key_self,
    value_self,
    out_self,
    bias_table,
    norm_cross,
    query_cross,
    key_cross,
    value_cross,
    out_cross,
    norm_ffn,
    ffn_in,
    ffn_out,
):
    examples = target_lengths.shape[0]
    local_rows = tokens.shape[0]
    parts = lax.axis_size("mp")
    device_rank = lax.axis_index("mp")
    local_pos = local_rows // examples
    total_pos = local_pos * parts
    memory_local = memory.shape[0]
    memory_total = memory_local * parts
    memory_pos = memory_total // examples
    inner_local = query_self.shape[1]
    heads = inner_local // HEAD_DIM
    total_rows = local_rows * parts
    group_count = jnp.sum(target_lengths).astype(jnp.float32)
    total_count = lax.psum(group_count, "dp")
    token_scale = lax.axis_size("dp") * group_count / total_count
    positions = device_rank * local_pos + jnp.arange(local_pos, dtype=jnp.int32)
    live_rows = (
        (positions[:, None] < target_lengths[None, :]).astype(jnp.float32).reshape(local_rows, 1)
    )
    target_pos = jnp.arange(total_pos, dtype=jnp.int32)
    distance = jnp.maximum(target_pos[:, None] - target_pos[None, :], 0)
    buckets = jnp.sum(
        (distance[:, :, None] >= jnp.asarray(bucket_edges())[None, None, :]).astype(jnp.int32),
        axis=-1,
    )
    table_hot = (buckets[:, :, None] == jnp.arange(BUCKETS, dtype=jnp.int32)[None, None, :]).astype(
        jnp.float32
    )
    causal = target_pos[None, :] <= target_pos[:, None]
    self_mask = causal[None, None] & (
        target_pos[None, None, None, :] < target_lengths[:, None, None, None]
    )
    cross_pos = jnp.arange(memory_pos, dtype=jnp.int32)
    cross_mask = cross_pos[None, None, None, :] < memory_lengths[:, None, None, None]
    score_bias = jnp.einsum(
        "qkb,bh->hqk", table_hot, bias_table.astype(jnp.float32), precision=highest
    )

    def target_view(value):
        return value.reshape(total_pos, examples, heads, HEAD_DIM)

    def memory_view(value):
        return value.reshape(memory_pos, examples, heads, HEAD_DIM)

    tokens_float = tokens.astype(jnp.float32)
    normed_one = rms_norm(tokens_float, norm_self.astype(jnp.float32)).astype(jnp.bfloat16)
    rows_one = gather_rows(normed_one)
    self_weights = jnp.concatenate([query_self, key_self, value_self], axis=1)
    projected = matmul(rows_one, self_weights).astype(jnp.bfloat16)
    query_one = target_view(projected[:, :inner_local])
    keys_one = target_view(projected[:, inner_local : 2 * inner_local])
    values_one = target_view(projected[:, 2 * inner_local :])
    probs_one, low_one, mixed_one = attend_forward(
        query_one, keys_one, values_one, score_bias, self_mask
    )
    mixed_rows_one = mixed_one.reshape(total_rows, inner_local)
    resid_one = tokens_float + spread_rows(matmul(mixed_rows_one, out_self))
    normed_two = rms_norm(resid_one, norm_cross.astype(jnp.float32)).astype(jnp.bfloat16)
    rows_two = gather_rows(normed_two)
    query_two = target_view(matmul(rows_two, query_cross).astype(jnp.bfloat16))
    memory_all = lax.all_gather(memory, "mp", axis=0, tiled=True)
    cross_kv = matmul(memory_all, jnp.concatenate([key_cross, value_cross], axis=1)).astype(
        jnp.bfloat16
    )
    keys_flat = cross_kv[:, :inner_local]
    values_flat = cross_kv[:, inner_local:]
    keys_two = memory_view(keys_flat)
    values_two = memory_view(values_flat)
    probs_two, low_two, mixed_two = attend_forward(
        query_two, keys_two, values_two, None, cross_mask
    )
    mixed_rows_two = mixed_two.reshape(total_rows, inner_local)
    resid_two = resid_one + spread_rows(matmul(mixed_rows_two, out_cross))
    normed_three = rms_norm(resid_two, norm_ffn.astype(jnp.float32)).astype(jnp.bfloat16)
    rows_three = gather_rows(normed_three)
    pre_act = matmul(rows_three, ffn_in)
    hidden = jax.nn.gelu(pre_act).astype(jnp.bfloat16)
    block_out = resid_two + spread_rows(matmul(hidden, ffn_out))
    grad_out = cotangent.astype(jnp.float32) * live_rows * token_scale
    grad_rows_three = gather_rows(grad_out.astype(jnp.bfloat16))
    ffn_out_grad = left_product(hidden, grad_rows_three)
    grad_hidden = right_product(grad_rows_three, ffn_out)
    gelu_back = jax.vjp(jax.nn.gelu, pre_act)[1]
    grad_pre = gelu_back(grad_hidden)[0].astype(jnp.bfloat16)
    ffn_in_grad = left_product(rows_three, grad_pre)
    grad_normed_three = spread_rows(right_product(grad_pre, ffn_in))
    grad_resid_three, gain_three = norm_backward(resid_two, norm_ffn, grad_normed_three)
    grad_two = grad_out + grad_resid_three
    grad_rows_two = gather_rows(grad_two.astype(jnp.bfloat16))
    out_cross_grad = left_product(mixed_rows_two, grad_rows_two)
    grad_mixed_two = target_view(right_product(grad_rows_two, out_cross).astype(jnp.bfloat16))
    cross_back = attend_backward(
        query_two, keys_two, values_two, probs_two, low_two, grad_mixed_two
    )
    grad_query_two = cross_back[1].reshape(total_rows, inner_local)
    grad_keys_two = cross_back[2].reshape(memory_total, inner_local)
    grad_values_two = cross_back[3].reshape(memory_total, inner_local)
    query_cross_grad = left_product(rows_two, grad_query_two)
    grad_normed_two = spread_rows(right_product(grad_query_two, query_cross))
    key_cross_grad = left_product(memory_all, grad_keys_two)
    value_cross_grad = left_product(memory_all, grad_values_two)
    memory_terms = right_product(grad_keys_two, key_cross) + right_product(
        grad_values_two, value_cross
    )
    memory_grad = lax.psum_scatter(memory_terms, "mp", scatter_dimension=0, tiled=True)
    grad_resid_two, gain_two = norm_backward(resid_one, norm_cross, grad_normed_two)
    grad_one = grad_two + grad_resid_two
    grad_rows_one = gather_rows(grad_one.astype(jnp.bfloat16))
    out_self_grad = left_product(mixed_rows_one, grad_rows_one)
    grad_mixed_one = target_view(right_product(grad_rows_one, out_self).astype(jnp.bfloat16))
    self_back = attend_backward(query_one, keys_one, values_one, probs_one, low_one, grad_mixed_one)
    bias_table_grad = jnp.einsum(
        "ehqk,qkb->bh", self_back[0].astype(jnp.float32), table_hot, precision=highest
    )
    grad_projected = jnp.concatenate(
        [
            self_back[1].reshape(total_rows, inner_local),
            self_back[2].reshape(total_rows, inner_local),
            self_back[3].reshape(total_rows, inner_local),
        ],
        axis=1,
    )
    self_weight_grad = left_product(rows_one, grad_projected)
    grad_normed_one = spread_rows(right_product(grad_projected, self_weights))
    grad_resid_one, gain_one = norm_backward(tokens_float, norm_self, grad_normed_one)
    tokens_grad = grad_one + grad_resid_one
    summed = lax.psum(
        (
            self_weight_grad[:, :inner_local],
            self_weight_grad[:, inner_local : 2 * inner_local],
            self_weight_grad[:, 2 * inner_local :],
            out_self_grad,
            bias_table_grad,
            query_cross_grad,
            key_cross_grad,
            value_cross_grad,
            out_cross_grad,
            ffn_in_grad,
            ffn_out_grad,
        ),
        "dp",
    )
    gains = lax.psum((gain_one, gain_two, gain_three), ("dp", "mp"))
    return (
        block_out.astype(jnp.bfloat16),
        tokens_grad.astype(jnp.bfloat16),
        memory_grad.astype(jnp.bfloat16),
        gains[0],
        summed[0],
        summed[1],
        summed[2],
        summed[3],
        summed[4],
        gains[1],
        summed[5],
        summed[6],
        summed[7],
        summed[8],
        gains[2],
        summed[9],
        summed[10],
    )


def links(dp_size):
    total = 2 * dp_size

    def swap(bit):
        return [(at, at ^ bit) for at in range(total)]

    def turned(at):
        return (at & ~3) | ((at & 1) << 1) | ((at >> 1) & 1)

    return {
        "turn": [(at, turned(at)) for at in range(total) if at != turned(at)],
        "give": [(at, at ^ 2) for at in range(total) if (at & 1) == ((at >> 1) & 1)],
        "take": [(at, at ^ 2) for at in range(total) if (at & 1) != ((at >> 1) & 1)],
        "y": swap(1),
        "core": swap(2),
        "x": swap(4),
        "zl": swap(8),
        "zh": swap(16),
    }


def permute(value, pairs):
    return lax.ppermute(value, ("dp", "mp"), pairs)


def reorder_kernel(inverse, examples, info, held, arrived, target):
    block = 256
    chunk = block // examples

    def write(source):
        high = lax.broadcasted_iota(jnp.int32, (block, block), 0)
        low = lax.broadcasted_iota(jnp.int32, (block, block), 1)
        if inverse:
            hot = low == (high % examples) * chunk + high // examples
            for i in range(target.shape[0] // block):
                value = source[:, chunk * i : chunk * (i + 1), :].reshape(block, -1)
                moved = nn(hot.astype(jnp.bfloat16), value).astype(jnp.bfloat16)
                target[block * i : block * (i + 1), :] = moved
        else:
            hot = low == (high % chunk) * examples + high // chunk
            for i in range(source.shape[0] // block):
                value = source[block * i : block * (i + 1), :]
                moved = nn(hot.astype(jnp.bfloat16), value).astype(jnp.bfloat16)
                target[:, chunk * i : chunk * (i + 1), :] = moved.reshape(examples, chunk, -1)

    @pl.when(info[0] == 1)
    def _():
        write(held)

    @pl.when(info[0] == 0)
    def _():
        write(arrived)


def reorder(inverse, held, arrived, settled, examples):
    rows, width = held.shape
    block = min(rows, 512)
    flat = pl.BlockSpec((block, width), lambda i, s: (i, 0))
    flat_shape = (rows, width)
    split_shape = (examples, rows // examples, width)
    split_block = (examples, block // examples, width)
    if inverse:
        held, arrived = held.reshape(split_shape), arrived.reshape(split_shape)
        in_specs = [
            pl.BlockSpec(split_block, lambda i, s: (0, i * s[0], 0)),
            pl.BlockSpec(split_block, lambda i, s: (0, i * (1 - s[0]), 0)),
        ]
        out_spec, out_shape = flat, flat_shape
    else:
        in_specs = [
            pl.BlockSpec((block, width), lambda i, s: (i * s[0], 0)),
            pl.BlockSpec((block, width), lambda i, s: (i * (1 - s[0]), 0)),
        ]
        out_spec = pl.BlockSpec(split_block, lambda i, s: (0, i, 0))
        out_shape = split_shape
    return pl.pallas_call(
        functools.partial(reorder_kernel, inverse, examples),
        grid_spec=pltpu.PrefetchScalarGridSpec(
            num_scalar_prefetch=1,
            grid=(rows // block,),
            in_specs=in_specs,
            out_specs=out_spec,
        ),
        out_shape=jax.ShapeDtypeStruct(out_shape, held.dtype),
        cost_estimate=cost(2 * rows * width * block, 4 * rows * width),
        compiler_params=pltpu.CompilerParams(vmem_limit_bytes=SMALL_VMEM),
    )(settled, held, arrived).reshape(flat_shape)


def memory_kernel(examples, info, *refs):
    sources, weight, rows_out, kv_out = refs[:6], refs[6], refs[7], refs[8]
    block = 256
    chunk = block // examples
    high = lax.broadcasted_iota(jnp.int32, (block, block), 0)
    low = lax.broadcasted_iota(jnp.int32, (block, block), 1)
    hot = (low == (high % chunk) * examples + high // chunk).astype(jnp.bfloat16)

    def write(source):
        parts = []
        for start in range(0, source.shape[0], block):
            moved = nn(hot, source[start : start + block, :]).astype(jnp.bfloat16)
            parts.append(moved.reshape(examples, chunk, moved.shape[1]))
        moved = jnp.concatenate(parts, axis=1)
        rows_out[...] = moved.reshape(rows_out.shape)
        moved = nn(moved.reshape(source.shape), weight[...]).astype(jnp.bfloat16)
        kv_out[...] = moved.reshape(kv_out.shape)

    late = pl.program_id(1) >= 1
    kind = jnp.where(pl.program_id(0) == 0, 0, jnp.where(late, 4, 2)) + info[1]
    for i in range(6):
        pl.when(kind == i)(functools.partial(write, sources[i]))


def memory_rows(y_half, settled, sources, weight, examples):
    rows, width = sources[0].shape
    block = 512
    blocks = rows // block
    shape = (2, examples, rows // examples, width)
    kv_shape = shape[:3] + (weight.shape[1],)

    def source(which):
        half, part = (0, 0) if which < 2 else (1, which // 2 - 1)
        start = part
        last = (blocks if half == 0 else 1 if part == 0 else blocks - 1) - 1

        def index(p, i, s):
            held = jnp.clip(i - start, 0, last)
            return (jnp.where((p == half) & (s[1] == which % 2), held, 0), 0)

        return pl.BlockSpec((block, width), index)

    def out(columns):
        return pl.BlockSpec(
            (1, examples, block // examples, columns),
            lambda p, i, s: ((p + s[0]) & 1, 0, i, 0),
        )

    return pl.pallas_call(
        functools.partial(memory_kernel, examples),
        grid_spec=pltpu.PrefetchScalarGridSpec(
            num_scalar_prefetch=1,
            grid=(2, blocks),
            in_specs=[source(i) for i in range(6)]
            + [pl.BlockSpec(weight.shape, lambda p, i, s: (0, 0))],
            out_specs=[out(width), out(weight.shape[1])],
        ),
        out_shape=[
            jax.ShapeDtypeStruct(shape, weight.dtype),
            jax.ShapeDtypeStruct(kv_shape, weight.dtype),
        ],
        cost_estimate=cost(4 * rows * width * (weight.shape[1] + 256), 12 * rows * width),
        compiler_params=pltpu.CompilerParams(vmem_limit_bytes=ATTEND_VMEM),
    )(jnp.stack([y_half, settled]), *sources, weight)


def nt(left, right):
    return lax.dot_general(
        left, right, (((1,), (1,)), ((), ())), preferred_element_type=jnp.float32
    )


def tn(left, right):
    return lax.dot_general(
        left, right, (((0,), (0,)), ((), ())), preferred_element_type=jnp.float32
    )


def nn(left, right):
    return jnp.dot(left, right, preferred_element_type=jnp.float32)


def one_head(value, head):
    lane = lax.broadcasted_iota(jnp.int32, value.shape, 1)
    return jnp.where(lane // HEAD_DIM == head, value, jnp.zeros_like(value))


def toeplitz(row, size):
    return pltpu.roll(jnp.broadcast_to(row, (size, size)), 0, 1, stride=1, stride_axis=0)


def diagonals(square):
    size = square.shape[0]
    row = lax.broadcasted_iota(jnp.int32, square.shape, 0)
    turned, step = square, 1
    while step < size:
        moved = pltpu.roll(turned, size - step, 1)
        turned = jnp.where((row & step) != 0, moved, turned)
        step *= 2
    return jnp.sum(turned, axis=0, keepdims=True)


def heads_joined(first, second):
    return jnp.concatenate([first, second], axis=0).T


def head_rows(value, head):
    return value[HEAD_DIM * head : HEAD_DIM * (head + 1)]


def self_heads(core, rows, scratch, example):
    half = scratch.shape[1] // 2
    at = pl.ds(example * half, half)
    scratch[example, pl.ds(pl.multiple_of(core * half, half), half), :] = rows[0, at, :]
    scratch[example, pl.ds(pl.multiple_of((1 - core) * half, half), half), :] = rows[1, at, :]
    return scratch[example]


def self_store(core, value, scratch, out, example):
    half = scratch.shape[1] // 2
    at = pl.ds(example * half, half)
    scratch[example] = value
    out[0, at, :] = scratch[example, pl.ds(pl.multiple_of(core * half, half), half), :]
    out[1, at, :] = scratch[example, pl.ds(pl.multiple_of((1 - core) * half, half), half), :]


def self_masks(size, length):
    key_at = lax.broadcasted_iota(jnp.int32, (size, size), 0)
    query_at = lax.broadcasted_iota(jnp.int32, (size, size), 1)
    return jnp.where((key_at <= query_at) & (key_at < length), 0.0, masked_score)


def side_by_side(value):
    return jnp.concatenate([one_head(value, head) for head in range(2)], axis=0)


def own_blocks(value, size):
    return value[:HEAD_DIM, :size], value[HEAD_DIM:, size:]


def self_forward_kernel(examples, info, rows, bias, out, mixed, level, scratch, out_scratch):
    core = info[0]
    size = scratch.shape[1]
    slopes = jnp.concatenate(
        [toeplitz(bias[0, head : head + 1, :], size) for head in range(2)], axis=1
    )
    for example in range(examples):
        joined = self_heads(core, rows, scratch, example)
        query, keys = joined[:, :128], joined[:, 128:256]
        mask = self_masks(size, info[1 + example])
        scores = nt(keys, side_by_side(query)) + slopes + jnp.concatenate([mask, mask], axis=1)
        top = jnp.max(scores, axis=0, keepdims=True)
        weights = jnp.exp(scores - top)
        total = jnp.sum(weights, axis=0, keepdims=True)
        probs = (weights * (1.0 / total)).astype(jnp.bfloat16)
        sums = nn(joined[:, 256:].T, probs)
        parts = own_blocks(sums, size)
        levels = top + jnp.log(total)
        for head in range(2):
            level[0, example, head : head + 1, :] = levels[:, size * head : size * (head + 1)]
            mixed[0, example, HEAD_DIM * head : HEAD_DIM * (head + 1), :] = parts[head]
        result = heads_joined(*parts).astype(jnp.bfloat16)
        self_store(core, result, out_scratch, out, example)


def by_length(length, span, body):
    quarter = span // 4
    for part in range(1, 5):
        keys = part * quarter
        inside = length > keys - quarter
        if part < 4:
            inside = inside & (length <= keys)

        @pl.when(inside)
        def _():
            body(keys)


def masked_tail(scores, length, quarter):
    keys, count = scores.shape
    key_at = keys - quarter + lax.broadcasted_iota(jnp.int32, (quarter, count), 0)
    tail = scores[keys - quarter :] + jnp.where(key_at < length, 0.0, masked_score)
    if keys == quarter:
        return tail
    return jnp.concatenate([scores[: keys - quarter], tail], axis=0)


def cross_forward_kernel(info, queries, kv, out, mixed, level):
    length = info[pl.program_id(0)]
    count = 2 * queries.shape[1]
    span = 2 * kv.shape[1]

    def body(keys):
        for pair in range(queries.shape[2] // 128):
            columns = slice(128 * pair, 128 * (pair + 1))
            heads = side_by_side(queries[:, :, columns].reshape(-1, 128))
            joined = kv[:, :, 256 * pair : 256 * (pair + 1)].reshape(span, 256)[:keys]
            scores = masked_tail(nt(joined[:, :128], heads), length, span // 4)
            top = jnp.max(scores, axis=0, keepdims=True)
            weights = jnp.exp(scores - top)
            total = jnp.sum(weights, axis=0, keepdims=True)
            probs = (weights * (1.0 / total)).astype(jnp.bfloat16)
            parts = own_blocks(nn(joined[:, 128:].T, probs), count)
            levels = top + jnp.log(total)
            for head in range(2):
                mixed[0, pair, HEAD_DIM * head : HEAD_DIM * (head + 1), :] = parts[head]
                level[0, pair, head : head + 1, :] = levels[:, count * head : count * (head + 1)]
            out[:, :, columns] = (
                heads_joined(*parts).astype(jnp.bfloat16).reshape(2, count // 2, 128)
            )

    by_length(length, span, body)


def cross_backward_kernel(info, queries, kv, grads, mixed, level, dq, dkv):
    length = info[pl.program_id(0)]
    count = 2 * queries.shape[1]
    span = 2 * kv.shape[1]

    def body(keys):
        for pair in range(queries.shape[2] // 128):
            columns = slice(128 * pair, 128 * (pair + 1))
            wide = slice(256 * pair, 256 * (pair + 1))
            grad = grads[:, :, columns].reshape(-1, 128)
            heads = side_by_side(queries[:, :, columns].reshape(-1, 128))
            grad_heads = side_by_side(grad)
            products = grad.astype(jnp.float32).T * mixed[0, pair]
            inner = jnp.concatenate(
                [jnp.sum(head_rows(products, head), axis=0, keepdims=True) for head in range(2)],
                axis=1,
            )
            levels = jnp.concatenate([level[0, pair, 0:1, :], level[0, pair, 1:2, :]], axis=1)
            joined = kv[:, :, wide].reshape(span, 256)[:keys]
            scores = masked_tail(nt(joined[:, :128], heads), length, span // 4)
            probs = jnp.exp(scores - levels)
            grad_scores = (probs * (nt(joined[:, 128:], grad_heads) - inner)).astype(
                jnp.bfloat16
            )
            result = jnp.concatenate(
                [nn(grad_scores, heads), nn(probs.astype(jnp.bfloat16), grad_heads)], axis=1
            ).astype(jnp.bfloat16)
            if keys < span:
                result = jnp.concatenate(
                    [result, jnp.zeros((span - keys, 256), jnp.bfloat16)], axis=0
                )
            dkv[:, :, wide] = result.reshape(2, span // 2, 256)
            sums = nn(joined[:, :128].T, grad_scores)
            dq[:, :, columns] = (
                heads_joined(*own_blocks(sums, count))
                .astype(jnp.bfloat16)
                .reshape(2, count // 2, 128)
            )

    by_length(length, span, body)


MIB = 1024 * 1024


def cost(flops, moved, exps=0):
    return pl.CostEstimate(
        flops=int(flops), bytes_accessed=int(moved), transcendentals=int(exps)
    )


SMALL_VMEM = 12 * MIB
ATTEND_VMEM = 24 * MIB
FFN_VMEM = 44 * MIB
SETTLE_VMEM = 48 * MIB
MESH = pl.DeviceIdType.MESH
SMEM_SPEC = pl.BlockSpec(memory_space=pltpu.SMEM)


def self_forward(info, rows, bias, examples):
    _, count, width = rows.shape
    pairs, size = width // 384, count // examples
    return pl.pallas_call(
        functools.partial(self_forward_kernel, examples),
        grid=(pairs,),
        in_specs=[
            SMEM_SPEC,
            pl.BlockSpec((2, count, 384), lambda h: (0, 0, h)),
            pl.BlockSpec((1, 2, 2 * size), lambda h: (h, 0, 0)),
        ],
        out_specs=[
            pl.BlockSpec((2, count, 128), lambda h: (0, 0, h)),
            pl.BlockSpec((1, examples, 128, 2 * size), lambda h: (h, 0, 0, 0)),
            pl.BlockSpec((1, examples, 2, 2 * size), lambda h: (h, 0, 0, 0)),
        ],
        out_shape=[
            jax.ShapeDtypeStruct((2, count, pairs * 128), jnp.bfloat16),
            jax.ShapeDtypeStruct((pairs, examples, 128, 2 * size), jnp.float32),
            jax.ShapeDtypeStruct((pairs, examples, 2, 2 * size), jnp.float32),
        ],
        scratch_shapes=[
            pltpu.VMEM((examples, 2 * size, 384), jnp.bfloat16),
            pltpu.VMEM((examples, 2 * size, 128), jnp.bfloat16),
        ],
        cost_estimate=cost(
            2 * 2 * examples * 2 * pairs * (2 * size) ** 2 * 256 * 2,
            8 * rows.size,
            examples * 2 * pairs * (2 * size) ** 2,
        ),
        compiler_params=pltpu.CompilerParams(vmem_limit_bytes=ATTEND_VMEM),
    )(info, rows, bias)


def cross_forward(info, queries, kv, examples):
    _, count, width = queries.shape
    pairs, size, span = width // 128, count // examples, kv.shape[1] // examples
    thin = pl.BlockSpec((2, size, 256), lambda e, h: (0, e, h))
    wide = pl.BlockSpec((2, span, 512), lambda e, h: (0, e, h))
    return pl.pallas_call(
        cross_forward_kernel,
        grid=(examples, pairs // 2),
        in_specs=[SMEM_SPEC, thin, wide],
        out_specs=[
            thin,
            pl.BlockSpec((1, 2, 128, 2 * size), lambda e, h: (e, h, 0, 0)),
            pl.BlockSpec((1, 2, 2, 2 * size), lambda e, h: (e, h, 0, 0)),
        ],
        out_shape=[
            jax.ShapeDtypeStruct(queries.shape, jnp.bfloat16),
            jax.ShapeDtypeStruct((examples, pairs, 128, 2 * size), jnp.float32),
            jax.ShapeDtypeStruct((examples, pairs, 2, 2 * size), jnp.float32),
        ],
        cost_estimate=cost(
            2 * 2 * examples * 2 * pairs * 4 * size * span * 256,
            4 * kv.size,
            examples * 2 * pairs * 4 * size * span,
        ),
        compiler_params=pltpu.CompilerParams(vmem_limit_bytes=32 * MIB),
    )(info, queries, kv)


def cross_backward(info, queries, kv, grads, mixed, level, examples):
    _, count, width = queries.shape
    pairs, size, span = width // 128, count // examples, kv.shape[1] // examples
    thin = pl.BlockSpec((2, size, 256), lambda e, h: (0, e, h))
    wide = pl.BlockSpec((2, span, 512), lambda e, h: (0, e, h))
    return pl.pallas_call(
        cross_backward_kernel,
        grid=(examples, pairs // 2),
        in_specs=[
            SMEM_SPEC,
            thin,
            wide,
            thin,
            pl.BlockSpec((1, 2, 128, 2 * size), lambda e, h: (e, h, 0, 0)),
            pl.BlockSpec((1, 2, 2, 2 * size), lambda e, h: (e, h, 0, 0)),
        ],
        out_specs=[thin, wide],
        out_shape=[
            jax.ShapeDtypeStruct(queries.shape, jnp.bfloat16),
            jax.ShapeDtypeStruct(kv.shape, jnp.bfloat16),
        ],
        cost_estimate=cost(
            5 * 2 * examples * 2 * pairs * 4 * size * span * 256,
            6 * kv.size,
            examples * 2 * pairs * 4 * size * span,
        ),
        compiler_params=pltpu.CompilerParams(vmem_limit_bytes=58 * MIB),
    )(info, queries, kv, grads, mixed, level)


root = math.sqrt(2.0 / math.pi)
cubic = 0.044715


def ffn_rows_kernel(normed, grad, into, outof, out, back, hidden_out, pre_out, out_sum, back_sum):
    step = pl.program_id(0)

    @pl.when(step == 0)
    def _():
        out_sum[...] = jnp.zeros_like(out_sum)
        back_sum[...] = jnp.zeros_like(back_sum)

    pre = nn(normed[...], into[...])
    grad_hidden = nt(grad[...], outof[...])
    bend = jnp.tanh(root * (pre + cubic * (pre * pre * pre)))
    hidden = (0.5 * pre * (1.0 + bend)).astype(jnp.bfloat16)
    slope = 0.5 * (1.0 + bend) + 0.5 * pre * (1.0 - bend * bend) * (
        root * (1.0 + 3.0 * cubic * (pre * pre))
    )
    grad_pre = (grad_hidden * slope).astype(jnp.bfloat16)
    hidden_out[...] = hidden
    pre_out[...] = grad_pre
    out_sum[...] += nn(hidden, outof[...])
    back_sum[...] += nt(grad_pre, into[...])

    @pl.when(step == pl.num_programs(0) - 1)
    def _():
        out[...] = out_sum[...].astype(out.dtype)
        back[...] = back_sum[...].astype(back.dtype)


def ffn_rows(normed, grad, into, outof, kind):
    rows, width = normed.shape
    units = into.shape[1]
    tile = 512
    whole = pl.BlockSpec((rows, width), lambda i: (0, 0))
    tall = pl.BlockSpec((width, tile), lambda i: (0, i))
    flat = pl.BlockSpec((tile, width), lambda i: (i, 0))
    thin = pl.BlockSpec((rows, tile), lambda i: (0, i))
    return pl.pallas_call(
        ffn_rows_kernel,
        grid=(units // tile,),
        in_specs=[whole, whole, tall, flat],
        out_specs=[whole, whole, thin, thin],
        out_shape=[jax.ShapeDtypeStruct((rows, width), kind)] * 2
        + [jax.ShapeDtypeStruct((rows, units), jnp.bfloat16)] * 2,
        scratch_shapes=[pltpu.VMEM((rows, width), jnp.float32)] * 2,
        cost_estimate=cost(
            4 * 2 * rows * width * units, 12 * rows * width + 4 * width * units, rows * units
        ),
        compiler_params=pltpu.CompilerParams(vmem_limit_bytes=ATTEND_VMEM),
    )(normed, grad, into, outof)


def ffn_weights_kernel(n_own, n_far, g_own, g_far, h_own, h_far, p_own, p_far, out):
    step = pl.program_id(0)
    half = pl.num_programs(0) // 2

    @pl.when(step < half)
    def _():
        out[...] = (tn(h_own[...], g_own[...]) + tn(h_far[...], g_far[...])).astype(out.dtype)

    @pl.when(step >= half)
    def _():
        out[...] = (tn(p_own[...], n_own[...]) + tn(p_far[...], n_far[...])).astype(out.dtype)


def ffn_weights(normed, grads, hiddens, pres):
    rows, width = normed[0].shape
    units = hiddens[0].shape[1]
    tile = 512
    steps = units // tile
    whole = pl.BlockSpec((rows, width), lambda i: (0, 0))
    first = pl.BlockSpec((rows, tile), lambda i: (0, jnp.minimum(i, steps - 1)))
    second = pl.BlockSpec((rows, tile), lambda i: (0, jnp.maximum(i - steps, 0)))
    return pl.pallas_call(
        ffn_weights_kernel,
        grid=(2 * steps,),
        in_specs=[whole] * 4 + [first] * 2 + [second] * 2,
        out_specs=pl.BlockSpec((tile, width), lambda i: (i, 0)),
        out_shape=jax.ShapeDtypeStruct((2 * units, width), jnp.bfloat16),
        cost_estimate=cost(
            4 * 2 * rows * width * units, 8 * rows * width + 4 * width * units
        ),
        compiler_params=pltpu.CompilerParams(vmem_limit_bytes=30 * MIB),
    )(*normed, *grads, *hiddens, *pres)


def gather_kernel(groups, examples, tokens, memory, facts, counts, *refs):
    weights, refs = refs[:8], refs[8:]
    tok_out, mem_out, facts_out, counts_out, self_in, cross_q, cross_kv = refs[:7]
    self_out, cross_out = refs[7:9]
    raw, landed, round_in, near_send, near_get, send, get = refs[9:]
    index, y = lax.axis_index("dp"), lax.axis_index("mp")
    core, x, z = index % 2, (index // 2) % 2, index // 4
    deep = groups // 4

    def at(c, yy, xx, zz):
        return (zz * 4 + xx * 2 + c, yy)

    z_near = z + 1 - 2 * (z % 2)
    x_side, z_side = at(core, y, 1 - x, z), at(core, y, x, z_near)
    turned = at(1 - core, 1 - y, x, z)
    rounds = [at(1 - core, y, x, z), x_side, z_side]
    step = 2
    while step < deep:
        rounds.append(at(core, y, x, z + step - 2 * step * ((z // step) % 2)))
        step *= 2
    barrier = pltpu.get_barrier_semaphore()
    for partner in rounds:
        pl.semaphore_signal(barrier, inc=1, device_id=partner, device_id_type=MESH)

    @pl.when(core != y)
    def _():
        pl.semaphore_signal(barrier, inc=1, device_id=turned, device_id_type=MESH)
        pl.semaphore_wait(barrier, len(rounds) + 1)

    @pl.when(core == y)
    def _():
        pl.semaphore_wait(barrier, len(rounds))

    homes = [raw.at[0], raw.at[1], raw.at[2], cross_q, raw.at[3], raw.at[4], self_out, cross_out]

    def remote(source, target, sems, slot, device):
        return pltpu.make_async_remote_copy(
            src_ref=source,
            dst_ref=target,
            send_sem=sems[0].at[slot],
            recv_sem=sems[1].at[slot],
            device_id=device,
            device_id_type=MESH,
        )

    mine = x * 2 + z % 2

    def quarter(w, which, first=0, parts=1):
        rows = homes[w].shape[0] // 4
        size = rows // parts
        return homes[w].at[pl.ds(pl.multiple_of(which * rows + first * size, size), size)]

    def along_y(w):
        rows = homes[w].shape[0] // 4
        sent = mine * rows
        return remote(
            weights[w].at[pl.ds(pl.multiple_of(sent, rows), rows)],
            quarter(w, mine),
            (send, get),
            w,
            turned,
        )

    def direct(w, which):
        piece = quarter(w, mine)
        return remote(piece, piece, (send, get), 8 + 2 * w + which, (x_side, z_side)[which])

    def passed(w, which):
        other = mine + (2 - 4 * x if which == 0 else 1 - 2 * (z % 2))
        piece = quarter(w, other, which, 2)
        return remote(piece, piece, (send, get), 24 + 2 * w + which, (z_side, x_side)[which])

    token_copy = remote(tokens, landed, (send, get), 40, turned)
    facts_copy = remote(facts, facts_out, (send, get), 41, turned)
    early = memory.at[pl.ds(0, mem_out.shape[0])]
    memory_copy = remote(early, mem_out, (send, get), 42 + len(rounds), turned)

    @pl.when(core != y)
    def _():
        facts_copy.start()
        for w in range(8):
            along_y(w).start()
        token_copy.start()
        memory_copy.start()

    @pl.when(core == y)
    def _():
        pltpu.make_async_copy(tokens, landed, near_get.at[0]).start()
        pltpu.make_async_copy(facts, facts_out, near_get.at[1]).start()
        for w in range(8):
            pltpu.make_async_copy(weights[w], homes[w], near_get.at[2 + w]).start()

    def count_copy(i):
        return remote(counts_out, round_in.at[i], (near_send, get), 42 + i, rounds[i])

    def count_round(w):
        if w % 2 == 1 and w // 2 < len(rounds):
            count_copy(w // 2).start()
        if w % 2 == 0 and 0 < w <= 2 * len(rounds):
            count_copy(w // 2 - 1).wait()
            counts_out[...] += round_in[w // 2 - 1]

    counts_out[...] = counts[...]
    @pl.when(core == y)
    def _():
        pltpu.make_async_copy(tokens, landed, near_get.at[0]).wait()
        pltpu.make_async_copy(facts, facts_out, near_get.at[1]).wait()
        for w in range(8):
            pltpu.make_async_copy(weights[w], homes[w], near_get.at[2 + w]).wait()

    def share(w):
        if w < 8:
            along_y(w).wait()
            for which in range(2):
                direct(w, which).start()
        if w > 0:
            for which in range(2):
                direct(w - 1, which).wait()
            for which in range(2):
                passed(w - 1, which).start()

    for w in range(9):
        pl.when(core != y)(functools.partial(share, w))
        count_round(w)

    @pl.when(core != y)
    def _():
        facts_copy.wait()
        token_copy.wait()

    rows = landed.shape[0]
    block = 256
    chunk = block // examples
    high = lax.broadcasted_iota(jnp.int32, (block, block), 0)
    low = lax.broadcasted_iota(jnp.int32, (block, block), 1)
    hot = (low == (high % chunk) * examples + high // chunk).astype(jnp.bfloat16)
    for i in range(rows // block):
        moved = nn(hot, landed[pl.ds(i * block, block), :]).astype(jnp.bfloat16)
        tok_out[:, pl.ds(i * chunk, chunk), :] = moved.reshape(examples, chunk, moved.shape[1])

    @pl.when(core != y)
    def _():
        for w in range(8):
            for which in range(2):
                passed(w, which).wait()
        memory_copy.wait()

    for h in range(raw.shape[2] // 128):
        for i in range(3):
            self_in[:, 384 * h + 128 * i : 384 * h + 128 * i + 128] = raw[
                i, :, 128 * h : 128 * h + 128
            ]
        for i in range(2):
            cross_kv[:, 256 * h + 128 * i : 256 * h + 128 * i + 128] = raw[
                3 + i, :, 128 * h : 128 * h + 128
            ]


def gather(tokens, memory, facts, counts, weights, groups, examples):
    rows, width = tokens.shape
    inner = weights[0].shape[1]
    rounds = 2 + (groups // 4).bit_length() - 1
    anywhere = pl.BlockSpec(memory_space=pl.ANY)
    whole = pl.BlockSpec(memory_space=pltpu.VMEM)

    def half(*shape):
        return jax.ShapeDtypeStruct(shape, jnp.bfloat16)

    return pl.pallas_call(
        functools.partial(gather_kernel, groups, examples),
        in_specs=[anywhere, anywhere, whole, whole] + [anywhere] * 8,
        out_specs=[whole] * 9,
        out_shape=[
            half(examples, rows // examples, width),
            half(memory.shape[0] // 4, width),
            jax.ShapeDtypeStruct(facts.shape, facts.dtype),
            jax.ShapeDtypeStruct(counts.shape, counts.dtype),
            half(width, 3 * inner),
            half(width, inner),
            half(width, 2 * inner),
            half(inner, width),
            half(inner, width),
        ],
        scratch_shapes=[
            pltpu.VMEM((5, width, inner), jnp.bfloat16),
            pltpu.VMEM((rows, width), jnp.bfloat16),
            pltpu.VMEM((rounds,) + counts.shape, counts.dtype),
            pltpu.SemaphoreType.DMA((42 + rounds,)),
            pltpu.SemaphoreType.DMA((10,)),
            pltpu.SemaphoreType.DMA((43 + rounds,)),
            pltpu.SemaphoreType.DMA((43 + rounds,)),
        ],
        cost_estimate=cost(0, 150 * MIB),
        compiler_params=pltpu.CompilerParams(
            collective_id=1, has_side_effects=True, vmem_limit_bytes=SETTLE_VMEM
        ),
    )(tokens, memory, facts, counts, *weights)


def add_low(left, right):
    return (left.astype(jnp.float32) + right.astype(jnp.float32)).astype(jnp.bfloat16)


def pick(value, index):
    return lax.dynamic_index_in_dim(value, index, 0, keepdims=False)


def tie(*values):
    return lax.optimization_barrier(values)


def settle_kernel(groups, examples, *refs):
    parts, small, info, qkv = refs[:4], refs[4], refs[5], refs[6]
    bias, grads, mixed, level, normed, self_in, tok, grad_rest, gain = refs[7:16]
    result_out, small_out, tok_grad, tok_back = refs[16:20]
    value, first, second, third, small_in, rows_held, placed, grad_placed, result = refs[20:29]
    far_sent, far_found, send, receive, small_send, small_get, load, single = refs[29:37]
    out, leave = refs[37:]
    count = len(parts)
    index, y = lax.axis_index("dp"), lax.axis_index("mp")
    core, x, z = index % 2, (index // 2) % 2, index // 4
    deep = groups // 4
    chunks, rows = first.shape[0], first.shape[3]

    def at(c, yy, xx, zz):
        return (zz * 4 + xx * 2 + c, yy)

    def part(k):
        return pl.ds(pl.multiple_of(k * rows, rows), rows)

    fetch = pltpu.make_async_copy(qkv, rows_held, load.at[count])
    fetch.start()
    loads, starts = [], [0]
    for i, ref in enumerate(parts):
        size = ref.shape[1]
        target = value.at[:, pl.ds(starts[-1], size)]
        loads.append(pltpu.make_async_copy(ref, target, load.at[i]))
        loads[-1].start()
        starts.append(starts[-1] + size)
    partners = [at(1 - core, y, x, z), at(core, 1 - y, x, z), at(1 - core, 1 - y, x, z)]
    partners.append(at(core, y, 1 - x, z))
    for step in range(1, deep):
        partners.append(at(core, y, x, (z + step) % deep))
    barrier = pltpu.get_barrier_semaphore()
    for partner in partners:
        pl.semaphore_signal(barrier, inc=1, device_id=partner, device_id_type=MESH)
    pl.semaphore_wait(barrier, len(partners))

    def copy(source, target, slot, k, device):
        return pltpu.make_async_remote_copy(
            src_ref=source,
            dst_ref=target,
            send_sem=send.at[k, slot],
            recv_sem=receive.at[k, slot],
            device_id=device,
            device_id_type=MESH,
        )

    def quarter(k, q):
        return value.at[pl.ds(q * 8, 8), part(k)]

    def to_core(k):
        return copy(quarter(k, 1 - core), first.at[k, 0], 0, k, at(1 - core, core, x, z))

    def to_turned(k):
        return copy(quarter(k, 1 - core), first.at[k, 1], 1, k, at(1 - core, core, x, z))

    def to_same(k):
        return copy(quarter(k, core), first.at[k, 1], 2, k, at(core, core, x, z))

    def arrived(k, slot):
        return copy(quarter(k, core), first.at[k, 1 if slot else 0], slot, k, at(1 - core, y, x, z))

    def along_x(k):
        return copy(
            first.at[k, 1, pl.ds((1 - x) * 4, 4)], second.at[k], 3, k, at(core, y, 1 - x, z)
        )

    def along_z(k, step):
        far = (z + step) % deep
        return copy(
            second.at[k, far], third.at[k, step - 1], 3 + step, k, at(core, y, x, far)
        )

    def back_z(k, step):
        far = (z + step) % deep
        piece = core * 8 + x * 4 + z
        return copy(
            out.at[piece, part(k)], out.at[piece, part(k)], 6 + step, k, at(core, y, x, far)
        )

    def back_x(k):
        held = out.at[pl.ds(core * 8 + x * 4, 4), part(k)]
        return copy(held, held, 10, k, at(core, y, 1 - x, z))

    def back_core(k):
        held = out.at[pl.ds(core * 8, 8), part(k)]
        return copy(held, held, 11, k, at(1 - core, y, x, z))

    rounds = [at(core, 1 - y, x, z), at(core, y, 1 - x, z)]
    step = 1
    while step < deep:
        rounds.append(at(core, y, x, z + step - 2 * step * ((z // step) % 2)))
        step *= 2
    rounds.append(at(1 - core, y, x, z))
    small_out[0] = small[...]

    def small_copy(i):
        return pltpu.make_async_remote_copy(
            src_ref=small_out.at[0],
            dst_ref=small_in.at[i],
            send_sem=small_send.at[i],
            recv_sem=small_get.at[i],
            device_id=rounds[i],
            device_id_type=MESH,
        )

    def small_wait(i):
        small_copy(i).wait()
        if i < len(rounds) - 1:
            small_out[0] = small_out[0] + small_in[i]
        else:
            small_out[1] = small_in[i]

    def single_copy(i, source, target, device):
        return pltpu.make_async_remote_copy(
            src_ref=source,
            dst_ref=target,
            send_sem=single.at[i, 0],
            recv_sem=single.at[i, 1],
            device_id=device,
            device_id_type=MESH,
        )

    far_copy = single_copy(0, far_sent, far_found, at(1 - core, y, x, z))
    turn_copy = single_copy(1, tok_grad, tok_back, at(1 - core, 1 - y, x, z))
    width = tok.shape[1]

    def attend(pair):
        size = placed.shape[1]
        half = size // 2
        columns = slice(384 * pair, 384 * (pair + 1))
        near = pl.ds(pl.multiple_of(core * half, half), half)
        away = pl.ds(pl.multiple_of((1 - core) * half, half), half)
        slopes = jnp.concatenate(
            [toeplitz(bias[pair, head : head + 1, :], size) for head in range(2)], axis=1
        )
        sums = None
        for example in range(examples):
            held = slice(half * example, half * (example + 1))
            placed[example, near, :] = rows_held[0, held, columns]
            placed[example, away, :] = rows_held[1, held, columns]
            grad_placed[example, near, :] = grads[0, held, 128 * pair : 128 * (pair + 1)]
            grad_placed[example, away, :] = grads[1, held, 128 * pair : 128 * (pair + 1)]
            joined, grad = placed[example], grad_placed[example]
            query, keys, values = joined[:, :128], joined[:, 128:256], joined[:, 256:]
            products = grad.astype(jnp.float32).T * mixed[pair, example]
            inner = jnp.concatenate(
                [jnp.sum(head_rows(products, head), axis=0, keepdims=True) for head in range(2)],
                axis=1,
            )
            levels = jnp.concatenate(
                [level[pair, example, 0:1, :], level[pair, example, 1:2, :]], axis=1
            )
            mask = self_masks(size, info[example])
            heads, grad_heads = side_by_side(query), side_by_side(grad)
            scores = nt(keys, heads) + slopes + jnp.concatenate([mask, mask], axis=1)
            probs = jnp.exp(scores - levels)
            grad_scores = (probs * (nt(values, grad_heads) - inner)).astype(jnp.bfloat16)
            square = grad_scores.astype(jnp.float32)
            sums = square if sums is None else sums + square
            result[example] = jnp.concatenate(
                [
                    heads_joined(*own_blocks(nn(keys.T, grad_scores), size)),
                    nn(grad_scores, heads),
                    nn(probs.astype(jnp.bfloat16), grad_heads),
                ],
                axis=1,
            ).astype(jnp.bfloat16)
            rows_held[0, held, columns] = result[example, near, :]
            rows_held[1, held, columns] = result[example, away, :]
        for head in range(2):
            at_column = 512 * (pair % 2) + 256 * head
            small_out[0, 4 + pair // 2 : 5 + pair // 2, at_column : at_column + size] = diagonals(
                sums[:, size * head : size * (head + 1)]
            )
        both_rows = rows_held[:, :, columns].reshape(-1, 384)
        piece = tn(both_rows, normed[...].reshape(-1, width)).astype(jnp.bfloat16)
        value[4 * pair : 4 * pair + 4, starts[count] :, :] = piece.reshape(4, 96, width)

    def heads_sent():
        lax.fori_loop(starts[count] // rows, chunks, start, 0)
        far_sent[...] = nt(rows_held[1], self_in[...]).astype(jnp.bfloat16)
        far_copy.start()

    def tokens_done():
        far_copy.wait()
        back = nt(rows_held[0], self_in[...]) + far_found[...].astype(jnp.float32)
        held = tok[...].astype(jnp.float32)
        size = lax.rsqrt(jnp.mean(held * held, axis=-1, keepdims=True) + epsilon)
        small_out[0, 0:1, :] = jnp.sum(back * held * size, axis=0, keepdims=True)
        back = back * gain[...]
        inner = jnp.mean(back * held, axis=-1, keepdims=True)
        back = back * size - held * (size * size * size * inner)
        tok_grad[...] = (grad_rest[...] + back).astype(jnp.bfloat16)
        small_copy(0).start()

        @pl.when(core != y)
        def _():
            turn_copy.start()

    def start(k, carry):
        @pl.when(core == y)
        def _():
            to_core(k).start()

        @pl.when(core != y)
        def _():
            to_same(k).start()
            to_turned(k).start()

        return carry

    for i in range(count):
        loads[i].wait()
        lax.fori_loop(starts[i] // rows, starts[i + 1] // rows, start, 0)
    fetch.wait()

    def total(left, right):
        return (left.astype(jnp.float32) + right.astype(jnp.float32)).astype(jnp.bfloat16)

    pairs = bias.shape[0]
    work = [functools.partial(attend, pair) for pair in range(pairs)] + [heads_sent, tokens_done]

    def leaving(k):
        return pltpu.make_async_copy(out.at[:, part(k)], result_out.at[:, part(k)], leave.at[k])

    def tick(t, carry):
        for i, piece_of_work in enumerate(work):
            pl.when(t == i)(piece_of_work)
        for i in range(len(rounds) - 1):

            @pl.when(t == chunks + 1 + i)
            def _():
                small_wait(i)
                small_copy(i + 1).start()

        @pl.when(t < chunks)
        def _():
            k = jnp.minimum(t, chunks - 1)

            @pl.when(core == y)
            def _():
                arrived(k, 2).wait_recv()

                def add(i, c):
                    first[k, 1, i] = total(value[core * 8 + i, part(k)], first[k, 1, i])
                    return c

                lax.fori_loop(0, 8, add, 0)

            @pl.when(core != y)
            def _():
                arrived(k, 0).wait_recv()
                arrived(k, 1).wait_recv()

                def add(i, c):
                    first[k, 1, i] = total(first[k, 0, i], first[k, 1, i])
                    return c

                lax.fori_loop(0, 8, add, 0)

            along_x(k).start()

        @pl.when((t >= 1) & (t < chunks + 1))
        def _():
            k = t - 1
            along_x(k).wait_recv()

            def add(i, c):
                second[k, i] = total(first[k, 1, x * 4 + i], second[k, i])
                return c

            lax.fori_loop(0, deep, add, 0)
            for step in range(1, deep):
                along_z(k, step).start()

        @pl.when((t >= 2) & (t < chunks + 2))
        def _():
            k = t - 2
            for step in range(1, deep):
                along_z(k, step).wait_recv()
            summed = second[k, z].astype(jnp.float32)
            for step in range(1, deep):
                summed = summed + third[k, step - 1].astype(jnp.float32)
            out[core * 8 + x * 4 + z, part(k)] = summed.astype(jnp.bfloat16)
            for step in range(1, deep):
                back_z(k, step).start()

        @pl.when((t >= 3) & (t < chunks + 3))
        def _():
            k = t - 3
            for step in range(1, deep):
                back_z(k, step).wait_recv()
            back_x(k).start()

        @pl.when((t >= 4) & (t < chunks + 4))
        def _():
            k = t - 4
            back_x(k).wait_recv()
            back_core(k).start()

        @pl.when(t >= 5)
        def _():
            back_core(t - 5).wait_recv()
            leaving(t - 5).start()

        return carry

    lax.fori_loop(0, chunks + 5, tick, 0)
    small_wait(len(rounds) - 1)

    @pl.when(core != y)
    def _():
        turn_copy.wait()


    def finish_sends(k, carry):
        @pl.when(core == y)
        def _():
            to_core(k).wait_send()

        @pl.when(core != y)
        def _():
            to_same(k).wait_send()
            to_turned(k).wait_send()

        along_x(k).wait_send()
        for step in range(1, deep):
            along_z(k, step).wait_send()
            back_z(k, step).wait_send()
        back_x(k).wait_send()
        back_core(k).wait_send()
        leaving(k).wait()
        return carry

    lax.fori_loop(0, chunks, finish_sends, 0)


def settle(parts, small, info, attention, rows_in, groups, examples):
    qkv, bias, grads, mixed, level = attention
    normed, self_in, tok, grad_rest, gain = rows_in
    count, _, width = parts[0].shape
    kind = parts[0].dtype
    rows = sum(part.shape[1] for part in parts) + qkv.shape[2] // count
    chunk = 16
    chunks = rows // chunk
    deep = groups // 4
    rounds = 3 + deep.bit_length() - 1
    size = 2 * qkv.shape[1] // examples
    whole = pl.BlockSpec(memory_space=pltpu.VMEM)
    anywhere = pl.BlockSpec(memory_space=pl.ANY)
    return pl.pallas_call(
        functools.partial(settle_kernel, groups, examples),
        in_specs=[anywhere] * len(parts) + [whole, SMEM_SPEC, anywhere] + [whole] * 9,
        out_specs=[anywhere] + [whole] * 3,
        out_shape=[
            jax.ShapeDtypeStruct((count, rows, width), kind),
            jax.ShapeDtypeStruct((2,) + small.shape, small.dtype),
            jax.ShapeDtypeStruct(tok.shape, tok.dtype),
            jax.ShapeDtypeStruct(tok.shape, tok.dtype),
        ],
        scratch_shapes=[
            pltpu.VMEM((count, rows, width), kind),
            pltpu.VMEM((chunks, 2, count // 2, chunk, width), kind),
            pltpu.VMEM((chunks, deep, chunk, width), kind),
            pltpu.VMEM((chunks, deep - 1, chunk, width), kind),
            pltpu.VMEM((rounds,) + small.shape, small.dtype),
            pltpu.VMEM(qkv.shape, kind),
            pltpu.VMEM((examples, size, 384), kind),
            pltpu.VMEM((examples, size, 128), kind),
            pltpu.VMEM((examples, size, 384), kind),
            pltpu.VMEM(tok.shape, kind),
            pltpu.VMEM(tok.shape, kind),
            pltpu.SemaphoreType.DMA((chunks, 12)),
            pltpu.SemaphoreType.DMA((chunks, 12)),
            pltpu.SemaphoreType.DMA((rounds,)),
            pltpu.SemaphoreType.DMA((rounds,)),
            pltpu.SemaphoreType.DMA((len(parts) + 1,)),
            pltpu.SemaphoreType.DMA((2, 2)),
            pltpu.VMEM((count, rows, width), kind),
            pltpu.SemaphoreType.DMA((chunks,)),
        ],
        cost_estimate=cost(0, 60 * count * rows * width),
        compiler_params=pltpu.CompilerParams(
            collective_id=0, has_side_effects=True, vmem_limit_bytes=62 * MIB
        ),
    )(*parts, small, info, qkv, bias, grads, mixed, level, normed, self_in, tok, grad_rest, gain)


def unpack_kernel(pairs, source, key, val, cross_out, self_out, cross_q, *self_in):
    wide = key.shape[0] // 4
    thin = cross_out.shape[0] // 4

    def taken(row, rows):
        block = source[:, row : row + rows, :].astype(jnp.float32)
        return block.reshape(4 * rows, block.shape[2])

    kv = taken(0, wide)
    for i in range(pairs):
        key[:, 128 * i : 128 * i + 128] = kv[:, 256 * i : 256 * i + 128]
        val[:, 128 * i : 128 * i + 128] = kv[:, 256 * i + 128 : 256 * i + 256]
    cross_out[...] = taken(wide, thin)
    self_out[...] = taken(wide + thin, thin)
    cross_q[...] = taken(wide + 2 * thin, thin).T
    rest = taken(wide + 3 * thin, 3 * thin)
    for i in range(3):
        self_in[i][...] = rest[4 * thin * i : 4 * thin * (i + 1)].T


def unpack(value, inner):
    count, rows, width = value.shape
    tall = jax.ShapeDtypeStruct((width, inner), jnp.float32)
    flat = jax.ShapeDtypeStruct((inner, width), jnp.float32)
    by_row = pl.BlockSpec((width // 4, inner), lambda i: (i, 0))
    by_out = pl.BlockSpec((inner // 4, width), lambda i: (i, 0))
    by_column = pl.BlockSpec((width, inner // 4), lambda i: (0, i))
    return pl.pallas_call(
        functools.partial(unpack_kernel, inner // 128),
        grid=(4,),
        in_specs=[pl.BlockSpec((4, rows, width), lambda i: (i, 0, 0))],
        out_specs=[by_row, by_row, by_out, by_out] + [by_column] * 4,
        out_shape=[tall, tall, flat, flat] + [tall] * 4,
        cost_estimate=cost(0, 6 * value.size),
        compiler_params=pltpu.CompilerParams(vmem_limit_bytes=58 * MIB),
    )(value)


def widen_kernel(first, second, out_first, out_second):
    out_first[...] = first[...].astype(jnp.float32)
    out_second[...] = second[...].astype(jnp.float32).T


def widen(value):
    rows, width = value.shape[0] // 2, value.shape[1]
    steps = 4
    block = rows // steps
    return pl.pallas_call(
        widen_kernel,
        grid=(steps,),
        in_specs=[
            pl.BlockSpec((block, width), lambda i: (i, 0)),
            pl.BlockSpec((block, width), lambda i: (steps + i, 0)),
        ],
        out_specs=[
            pl.BlockSpec((block, width), lambda i: (i, 0)),
            pl.BlockSpec((width, block), lambda i: (0, i)),
        ],
        out_shape=[
            jax.ShapeDtypeStruct((rows, width), jnp.float32),
            jax.ShapeDtypeStruct((width, rows), jnp.float32),
        ],
        cost_estimate=cost(0, 12 * rows * width),
        compiler_params=pltpu.CompilerParams(vmem_limit_bytes=58 * MIB),
    )(value, value)


def pieces(value):
    return value.reshape(16, value.shape[0] // 16, value.shape[1])


def low(value):
    return value.astype(jnp.bfloat16)


def on_chip_group(
    tokens,
    memory,
    cotangent,
    target_lengths,
    memory_lengths,
    norm_self,
    query_self,
    key_self,
    value_self,
    out_self,
    bias_table,
    norm_cross,
    query_cross,
    key_cross,
    value_cross,
    out_cross,
    norm_ffn,
    ffn_in,
    ffn_out,
):
    examples = target_lengths.shape[0]
    groups = lax.axis_size("dp")
    net = links(groups)
    index = lax.axis_index("dp")
    place = {
        "y": lax.axis_index("mp"),
        "core": index & 1,
        "x": (index >> 1) & 1,
        "zl": (index >> 2) & 1,
        "zh": (index >> 3) & 1,
    }
    core = place["core"]
    settled = (core == place["y"]).astype(jnp.int32)
    place["settled"] = settled[None]
    rows, width = tokens.shape
    half_pos = rows // examples
    inner = query_self.shape[1]
    pairs = inner // 128

    def swap(value):
        return permute(value, net["core"])

    def both(value):
        return jnp.stack([value, swap(value)])

    def flat(value):
        return value.reshape(-1, value.shape[2])

    def turn(value):
        return permute(value, net["turn"])

    lengths = jnp.concatenate([target_lengths, memory_lengths]).astype(jnp.float32)
    table_rows = bias_table.astype(jnp.float32).reshape(-1, 128)
    facts = jnp.concatenate(
        [jnp.pad(lengths, (0, 128 - lengths.size))[None], table_rows], axis=0
    )
    facts = jnp.pad(facts, ((0, 8 - facts.shape[0]), (0, 0)))
    counts = jnp.broadcast_to(jnp.sum(target_lengths).astype(jnp.float32), (8, 128))
    mem_near = permute(memory, net["give"])
    held = gather(
        tokens,
        memory,
        facts,
        counts,
        [query_self, key_self, value_self, query_cross, key_cross, value_cross, out_self, out_cross],
        groups,
        examples,
    )
    tok, mem_first, facts, counts, self_in, cross_q, cross_kv = held[:7]
    self_out, cross_out = held[7:]
    tok = tok.reshape(rows, width)
    target_len = facts[0, :examples].astype(jnp.int32)
    memory_len = facts[0, examples : 2 * examples].astype(jnp.int32)
    table = facts[1 : 1 + table_rows.shape[0]].reshape(bias_table.shape)
    group_count = jnp.sum(target_len).astype(jnp.float32)
    token_scale = groups * group_count / counts[0, 0]
    self_info = jnp.concatenate([core[None], target_len])
    mem_sent, tok = tie(memory[mem_first.shape[0] :], tok)
    mem_rest = turn(mem_sent)
    first_far = permute(mem_first, net["take"])

    span = 2 * half_pos
    distance = jnp.arange(span, dtype=jnp.int32)
    level = jnp.sum(
        (distance[:, None] >= jnp.asarray(bucket_edges())[None, :]).astype(jnp.int32), axis=-1
    )
    level_hot = (level[:, None] == jnp.arange(BUCKETS, dtype=jnp.int32)[None, :]).astype(
        jnp.float32
    )
    bias = jnp.einsum("db,bh->hd", level_hot, table, precision=highest).reshape(-1, 2, span)

    tok_float = tok.astype(jnp.float32)
    n1 = both(low(rms_norm(tok_float, norm_self.astype(jnp.float32))))
    qkv = low(nn(flat(n1), self_in)).reshape(2, rows, -1)
    cot_after, qkv = tie(cotangent, qkv)
    cot_raw = turn(cot_after)
    a1, mixed_one, level_one = self_forward(self_info, qkv, bias, examples)
    r1 = tok_float + (nn(a1[0], self_out) + swap(low(nn(a1[1], self_out))).astype(jnp.float32))

    n2 = low(rms_norm(r1, norm_cross.astype(jnp.float32)))
    mem_rest, n2 = tie(mem_rest, n2)
    n2 = both(n2)
    q2 = low(nn(flat(n2), cross_q)).reshape(2, rows, -1)
    rest_far = permute(mem_rest, net["take"])
    mem, kv = memory_rows(
        place["y"],
        settled,
        [mem_near, memory, mem_first, first_far, mem_rest, rest_far],
        cross_kv,
        examples,
    )
    mem = mem.reshape(2, -1, width)
    kv = kv.reshape(2, -1, 2 * inner)
    kv, cot_raw = tie(kv, cot_raw)
    cot = reorder(False, cotangent, cot_raw, place["settled"], examples)
    positions = core * half_pos + jnp.arange(half_pos, dtype=jnp.int32)
    live = (positions[None, :] < target_len[:, None]).astype(jnp.float32).reshape(rows, 1)
    dy = cot.astype(jnp.float32) * live * token_scale
    gy = low(dy)
    gy_far = permute(gy, net["y"])

    a2, mixed_two, level_two = cross_forward(memory_len, q2, kv, examples)
    a2, gy_far = tie(a2, gy_far)
    r2 = r1 + (nn(a2[0], cross_out) + swap(low(nn(a2[1], cross_out))).astype(jnp.float32))

    n3 = low(rms_norm(r2, norm_ffn.astype(jnp.float32)))
    n3_far = permute(n3, net["y"])
    out_own, dn_own, h_own, p_own = ffn_rows(n3, gy, ffn_in, ffn_out, jnp.float32)
    out_own, n3_far = tie(out_own, n3_far)
    out_far, dn_far, h_far, p_far = ffn_rows(n3_far, gy_far, ffn_in, ffn_out, jnp.bfloat16)
    dn_far = permute(dn_far, net["y"])
    ffn_part = ffn_weights((n3, n3_far), (gy, gy_far), (h_own, h_far), (p_own, p_far))
    dn_far, ffn_part = tie(dn_far, ffn_part)
    ffn_piece = lax.psum_scatter(ffn_part, "dp", scatter_dimension=0, tiled=True)
    dn3 = dn_own + dn_far.astype(jnp.float32)
    back, gain_three = norm_backward(r2, norm_ffn, dn3)
    dr2 = dy + back

    g2 = both(low(dr2))
    da2 = low(nt(flat(g2), cross_out)).reshape(2, rows, -1)
    da2, out_far = tie(da2, out_far)
    out_far = permute(out_far, net["y"])
    dq2, dkv = cross_backward(memory_len, q2, kv, da2, mixed_two, level_two, examples)
    dkv, out_far = tie(dkv, out_far)
    block_out = low(r2 + (out_own + out_far.astype(jnp.float32)))
    block_back = turn(block_out)
    dkv_swapped = swap(low(nt(pick(dkv, 1 - core), cross_kv)))
    cross_kv_part = low(tn(flat(mem), flat(dkv)))
    dkv_swapped, cross_kv_part = tie(dkv_swapped, cross_kv_part)
    memory_grad = low(nt(pick(dkv, core), cross_kv) + dkv_swapped.astype(jnp.float32))
    memory_grad, cross_kv_part, dq2 = tie(memory_grad, cross_kv_part, dq2)
    memory_back = turn(memory_grad)
    dn2 = nt(dq2[0], cross_q) + swap(low(nt(dq2[1], cross_q))).astype(jnp.float32)
    back, gain_two = norm_backward(r1, norm_cross, dn2)
    dr1 = dr2 + back
    cross_out_part = low(tn(flat(a2), flat(g2)))
    cross_q_part = low(tn(flat(dq2), flat(n2)))

    g1 = both(low(dr1))
    self_out_part = low(tn(flat(a1), flat(g1)))
    da1 = low(nt(flat(g1), self_out)).reshape(2, rows, -1)
    head_parts = [cross_kv_part, cross_out_part, self_out_part, cross_q_part]
    head_parts = [pieces(part) for part in head_parts]
    zero = jnp.zeros((1, width), jnp.float32)
    small = jnp.concatenate([zero, gain_two[None], gain_three[None], jnp.tile(zero, (5, 1))])
    da1, head_parts, small, ffn_piece, block_back = tie(
        da1, head_parts, small, ffn_piece, block_back
    )
    ffn_whole = lax.all_gather(ffn_piece, "dp", axis=0, tiled=True)

    heads_done, small, tokens_grad, tokens_back = settle(
        head_parts,
        small,
        target_len,
        (qkv, bias, da1, mixed_one, level_one),
        (n1, self_in, tok, dr1, norm_self.astype(jnp.float32)[None]),
        groups,
        examples,
    )
    small, ffn_whole, block_back, memory_back = tie(small, ffn_whole, block_back, memory_back)
    gains = small[0, :3] + small[1, :3]
    by_distance = jnp.where(settled == 1, small[0, 4:6], small[1, 4:6]).reshape(-1, span)
    bias_grad = jnp.einsum("hd,db->bh", by_distance, level_hot, precision=highest)
    block_out = reorder(True, block_out, block_back, place["settled"], examples)
    tokens_grad = reorder(True, tokens_grad, tokens_back, place["settled"], examples)
    memory_grad = reorder(True, memory_grad, memory_back, place["settled"], examples)

    ffn_out_grad, ffn_in_grad = widen(ffn_whole)
    (
        key_cross_grad,
        value_cross_grad,
        out_cross_grad,
        out_self_grad,
        query_cross_grad,
        query_self_grad,
        key_self_grad,
        value_self_grad,
    ) = unpack(heads_done, inner)
    return (
        block_out,
        tokens_grad,
        memory_grad,
        gains[0],
        query_self_grad,
        key_self_grad,
        value_self_grad,
        out_self_grad,
        bias_grad,
        gains[1],
        query_cross_grad,
        key_cross_grad,
        value_cross_grad,
        out_cross_grad,
        gains[2],
        ffn_in_grad,
        ffn_out_grad,
    )


def solution(mesh):
    placed = (
        P(("dp", "mp"), None),
        P(("dp", "mp"), None),
        P(("dp", "mp"), None),
        P("dp"),
        P("dp"),
        P(),
        P(None, "mp"),
        P(None, "mp"),
        P(None, "mp"),
        P("mp", None),
        P(None, "mp"),
        P(),
        P(None, "mp"),
        P(None, "mp"),
        P(None, "mp"),
        P("mp", None),
        P(),
        P(None, "mp"),
        P("mp", None),
    )
    near = mesh.shape["mp"] == 2 and mesh.shape["dp"] == 16
    return jax.shard_map(
        on_chip_group if near else on_device,
        mesh=mesh,
        in_specs=placed,
        out_specs=(
            P(("dp", "mp"), None),
            P(("dp", "mp"), None),
            P(("dp", "mp"), None),
            P(),
            P(None, "mp"),
            P(None, "mp"),
            P(None, "mp"),
            P("mp", None),
            P(None, "mp"),
            P(),
            P(None, "mp"),
            P(None, "mp"),
            P(None, "mp"),
            P("mp", None),
            P(),
            P(None, "mp"),
            P("mp", None),
        ),
        check_vma=False,
    )
```

```python
import functools
import math

import jax
import jax.numpy as jnp
import numpy as np
from jax import lax
from jax.experimental import pallas as pl
from jax.experimental.pallas import tpu as pltpu
from jax.sharding import PartitionSpec as P

HEAD_DIM = 64
BUCKETS = 32


epsilon = 1e-06
masked_score = -1e30
highest = lax.Precision.HIGHEST


def bucket_edges():
    exact = list(range(1, 17))
    spaced = [int(math.ceil(16.0 * 8.0 ** ((level - 16) / 16.0))) for level in range(17, 32)]
    return np.array(exact + spaced, dtype=np.int32)


def rms_norm(value, gain):
    factor = lax.rsqrt(jnp.mean(value * value, axis=-1, keepdims=True) + epsilon)
    return value * factor * gain


def gather_rows(value):
    return lax.all_gather(value, "mp", axis=0, tiled=True)


def spread_rows(value):
    return lax.psum_scatter(value, "mp", scatter_dimension=0, tiled=True)


def matmul(left, right):
    return jnp.dot(left, right, preferred_element_type=jnp.float32)


def left_product(left, right):
    return lax.dot_general(
        left, right, (((0,), (0,)), ((), ())), preferred_element_type=jnp.float32
    )


def right_product(left, right):
    return lax.dot_general(
        left, right, (((1,), (1,)), ((), ())), preferred_element_type=jnp.float32
    )


def attend_forward(query, key_rows, value_rows, score_bias, mask):
    scores = jnp.einsum("pehd,kehd->ehpk", query, key_rows, preferred_element_type=jnp.float32)
    if score_bias is not None:
        scores = scores + score_bias[None]
    scores = jnp.where(mask, scores, masked_score)
    row_max = jnp.max(scores, axis=-1, keepdims=True)
    weights = jnp.exp(scores - row_max)
    probs = weights / jnp.sum(weights, axis=-1, keepdims=True)
    probs_low = probs.astype(jnp.bfloat16)
    output = jnp.einsum(
        "ehpk,kehd->pehd", probs_low, value_rows, preferred_element_type=jnp.float32
    )
    return (probs, probs_low, output.astype(jnp.bfloat16))


def attend_backward(query, key_rows, value_rows, probs, probs_low, grad_mixed):
    grad_probs = jnp.einsum(
        "pehd,kehd->ehpk", grad_mixed, value_rows, preferred_element_type=jnp.float32
    )
    inner_sum = jnp.sum(probs * grad_probs, axis=-1, keepdims=True)
    grad_scores = (probs * (grad_probs - inner_sum)).astype(jnp.bfloat16)
    grad_query = jnp.einsum(
        "ehpk,kehd->pehd", grad_scores, key_rows, preferred_element_type=jnp.float32
    )
    grad_keys = jnp.einsum(
        "ehpk,pehd->kehd", grad_scores, query, preferred_element_type=jnp.float32
    )
    grad_values = jnp.einsum(
        "ehpk,pehd->kehd", probs_low, grad_mixed, preferred_element_type=jnp.float32
    )
    return (
        grad_scores,
        grad_query.astype(jnp.bfloat16),
        grad_keys.astype(jnp.bfloat16),
        grad_values.astype(jnp.bfloat16),
    )


def norm_backward(value, gain, grad_normed):
    pullback = jax.vjp(rms_norm, value, gain.astype(jnp.float32))[1]
    return pullback(grad_normed)


def on_device(
    tokens,
    memory,
    cotangent,
    target_lengths,
    memory_lengths,
    norm_self,
    query_self,
    key_self,
    value_self,
    out_self,
    bias_table,
    norm_cross,
    query_cross,
    key_cross,
    value_cross,
    out_cross,
    norm_ffn,
    ffn_in,
    ffn_out,
):
    examples = target_lengths.shape[0]
    local_rows = tokens.shape[0]
    parts = lax.axis_size("mp")
    device_rank = lax.axis_index("mp")
    local_pos = local_rows // examples
    total_pos = local_pos * parts
    memory_local = memory.shape[0]
    memory_total = memory_local * parts
    memory_pos = memory_total // examples
    inner_local = query_self.shape[1]
    heads = inner_local // HEAD_DIM
    total_rows = local_rows * parts
    group_count = jnp.sum(target_lengths).astype(jnp.float32)
    total_count = lax.psum(group_count, "dp")
    token_scale = lax.axis_size("dp") * group_count / total_count
    positions = device_rank * local_pos + jnp.arange(local_pos, dtype=jnp.int32)
    live_rows = (
        (positions[:, None] < target_lengths[None, :]).astype(jnp.float32).reshape(local_rows, 1)
    )
    target_pos = jnp.arange(total_pos, dtype=jnp.int32)
    distance = jnp.maximum(target_pos[:, None] - target_pos[None, :], 0)
    buckets = jnp.sum(
        (distance[:, :, None] >= jnp.asarray(bucket_edges())[None, None, :]).astype(jnp.int32),
        axis=-1,
    )
    table_hot = (buckets[:, :, None] == jnp.arange(BUCKETS, dtype=jnp.int32)[None, None, :]).astype(
        jnp.float32
    )
    causal = target_pos[None, :] <= target_pos[:, None]
    self_mask = causal[None, None] & (
        target_pos[None, None, None, :] < target_lengths[:, None, None, None]
    )
    cross_pos = jnp.arange(memory_pos, dtype=jnp.int32)
    cross_mask = cross_pos[None, None, None, :] < memory_lengths[:, None, None, None]
    score_bias = jnp.einsum(
        "qkb,bh->hqk", table_hot, bias_table.astype(jnp.float32), precision=highest
    )

    def target_view(value):
        return value.reshape(total_pos, examples, heads, HEAD_DIM)

    def memory_view(value):
        return value.reshape(memory_pos, examples, heads, HEAD_DIM)

    tokens_float = tokens.astype(jnp.float32)
    normed_one = rms_norm(tokens_float, norm_self.astype(jnp.float32)).astype(jnp.bfloat16)
    rows_one = gather_rows(normed_one)
    self_weights = jnp.concatenate([query_self, key_self, value_self], axis=1)
    projected = matmul(rows_one, self_weights).astype(jnp.bfloat16)
    query_one = target_view(projected[:, :inner_local])
    keys_one = target_view(projected[:, inner_local : 2 * inner_local])
    values_one = target_view(projected[:, 2 * inner_local :])
    probs_one, low_one, mixed_one = attend_forward(
        query_one, keys_one, values_one, score_bias, self_mask
    )
    mixed_rows_one = mixed_one.reshape(total_rows, inner_local)
    resid_one = tokens_float + spread_rows(matmul(mixed_rows_one, out_self))
    normed_two = rms_norm(resid_one, norm_cross.astype(jnp.float32)).astype(jnp.bfloat16)
    rows_two = gather_rows(normed_two)
    query_two = target_view(matmul(rows_two, query_cross).astype(jnp.bfloat16))
    memory_all = lax.all_gather(memory, "mp", axis=0, tiled=True)
    cross_kv = matmul(memory_all, jnp.concatenate([key_cross, value_cross], axis=1)).astype(
        jnp.bfloat16
    )
    keys_flat = cross_kv[:, :inner_local]
    values_flat = cross_kv[:, inner_local:]
    keys_two = memory_view(keys_flat)
    values_two = memory_view(values_flat)
    probs_two, low_two, mixed_two = attend_forward(
        query_two, keys_two, values_two, None, cross_mask
    )
    mixed_rows_two = mixed_two.reshape(total_rows, inner_local)
    resid_two = resid_one + spread_rows(matmul(mixed_rows_two, out_cross))
    normed_three = rms_norm(resid_two, norm_ffn.astype(jnp.float32)).astype(jnp.bfloat16)
    rows_three = gather_rows(normed_three)
    pre_act = matmul(rows_three, ffn_in)
    hidden = jax.nn.gelu(pre_act).astype(jnp.bfloat16)
    block_out = resid_two + spread_rows(matmul(hidden, ffn_out))
    grad_out = cotangent.astype(jnp.float32) * live_rows * token_scale
    grad_rows_three = gather_rows(grad_out.astype(jnp.bfloat16))
    ffn_out_grad = left_product(hidden, grad_rows_three)
    grad_hidden = right_product(grad_rows_three, ffn_out)
    gelu_back = jax.vjp(jax.nn.gelu, pre_act)[1]
    grad_pre = gelu_back(grad_hidden)[0].astype(jnp.bfloat16)
    ffn_in_grad = left_product(rows_three, grad_pre)
    grad_normed_three = spread_rows(right_product(grad_pre, ffn_in))
    grad_resid_three, gain_three = norm_backward(resid_two, norm_ffn, grad_normed_three)
    grad_two = grad_out + grad_resid_three
    grad_rows_two = gather_rows(grad_two.astype(jnp.bfloat16))
    out_cross_grad = left_product(mixed_rows_two, grad_rows_two)
    grad_mixed_two = target_view(right_product(grad_rows_two, out_cross).astype(jnp.bfloat16))
    cross_back = attend_backward(
        query_two, keys_two, values_two, probs_two, low_two, grad_mixed_two
    )
    grad_query_two = cross_back[1].reshape(total_rows, inner_local)
    grad_keys_two = cross_back[2].reshape(memory_total, inner_local)
    grad_values_two = cross_back[3].reshape(memory_total, inner_local)
    query_cross_grad = left_product(rows_two, grad_query_two)
    grad_normed_two = spread_rows(right_product(grad_query_two, query_cross))
    key_cross_grad = left_product(memory_all, grad_keys_two)
    value_cross_grad = left_product(memory_all, grad_values_two)
    memory_terms = right_product(grad_keys_two, key_cross) + right_product(
        grad_values_two, value_cross
    )
    memory_grad = lax.psum_scatter(memory_terms, "mp", scatter_dimension=0, tiled=True)
    grad_resid_two, gain_two = norm_backward(resid_one, norm_cross, grad_normed_two)
    grad_one = grad_two + grad_resid_two
    grad_rows_one = gather_rows(grad_one.astype(jnp.bfloat16))
    out_self_grad = left_product(mixed_rows_one, grad_rows_one)
    grad_mixed_one = target_view(right_product(grad_rows_one, out_self).astype(jnp.bfloat16))
    self_back = attend_backward(query_one, keys_one, values_one, probs_one, low_one, grad_mixed_one)
    bias_table_grad = jnp.einsum(
        "ehqk,qkb->bh", self_back[0].astype(jnp.float32), table_hot, precision=highest
    )
    grad_projected = jnp.concatenate(
        [
            self_back[1].reshape(total_rows, inner_local),
            self_back[2].reshape(total_rows, inner_local),
            self_back[3].reshape(total_rows, inner_local),
        ],
        axis=1,
    )
    self_weight_grad = left_product(rows_one, grad_projected)
    grad_normed_one = spread_rows(right_product(grad_projected, self_weights))
    grad_resid_one, gain_one = norm_backward(tokens_float, norm_self, grad_normed_one)
    tokens_grad = grad_one + grad_resid_one
    summed = lax.psum(
        (
            self_weight_grad[:, :inner_local],
            self_weight_grad[:, inner_local : 2 * inner_local],
            self_weight_grad[:, 2 * inner_local :],
            out_self_grad,
            bias_table_grad,
            query_cross_grad,
            key_cross_grad,
            value_cross_grad,
            out_cross_grad,
            ffn_in_grad,
            ffn_out_grad,
        ),
        "dp",
    )
    gains = lax.psum((gain_one, gain_two, gain_three), ("dp", "mp"))
    return (
        block_out.astype(jnp.bfloat16),
        tokens_grad.astype(jnp.bfloat16),
        memory_grad.astype(jnp.bfloat16),
        gains[0],
        summed[0],
        summed[1],
        summed[2],
        summed[3],
        summed[4],
        gains[1],
        summed[5],
        summed[6],
        summed[7],
        summed[8],
        gains[2],
        summed[9],
        summed[10],
    )


def links(dp_size):
    total = 2 * dp_size

    def swap(bit):
        return [(at, at ^ bit) for at in range(total)]

    def turned(at):
        return (at & ~3) | ((at & 1) << 1) | ((at >> 1) & 1)

    return {
        "turn": [(at, turned(at)) for at in range(total) if at != turned(at)],
        "give": [(at, at ^ 2) for at in range(total) if (at & 1) == ((at >> 1) & 1)],
        "take": [(at, at ^ 2) for at in range(total) if (at & 1) != ((at >> 1) & 1)],
        "y": swap(1),
        "core": swap(2),
        "x": swap(4),
        "zl": swap(8),
        "zh": swap(16),
    }


def permute(value, pairs):
    return lax.ppermute(value, ("dp", "mp"), pairs)


def reorder_kernel(inverse, examples, info, held, *refs):
    arrived, target = refs[:-1], refs[-1]
    block = 256
    chunk = block // examples

    def write(*sources):
        source = sources[0]
        high = lax.broadcasted_iota(jnp.int32, (block, block), 0)
        low = lax.broadcasted_iota(jnp.int32, (block, block), 1)
        if inverse:
            hot = low == (high % examples) * chunk + high // examples
            for i in range(target.shape[0] // block):
                held_rows = slice(chunk * i, chunk * (i + 1))
                value = jnp.concatenate([part[:, held_rows, :] for part in sources], axis=0)
                value = value.reshape(block, -1)
                moved = nn(hot.astype(jnp.bfloat16), value).astype(jnp.bfloat16)
                target[block * i : block * (i + 1), :] = moved
        else:
            hot = low == (high % chunk) * examples + high // chunk
            for i in range(source.shape[0] // block):
                value = source[block * i : block * (i + 1), :]
                moved = nn(hot.astype(jnp.bfloat16), value).astype(jnp.bfloat16)
                target[:, chunk * i : chunk * (i + 1), :] = moved.reshape(examples, chunk, -1)

    @pl.when(info[0] == 1)
    def _():
        write(held)

    @pl.when(info[0] == 0)
    def _():
        write(*arrived)


def reorder(inverse, held, arrived, settled, examples):
    rows, width = held.shape
    block = min(rows, 512)
    flat = pl.BlockSpec((block, width), lambda i, s: (i, 0))
    flat_shape = (rows, width)
    split_shape = (examples, rows // examples, width)
    split_block = (examples, block // examples, width)
    arrived = arrived if isinstance(arrived, tuple) else (arrived,)
    if inverse:
        held = held.reshape(split_shape)
        share = examples // len(arrived)
        arrived = [part.reshape((share,) + split_shape[1:]) for part in arrived]
        in_specs = [pl.BlockSpec(split_block, lambda i, s: (0, i * s[0], 0))] + [
            pl.BlockSpec((share,) + split_block[1:], lambda i, s: (0, i * (1 - s[0]), 0))
        ] * len(arrived)
        out_spec, out_shape = flat, flat_shape
    else:
        in_specs = [
            pl.BlockSpec((block, width), lambda i, s: (i * s[0], 0)),
            pl.BlockSpec((block, width), lambda i, s: (i * (1 - s[0]), 0)),
        ]
        out_spec = pl.BlockSpec(split_block, lambda i, s: (0, i, 0))
        out_shape = split_shape
    return pl.pallas_call(
        functools.partial(reorder_kernel, inverse, examples),
        grid_spec=pltpu.PrefetchScalarGridSpec(
            num_scalar_prefetch=1,
            grid=(rows // block,),
            in_specs=in_specs,
            out_specs=out_spec,
        ),
        out_shape=jax.ShapeDtypeStruct(out_shape, held.dtype),
        cost_estimate=cost(2 * rows * width * block, 4 * rows * width),
        compiler_params=pltpu.CompilerParams(vmem_limit_bytes=SMALL_VMEM),
    )(settled, held, *arrived).reshape(flat_shape)


def memory_kernel(examples, info, *refs):
    sources, weight, rows_out, kv_out = refs[:6], refs[6], refs[7], refs[8]
    block = 256
    chunk = block // examples
    high = lax.broadcasted_iota(jnp.int32, (block, block), 0)
    low = lax.broadcasted_iota(jnp.int32, (block, block), 1)
    hot = (low == (high % chunk) * examples + high // chunk).astype(jnp.bfloat16)

    def write(source):
        parts = []
        for start in range(0, source.shape[0], block):
            moved = nn(hot, source[start : start + block, :]).astype(jnp.bfloat16)
            parts.append(moved.reshape(examples, chunk, moved.shape[1]))
        moved = jnp.concatenate(parts, axis=1)
        rows_out[...] = moved.reshape(rows_out.shape)
        moved = nn(moved.reshape(source.shape), weight[...]).astype(jnp.bfloat16)
        kv_out[...] = moved.reshape(kv_out.shape)

    late = pl.program_id(1) >= 1
    kind = jnp.where(pl.program_id(0) == 0, 0, jnp.where(late, 4, 2)) + info[1]
    for i in range(6):
        pl.when(kind == i)(functools.partial(write, sources[i]))


def memory_rows(y_half, settled, sources, weight, examples):
    rows, width = sources[0].shape
    block = 512
    blocks = rows // block
    shape = (2, examples, rows // examples, width)
    kv_shape = shape[:3] + (weight.shape[1],)

    def source(which):
        half, part = (0, 0) if which < 2 else (1, which // 2 - 1)
        start = part
        last = (blocks if half == 0 else 1 if part == 0 else blocks - 1) - 1

        def index(p, i, s):
            held = jnp.clip(i - start, 0, last)
            return (jnp.where((p == half) & (s[1] == which % 2), held, 0), 0)

        return pl.BlockSpec((block, width), index)

    def out(columns):
        return pl.BlockSpec(
            (1, examples, block // examples, columns),
            lambda p, i, s: ((p + s[0]) & 1, 0, i, 0),
        )

    return pl.pallas_call(
        functools.partial(memory_kernel, examples),
        grid_spec=pltpu.PrefetchScalarGridSpec(
            num_scalar_prefetch=1,
            grid=(2, blocks),
            in_specs=[source(i) for i in range(6)]
            + [pl.BlockSpec(weight.shape, lambda p, i, s: (0, 0))],
            out_specs=[out(width), out(weight.shape[1])],
        ),
        out_shape=[
            jax.ShapeDtypeStruct(shape, weight.dtype),
            jax.ShapeDtypeStruct(kv_shape, weight.dtype),
        ],
        cost_estimate=cost(4 * rows * width * (weight.shape[1] + 256), 12 * rows * width),
        compiler_params=pltpu.CompilerParams(vmem_limit_bytes=ATTEND_VMEM),
    )(jnp.stack([y_half, settled]), *sources, weight)


def nt(left, right):
    return lax.dot_general(
        left, right, (((1,), (1,)), ((), ())), preferred_element_type=jnp.float32
    )


def tn(left, right):
    return lax.dot_general(
        left, right, (((0,), (0,)), ((), ())), preferred_element_type=jnp.float32
    )


def nn(left, right):
    return jnp.dot(left, right, preferred_element_type=jnp.float32)


def one_head(value, head):
    lane = lax.broadcasted_iota(jnp.int32, value.shape, 1)
    return jnp.where(lane // HEAD_DIM == head, value, jnp.zeros_like(value))


def toeplitz(row, size):
    return pltpu.roll(jnp.broadcast_to(row, (size, size)), 0, 1, stride=1, stride_axis=0)


def diagonals(square):
    size = square.shape[0]
    row = lax.broadcasted_iota(jnp.int32, square.shape, 0)
    turned, step = square, 1
    while step < size:
        moved = pltpu.roll(turned, size - step, 1)
        turned = jnp.where((row & step) != 0, moved, turned)
        step *= 2
    return jnp.sum(turned, axis=0, keepdims=True)


def heads_joined(first, second):
    return jnp.concatenate([first, second], axis=0).T


def head_rows(value, head):
    return value[HEAD_DIM * head : HEAD_DIM * (head + 1)]


def self_heads(core, rows, scratch, example):
    half = scratch.shape[1] // 2
    at = pl.ds(example * half, half)
    scratch[example, pl.ds(pl.multiple_of(core * half, half), half), :] = rows[0, at, :]
    scratch[example, pl.ds(pl.multiple_of((1 - core) * half, half), half), :] = rows[1, at, :]
    return scratch[example]


def self_store(core, value, scratch, out, example):
    half = scratch.shape[1] // 2
    at = pl.ds(example * half, half)
    scratch[example] = value
    out[0, at, :] = scratch[example, pl.ds(pl.multiple_of(core * half, half), half), :]
    out[1, at, :] = scratch[example, pl.ds(pl.multiple_of((1 - core) * half, half), half), :]


def self_masks(size, length):
    key_at = lax.broadcasted_iota(jnp.int32, (size, size), 0)
    query_at = lax.broadcasted_iota(jnp.int32, (size, size), 1)
    return jnp.where((key_at <= query_at) & (key_at < length), 0.0, masked_score)


def side_by_side(value):
    return jnp.concatenate([one_head(value, head) for head in range(2)], axis=0)


def own_blocks(value, size):
    return value[:HEAD_DIM, :size], value[HEAD_DIM:, size:]


def self_forward_kernel(examples, info, rows, bias, out, mixed, level, scratch, out_scratch):
    core = info[0]
    size = scratch.shape[1]
    slopes = jnp.concatenate(
        [toeplitz(bias[0, head : head + 1, :], size) for head in range(2)], axis=1
    )
    for example in range(examples):
        joined = self_heads(core, rows, scratch, example)
        query, keys = joined[:, :128], joined[:, 128:256]
        mask = self_masks(size, info[1 + example])
        scores = nt(keys, side_by_side(query)) + slopes + jnp.concatenate([mask, mask], axis=1)
        top = jnp.max(scores, axis=0, keepdims=True)
        weights = jnp.exp(scores - top)
        total = jnp.sum(weights, axis=0, keepdims=True)
        probs = (weights * (1.0 / total)).astype(jnp.bfloat16)
        sums = nn(joined[:, 256:].T, probs)
        parts = own_blocks(sums, size)
        levels = top + jnp.log(total)
        for head in range(2):
            level[0, example, head : head + 1, :] = levels[:, size * head : size * (head + 1)]
            mixed[0, example, HEAD_DIM * head : HEAD_DIM * (head + 1), :] = parts[head]
        result = heads_joined(*parts).astype(jnp.bfloat16)
        self_store(core, result, out_scratch, out, example)


def by_length(length, span, body):
    quarter = span // 4
    for part in range(1, 5):
        keys = part * quarter
        inside = length > keys - quarter
        if part < 4:
            inside = inside & (length <= keys)

        @pl.when(inside)
        def _():
            body(keys)


def masked_tail(scores, length, quarter):
    keys, count = scores.shape
    key_at = keys - quarter + lax.broadcasted_iota(jnp.int32, (quarter, count), 0)
    tail = scores[keys - quarter :] + jnp.where(key_at < length, 0.0, masked_score)
    if keys == quarter:
        return tail
    return jnp.concatenate([scores[: keys - quarter], tail], axis=0)


def cross_forward_kernel(info, queries, kv, out, mixed, level):
    length = info[pl.program_id(0)]
    count = 2 * queries.shape[1]
    span = 2 * kv.shape[1]

    def body(keys):
        for pair in range(queries.shape[2] // 128):
            columns = slice(128 * pair, 128 * (pair + 1))
            heads = side_by_side(queries[:, :, columns].reshape(-1, 128))
            joined = kv[:, :, 256 * pair : 256 * (pair + 1)].reshape(span, 256)[:keys]
            scores = masked_tail(nt(joined[:, :128], heads), length, span // 4)
            top = jnp.max(scores, axis=0, keepdims=True)
            weights = jnp.exp(scores - top)
            total = jnp.sum(weights, axis=0, keepdims=True)
            probs = (weights * (1.0 / total)).astype(jnp.bfloat16)
            parts = own_blocks(nn(joined[:, 128:].T, probs), count)
            levels = top + jnp.log(total)
            for head in range(2):
                mixed[0, pair, HEAD_DIM * head : HEAD_DIM * (head + 1), :] = parts[head]
                level[0, pair, head : head + 1, :] = levels[:, count * head : count * (head + 1)]
            out[:, :, columns] = (
                heads_joined(*parts).astype(jnp.bfloat16).reshape(2, count // 2, 128)
            )

    by_length(length, span, body)


def cross_backward_kernel(info, queries, kv, grads, mixed, level, dq, dkv):
    length = info[pl.program_id(0)]
    count = 2 * queries.shape[1]
    span = 2 * kv.shape[1]

    def body(keys):
        for pair in range(queries.shape[2] // 128):
            columns = slice(128 * pair, 128 * (pair + 1))
            wide = slice(256 * pair, 256 * (pair + 1))
            grad = grads[:, :, columns].reshape(-1, 128)
            heads = side_by_side(queries[:, :, columns].reshape(-1, 128))
            grad_heads = side_by_side(grad)
            products = grad.astype(jnp.float32).T * mixed[0, pair]
            inner = jnp.concatenate(
                [jnp.sum(head_rows(products, head), axis=0, keepdims=True) for head in range(2)],
                axis=1,
            )
            levels = jnp.concatenate([level[0, pair, 0:1, :], level[0, pair, 1:2, :]], axis=1)
            joined = kv[:, :, wide].reshape(span, 256)[:keys]
            scores = masked_tail(nt(joined[:, :128], heads), length, span // 4)
            probs = jnp.exp(scores - levels)
            grad_scores = (probs * (nt(joined[:, 128:], grad_heads) - inner)).astype(
                jnp.bfloat16
            )
            result = jnp.concatenate(
                [nn(grad_scores, heads), nn(probs.astype(jnp.bfloat16), grad_heads)], axis=1
            ).astype(jnp.bfloat16)
            if keys < span:
                result = jnp.concatenate(
                    [result, jnp.zeros((span - keys, 256), jnp.bfloat16)], axis=0
                )
            dkv[:, :, wide] = result.reshape(2, span // 2, 256)
            sums = nn(joined[:, :128].T, grad_scores)
            dq[:, :, columns] = (
                heads_joined(*own_blocks(sums, count))
                .astype(jnp.bfloat16)
                .reshape(2, count // 2, 128)
            )

    by_length(length, span, body)


MIB = 1024 * 1024


def cost(flops, moved, exps=0):
    return pl.CostEstimate(
        flops=int(flops), bytes_accessed=int(moved), transcendentals=int(exps)
    )


SMALL_VMEM = 12 * MIB
ATTEND_VMEM = 24 * MIB
FFN_VMEM = 44 * MIB
SETTLE_VMEM = 48 * MIB
MESH = pl.DeviceIdType.MESH
SMEM_SPEC = pl.BlockSpec(memory_space=pltpu.SMEM)


def self_forward(info, rows, bias, examples):
    _, count, width = rows.shape
    pairs, size = width // 384, count // examples
    return pl.pallas_call(
        functools.partial(self_forward_kernel, examples),
        grid=(pairs,),
        in_specs=[
            SMEM_SPEC,
            pl.BlockSpec((2, count, 384), lambda h: (0, 0, h)),
            pl.BlockSpec((1, 2, 2 * size), lambda h: (h, 0, 0)),
        ],
        out_specs=[
            pl.BlockSpec((2, count, 128), lambda h: (0, 0, h)),
            pl.BlockSpec((1, examples, 128, 2 * size), lambda h: (h, 0, 0, 0)),
            pl.BlockSpec((1, examples, 2, 2 * size), lambda h: (h, 0, 0, 0)),
        ],
        out_shape=[
            jax.ShapeDtypeStruct((2, count, pairs * 128), jnp.bfloat16),
            jax.ShapeDtypeStruct((pairs, examples, 128, 2 * size), jnp.float32),
            jax.ShapeDtypeStruct((pairs, examples, 2, 2 * size), jnp.float32),
        ],
        scratch_shapes=[
            pltpu.VMEM((examples, 2 * size, 384), jnp.bfloat16),
            pltpu.VMEM((examples, 2 * size, 128), jnp.bfloat16),
        ],
        cost_estimate=cost(
            2 * 2 * examples * 2 * pairs * (2 * size) ** 2 * 256 * 2,
            8 * rows.size,
            examples * 2 * pairs * (2 * size) ** 2,
        ),
        compiler_params=pltpu.CompilerParams(vmem_limit_bytes=ATTEND_VMEM),
    )(info, rows, bias)


def cross_forward(info, queries, kv, examples):
    _, count, width = queries.shape
    pairs, size, span = width // 128, count // examples, kv.shape[1] // examples
    thin = pl.BlockSpec((2, size, 256), lambda e, h: (0, e, h))
    wide = pl.BlockSpec((2, span, 512), lambda e, h: (0, e, h))
    return pl.pallas_call(
        cross_forward_kernel,
        grid=(examples, pairs // 2),
        in_specs=[SMEM_SPEC, thin, wide],
        out_specs=[
            thin,
            pl.BlockSpec((1, 2, 128, 2 * size), lambda e, h: (e, h, 0, 0)),
            pl.BlockSpec((1, 2, 2, 2 * size), lambda e, h: (e, h, 0, 0)),
        ],
        out_shape=[
            jax.ShapeDtypeStruct(queries.shape, jnp.bfloat16),
            jax.ShapeDtypeStruct((examples, pairs, 128, 2 * size), jnp.float32),
            jax.ShapeDtypeStruct((examples, pairs, 2, 2 * size), jnp.float32),
        ],
        cost_estimate=cost(
            2 * 2 * examples * 2 * pairs * 4 * size * span * 256,
            4 * kv.size,
            examples * 2 * pairs * 4 * size * span,
        ),
        compiler_params=pltpu.CompilerParams(vmem_limit_bytes=32 * MIB),
    )(info, queries, kv)


def cross_backward(info, queries, kv, grads, mixed, level, examples):
    _, count, width = queries.shape
    pairs, size, span = width // 128, count // examples, kv.shape[1] // examples
    thin = pl.BlockSpec((2, size, 256), lambda e, h: (0, e, h))
    wide = pl.BlockSpec((2, span, 512), lambda e, h: (0, e, h))
    return pl.pallas_call(
        cross_backward_kernel,
        grid=(examples, pairs // 2),
        in_specs=[
            SMEM_SPEC,
            thin,
            wide,
            thin,
            pl.BlockSpec((1, 2, 128, 2 * size), lambda e, h: (e, h, 0, 0)),
            pl.BlockSpec((1, 2, 2, 2 * size), lambda e, h: (e, h, 0, 0)),
        ],
        out_specs=[thin, wide],
        out_shape=[
            jax.ShapeDtypeStruct(queries.shape, jnp.bfloat16),
            jax.ShapeDtypeStruct(kv.shape, jnp.bfloat16),
        ],
        cost_estimate=cost(
            5 * 2 * examples * 2 * pairs * 4 * size * span * 256,
            6 * kv.size,
            examples * 2 * pairs * 4 * size * span,
        ),
        compiler_params=pltpu.CompilerParams(vmem_limit_bytes=58 * MIB),
    )(info, queries, kv, grads, mixed, level)


root = math.sqrt(2.0 / math.pi)
cubic = 0.044715


def ffn_rows_kernel(normed, grad, into, outof, out, back, hidden_out, pre_out, out_sum, back_sum):
    step = pl.program_id(0)

    @pl.when(step == 0)
    def _():
        out_sum[...] = jnp.zeros_like(out_sum)
        back_sum[...] = jnp.zeros_like(back_sum)

    pre = nn(normed[...], into[...])
    grad_hidden = nt(grad[...], outof[...])
    bend = jnp.tanh(root * (pre + cubic * (pre * pre * pre)))
    hidden = (0.5 * pre * (1.0 + bend)).astype(jnp.bfloat16)
    slope = 0.5 * (1.0 + bend) + 0.5 * pre * (1.0 - bend * bend) * (
        root * (1.0 + 3.0 * cubic * (pre * pre))
    )
    grad_pre = (grad_hidden * slope).astype(jnp.bfloat16)
    hidden_out[...] = hidden
    pre_out[...] = grad_pre
    out_sum[...] += nn(hidden, outof[...])
    back_sum[...] += nt(grad_pre, into[...])

    @pl.when(step == pl.num_programs(0) - 1)
    def _():
        out[...] = out_sum[...].astype(out.dtype)
        back[...] = back_sum[...].astype(back.dtype)


def ffn_rows(normed, grad, into, outof, kind):
    rows, width = normed.shape
    units = into.shape[1]
    tile = 512
    whole = pl.BlockSpec((rows, width), lambda i: (0, 0))
    tall = pl.BlockSpec((width, tile), lambda i: (0, i))
    flat = pl.BlockSpec((tile, width), lambda i: (i, 0))
    thin = pl.BlockSpec((rows, tile), lambda i: (0, i))
    return pl.pallas_call(
        ffn_rows_kernel,
        grid=(units // tile,),
        in_specs=[whole, whole, tall, flat],
        out_specs=[whole, whole, thin, thin],
        out_shape=[jax.ShapeDtypeStruct((rows, width), kind)] * 2
        + [jax.ShapeDtypeStruct((rows, units), jnp.bfloat16)] * 2,
        scratch_shapes=[pltpu.VMEM((rows, width), jnp.float32)] * 2,
        cost_estimate=cost(
            4 * 2 * rows * width * units, 12 * rows * width + 4 * width * units, rows * units
        ),
        compiler_params=pltpu.CompilerParams(vmem_limit_bytes=ATTEND_VMEM),
    )(normed, grad, into, outof)


def ffn_weights_kernel(n_own, n_far, g_own, g_far, h_own, h_far, p_own, p_far, out):
    step = pl.program_id(0)
    half = pl.num_programs(0) // 2

    @pl.when(step < half)
    def _():
        out[...] = (tn(h_own[...], g_own[...]) + tn(h_far[...], g_far[...])).astype(out.dtype)

    @pl.when(step >= half)
    def _():
        out[...] = (tn(p_own[...], n_own[...]) + tn(p_far[...], n_far[...])).astype(out.dtype)


def ffn_weights(normed, grads, hiddens, pres):
    rows, width = normed[0].shape
    units = hiddens[0].shape[1]
    tile = 512
    steps = units // tile
    whole = pl.BlockSpec((rows, width), lambda i: (0, 0))
    first = pl.BlockSpec((rows, tile), lambda i: (0, jnp.minimum(i, steps - 1)))
    second = pl.BlockSpec((rows, tile), lambda i: (0, jnp.maximum(i - steps, 0)))
    return pl.pallas_call(
        ffn_weights_kernel,
        grid=(2 * steps,),
        in_specs=[whole] * 4 + [first] * 2 + [second] * 2,
        out_specs=pl.BlockSpec((tile, width), lambda i: (i, 0)),
        out_shape=jax.ShapeDtypeStruct((2 * units, width), jnp.bfloat16),
        cost_estimate=cost(
            4 * 2 * rows * width * units, 8 * rows * width + 4 * width * units
        ),
        compiler_params=pltpu.CompilerParams(vmem_limit_bytes=30 * MIB),
    )(*normed, *grads, *hiddens, *pres)


def gather_kernel(groups, examples, tokens, memory, facts, counts, *refs):
    weights, refs = refs[:8], refs[8:]
    tok_out, mem_out, facts_out, counts_out, self_in, cross_q, cross_kv = refs[:7]
    self_out, cross_out = refs[7:9]
    raw, landed, round_in, near_send, near_get, send, get = refs[9:]
    index, y = lax.axis_index("dp"), lax.axis_index("mp")
    core, x, z = index % 2, (index // 2) % 2, index // 4
    deep = groups // 4

    def at(c, yy, xx, zz):
        return (zz * 4 + xx * 2 + c, yy)

    z_near = z + 1 - 2 * (z % 2)
    x_side, z_side = at(core, y, 1 - x, z), at(core, y, x, z_near)
    turned = at(1 - core, 1 - y, x, z)
    rounds = [at(1 - core, y, x, z), x_side, z_side]
    step = 2
    while step < deep:
        rounds.append(at(core, y, x, z + step - 2 * step * ((z // step) % 2)))
        step *= 2
    barrier = pltpu.get_barrier_semaphore()
    for partner in rounds:
        pl.semaphore_signal(barrier, inc=1, device_id=partner, device_id_type=MESH)

    @pl.when(core != y)
    def _():
        pl.semaphore_signal(barrier, inc=1, device_id=turned, device_id_type=MESH)
        pl.semaphore_wait(barrier, len(rounds) + 1)

    @pl.when(core == y)
    def _():
        pl.semaphore_wait(barrier, len(rounds))

    homes = [raw.at[0], raw.at[1], raw.at[2], cross_q, raw.at[3], raw.at[4], self_out, cross_out]

    def remote(source, target, sems, slot, device):
        return pltpu.make_async_remote_copy(
            src_ref=source,
            dst_ref=target,
            send_sem=sems[0].at[slot],
            recv_sem=sems[1].at[slot],
            device_id=device,
            device_id_type=MESH,
        )

    mine = x * 2 + z % 2

    def quarter(w, which, first=0, parts=1):
        rows = homes[w].shape[0] // 4
        size = rows // parts
        return homes[w].at[pl.ds(pl.multiple_of(which * rows + first * size, size), size)]

    def along_y(w):
        rows = homes[w].shape[0] // 4
        sent = mine * rows
        return remote(
            weights[w].at[pl.ds(pl.multiple_of(sent, rows), rows)],
            quarter(w, mine),
            (send, get),
            w,
            turned,
        )

    def direct(w, which):
        piece = quarter(w, mine)
        return remote(piece, piece, (send, get), 8 + 2 * w + which, (x_side, z_side)[which])

    def passed(w, which):
        other = mine + (2 - 4 * x if which == 0 else 1 - 2 * (z % 2))
        piece = quarter(w, other, which, 2)
        return remote(piece, piece, (send, get), 24 + 2 * w + which, (z_side, x_side)[which])

    token_copy = remote(tokens, landed, (send, get), 40, turned)
    facts_copy = remote(facts, facts_out, (send, get), 41, turned)
    early = memory.at[pl.ds(0, mem_out.shape[0])]
    memory_copy = remote(early, mem_out, (send, get), 42 + len(rounds), turned)

    @pl.when(core != y)
    def _():
        facts_copy.start()
        for w in range(8):
            along_y(w).start()
        token_copy.start()
        memory_copy.start()

    @pl.when(core == y)
    def _():
        pltpu.make_async_copy(tokens, landed, near_get.at[0]).start()
        pltpu.make_async_copy(facts, facts_out, near_get.at[1]).start()
        for w in range(8):
            pltpu.make_async_copy(weights[w], homes[w], near_get.at[2 + w]).start()

    def count_copy(i):
        return remote(counts_out, round_in.at[i], (near_send, get), 42 + i, rounds[i])

    def count_round(w):
        if w % 2 == 1 and w // 2 < len(rounds):
            count_copy(w // 2).start()
        if w % 2 == 0 and 0 < w <= 2 * len(rounds):
            count_copy(w // 2 - 1).wait()
            counts_out[...] += round_in[w // 2 - 1]

    counts_out[...] = counts[...]
    @pl.when(core == y)
    def _():
        pltpu.make_async_copy(tokens, landed, near_get.at[0]).wait()
        pltpu.make_async_copy(facts, facts_out, near_get.at[1]).wait()
        for w in range(8):
            pltpu.make_async_copy(weights[w], homes[w], near_get.at[2 + w]).wait()

    def share(w):
        if w < 8:
            along_y(w).wait()
            for which in range(2):
                direct(w, which).start()
        if w > 0:
            for which in range(2):
                direct(w - 1, which).wait()
            for which in range(2):
                passed(w - 1, which).start()

    for w in range(9):
        pl.when(core != y)(functools.partial(share, w))
        count_round(w)

    @pl.when(core != y)
    def _():
        facts_copy.wait()
        token_copy.wait()

    rows = landed.shape[0]
    block = 256
    chunk = block // examples
    high = lax.broadcasted_iota(jnp.int32, (block, block), 0)
    low = lax.broadcasted_iota(jnp.int32, (block, block), 1)
    hot = (low == (high % chunk) * examples + high // chunk).astype(jnp.bfloat16)
    for i in range(rows // block):
        moved = nn(hot, landed[pl.ds(i * block, block), :]).astype(jnp.bfloat16)
        tok_out[:, pl.ds(i * chunk, chunk), :] = moved.reshape(examples, chunk, moved.shape[1])

    @pl.when(core != y)
    def _():
        for w in range(8):
            for which in range(2):
                passed(w, which).wait()
        memory_copy.wait()

    for h in range(raw.shape[2] // 128):
        for i in range(3):
            self_in[:, 384 * h + 128 * i : 384 * h + 128 * i + 128] = raw[
                i, :, 128 * h : 128 * h + 128
            ]
        for i in range(2):
            cross_kv[:, 256 * h + 128 * i : 256 * h + 128 * i + 128] = raw[
                3 + i, :, 128 * h : 128 * h + 128
            ]


def gather(tokens, memory, facts, counts, weights, groups, examples):
    rows, width = tokens.shape
    inner = weights[0].shape[1]
    rounds = 2 + (groups // 4).bit_length() - 1
    anywhere = pl.BlockSpec(memory_space=pl.ANY)
    whole = pl.BlockSpec(memory_space=pltpu.VMEM)

    def half(*shape):
        return jax.ShapeDtypeStruct(shape, jnp.bfloat16)

    return pl.pallas_call(
        functools.partial(gather_kernel, groups, examples),
        in_specs=[anywhere, anywhere, whole, whole] + [anywhere] * 8,
        out_specs=[whole] * 9,
        out_shape=[
            half(examples, rows // examples, width),
            half(memory.shape[0] // 4, width),
            jax.ShapeDtypeStruct(facts.shape, facts.dtype),
            jax.ShapeDtypeStruct(counts.shape, counts.dtype),
            half(width, 3 * inner),
            half(width, inner),
            half(width, 2 * inner),
            half(inner, width),
            half(inner, width),
        ],
        scratch_shapes=[
            pltpu.VMEM((5, width, inner), jnp.bfloat16),
            pltpu.VMEM((rows, width), jnp.bfloat16),
            pltpu.VMEM((rounds,) + counts.shape, counts.dtype),
            pltpu.SemaphoreType.DMA((42 + rounds,)),
            pltpu.SemaphoreType.DMA((10,)),
            pltpu.SemaphoreType.DMA((43 + rounds,)),
            pltpu.SemaphoreType.DMA((43 + rounds,)),
        ],
        cost_estimate=cost(0, 150 * MIB),
        compiler_params=pltpu.CompilerParams(
            collective_id=1, has_side_effects=True, vmem_limit_bytes=SETTLE_VMEM
        ),
    )(tokens, memory, facts, counts, *weights)


def add_low(left, right):
    return (left.astype(jnp.float32) + right.astype(jnp.float32)).astype(jnp.bfloat16)


def pick(value, index):
    return lax.dynamic_index_in_dim(value, index, 0, keepdims=False)


def tie(*values):
    return lax.optimization_barrier(values)


def settle_kernel(groups, examples, *refs):
    parts, small, info, qkv = refs[:4], refs[4], refs[5], refs[6]
    bias, grads, mixed, level, normed, self_in, tok, grad_rest, gain = refs[7:16]
    result_out, small_out, tok_grad, tok_back = refs[16:20]
    value, first, second, third, small_in, rows_held, placed, grad_placed, result = refs[20:29]
    far_sent, far_found, send, receive, small_send, small_get, load, single = refs[29:37]
    out, leave = refs[37:]
    count = len(parts)
    index, y = lax.axis_index("dp"), lax.axis_index("mp")
    core, x, z = index % 2, (index // 2) % 2, index // 4
    deep = groups // 4
    chunks, rows = first.shape[0], first.shape[3]

    def at(c, yy, xx, zz):
        return (zz * 4 + xx * 2 + c, yy)

    def part(k):
        return pl.ds(pl.multiple_of(k * rows, rows), rows)

    fetch = pltpu.make_async_copy(qkv, rows_held, load.at[count])
    fetch.start()
    loads, starts = [], [0]
    for i, ref in enumerate(parts):
        size = ref.shape[1]
        target = value.at[:, pl.ds(starts[-1], size)]
        loads.append(pltpu.make_async_copy(ref, target, load.at[i]))
        loads[-1].start()
        starts.append(starts[-1] + size)
    partners = [at(1 - core, y, x, z), at(core, 1 - y, x, z), at(1 - core, 1 - y, x, z)]
    partners.append(at(core, y, 1 - x, z))
    for step in range(1, deep):
        partners.append(at(core, y, x, (z + step) % deep))
    barrier = pltpu.get_barrier_semaphore()
    for partner in partners:
        pl.semaphore_signal(barrier, inc=1, device_id=partner, device_id_type=MESH)
    pl.semaphore_wait(barrier, len(partners))

    def copy(source, target, slot, k, device):
        return pltpu.make_async_remote_copy(
            src_ref=source,
            dst_ref=target,
            send_sem=send.at[k, slot],
            recv_sem=receive.at[k, slot],
            device_id=device,
            device_id_type=MESH,
        )

    def quarter(k, q):
        return value.at[pl.ds(q * 8, 8), part(k)]

    def to_core(k):
        return copy(quarter(k, 1 - core), first.at[k, 0], 0, k, at(1 - core, core, x, z))

    def to_turned(k):
        return copy(quarter(k, 1 - core), first.at[k, 1], 1, k, at(1 - core, core, x, z))

    def to_same(k):
        return copy(quarter(k, core), first.at[k, 1], 2, k, at(core, core, x, z))

    def arrived(k, slot):
        return copy(quarter(k, core), first.at[k, 1 if slot else 0], slot, k, at(1 - core, y, x, z))

    def along_x(k):
        return copy(
            first.at[k, 1, pl.ds((1 - x) * 4, 4)], second.at[k], 3, k, at(core, y, 1 - x, z)
        )

    def along_z(k, step):
        far = (z + step) % deep
        return copy(
            second.at[k, far], third.at[k, step - 1], 3 + step, k, at(core, y, x, far)
        )

    def back_z(k, step):
        far = (z + step) % deep
        piece = core * 8 + x * 4 + z
        return copy(
            out.at[piece, part(k)], out.at[piece, part(k)], 6 + step, k, at(core, y, x, far)
        )

    def back_x(k):
        held = out.at[pl.ds(core * 8 + x * 4, 4), part(k)]
        return copy(held, held, 10, k, at(core, y, 1 - x, z))

    def back_core(k):
        held = out.at[pl.ds(core * 8, 8), part(k)]
        return copy(held, held, 11, k, at(1 - core, y, x, z))

    rounds = [at(core, 1 - y, x, z), at(core, y, 1 - x, z)]
    step = 1
    while step < deep:
        rounds.append(at(core, y, x, z + step - 2 * step * ((z // step) % 2)))
        step *= 2
    rounds.append(at(1 - core, y, x, z))
    small_out[0] = small[...]

    def small_copy(i):
        return pltpu.make_async_remote_copy(
            src_ref=small_out.at[0],
            dst_ref=small_in.at[i],
            send_sem=small_send.at[i],
            recv_sem=small_get.at[i],
            device_id=rounds[i],
            device_id_type=MESH,
        )

    def small_wait(i):
        small_copy(i).wait()
        if i < len(rounds) - 1:
            small_out[0] = small_out[0] + small_in[i]
        else:
            small_out[1] = small_in[i]

    def single_copy(i, source, target, device):
        return pltpu.make_async_remote_copy(
            src_ref=source,
            dst_ref=target,
            send_sem=single.at[i, 0],
            recv_sem=single.at[i, 1],
            device_id=device,
            device_id_type=MESH,
        )

    far_copy = single_copy(0, far_sent, far_found, at(1 - core, y, x, z))
    turn_copy = single_copy(1, tok_grad, tok_back, at(1 - core, 1 - y, x, z))
    width = tok.shape[1]

    def attend(pair):
        size = placed.shape[1]
        half = size // 2
        columns = slice(384 * pair, 384 * (pair + 1))
        near = pl.ds(pl.multiple_of(core * half, half), half)
        away = pl.ds(pl.multiple_of((1 - core) * half, half), half)
        slopes = jnp.concatenate(
            [toeplitz(bias[pair, head : head + 1, :], size) for head in range(2)], axis=1
        )
        sums = None
        for example in range(examples):
            held = slice(half * example, half * (example + 1))
            placed[example, near, :] = rows_held[0, held, columns]
            placed[example, away, :] = rows_held[1, held, columns]
            grad_placed[example, near, :] = grads[0, held, 128 * pair : 128 * (pair + 1)]
            grad_placed[example, away, :] = grads[1, held, 128 * pair : 128 * (pair + 1)]
            joined, grad = placed[example], grad_placed[example]
            query, keys, values = joined[:, :128], joined[:, 128:256], joined[:, 256:]
            products = grad.astype(jnp.float32).T * mixed[pair, example]
            inner = jnp.concatenate(
                [jnp.sum(head_rows(products, head), axis=0, keepdims=True) for head in range(2)],
                axis=1,
            )
            levels = jnp.concatenate(
                [level[pair, example, 0:1, :], level[pair, example, 1:2, :]], axis=1
            )
            mask = self_masks(size, info[example])
            heads, grad_heads = side_by_side(query), side_by_side(grad)
            scores = nt(keys, heads) + slopes + jnp.concatenate([mask, mask], axis=1)
            probs = jnp.exp(scores - levels)
            grad_scores = (probs * (nt(values, grad_heads) - inner)).astype(jnp.bfloat16)
            square = grad_scores.astype(jnp.float32)
            sums = square if sums is None else sums + square
            result[example] = jnp.concatenate(
                [
                    heads_joined(*own_blocks(nn(keys.T, grad_scores), size)),
                    nn(grad_scores, heads),
                    nn(probs.astype(jnp.bfloat16), grad_heads),
                ],
                axis=1,
            ).astype(jnp.bfloat16)
            rows_held[0, held, columns] = result[example, near, :]
            rows_held[1, held, columns] = result[example, away, :]
        for head in range(2):
            at_column = 512 * (pair % 2) + 256 * head
            small_out[0, 4 + pair // 2 : 5 + pair // 2, at_column : at_column + size] = diagonals(
                sums[:, size * head : size * (head + 1)]
            )
        both_rows = rows_held[:, :, columns].reshape(-1, 384)
        piece = tn(both_rows, normed[...].reshape(-1, width)).astype(jnp.bfloat16)
        value[4 * pair : 4 * pair + 4, starts[count] :, :] = piece.reshape(4, 96, width)

    def heads_sent():
        lax.fori_loop(starts[count] // rows, chunks, start, 0)
        far_sent[...] = nt(rows_held[1], self_in[...]).astype(jnp.bfloat16)
        far_copy.start()

    def tokens_done():
        far_copy.wait()
        back = nt(rows_held[0], self_in[...]) + far_found[...].astype(jnp.float32)
        held = tok[...].astype(jnp.float32)
        size = lax.rsqrt(jnp.mean(held * held, axis=-1, keepdims=True) + epsilon)
        small_out[0, 0:1, :] = jnp.sum(back * held * size, axis=0, keepdims=True)
        back = back * gain[...]
        inner = jnp.mean(back * held, axis=-1, keepdims=True)
        back = back * size - held * (size * size * size * inner)
        tok_grad[...] = (grad_rest[...] + back).astype(jnp.bfloat16)
        small_copy(0).start()

        @pl.when(core != y)
        def _():
            turn_copy.start()

    def start(k, carry):
        @pl.when(core == y)
        def _():
            to_core(k).start()

        @pl.when(core != y)
        def _():
            to_same(k).start()
            to_turned(k).start()

        return carry

    for i in range(count):
        loads[i].wait()
        lax.fori_loop(starts[i] // rows, starts[i + 1] // rows, start, 0)
    fetch.wait()

    def total(left, right):
        return (left.astype(jnp.float32) + right.astype(jnp.float32)).astype(jnp.bfloat16)

    pairs = bias.shape[0]
    work = [functools.partial(attend, pair) for pair in range(pairs)] + [heads_sent, tokens_done]

    def leaving(k):
        return pltpu.make_async_copy(out.at[:, part(k)], result_out.at[:, part(k)], leave.at[k])

    def tick(t, carry):
        for i, piece_of_work in enumerate(work):
            pl.when(t == i)(piece_of_work)
        for i in range(len(rounds) - 1):

            @pl.when(t == chunks + 1 + i)
            def _():
                small_wait(i)
                small_copy(i + 1).start()

        @pl.when(t < chunks)
        def _():
            k = jnp.minimum(t, chunks - 1)

            @pl.when(core == y)
            def _():
                arrived(k, 2).wait_recv()

                def add(i, c):
                    first[k, 1, i] = total(value[core * 8 + i, part(k)], first[k, 1, i])
                    return c

                lax.fori_loop(0, 8, add, 0)

            @pl.when(core != y)
            def _():
                arrived(k, 0).wait_recv()
                arrived(k, 1).wait_recv()

                def add(i, c):
                    first[k, 1, i] = total(first[k, 0, i], first[k, 1, i])
                    return c

                lax.fori_loop(0, 8, add, 0)

            along_x(k).start()

        @pl.when((t >= 1) & (t < chunks + 1))
        def _():
            k = t - 1
            along_x(k).wait_recv()

            def add(i, c):
                second[k, i] = total(first[k, 1, x * 4 + i], second[k, i])
                return c

            lax.fori_loop(0, deep, add, 0)
            for step in range(1, deep):
                along_z(k, step).start()

        @pl.when((t >= 2) & (t < chunks + 2))
        def _():
            k = t - 2
            for step in range(1, deep):
                along_z(k, step).wait_recv()
            summed = second[k, z].astype(jnp.float32)
            for step in range(1, deep):
                summed = summed + third[k, step - 1].astype(jnp.float32)
            out[core * 8 + x * 4 + z, part(k)] = summed.astype(jnp.bfloat16)
            for step in range(1, deep):
                back_z(k, step).start()

        @pl.when((t >= 3) & (t < chunks + 3))
        def _():
            k = t - 3
            for step in range(1, deep):
                back_z(k, step).wait_recv()
            back_x(k).start()

        @pl.when((t >= 4) & (t < chunks + 4))
        def _():
            k = t - 4
            back_x(k).wait_recv()
            back_core(k).start()

        @pl.when(t >= 5)
        def _():
            back_core(t - 5).wait_recv()
            leaving(t - 5).start()

        return carry

    lax.fori_loop(0, chunks + 5, tick, 0)
    small_wait(len(rounds) - 1)

    @pl.when(core != y)
    def _():
        turn_copy.wait()


    def finish_sends(k, carry):
        @pl.when(core == y)
        def _():
            to_core(k).wait_send()

        @pl.when(core != y)
        def _():
            to_same(k).wait_send()
            to_turned(k).wait_send()

        along_x(k).wait_send()
        for step in range(1, deep):
            along_z(k, step).wait_send()
            back_z(k, step).wait_send()
        back_x(k).wait_send()
        back_core(k).wait_send()
        leaving(k).wait()
        return carry

    lax.fori_loop(0, chunks, finish_sends, 0)


def settle(parts, small, info, attention, rows_in, groups, examples):
    qkv, bias, grads, mixed, level = attention
    normed, self_in, tok, grad_rest, gain = rows_in
    count, _, width = parts[0].shape
    kind = parts[0].dtype
    rows = sum(part.shape[1] for part in parts) + qkv.shape[2] // count
    chunk = 16
    chunks = rows // chunk
    deep = groups // 4
    rounds = 3 + deep.bit_length() - 1
    size = 2 * qkv.shape[1] // examples
    whole = pl.BlockSpec(memory_space=pltpu.VMEM)
    anywhere = pl.BlockSpec(memory_space=pl.ANY)
    return pl.pallas_call(
        functools.partial(settle_kernel, groups, examples),
        in_specs=[anywhere] * len(parts) + [whole, SMEM_SPEC, anywhere] + [whole] * 9,
        out_specs=[anywhere] + [whole] * 3,
        out_shape=[
            jax.ShapeDtypeStruct((count, rows, width), kind),
            jax.ShapeDtypeStruct((2,) + small.shape, small.dtype),
            jax.ShapeDtypeStruct(tok.shape, tok.dtype),
            jax.ShapeDtypeStruct(tok.shape, tok.dtype),
        ],
        scratch_shapes=[
            pltpu.VMEM((count, rows, width), kind),
            pltpu.VMEM((chunks, 2, count // 2, chunk, width), kind),
            pltpu.VMEM((chunks, deep, chunk, width), kind),
            pltpu.VMEM((chunks, deep - 1, chunk, width), kind),
            pltpu.VMEM((rounds,) + small.shape, small.dtype),
            pltpu.VMEM(qkv.shape, kind),
            pltpu.VMEM((examples, size, 384), kind),
            pltpu.VMEM((examples, size, 128), kind),
            pltpu.VMEM((examples, size, 384), kind),
            pltpu.VMEM(tok.shape, kind),
            pltpu.VMEM(tok.shape, kind),
            pltpu.SemaphoreType.DMA((chunks, 12)),
            pltpu.SemaphoreType.DMA((chunks, 12)),
            pltpu.SemaphoreType.DMA((rounds,)),
            pltpu.SemaphoreType.DMA((rounds,)),
            pltpu.SemaphoreType.DMA((len(parts) + 1,)),
            pltpu.SemaphoreType.DMA((2, 2)),
            pltpu.VMEM((count, rows, width), kind),
            pltpu.SemaphoreType.DMA((chunks,)),
        ],
        cost_estimate=cost(0, 60 * count * rows * width),
        compiler_params=pltpu.CompilerParams(
            collective_id=0, has_side_effects=True, vmem_limit_bytes=62 * MIB
        ),
    )(*parts, small, info, qkv, bias, grads, mixed, level, normed, self_in, tok, grad_rest, gain)


def unpack_kernel(pairs, source, key, val, cross_out, self_out, cross_q, *self_in):
    wide = key.shape[0] // 4
    thin = cross_out.shape[0] // 4

    def taken(row, rows):
        block = source[:, row : row + rows, :].astype(jnp.float32)
        return block.reshape(4 * rows, block.shape[2])

    kv = taken(0, wide)
    for i in range(pairs):
        key[:, 128 * i : 128 * i + 128] = kv[:, 256 * i : 256 * i + 128]
        val[:, 128 * i : 128 * i + 128] = kv[:, 256 * i + 128 : 256 * i + 256]
    cross_out[...] = taken(wide, thin)
    self_out[...] = taken(wide + thin, thin)
    cross_q[...] = taken(wide + 2 * thin, thin).T
    rest = taken(wide + 3 * thin, 3 * thin)
    for i in range(3):
        self_in[i][...] = rest[4 * thin * i : 4 * thin * (i + 1)].T


def unpack(value, inner):
    count, rows, width = value.shape
    tall = jax.ShapeDtypeStruct((width, inner), jnp.float32)
    flat = jax.ShapeDtypeStruct((inner, width), jnp.float32)
    by_row = pl.BlockSpec((width // 4, inner), lambda i: (i, 0))
    by_out = pl.BlockSpec((inner // 4, width), lambda i: (i, 0))
    by_column = pl.BlockSpec((width, inner // 4), lambda i: (0, i))
    return pl.pallas_call(
        functools.partial(unpack_kernel, inner // 128),
        grid=(4,),
        in_specs=[pl.BlockSpec((4, rows, width), lambda i: (i, 0, 0))],
        out_specs=[by_row, by_row, by_out, by_out] + [by_column] * 4,
        out_shape=[tall, tall, flat, flat] + [tall] * 4,
        cost_estimate=cost(0, 6 * value.size),
        compiler_params=pltpu.CompilerParams(vmem_limit_bytes=58 * MIB),
    )(value)


def widen_kernel(first, second, out_first, out_second):
    out_first[...] = first[...].astype(jnp.float32)
    out_second[...] = second[...].astype(jnp.float32).T


def widen(value):
    rows, width = value.shape[0] // 2, value.shape[1]
    steps = 4
    block = rows // steps
    return pl.pallas_call(
        widen_kernel,
        grid=(steps,),
        in_specs=[
            pl.BlockSpec((block, width), lambda i: (i, 0)),
            pl.BlockSpec((block, width), lambda i: (steps + i, 0)),
        ],
        out_specs=[
            pl.BlockSpec((block, width), lambda i: (i, 0)),
            pl.BlockSpec((width, block), lambda i: (0, i)),
        ],
        out_shape=[
            jax.ShapeDtypeStruct((rows, width), jnp.float32),
            jax.ShapeDtypeStruct((width, rows), jnp.float32),
        ],
        cost_estimate=cost(0, 12 * rows * width),
        compiler_params=pltpu.CompilerParams(vmem_limit_bytes=58 * MIB),
    )(value, value)


def pieces(value):
    return value.reshape(16, value.shape[0] // 16, value.shape[1])


def low(value):
    return value.astype(jnp.bfloat16)


def on_chip_group(
    tokens,
    memory,
    cotangent,
    target_lengths,
    memory_lengths,
    norm_self,
    query_self,
    key_self,
    value_self,
    out_self,
    bias_table,
    norm_cross,
    query_cross,
    key_cross,
    value_cross,
    out_cross,
    norm_ffn,
    ffn_in,
    ffn_out,
):
    examples = target_lengths.shape[0]
    groups = lax.axis_size("dp")
    net = links(groups)
    index = lax.axis_index("dp")
    place = {
        "y": lax.axis_index("mp"),
        "core": index & 1,
        "x": (index >> 1) & 1,
        "zl": (index >> 2) & 1,
        "zh": (index >> 3) & 1,
    }
    core = place["core"]
    settled = (core == place["y"]).astype(jnp.int32)
    place["settled"] = settled[None]
    rows, width = tokens.shape
    half_pos = rows // examples
    inner = query_self.shape[1]
    pairs = inner // 128

    def swap(value):
        return permute(value, net["core"])

    def both(value):
        return jnp.stack([value, swap(value)])

    def flat(value):
        return value.reshape(-1, value.shape[2])

    def turn(value):
        return permute(value, net["turn"])

    lengths = jnp.concatenate([target_lengths, memory_lengths]).astype(jnp.float32)
    table_rows = bias_table.astype(jnp.float32).reshape(-1, 128)
    facts = jnp.concatenate(
        [jnp.pad(lengths, (0, 128 - lengths.size))[None], table_rows], axis=0
    )
    facts = jnp.pad(facts, ((0, 8 - facts.shape[0]), (0, 0)))
    counts = jnp.broadcast_to(jnp.sum(target_lengths).astype(jnp.float32), (8, 128))
    mem_near = permute(memory, net["give"])
    held = gather(
        tokens,
        memory,
        facts,
        counts,
        [query_self, key_self, value_self, query_cross, key_cross, value_cross, out_self, out_cross],
        groups,
        examples,
    )
    tok, mem_first, facts, counts, self_in, cross_q, cross_kv = held[:7]
    self_out, cross_out = held[7:]
    tok = tok.reshape(rows, width)
    target_len = facts[0, :examples].astype(jnp.int32)
    memory_len = facts[0, examples : 2 * examples].astype(jnp.int32)
    table = facts[1 : 1 + table_rows.shape[0]].reshape(bias_table.shape)
    group_count = jnp.sum(target_len).astype(jnp.float32)
    token_scale = groups * group_count / counts[0, 0]
    self_info = jnp.concatenate([core[None], target_len])
    mem_sent, tok = tie(memory[mem_first.shape[0] :], tok)
    mem_rest = turn(mem_sent)
    first_far = permute(mem_first, net["take"])

    span = 2 * half_pos
    distance = jnp.arange(span, dtype=jnp.int32)
    level = jnp.sum(
        (distance[:, None] >= jnp.asarray(bucket_edges())[None, :]).astype(jnp.int32), axis=-1
    )
    level_hot = (level[:, None] == jnp.arange(BUCKETS, dtype=jnp.int32)[None, :]).astype(
        jnp.float32
    )
    bias = jnp.einsum("db,bh->hd", level_hot, table, precision=highest).reshape(-1, 2, span)

    tok_float = tok.astype(jnp.float32)
    n1 = both(low(rms_norm(tok_float, norm_self.astype(jnp.float32))))
    qkv = low(nn(flat(n1), self_in)).reshape(2, rows, -1)
    cot_after, qkv = tie(cotangent, qkv)
    cot_raw = turn(cot_after)
    a1, mixed_one, level_one = self_forward(self_info, qkv, bias, examples)
    r1 = tok_float + (nn(a1[0], self_out) + swap(low(nn(a1[1], self_out))).astype(jnp.float32))

    n2 = low(rms_norm(r1, norm_cross.astype(jnp.float32)))
    mem_rest, n2 = tie(mem_rest, n2)
    n2 = both(n2)
    q2 = low(nn(flat(n2), cross_q)).reshape(2, rows, -1)
    rest_far = permute(mem_rest, net["take"])
    mem, kv = memory_rows(
        place["y"],
        settled,
        [mem_near, memory, mem_first, first_far, mem_rest, rest_far],
        cross_kv,
        examples,
    )
    mem = mem.reshape(2, -1, width)
    kv = kv.reshape(2, -1, 2 * inner)
    kv, cot_raw = tie(kv, cot_raw)
    cot = reorder(False, cotangent, cot_raw, place["settled"], examples)
    positions = core * half_pos + jnp.arange(half_pos, dtype=jnp.int32)
    live = (positions[None, :] < target_len[:, None]).astype(jnp.float32).reshape(rows, 1)
    dy = cot.astype(jnp.float32) * live * token_scale
    gy = low(dy)
    gy_far = permute(gy, net["y"])

    a2, mixed_two, level_two = cross_forward(memory_len, q2, kv, examples)
    a2, gy_far = tie(a2, gy_far)
    r2 = r1 + (nn(a2[0], cross_out) + swap(low(nn(a2[1], cross_out))).astype(jnp.float32))

    n3 = low(rms_norm(r2, norm_ffn.astype(jnp.float32)))
    n3_far = permute(n3, net["y"])
    out_own, dn_own, h_own, p_own = ffn_rows(n3, gy, ffn_in, ffn_out, jnp.float32)
    out_own, n3_far = tie(out_own, n3_far)
    out_far, dn_far, h_far, p_far = ffn_rows(n3_far, gy_far, ffn_in, ffn_out, jnp.bfloat16)
    dn_far = permute(dn_far, net["y"])
    ffn_part = ffn_weights((n3, n3_far), (gy, gy_far), (h_own, h_far), (p_own, p_far))
    dn_far, ffn_part = tie(dn_far, ffn_part)
    ffn_piece = lax.psum_scatter(ffn_part, "dp", scatter_dimension=0, tiled=True)
    dn3 = dn_own + dn_far.astype(jnp.float32)
    back, gain_three = norm_backward(r2, norm_ffn, dn3)
    dr2 = dy + back

    g2 = both(low(dr2))
    da2 = low(nt(flat(g2), cross_out)).reshape(2, rows, -1)
    da2, out_far = tie(da2, out_far)
    out_far = permute(out_far, net["y"])
    dq2, dkv = cross_backward(memory_len, q2, kv, da2, mixed_two, level_two, examples)
    dkv, out_far = tie(dkv, out_far)
    block_out = low(r2 + (out_own + out_far.astype(jnp.float32)))
    block_back = turn(block_out)
    dkv_swapped = swap(low(nt(pick(dkv, 1 - core), cross_kv)))
    cross_kv_part = low(tn(flat(mem), flat(dkv)))
    dkv_swapped, cross_kv_part = tie(dkv_swapped, cross_kv_part)
    memory_grad = low(nt(pick(dkv, core), cross_kv) + dkv_swapped.astype(jnp.float32))
    memory_grad, cross_kv_part, dq2 = tie(memory_grad, cross_kv_part, dq2)
    half = memory_grad.shape[0] // 2
    memory_back, memory_late = turn(memory_grad[:half]), turn(memory_grad[half:])
    dn2 = nt(dq2[0], cross_q) + swap(low(nt(dq2[1], cross_q))).astype(jnp.float32)
    back, gain_two = norm_backward(r1, norm_cross, dn2)
    dr1 = dr2 + back
    cross_out_part = low(tn(flat(a2), flat(g2)))
    cross_q_part = low(tn(flat(dq2), flat(n2)))

    g1 = both(low(dr1))
    self_out_part = low(tn(flat(a1), flat(g1)))
    da1 = low(nt(flat(g1), self_out)).reshape(2, rows, -1)
    head_parts = [cross_kv_part, cross_out_part, self_out_part, cross_q_part]
    head_parts = [pieces(part) for part in head_parts]
    zero = jnp.zeros((1, width), jnp.float32)
    small = jnp.concatenate([zero, gain_two[None], gain_three[None], jnp.tile(zero, (5, 1))])
    da1, head_parts, small, ffn_piece, block_back, memory_back = tie(
        da1, head_parts, small, ffn_piece, block_back, memory_back
    )
    ffn_whole = lax.all_gather(ffn_piece, "dp", axis=0, tiled=True)

    heads_done, small, tokens_grad, tokens_back = settle(
        head_parts,
        small,
        target_len,
        (qkv, bias, da1, mixed_one, level_one),
        (n1, self_in, tok, dr1, norm_self.astype(jnp.float32)[None]),
        groups,
        examples,
    )
    small, ffn_whole, block_back, memory_late = tie(small, ffn_whole, block_back, memory_late)
    memory_back = (memory_back, memory_late)
    gains = small[0, :3] + small[1, :3]
    by_distance = jnp.where(settled == 1, small[0, 4:6], small[1, 4:6]).reshape(-1, span)
    bias_grad = jnp.einsum("hd,db->bh", by_distance, level_hot, precision=highest)
    block_out = reorder(True, block_out, block_back, place["settled"], examples)
    tokens_grad = reorder(True, tokens_grad, tokens_back, place["settled"], examples)
    memory_grad = reorder(True, memory_grad, memory_back, place["settled"], examples)

    ffn_out_grad, ffn_in_grad = widen(ffn_whole)
    (
        key_cross_grad,
        value_cross_grad,
        out_cross_grad,
        out_self_grad,
        query_cross_grad,
        query_self_grad,
        key_self_grad,
        value_self_grad,
    ) = unpack(heads_done, inner)
    return (
        block_out,
        tokens_grad,
        memory_grad,
        gains[0],
        query_self_grad,
        key_self_grad,
        value_self_grad,
        out_self_grad,
        bias_grad,
        gains[1],
        query_cross_grad,
        key_cross_grad,
        value_cross_grad,
        out_cross_grad,
        gains[2],
        ffn_in_grad,
        ffn_out_grad,
    )


def solution(mesh):
    placed = (
        P(("dp", "mp"), None),
        P(("dp", "mp"), None),
        P(("dp", "mp"), None),
        P("dp"),
        P("dp"),
        P(),
        P(None, "mp"),
        P(None, "mp"),
        P(None, "mp"),
        P("mp", None),
        P(None, "mp"),
        P(),
        P(None, "mp"),
        P(None, "mp"),
        P(None, "mp"),
        P("mp", None),
        P(),
        P(None, "mp"),
        P("mp", None),
    )
    near = mesh.shape["mp"] == 2 and mesh.shape["dp"] == 16
    return jax.shard_map(
        on_chip_group if near else on_device,
        mesh=mesh,
        in_specs=placed,
        out_specs=(
            P(("dp", "mp"), None),
            P(("dp", "mp"), None),
            P(("dp", "mp"), None),
            P(),
            P(None, "mp"),
            P(None, "mp"),
            P(None, "mp"),
            P("mp", None),
            P(None, "mp"),
            P(),
            P(None, "mp"),
            P(None, "mp"),
            P(None, "mp"),
            P("mp", None),
            P(),
            P(None, "mp"),
            P("mp", None),
        ),
        check_vma=False,
    )
```
